128 devices in a mesh: seq: 32 (over y_lo, z, x), head: 4 (over y_hi, core).
Axes of the slice: x: 4, y: 4 (y_hi: 2, y_lo: 2; y = y_hi * 2 + y_lo), z: 4, core: 2. Of those that a mesh axis runs over, the one named last changes fastest.
Arguments:
- queries: bfloat16 [8192, 1536], P('seq', 'head'), may hold values from -6 to 6
- keys: bfloat16 [8192, 1536], P('seq', 'head'), may hold values from -6 to 6
- values: bfloat16 [8192, 1536], P('seq', 'head'), may hold values from -6 to 6
- text_keys: bfloat16 [512, 1536], P('seq', 'head'), may hold values from -6 to 6
- text_values: bfloat16 [512, 1536], P('seq', 'head'), may hold values from -6 to 6
- head_bias: float32 [12], P('head'), may hold values from 2 to 4
- out_weight: bfloat16 [1536, 3072], P('head'), may hold values from -0.15625 to 0.15625
- grad_out: bfloat16 [8192, 3072], P('seq', 'head'), may hold values from -6 to 6
- clip_lengths: int32 [4], replicated, may hold values from 1 to 4096, 8192 in all
- tile_mask: int32 [128, 128], replicated, may hold values 0 or 1
- caption_order: int32 [512], replicated, may hold values from 0 to 511, each once
Outputs:
- out: bfloat16 [8192, 3072], P('seq', 'head')
- grad_queries: bfloat16 [8192, 1536], P('seq', 'head')
- grad_keys: bfloat16 [8192, 1536], P('seq', 'head')
- grad_values: bfloat16 [8192, 1536], P('seq', 'head')
- grad_text_keys: bfloat16 [512, 1536], P('seq', 'head')
- grad_text_values: bfloat16 [512, 1536], P('seq', 'head')
The draws below stay inside these ranges and needn't reach their ends.
Inputs may be any that keep to these rules, and one draw needn't show every extreme that they name: `clip_lengths`: the 4 clip lengths sum to 8192, and the longest clip has exactly 4096 tokens. `tile_mask`: 0/1 entries. Each caption row appears once; clip c's caption is the rows caption_order[c * 128] to caption_order[(c + 1) * 128 - 1].
All inputs are finite; a program needn't handle non-finite values.
Results may differ from the reference program's by a relative error of at most 0.015.
Values may be sent and summed in bfloat16 or wider, within the bound.
A program may use at most 192 MiB of HBM per device.

```python
import math
import jax
import jax.numpy as jnp
import numpy as np
from jax import lax

D = 3072
HD = 128
HEADS = 12
NCLIP = 4
TILE = 64
TOKENS = 8192
TEXT = 512
CAP = 128
NT = 128


def touch_ends(drawn, rng, least, top_value):
    longest = drawn.shape.index(max(drawn.shape))
    spots = []
    for shift in (0, 1):
        where = [jax.random.randint(jax.random.fold_in(rng, axis), (), 0, length) for axis, length in enumerate(drawn.shape)]
        where[longest] = (where[longest] + shift) % drawn.shape[longest]
        spots.append(tuple(where))
    return drawn.at[spots[0]].set(least).at[spots[1]].set(top_value)


def steps_of(key, extent, cuts, least, largest):
    gain, own = 1.0, jax.random.fold_in(key, 6)
    for axis_at, shards_of in cuts:
        steps = jnp.exp(jax.random.uniform(jax.random.fold_in(own, axis_at), (shards_of,), jnp.float32, least / len(cuts), largest / len(cuts)))
        gain = gain * jnp.repeat(steps, extent[axis_at] // shards_of).reshape([-1 if axis == axis_at else 1 for axis in range(len(extent))])
    return gain


def split_up(amount, total, bound, slope):
    weights = [(1 << 20) // math.isqrt(rank ** slope) + 1 for rank in range(2, amount + 1)]
    rest, counts = total - bound - (amount - 1), [1] * (amount - 1)
    while rest > 0:
        candidates = [i for i in range(amount - 1) if counts[i] < bound]
        pool, remaining = sum([weights[i] for i in candidates]), rest
        for i in candidates:
            extra = min(bound - counts[i], max(1, remaining * weights[i] // pool), rest)
            counts[i] = counts[i] + extra
            rest = rest - extra
    return np.array([bound] + counts)


def uneven(rng, count, total, bound, skew):
    if count == 2:
        one = jax.random.randint(rng, (), max(1, total - bound), min(bound, total - 1) + 1)
        return jnp.stack([one, total - one])
    sizes = jnp.asarray(split_up(count, total, bound, skew), jnp.int32)
    twos = (count - 1) // 2
    donor, taker = sizes[1:1 + 2 * twos:2], sizes[2:2 + 2 * twos:2]
    margin = jnp.minimum(donor - 1, bound - taker)
    passed = jax.random.randint(jax.random.fold_in(rng, 1), (twos,), 0, 1 << 20) % (margin + 1)
    sizes = sizes.at[1:1 + 2 * twos:2].set(donor - passed).at[2:2 + 2 * twos:2].set(taker + passed)
    return sizes[jax.random.permutation(jax.random.fold_in(rng, 2), count)]


def noise(own_key, dims, deviation, reach, cuts=(), kind=jnp.bfloat16):
    level = steps_of(own_key, dims, cuts, -0.22, 0.18) if cuts else 1.0
    drawn = jax.random.normal(own_key, dims, jnp.float32) * deviation * level
    return jnp.minimum(jnp.maximum(drawn, -reach), reach).astype(kind)


def setup_inputs(seed: int = 0) -> dict:
    key_list = jax.random.split(jax.random.key(seed), 12)
    queries = noise(key_list[0], (TOKENS, HEADS * HD), 1.0, 6.0, ((0, 32), (1, 4)))
    keys = noise(key_list[1], (TOKENS, HEADS * HD), 1.0, 6.0, ((0, 32), (1, 4)))
    values = noise(key_list[2], (TOKENS, HEADS * HD), 1.0, 6.0, ((0, 32), (1, 4)))
    text_keys = noise(key_list[3], (TEXT, HEADS * HD), 1.0, 6.0, ((0, 32), (1, 4)))
    text_values = noise(key_list[4], (TEXT, HEADS * HD), 1.0, 6.0, ((0, 32), (1, 4)))
    head_bias = jnp.clip(2.0 + 2.0 * jax.random.uniform(key_list[5], (HEADS,), jnp.float32) ** steps_of(key_list[5], (HEADS,), ((0, 4),), -0.2, 0.2), 2.0, 4.0)
    out_weight = noise(key_list[6], (HEADS * HD, D), (HEADS * HD) ** -0.5, 0.15625, ((0, 4),))
    grad_out = noise(key_list[7], (TOKENS, D), 1.0, 6.0, ((0, 32), (1, 4)))
    clip_lengths = uneven(key_list[8], NCLIP, TOKENS, TOKENS // 2, 2).astype(jnp.int32)
    tile_mask = touch_ends((jax.random.randint(key_list[9], (NT, NT), 0, 2) < 1).astype(jnp.int32), jax.random.fold_in(key_list[9], 1), 0, 1)
    caption_order = jax.random.permutation(key_list[10], TEXT).astype(jnp.int32)
    return {"queries": queries, "keys": keys, "values": values, "text_keys": text_keys, "text_values": text_values, "head_bias": head_bias, "out_weight": out_weight, "grad_out": grad_out, "clip_lengths": clip_lengths, "tile_mask": tile_mask, "caption_order": caption_order}


def reference(queries, keys, values, text_keys, text_values, head_bias, out_weight, grad_out, clip_lengths, tile_mask, caption_order):
    factor = HD ** -0.5
    block = math.gcd(TOKENS, 512)
    position = jnp.arange(TOKENS, dtype=jnp.int32)
    clip_ends = jnp.cumsum(clip_lengths).astype(jnp.int32)
    clip_of = jnp.sum((position[:, None] >= clip_ends[None, :]).astype(jnp.int32), axis=1)
    caption_clip = jnp.zeros((TEXT,), jnp.int32).at[caption_order].set(jnp.arange(TEXT, dtype=jnp.int32) // CAP)
    tile_of = position // TILE
    tile_index = jnp.arange(NT, dtype=jnp.int32)
    tile_on = (tile_mask > 0) | (tile_index[:, None] == tile_index[None, :])
    offset = jnp.log((clip_lengths[clip_of] + CAP).astype(jnp.float32))
    grad_attn = jnp.dot(grad_out, out_weight.T, preferred_element_type=jnp.float32).astype(jnp.bfloat16)
    query_all = queries.astype(jnp.float32).reshape(TOKENS, HEADS, HD)
    key_all = keys.astype(jnp.float32).reshape(TOKENS, HEADS, HD)
    value_all = values.astype(jnp.float32).reshape(TOKENS, HEADS, HD)
    text_key_all = text_keys.astype(jnp.float32).reshape(TEXT, HEADS, HD)
    text_value_all = text_values.astype(jnp.float32).reshape(TEXT, HEADS, HD)
    grad_all = grad_attn.astype(jnp.float32).reshape(TOKENS, HEADS, HD)
    bias_column = head_bias[:, None, None]

    def visit(running, index):
        first_row = index * block
        query_block = lax.dynamic_slice_in_dim(query_all, first_row, block, 0)
        grad_block = lax.dynamic_slice_in_dim(grad_all, first_row, block, 0)
        clip_block = lax.dynamic_slice_in_dim(clip_of, first_row, block, 0)
        tile_block = lax.dynamic_slice_in_dim(tile_of, first_row, block, 0)
        offset_block = lax.dynamic_slice_in_dim(offset, first_row, block, 0)
        keep_pairs = (clip_block[:, None] == clip_of[None, :]) & tile_on[tile_block[:, None], tile_of[None, :]]
        keep_text = clip_block[:, None] == caption_clip[None, :]

        def attend(key_set, value_set, keep_set):
            scores = jnp.einsum("qhd,khd->hqk", query_block, key_set) * factor + bias_column - offset_block[None, :, None]
            weights = jnp.where(keep_set[None], jax.nn.sigmoid(scores), 0.0)
            rounded = lax.optimization_barrier(weights.astype(jnp.bfloat16)).astype(jnp.float32)
            product = jnp.einsum("qhd,khd->hqk", grad_block, value_set)
            slopes = jnp.where(keep_set[None], product * weights * (1.0 - weights), 0.0)
            slopes = lax.optimization_barrier(slopes.astype(jnp.bfloat16)).astype(jnp.float32)
            return rounded, slopes

        weights, slopes = attend(key_all, value_all, keep_pairs)
        text_weights, text_slopes = attend(text_key_all, text_value_all, keep_text)
        attn_block = jnp.einsum("hqk,khd->qhd", weights, value_all) + jnp.einsum("hqk,khd->qhd", text_weights, text_value_all)
        query_grad = (jnp.einsum("hqk,khd->qhd", slopes, key_all) + jnp.einsum("hqk,khd->qhd", text_slopes, text_key_all)) * factor
        key_acc, value_acc, text_key_acc, text_value_acc = running
        key_acc = key_acc + jnp.einsum("hqk,qhd->khd", slopes, query_block)
        value_acc = value_acc + jnp.einsum("hqk,qhd->khd", weights, grad_block)
        text_key_acc = text_key_acc + jnp.einsum("hqk,qhd->khd", text_slopes, query_block)
        text_value_acc = text_value_acc + jnp.einsum("hqk,qhd->khd", text_weights, grad_block)
        return (key_acc, value_acc, text_key_acc, text_value_acc), (attn_block.astype(jnp.bfloat16), query_grad.astype(jnp.bfloat16))

    token_zeros = jnp.zeros((TOKENS, HEADS, HD), jnp.float32)
    text_zeros = jnp.zeros((TEXT, HEADS, HD), jnp.float32)
    sums, blocks = lax.scan(visit, (token_zeros, token_zeros, text_zeros, text_zeros), jnp.arange(TOKENS // block, dtype=jnp.int32))
    attn = blocks[0].reshape(TOKENS, HEADS * HD)
    out = jnp.dot(attn, out_weight, preferred_element_type=jnp.float32).astype(jnp.bfloat16)
    grad_queries = blocks[1].reshape(TOKENS, HEADS * HD)
    grad_keys = (sums[0] * factor).astype(jnp.bfloat16).reshape(TOKENS, HEADS * HD)
    grad_values = sums[1].astype(jnp.bfloat16).reshape(TOKENS, HEADS * HD)
    grad_text_keys = (sums[2] * factor).astype(jnp.bfloat16).reshape(TEXT, HEADS * HD)
    grad_text_values = sums[3].astype(jnp.bfloat16).reshape(TEXT, HEADS * HD)
    return (out, grad_queries, grad_keys, grad_values, grad_text_keys, grad_text_values)
```

```python
import functools

import jax
import jax.numpy as jnp
from jax import lax
from jax.experimental import pallas as pl
from jax.experimental.pallas import tpu as pltpu
from jax.sharding import PartitionSpec as P

MESH = pl.DeviceIdType.MESH
BF = jnp.bfloat16
F32 = jnp.float32

NX, NZ, NY = 4, 4, 2
HS = 128
NH = 3
TR = 256
CR = 16
BR = TR + CR
HALF = TR // 2
CLIPS = 4
CAP = 128
TILE = 64
LAT = NY * NX * TR
ROWS = NY * NX * BR
MASKED = -32768.0
VMEM_LIMIT = 48 * 1024 * 1024


def place():
    seq = lax.axis_index("seq")
    head = lax.axis_index("head")
    y = seq // (NZ * NX)
    z = (seq // NX) % NZ
    x = seq % NX
    return seq, head, y, z, x


def peers(seq, head, y, z, x):
    def at(yy, zz, xx):
        return (yy * NZ + zz) * NX + xx

    other_head = (head + 2) % 4
    core_head = head + 1 - 2 * (head % 2)
    return {
        "pair": (at(1 - y, z, x), head),
        "back": (at(1 - y, z, x), other_head),
        "core": (seq, core_head),
        "right": (at(y, z, (x + 1) % NX), head),
        "left": (at(y, z, (x + NX - 1) % NX), head),
        "up": (at(y, (z + 1) % NZ, x), head),
        "down": (at(y, (z + NZ - 1) % NZ, x), head),
    }


def greet(peer):
    barrier = pltpu.get_barrier_semaphore()
    for device in peer.values():
        pl.semaphore_signal(barrier, inc=1, device_id=device, device_id_type=MESH)
    pl.semaphore_wait(barrier, len(peer))


def sender(peer, send_sem, recv_sem, sent):
    def send(n, src, dst, to):
        copy = pltpu.make_async_remote_copy(
            src_ref=src,
            dst_ref=dst,
            send_sem=send_sem.at[n],
            recv_sem=recv_sem.at[n],
            device_id=peer[to],
            device_id_type=MESH,
        )
        copy.start()
        sent.append(copy)

    def arrived(n, dst):
        pltpu.make_async_remote_copy(
            src_ref=dst,
            dst_ref=dst,
            send_sem=send_sem.at[n],
            recv_sem=recv_sem.at[n],
            device_id=peer["core"],
            device_id_type=MESH,
        ).wait_recv()

    return send, arrived


def dot_nt(a, b):
    return lax.dot_general(a, b, (((1,), (1,)), ((), ())), preferred_element_type=F32)


def dot_nn(a, b):
    return lax.dot_general(a, b, (((1,), (0,)), ((), ())), preferred_element_type=F32)


def dot_tn(a, b):
    return lax.dot_general(a, b, (((0,), (0,)), ((), ())), preferred_element_type=F32)


def gather_kernel(
    q_ref,
    k_ref,
    v_ref,
    tk_ref,
    tv_ref,
    go_ref,
    w_ref,
    qg_ref,
    kv_ref,
    st_own,
    st_pair,
    qz,
    q_pair,
    goall,
    relay,
    acc,
    send_sem,
    recv_sem,
    local_sem,
):
    seq, head, y, z, x = place()
    peer = peers(seq, head, y, z, x)
    zu, zd = (z + 1) % NZ, (z + NZ - 1) % NZ
    xr, xl = (x + 1) % NX, (x + NX - 1) % NX
    other_head = (head + 2) % 4
    core_head = head + 1 - 2 * (head % 2)
    first, second = pl.ds(0, HALF), pl.ds(HALF, HALF)
    sent = []
    send, arrived = sender(peer, send_sem, recv_sem, sent)
    cols = lambda h: slice(h * HS, (h + 1) * HS)
    by_y = lambda a, b: jnp.where(y == 0, a, b)

    greet(peer)

    send(0, go_ref.at[first], relay.at[0], "pair")
    send(1, go_ref.at[second], relay.at[1], "back")
    send(2, go_ref, goall.at[head], "core")

    for t, (ref, text) in enumerate(((k_ref, tk_ref), (v_ref, tv_ref))):
        st_own[t, 0, 0:TR] = by_y(ref[:, cols(0)], ref[:, cols(1)])
        st_own[t, 0, TR:BR] = by_y(text[:, cols(0)], text[:, cols(1)])
        st_own[t, 1, 0:TR] = ref[:, cols(2)]
        st_own[t, 1, TR:BR] = text[:, cols(2)]
        c = y * NX + x
        send(10 + 2 * t, st_own.at[t], kv_ref.at[t, c], "right")
        send(11 + 2 * t, st_own.at[t], kv_ref.at[t, c], "left")
        st_pair[t, 0, 0:TR] = by_y(ref[:, cols(1)], ref[:, cols(0)])
        st_pair[t, 0, TR:BR] = by_y(text[:, cols(1)], text[:, cols(0)])
        st_pair[t, 1, 0:TR] = ref[:, cols(2)]
        st_pair[t, 1, TR:BR] = text[:, cols(2)]
    qz[0, y] = by_y(q_ref[:, cols(0)], q_ref[:, cols(1)])
    qz[0, 2] = q_ref[:, cols(2)]
    q_pair[0] = by_y(q_ref[:, cols(1)], q_ref[:, cols(0)])
    own = []
    for t in range(2):
        copy = pltpu.make_async_copy(st_own.at[t], kv_ref.at[t, y * NX + x], local_sem.at[t])
        copy.start()
        own.append(copy)

    def z_send(t):
        base = 22 + 6 * t
        send(base + 0, qz.at[t, :, first], qg_ref.at[t, z, :, first], "up")
        send(base + 3, qz.at[t, :, second], qg_ref.at[t, z, :, second], "down")
        send(base + 1, qz.at[t, :, first], qg_ref.at[t, z, :, first], "down")
        send(base + 2, qz.at[t, :, second], qg_ref.at[t, z, :, second], "up")
        copy = pltpu.make_async_copy(qz.at[t], qg_ref.at[t, z], local_sem.at[2 + t])
        copy.start()
        own.append(copy)

    def z_forward(t):
        base = 22 + 6 * t
        arrived(base + 0, qg_ref.at[t, zd, :, first])
        send(base + 4, qg_ref.at[t, zd, :, first], qg_ref.at[t, zd, :, first], "up")
        arrived(base + 3, qg_ref.at[t, zu, :, second])
        send(base + 5, qg_ref.at[t, zu, :, second], qg_ref.at[t, zu, :, second], "down")

    def z_finish(t):
        base = 22 + 6 * t
        far = (z + 2) % NZ
        arrived(base + 1, qg_ref.at[t, zu, :, first])
        arrived(base + 2, qg_ref.at[t, zd, :, second])
        arrived(base + 4, qg_ref.at[t, far, :, first])
        arrived(base + 5, qg_ref.at[t, far, :, second])

    def x_forward(a, yy):
        base = 10 + 6 * a
        arrived(base + 0, kv_ref.at[0, yy * NX + xl])
        send(base + 4, kv_ref.at[0, yy * NX + xl], kv_ref.at[0, yy * NX + xl], "right")
        arrived(base + 3, kv_ref.at[1, yy * NX + xr])
        send(base + 5, kv_ref.at[1, yy * NX + xr], kv_ref.at[1, yy * NX + xr], "left")

    def x_finish(a, yy):
        base = 10 + 6 * a
        far = yy * NX + (x + 2) % NX
        arrived(base + 1, kv_ref.at[0, yy * NX + xr])
        arrived(base + 2, kv_ref.at[1, yy * NX + xl])
        arrived(base + 4, kv_ref.at[0, far])
        arrived(base + 5, kv_ref.at[1, far])

    def feature(n):
        return w_ref[:, pl.ds(pl.multiple_of(n * 768, 128), 768)]

    acc[...] = dot_nt(go_ref[...], feature(head))
    arrived(0, relay.at[0])
    send(3, relay.at[0], goall.at[head, first], "back")
    arrived(1, relay.at[1])
    send(4, relay.at[1], goall.at[other_head, second], "pair")
    send(6, q_pair.at[0], qz.at[0, y], "pair")
    for t in range(2):
        send(7 + t, st_pair.at[t], kv_ref.at[t, y * NX + x], "pair")
    arrived(2, goall.at[core_head])
    acc[...] += dot_nt(goall[core_head], feature(core_head))
    x_forward(0, y)
    arrived(3, goall.at[other_head, first])
    arrived(4, goall.at[other_head, second])
    send(5, goall.at[other_head], goall.at[other_head], "core")
    acc[...] += dot_nt(goall[other_head], feature(other_head))
    arrived(6, qz.at[0, 1 - y])
    z_send(0)
    last = core_head + 2 - 4 * (core_head // 2)
    arrived(5, goall.at[last])
    grad = (acc[...] + dot_nt(goall[last], feature(last))).astype(BF)
    q_pair[1] = by_y(grad[:, cols(1)], grad[:, cols(0)])
    send(9, q_pair.at[1], qz.at[1, y], "pair")
    qz[1, y] = by_y(grad[:, cols(0)], grad[:, cols(1)])
    qz[1, 2] = grad[:, cols(2)]
    for t in range(2):
        c = (1 - y) * NX + x
        arrived(7 + t, kv_ref.at[t, c])
        send(16 + 2 * t, kv_ref.at[t, c], kv_ref.at[t, c], "right")
        send(17 + 2 * t, kv_ref.at[t, c], kv_ref.at[t, c], "left")
    arrived(9, qz.at[1, 1 - y])
    z_send(1)
    z_forward(0)
    z_forward(1)
    x_forward(1, 1 - y)
    z_finish(0)
    z_finish(1)
    x_finish(0, y)
    x_finish(1, 1 - y)
    for copy in own:
        copy.wait()
    for copy in sent:
        copy.wait_send()


def attend_kernel(
    qg_ref,
    kv_ref,
    tile_ref,
    order_ref,
    len_ref,
    bias_ref,
    oq_ref,
    kvg_ref,
    kaug,
    vall,
    qaug,
    oacc,
    qacc,
    kacc,
    vacc,
):
    seq, head, y, z, x = place()
    factor = HS ** (-0.5)
    ends = [len_ref[0]]
    for c in range(1, CLIPS):
        ends.append(ends[-1] + len_ref[c])

    def clip_at(pos):
        total = 0
        for c in range(CLIPS - 1):
            total = total + jnp.where(pos >= ends[c], 1, 0)
        return total

    lane = lax.broadcasted_iota(jnp.int32, (1, HS), 1)
    tiles_here = (lane % 64) // 16 == z
    clip_lane = ((z + 1) % NZ) * 16
    bias_lane = clip_lane + CLIPS

    bias_ones = jnp.where((lane >= bias_lane) & (lane < bias_lane + 3), 1.0, 0.0)
    for c in range(NY * NX):
        first_pos = (c // NX) * (NZ * NX * TR) + z * (NX * TR) + (c % NX) * TR
        pos = first_pos + lax.broadcasted_iota(jnp.int32, (TR, HS), 0)
        hit = (tiles_here & (pos // TILE == lane)) | (clip_at(pos) == lane - clip_lane)
        aug = jnp.where(hit, 1.0, bias_ones).astype(BF)
        for s in range(2):
            kaug[s, c * TR : (c + 1) * TR, 0:HS] = kv_ref[0, c, s, 0:TR]
            kaug[s, c * TR : (c + 1) * TR, HS:] = aug
            vall[s, c * TR : (c + 1) * TR] = kv_ref[1, c, s, 0:TR]
            kaug[s, LAT + c * CR : LAT + (c + 1) * CR, 0:HS] = kv_ref[0, c, s, TR:BR]
            vall[s, LAT + c * CR : LAT + (c + 1) * CR] = kv_ref[1, c, s, TR:BR]
    text = lax.broadcasted_iota(jnp.int32, (NY * NX * CR, HS), 0)
    text_row = ((text // (NX * CR)) * NZ + z) * (NX * CR) + text % (NX * CR)
    aug = jnp.broadcast_to(bias_ones, text_row.shape)
    for c in range(CLIPS):
        listed = jnp.where(order_ref[c : c + 1, :] == text_row, 1.0, 0.0)
        found = jnp.max(listed, axis=1, keepdims=True)
        aug = jnp.where(lane == clip_lane + c, found, aug)
    for s in range(2):
        kaug[s, LAT:, HS:] = aug.astype(BF)

    kacc[...] = jnp.zeros_like(kacc)
    vacc[...] = jnp.zeros_like(vacc)

    log_len = [
        jnp.log(jnp.full((1, HS), len_ref[c] + CAP, jnp.int32).astype(F32)) for c in range(CLIPS)
    ]
    log2e = 1.4426950408889634

    def query_chunk(n, carry):
        zq = n // NH
        j = n % NH
        shared = j == 2
        slot = jnp.where(shared, 1, 0)
        yq = jnp.where(shared, y, j)
        own_head = jnp.where(shared, 2, y)
        start = ((yq * NZ + zq) * NX + x) * TR
        head_bias = bias_ref[own_head]
        pos = start + lax.broadcasted_iota(jnp.int32, (TR, HS), 0)
        clip = clip_at(pos)
        offset = jnp.broadcast_to(log_len[CLIPS - 1], (TR, HS))
        for c in range(CLIPS - 2, -1, -1):
            offset = jnp.where(pos < ends[c], log_len[c], offset)
        total = (head_bias - offset) * (HS**0.5)
        hi = total.astype(BF).astype(F32)
        mid = (total - hi).astype(BF).astype(F32)
        low = total - hi - mid
        in_bias = jnp.where(
            lane == bias_lane, hi, jnp.where(lane == bias_lane + 1, mid, low)
        )
        in_bias = jnp.where((lane >= bias_lane) & (lane < bias_lane + 3), in_bias, 0.0)
        in_clip = (lane >= clip_lane) & (lane < clip_lane + CLIPS) & (lane - clip_lane != clip)
        side = jnp.where(in_clip, MASKED, in_bias)
        for u in range(TR // TILE):
            tile = start // TILE + u
            off = (tile_ref[pl.ds(tile, 1), :] == 0) & (lane != tile) & tiles_here
            rows = slice(u * TILE, (u + 1) * TILE)
            qaug[rows, HS:] = jnp.where(off, MASKED, side[rows]).astype(BF)
        qaug[:, 0:HS] = qg_ref[0, zq, j]

        def block(first_row, count, fresh):
            rows = pl.ds(first_row, count)
            keys = kaug[slot, rows, :]
            queries = qaug[:, 0:HS]
            grads = qg_ref[1, zq, j]
            scores = dot_nt(qaug[...], keys)
            e = jnp.exp2(jnp.minimum(scores * (factor * log2e), 115.0))
            rest = pl.reciprocal(1.0 + e, approx=True)
            sig = e * rest
            weight = sig.astype(BF)
            product = dot_nt(grads, vall[slot, rows, :])
            slope = (product * (sig * rest)).astype(BF)
            o_part = dot_nn(weight, vall[slot, rows, :])
            q_part = dot_nn(slope, keys[:, 0:HS])
            if fresh:
                oacc[...] = o_part
                qacc[...] = q_part
            else:
                oacc[...] += o_part
                qacc[...] += q_part
            vacc[slot, rows, :] += dot_tn(weight, grads)
            kacc[slot, rows, :] += dot_tn(slope, queries)

        block(LAT, NY * NX * CR, True)
        q_low, q_high = clip_at(start), clip_at(start + TR - 1)
        width = 512
        for b in range(LAT // width):
            per_plane = NX * TR // width
            k_start = (b // per_plane) * (NZ * NX * TR) + z * (NX * TR) + (b % per_plane) * width
            k_low, k_high = clip_at(k_start), clip_at(k_start + width - 1)

            @pl.when((q_low <= k_high) & (k_low <= q_high))
            def _():
                block(b * width, width, False)

        oq_ref[0, zq, j] = oacc[...].astype(BF)
        oq_ref[1, zq, j] = qacc[...].astype(BF)
        return carry

    lax.fori_loop(0, NZ * NH, query_chunk, 0)
    for t, total in enumerate((kacc, vacc)):
        for c in range(NY * NX):
            for s in range(2):
                kvg_ref[t, c, s, 0:TR] = total[s, c * TR : (c + 1) * TR].astype(BF)
                kvg_ref[t, c, s, TR:BR] = total[s, LAT + c * CR : LAT + (c + 1) * CR].astype(BF)


def reduce_kernel(
    oq_ref,
    kvg_ref,
    w_ref,
    out_ref,
    gq_ref,
    gk_ref,
    gv_ref,
    gtk_ref,
    gtv_ref,
    z_in,
    z_sum,
    x_in,
    x_sum,
    yq_out,
    yq_in,
    yk_out,
    yk_in,
    keep_q,
    attn,
    part,
    core_in,
    pair_sum,
    relay,
    far_in,
    send_sem,
    recv_sem,
):
    seq, head, y, z, x = place()
    peer = peers(seq, head, y, z, x)
    zu, zd, zf = (z + 1) % NZ, (z + NZ - 1) % NZ, (z + 2) % NZ
    xr, xl, xf = (x + 1) % NX, (x + NX - 1) % NX, (x + 2) % NX
    other_head = (head + 2) % 4
    core_head = head + 1 - 2 * (head % 2)
    core_other = core_head + 2 - 4 * (core_head // 2)
    factor = HS ** (-0.5)
    first, second = pl.ds(0, HALF), pl.ds(HALF, HALF)
    sent = []
    send, arrived = sender(peer, send_sem, recv_sem, sent)
    by_y = lambda a, b: jnp.where(y == 0, a, b)
    cols = lambda h: slice(h * HS, (h + 1) * HS)
    wide = lambda a: a.astype(F32)

    greet(peer)

    def z_start(t):
        base = 6 * t
        send(base + 0, oq_ref.at[t, zf, :, first], z_in.at[t, 0], "up")
        send(base + 3, oq_ref.at[t, zf, :, second], z_in.at[t, 3], "down")
        send(base + 1, oq_ref.at[t, zd, :, first], z_in.at[t, 1], "down")
        send(base + 4, oq_ref.at[t, zu, :, second], z_in.at[t, 4], "up")

    def z_relay(t):
        base = 6 * t
        arrived(base + 0, z_in.at[t, 0])
        z_sum[t, 0] = (wide(z_in[t, 0]) + wide(oq_ref[t, zu, :, first])).astype(BF)
        send(base + 2, z_sum.at[t, 0], z_in.at[t, 2], "up")
        arrived(base + 3, z_in.at[t, 3])
        z_sum[t, 1] = (wide(z_in[t, 3]) + wide(oq_ref[t, zd, :, second])).astype(BF)
        send(base + 5, z_sum.at[t, 1], z_in.at[t, 5], "down")

    def z_total(t, scale):
        base = 6 * t
        for n in (1, 2, 4, 5):
            arrived(base + n, z_in.at[t, n])
        for h, rows, one, two in ((0, first, 1, 2), (1, second, 4, 5)):
            def total(j):
                value = wide(oq_ref[t, z, j, rows]) + wide(z_in[t, one, j]) + wide(z_in[t, two, j])
                return (value * scale).astype(BF) if scale != 1.0 else value.astype(BF)

            yq_out[t, rows] = total(1 - y)
            keep_q[t, 0, rows] = total(y)
            keep_q[t, 1, rows] = total(2)
        send(24 + t, yq_out.at[t], yq_in.at[t], "pair")

    def x_base(t, a):
        return 12 + 6 * t + 3 * a

    ring = (("right", "left"), ("left", "right"))
    ahead = ((xr, xl), (xl, xr))

    def x_start(t):
        for a in range(NY):
            send(x_base(t, a), kvg_ref.at[t, a * NX + xf], x_in.at[t, a, 0], ring[t][0])
        for a in range(NY):
            send(x_base(t, a) + 1, kvg_ref.at[t, a * NX + ahead[t][1]], x_in.at[t, a, 1], ring[t][1])

    def x_relay(t, a):
        arrived(x_base(t, a), x_in.at[t, a, 0])
        x_sum[t, a] = (wide(x_in[t, a, 0]) + wide(kvg_ref[t, a * NX + ahead[t][0]])).astype(BF)
        send(x_base(t, a) + 2, x_sum.at[t, a], x_in.at[t, a, 2], ring[t][0])

    def x_total(t, a):
        value = wide(kvg_ref[t, a * NX + x]) + wide(x_in[t, a, 1]) + wide(x_in[t, a, 2])
        return value * factor if t == 0 else value

    z_start(0)
    x_start(0)
    x_start(1)
    z_start(1)
    z_relay(0)
    for a in range(NY):
        for t in range(2):
            x_relay(t, a)
    z_total(0, 1.0)
    z_relay(1)
    arrived(24, yq_in.at[0])
    attn[:, cols(0)] = by_y(keep_q[0, 0], yq_in[0])
    attn[:, cols(1)] = by_y(yq_in[0], keep_q[0, 0])
    attn[:, cols(2)] = keep_q[0, 1]

    def project(n):
        return dot_nn(attn[...], w_ref[:, pl.ds(pl.multiple_of(n * 768, 128), 768)]).astype(BF)

    part[0] = project(core_other)
    send(28, part.at[0], core_in.at[0], "core")
    part[1] = project(core_head)
    send(29, part.at[1], core_in.at[1], "core")
    part[2] = project(other_head)
    arrived(28, core_in.at[0])
    pair_sum[...] = (wide(part[2]) + wide(core_in[0])).astype(BF)
    send(30, pair_sum.at[first], relay.at[0], "pair")
    send(31, pair_sum.at[second], relay.at[1], "back")
    part[3] = project(head)
    z_total(1, factor)
    for t in range(2):
        for a in range(NY):
            arrived(x_base(t, a) + 1, x_in.at[t, a, 1])
            arrived(x_base(t, a) + 2, x_in.at[t, a, 2])
        yk_out[t] = x_total(t, 1 - y).astype(BF)
        send(26 + t, yk_out.at[t], yk_in.at[t], "pair")
    arrived(30, relay.at[0])
    send(32, relay.at[0], far_in.at[first], "back")
    arrived(31, relay.at[1])
    send(33, relay.at[1], far_in.at[second], "pair")

    arrived(25, yq_in.at[1])
    gq_ref[:, cols(0)] = by_y(keep_q[1, 0], yq_in[1])
    gq_ref[:, cols(1)] = by_y(yq_in[1], keep_q[1, 0])
    gq_ref[:, cols(2)] = keep_q[1, 1]
    for t, (ref, text) in enumerate(((gk_ref, gtk_ref), (gv_ref, gtv_ref))):
        arrived(26 + t, yk_in.at[t])
        own = x_total(t, y)
        mine = own[0].astype(BF)
        other = yk_in[t, 0]
        both = (own[1] + wide(yk_in[t, 1])).astype(BF)
        for h, value in ((0, by_y(mine, other)), (1, by_y(other, mine)), (2, both)):
            ref[:, cols(h)] = value[0:TR]
            text[:, cols(h)] = value[TR:BR]
    arrived(29, core_in.at[1])
    arrived(32, far_in.at[first])
    arrived(33, far_in.at[second])
    out_ref[...] = (wide(part[3]) + wide(core_in[1]) + wide(far_in[...])).astype(BF)
    for copy in sent:
        copy.wait_send()


def shards(
    queries,
    keys,
    values,
    text_keys,
    text_values,
    head_bias,
    out_weight,
    grad_out,
    clip_lengths,
    tile_mask,
    caption_order,
):
    vmem = pl.BlockSpec(memory_space=pltpu.VMEM)
    smem = pl.BlockSpec(memory_space=pltpu.SMEM)
    anywhere = pl.BlockSpec(memory_space=pl.ANY)
    dma = pltpu.SemaphoreType.DMA
    qg_shape = (2, NZ, NH, TR, HS)
    kv_shape = (2, NY * NX, 2, BR, HS)
    out_cols = grad_out.shape[1]
    qg, kv = pl.pallas_call(
        gather_kernel,
        out_shape=(jax.ShapeDtypeStruct(qg_shape, BF), jax.ShapeDtypeStruct(kv_shape, BF)),
        in_specs=[vmem] * 7,
        out_specs=(anywhere, anywhere),
        scratch_shapes=[
            pltpu.VMEM((2, 2, BR, HS), BF),
            pltpu.VMEM((2, 2, BR, HS), BF),
            pltpu.VMEM((2, NH, TR, HS), BF),
            pltpu.VMEM((2, TR, HS), BF),
            pltpu.VMEM((4, TR, out_cols), BF),
            pltpu.VMEM((2, HALF, out_cols), BF),
            pltpu.VMEM((TR, NH * HS), F32),
            dma((34,)),
            dma((34,)),
            dma((4,)),
        ],
        compiler_params=pltpu.CompilerParams(
            collective_id=0, has_side_effects=True, vmem_limit_bytes=VMEM_LIMIT
        ),
    )(queries, keys, values, text_keys, text_values, grad_out, out_weight)

    oq, kvg = pl.pallas_call(
        attend_kernel,
        out_shape=(jax.ShapeDtypeStruct(qg_shape, BF), jax.ShapeDtypeStruct(kv_shape, BF)),
        in_specs=[vmem] * 4 + [smem] * 2,
        out_specs=(vmem, vmem),
        scratch_shapes=[
            pltpu.VMEM((2, ROWS, 2 * HS), BF),
            pltpu.VMEM((2, ROWS, HS), BF),
            pltpu.VMEM((TR, 2 * HS), BF),
            pltpu.VMEM((TR, HS), F32),
            pltpu.VMEM((TR, HS), F32),
            pltpu.VMEM((2, ROWS, HS), F32),
            pltpu.VMEM((2, ROWS, HS), F32),
        ],
        compiler_params=pltpu.CompilerParams(vmem_limit_bytes=VMEM_LIMIT),
    )(
        qg,
        kv,
        tile_mask,
        caption_order.reshape(CLIPS, CAP),
        clip_lengths,
        head_bias,
    )

    token_shape = jax.ShapeDtypeStruct((TR, NH * HS), BF)
    text_shape = jax.ShapeDtypeStruct((CR, NH * HS), BF)
    return pl.pallas_call(
        reduce_kernel,
        out_shape=(
            jax.ShapeDtypeStruct((TR, out_cols), BF),
            token_shape,
            token_shape,
            token_shape,
            text_shape,
            text_shape,
        ),
        in_specs=[vmem] * 3,
        out_specs=(vmem,) * 6,
        scratch_shapes=[
            pltpu.VMEM((2, 6, NH, HALF, HS), BF),
            pltpu.VMEM((2, 2, NH, HALF, HS), BF),
            pltpu.VMEM((2, NY, 3, 2, BR, HS), BF),
            pltpu.VMEM((2, NY, 2, BR, HS), BF),
            pltpu.VMEM((2, TR, HS), BF),
            pltpu.VMEM((2, TR, HS), BF),
            pltpu.VMEM((2, 2, BR, HS), BF),
            pltpu.VMEM((2, 2, BR, HS), BF),
            pltpu.VMEM((2, 2, TR, HS), BF),
            pltpu.VMEM((TR, NH * HS), BF),
            pltpu.VMEM((4, TR, out_cols), BF),
            pltpu.VMEM((2, TR, out_cols), BF),
            pltpu.VMEM((TR, out_cols), BF),
            pltpu.VMEM((2, HALF, out_cols), BF),
            pltpu.VMEM((TR, out_cols), BF),
            dma((34,)),
            dma((34,)),
        ],
        compiler_params=pltpu.CompilerParams(
            collective_id=1, has_side_effects=True, vmem_limit_bytes=VMEM_LIMIT
        ),
    )(oq, kvg, out_weight)


def solution(mesh):
    in_specs = (
        P("seq", "head"),
        P("seq", "head"),
        P("seq", "head"),
        P("seq", "head"),
        P("seq", "head"),
        P("head"),
        P("head", None),
        P("seq", "head"),
        P(),
        P(),
        P(),
    )
    out_specs = (P("seq", "head"),) * 6
    return jax.shard_map(shards, mesh=mesh, in_specs=in_specs, out_specs=out_specs, check_vma=False)
```

```python
import jax
import jax.numpy as jnp
from jax import lax
from jax.experimental import pallas as pl
from jax.experimental.pallas import tpu as pltpu
from jax.sharding import PartitionSpec as P

MESH = pl.DeviceIdType.MESH
BF = jnp.bfloat16
F32 = jnp.float32

NX, NZ, NY = 4, 4, 2
HS = 128
NH = 3
TR = 256
CR = 16
BR = TR + CR
HALF = TR // 2
CLIPS = 4
CAP = 128
TILE = 64
LAT = NY * NX * TR
ROWS = NY * NX * BR
MASKED = -32768.0
VMEM_LIMIT = 24 * 1024 * 1024


def place():
    seq = lax.axis_index("seq")
    head = lax.axis_index("head")
    y = seq // (NZ * NX)
    z = (seq // NX) % NZ
    x = seq % NX
    return seq, head, y, z, x


def peers(seq, head, y, z, x):
    def at(yy, zz, xx):
        return (yy * NZ + zz) * NX + xx

    other_head = (head + 2) % 4
    core_head = head + 1 - 2 * (head % 2)
    return {
        "pair": (at(1 - y, z, x), head),
        "back": (at(1 - y, z, x), other_head),
        "core": (seq, core_head),
        "right": (at(y, z, (x + 1) % NX), head),
        "left": (at(y, z, (x + NX - 1) % NX), head),
        "up": (at(y, (z + 1) % NZ, x), head),
        "down": (at(y, (z + NZ - 1) % NZ, x), head),
    }


def greet(peer):
    barrier = pltpu.get_barrier_semaphore()
    for device in peer.values():
        pl.semaphore_signal(barrier, inc=1, device_id=device, device_id_type=MESH)
    pl.semaphore_wait(barrier, len(peer))


def sender(peer, send_sem, recv_sem, sent):
    def send(n, src, dst, to):
        copy = pltpu.make_async_remote_copy(
            src_ref=src,
            dst_ref=dst,
            send_sem=send_sem.at[n],
            recv_sem=recv_sem.at[n],
            device_id=peer[to],
            device_id_type=MESH,
        )
        copy.start()
        sent.append(copy)

    def arrived(n, dst):
        pltpu.make_async_remote_copy(
            src_ref=dst,
            dst_ref=dst,
            send_sem=send_sem.at[n],
            recv_sem=recv_sem.at[n],
            device_id=peer["core"],
            device_id_type=MESH,
        ).wait_recv()

    return send, arrived


def dot_nt(a, b):
    return lax.dot_general(a, b, (((1,), (1,)), ((), ())), preferred_element_type=F32)


def dot_nn(a, b):
    return lax.dot_general(a, b, (((1,), (0,)), ((), ())), preferred_element_type=F32)


def gather_kernel(
    q_hbm,
    k_hbm,
    v_hbm,
    tk_hbm,
    tv_hbm,
    go_hbm,
    w_hbm,
    qg_hbm,
    kv_hbm,
    qg_ref,
    kv_ref,
    q_ref,
    k_ref,
    v_ref,
    tk_ref,
    tv_ref,
    go_ref,
    w_ref,
    st_pair,
    q_pair,
    goall,
    relay,
    acc,
    send_sem,
    recv_sem,
    local_sem,
):
    seq, head, y, z, x = place()
    peer = peers(seq, head, y, z, x)
    zu, zd, zf = (z + 1) % NZ, (z + NZ - 1) % NZ, (z + 2) % NZ
    xr, xl, xf = (x + 1) % NX, (x + NX - 1) % NX, (x + 2) % NX
    other_head = (head + 2) % 4
    core_head = head + 1 - 2 * (head % 2)
    core_other = core_head + 2 - 4 * (core_head // 2)
    first, second = pl.ds(0, HALF), pl.ds(HALF, HALF)
    sent = []
    send, arrived = sender(peer, send_sem, recv_sem, sent)
    cols = lambda h: slice(h * HS, (h + 1) * HS)
    by_y = lambda a, b: jnp.where(y == 0, a, b)

    load = []
    for n, (src, dst) in enumerate(
        (
            (k_hbm, k_ref),
            (tk_hbm, tk_ref),
            (v_hbm, v_ref),
            (tv_hbm, tv_ref),
            (q_hbm, q_ref),
            (go_hbm, go_ref),
            (w_hbm, w_ref),
        )
    ):
        copy = pltpu.make_async_copy(src, dst, local_sem.at[n])
        copy.start()
        load.append(copy)

    greet(peer)

    send(0, go_hbm.at[first], relay.at[0], "pair")
    send(1, go_hbm.at[second], relay.at[1], "back")
    send(2, go_hbm, goall.at[head], "core")

    stores = []

    def store(src, dst):
        copy = pltpu.make_async_copy(src, dst, local_sem.at[7 + len(stores)])
        copy.start()
        stores.append(copy)

    def x_send(a, t, yy):
        c = yy * NX + x
        send(10 + 6 * a + 2 * t, kv_ref.at[t, c], kv_ref.at[t, c], ("right", "left")[t])
        send(11 + 6 * a + 2 * t, kv_ref.at[t, c], kv_ref.at[t, c], ("left", "right")[t])

    def x_forward(a, yy):
        base = 10 + 6 * a
        left, right = yy * NX + xl, yy * NX + xr
        arrived(base + 0, kv_ref.at[0, left])
        send(base + 4, kv_ref.at[0, left], kv_ref.at[0, left], "right")
        arrived(base + 2, kv_ref.at[1, right])
        send(base + 5, kv_ref.at[1, right], kv_ref.at[1, right], "left")

    def x_finish(a, yy):
        base = 10 + 6 * a
        arrived(base + 1, kv_ref.at[0, yy * NX + xr])
        arrived(base + 3, kv_ref.at[1, yy * NX + xl])
        arrived(base + 4, kv_ref.at[0, yy * NX + xf])
        arrived(base + 5, kv_ref.at[1, yy * NX + xf])

    def z_own(t):
        base = 22 + 10 * t
        send(base + 0, qg_ref.at[t, z, 2], qg_ref.at[t, z, 2], "up")
        send(base + 1, qg_ref.at[t, z, y], qg_ref.at[t, z, y], "down")
        send(base + 2, qg_ref.at[t, z, y], qg_ref.at[t, z, y], "up")
        send(base + 3, qg_ref.at[t, z, 2], qg_ref.at[t, z, 2], "down")

    def z_own_forward(t):
        base = 22 + 10 * t
        arrived(base + 0, qg_ref.at[t, zd, 2])
        send(base + 4, qg_ref.at[t, zd, 2], qg_ref.at[t, zd, 2], "up")
        arrived(base + 1, qg_ref.at[t, zu, y])
        send(base + 5, qg_ref.at[t, zu, y], qg_ref.at[t, zu, y], "down")

    def z_pair(t):
        base = 22 + 10 * t
        send(base + 6, qg_ref.at[t, z, 1 - y], qg_ref.at[t, z, 1 - y], "up")
        send(base + 7, qg_ref.at[t, z, 1 - y], qg_ref.at[t, z, 1 - y], "down")

    def z_pair_forward(t):
        base = 22 + 10 * t
        arrived(base + 6, qg_ref.at[t, zd, 1 - y])
        src = qg_ref.at[t, zd, 1 - y, first]
        send(base + 8, src, src, "up")
        arrived(base + 7, qg_ref.at[t, zu, 1 - y])
        src = qg_ref.at[t, zu, 1 - y, second]
        send(base + 9, src, src, "down")

    def z_finish(t):
        base = 22 + 10 * t
        arrived(base + 2, qg_ref.at[t, zd, y])
        arrived(base + 3, qg_ref.at[t, zu, 2])
        arrived(base + 4, qg_ref.at[t, zf, 2])
        arrived(base + 5, qg_ref.at[t, zf, y])
        arrived(base + 8, qg_ref.at[t, zf, 1 - y, first])
        arrived(base + 9, qg_ref.at[t, zf, 1 - y, second])

    def feature(n):
        return w_ref[:, pl.ds(pl.multiple_of(n * 768, 128), 768)]

    c = y * NX + x
    for t, (ref, text) in enumerate(((k_ref, tk_ref), (v_ref, tv_ref))):
        load[2 * t].wait()
        load[2 * t + 1].wait()
        kv_ref[t, c, 0, 0:TR] = by_y(ref[:, cols(0)], ref[:, cols(1)])
        kv_ref[t, c, 0, TR:BR] = by_y(text[:, cols(0)], text[:, cols(1)])
        kv_ref[t, c, 1, 0:TR] = ref[:, cols(2)]
        kv_ref[t, c, 1, TR:BR] = text[:, cols(2)]
        x_send(0, t, y)
    load[4].wait()
    qg_ref[0, z, y] = by_y(q_ref[:, cols(0)], q_ref[:, cols(1)])
    qg_ref[0, z, 2] = q_ref[:, cols(2)]
    z_own(0)
    q_pair[0] = by_y(q_ref[:, cols(1)], q_ref[:, cols(0)])
    for t, (ref, text) in enumerate(((k_ref, tk_ref), (v_ref, tv_ref))):
        st_pair[t, 0, 0:TR] = by_y(ref[:, cols(1)], ref[:, cols(0)])
        st_pair[t, 0, TR:BR] = by_y(text[:, cols(1)], text[:, cols(0)])
        st_pair[t, 1, 0:TR] = ref[:, cols(2)]
        st_pair[t, 1, TR:BR] = text[:, cols(2)]
    load[5].wait()
    load[6].wait()
    acc[...] = dot_nt(go_ref[...], feature(head))

    arrived(0, relay.at[0])
    send(3, relay.at[0], goall.at[head, first], "back")
    arrived(1, relay.at[1])
    send(4, relay.at[1], goall.at[other_head, second], "pair")
    send(6, q_pair.at[0], qg_ref.at[0, z, y], "pair")
    z_own_forward(0)
    x_forward(0, y)
    arrived(2, goall.at[core_head])
    acc[...] += dot_nt(goall[core_head], feature(core_head))
    arrived(3, goall.at[other_head, first])
    arrived(4, goall.at[other_head, second])
    send(5, goall.at[other_head], goall.at[other_head], "core")
    for t in range(2):
        send(7 + t, st_pair.at[t], kv_ref.at[t, c], "pair")
    acc[...] += dot_nt(goall[other_head], feature(other_head))
    arrived(6, qg_ref.at[0, z, 1 - y])
    z_pair(0)
    arrived(5, goall.at[core_other])
    grad = (acc[...] + dot_nt(goall[core_other], feature(core_other))).astype(BF)
    q_pair[1] = by_y(grad[:, cols(1)], grad[:, cols(0)])
    send(9, q_pair.at[1], qg_ref.at[1, z, y], "pair")
    qg_ref[1, z, y] = by_y(grad[:, cols(0)], grad[:, cols(1)])
    qg_ref[1, z, 2] = grad[:, cols(2)]
    z_own(1)
    z_pair_forward(0)
    arrived(9, qg_ref.at[1, z, 1 - y])
    z_pair(1)
    for t in range(2):
        arrived(7 + t, kv_ref.at[t, (1 - y) * NX + x])
        x_send(1, t, 1 - y)
    z_own_forward(1)
    z_pair_forward(1)
    x_finish(0, y)
    plane = pl.ds(y * NX, NX)
    for t in range(2):
        store(kv_ref.at[t, plane], kv_hbm.at[t, plane])
    x_forward(1, 1 - y)
    z_finish(0)
    store(qg_ref.at[0], qg_hbm.at[0])
    z_finish(1)
    store(qg_ref.at[1], qg_hbm.at[1])
    x_finish(1, 1 - y)
    plane = pl.ds((1 - y) * NX, NX)
    for t in range(2):
        store(kv_ref.at[t, plane], kv_hbm.at[t, plane])
    for copy in sent:
        copy.wait_send()
    for copy in stores:
        copy.wait()


def attend_kernel(
    qg_ref,
    kv_ref,
    tile_ref,
    order_ref,
    len_ref,
    bias_ref,
    oq_ref,
    kvg_ref,
    kaug,
    vall,
    qaug,
    oacc,
    qacc,
    kacc,
    vacc,
    queries_t,
    grads_t,
):
    seq, head, y, z, x = place()
    factor = HS ** (-0.5)
    ends = [len_ref[0]]
    for c in range(1, CLIPS):
        ends.append(ends[-1] + len_ref[c])

    def clip_at(pos):
        total = 0
        for c in range(CLIPS - 1):
            total = total + jnp.where(pos >= ends[c], 1, 0)
        return total

    lane = lax.broadcasted_iota(jnp.int32, (1, HS), 1)
    tiles_here = (lane % 64) // 16 == z
    clip_lane = ((z + 1) % NZ) * 16
    bias_lane = clip_lane + CLIPS

    bias_ones = jnp.where((lane >= bias_lane) & (lane < bias_lane + 3), 1.0, 0.0)
    for c in range(NY * NX):
        first_pos = (c // NX) * (NZ * NX * TR) + z * (NX * TR) + (c % NX) * TR
        pos = first_pos + lax.broadcasted_iota(jnp.int32, (TR, HS), 0)
        hit = (tiles_here & (pos // TILE == lane)) | (clip_at(pos) == lane - clip_lane)
        aug = jnp.where(hit, 1.0, bias_ones).astype(BF)
        for s in range(2):
            kaug[s, c * TR : (c + 1) * TR, 0:HS] = kv_ref[0, c, s, 0:TR]
            kaug[s, c * TR : (c + 1) * TR, HS:] = aug
            vall[s, c * TR : (c + 1) * TR] = kv_ref[1, c, s, 0:TR]
            kaug[s, LAT + c * CR : LAT + (c + 1) * CR, 0:HS] = kv_ref[0, c, s, TR:BR]
            vall[s, LAT + c * CR : LAT + (c + 1) * CR] = kv_ref[1, c, s, TR:BR]
    text = lax.broadcasted_iota(jnp.int32, (NY * NX * CR, HS), 0)
    text_row = ((text // (NX * CR)) * NZ + z) * (NX * CR) + text % (NX * CR)
    aug = jnp.broadcast_to(bias_ones, text_row.shape)
    for c in range(CLIPS):
        listed = jnp.where(order_ref[c : c + 1, :] == text_row, 1.0, 0.0)
        found = jnp.max(listed, axis=1, keepdims=True)
        aug = jnp.where(lane == clip_lane + c, found, aug)
    for s in range(2):
        kaug[s, LAT:, HS:] = aug.astype(BF)

    kacc[...] = jnp.zeros_like(kacc)
    vacc[...] = jnp.zeros_like(vacc)

    log_len = [
        jnp.log(jnp.full((1, HS), len_ref[c] + CAP, jnp.int32).astype(F32)) for c in range(CLIPS)
    ]
    log2e = 1.4426950408889634

    def query_chunk(n, carry):
        zq = n // NH
        j = n % NH
        shared = j == 2
        slot = jnp.where(shared, 1, 0)
        yq = jnp.where(shared, y, j)
        own_head = jnp.where(shared, 2, y)
        start = ((yq * NZ + zq) * NX + x) * TR
        head_bias = bias_ref[own_head]
        pos = start + lax.broadcasted_iota(jnp.int32, (TR, HS), 0)
        clip = clip_at(pos)
        offset = jnp.broadcast_to(log_len[CLIPS - 1], (TR, HS))
        for c in range(CLIPS - 2, -1, -1):
            offset = jnp.where(pos < ends[c], log_len[c], offset)
        total = (head_bias - offset) * (HS**0.5)
        hi = total.astype(BF).astype(F32)
        mid = (total - hi).astype(BF).astype(F32)
        low = total - hi - mid
        in_bias = jnp.where(
            lane == bias_lane, hi, jnp.where(lane == bias_lane + 1, mid, low)
        )
        in_bias = jnp.where((lane >= bias_lane) & (lane < bias_lane + 3), in_bias, 0.0)
        in_clip = (lane >= clip_lane) & (lane < clip_lane + CLIPS) & (lane - clip_lane != clip)
        side = jnp.where(in_clip, MASKED, in_bias)
        for u in range(TR // TILE):
            tile = start // TILE + u
            off = (tile_ref[pl.ds(tile, 1), :] == 0) & (lane != tile) & tiles_here
            rows = slice(u * TILE, (u + 1) * TILE)
            qaug[rows, HS:] = jnp.where(off, MASKED, side[rows]).astype(BF)
        queries = qg_ref[0, zq, j]
        grads = qg_ref[1, zq, j]
        qaug[:, 0:HS] = queries
        queries_t[...] = queries.T
        grads_t[...] = grads.T

        def block(first_row, count, fresh):
            rows = pl.ds(first_row, count)
            keys = kaug[slot, rows, :]
            grads = qg_ref[1, zq, j]
            scores = dot_nt(qaug[...], keys)
            e = jnp.exp2(jnp.minimum(scores * (factor * log2e), 115.0))
            rest = pl.reciprocal(1.0 + e, approx=True)
            sig = e * rest
            weight = sig.astype(BF)
            product = dot_nt(grads, vall[slot, rows, :])
            slope = (product * (sig * rest)).astype(BF)
            o_part = dot_nn(weight, vall[slot, rows, :])
            q_part = dot_nn(slope, keys[:, 0:HS])
            if fresh:
                oacc[...] = o_part
                qacc[...] = q_part
            else:
                oacc[...] += o_part
                qacc[...] += q_part
            vacc[slot, :, rows] += dot_nn(grads_t[...], weight)
            kacc[slot, :, rows] += dot_nn(queries_t[...], slope)

        block(LAT, NY * NX * CR, True)
        q_low, q_high = clip_at(start), clip_at(start + TR - 1)
        width = 512
        for b in range(LAT // width):
            per_plane = NX * TR // width
            k_start = (b // per_plane) * (NZ * NX * TR) + z * (NX * TR) + (b % per_plane) * width
            k_low, k_high = clip_at(k_start), clip_at(k_start + width - 1)

            @pl.when((q_low <= k_high) & (k_low <= q_high))
            def _():
                block(b * width, width, False)

        oq_ref[0, zq, j] = oacc[...].astype(BF)
        oq_ref[1, zq, j] = qacc[...].astype(BF)
        return carry

    lax.fori_loop(0, NZ * NH, query_chunk, 0)
    for t, total in enumerate((kacc, vacc)):
        for c in range(NY * NX):
            for s in range(2):
                kvg_ref[t, c, s, 0:TR] = total[s, :, c * TR : (c + 1) * TR].astype(BF).T
        for s in range(2):
            text_rows = total[s, :, LAT:].astype(BF).T
            for c in range(NY * NX):
                kvg_ref[t, c, s, TR:BR] = text_rows[c * CR : (c + 1) * CR]


def reduce_kernel(
    oq_ref,
    kvg_ref,
    w_hbm,
    out_ref,
    gq_ref,
    gk_ref,
    gv_ref,
    gtk_ref,
    gtv_ref,
    z_in,
    z_sum,
    x_in,
    x_sum,
    yq_out,
    yq_in,
    yk_out,
    yk_in,
    keep_q,
    attn,
    part,
    core_in,
    pair_sum,
    relay,
    far_in,
    w_ref,
    send_sem,
    recv_sem,
    load_sem,
):
    seq, head, y, z, x = place()
    peer = peers(seq, head, y, z, x)
    zu, zd, zf = (z + 1) % NZ, (z + NZ - 1) % NZ, (z + 2) % NZ
    xr, xl, xf = (x + 1) % NX, (x + NX - 1) % NX, (x + 2) % NX
    other_head = (head + 2) % 4
    core_head = head + 1 - 2 * (head % 2)
    core_other = core_head + 2 - 4 * (core_head // 2)
    factor = HS ** (-0.5)
    first, second = pl.ds(0, HALF), pl.ds(HALF, HALF)
    sent = []
    send, arrived = sender(peer, send_sem, recv_sem, sent)
    by_y = lambda a, b: jnp.where(y == 0, a, b)
    cols = lambda h: slice(h * HS, (h + 1) * HS)
    wide = lambda a: a.astype(F32)
    load = pltpu.make_async_copy(w_hbm, w_ref, load_sem.at[0])
    load.start()

    greet(peer)

    def z_start(t):
        base = 6 * t
        send(base + 0, oq_ref.at[t, zf, :, first], z_in.at[t, 0], "up")
        send(base + 3, oq_ref.at[t, zf, :, second], z_in.at[t, 3], "down")
        send(base + 1, oq_ref.at[t, zd, :, first], z_in.at[t, 1], "down")
        send(base + 4, oq_ref.at[t, zu, :, second], z_in.at[t, 4], "up")

    def z_relay(t):
        base = 6 * t
        arrived(base + 0, z_in.at[t, 0])
        z_sum[t, 0] = (wide(z_in[t, 0]) + wide(oq_ref[t, zu, :, first])).astype(BF)
        send(base + 2, z_sum.at[t, 0], z_in.at[t, 2], "up")
        arrived(base + 3, z_in.at[t, 3])
        z_sum[t, 1] = (wide(z_in[t, 3]) + wide(oq_ref[t, zd, :, second])).astype(BF)
        send(base + 5, z_sum.at[t, 1], z_in.at[t, 5], "down")

    def z_total(t, scale):
        base = 6 * t
        for n in (1, 2, 4, 5):
            arrived(base + n, z_in.at[t, n])
        for h, rows, one, two in ((0, first, 1, 2), (1, second, 4, 5)):
            def total(j):
                value = wide(oq_ref[t, z, j, rows]) + wide(z_in[t, one, j]) + wide(z_in[t, two, j])
                return (value * scale).astype(BF) if scale != 1.0 else value.astype(BF)

            yq_out[t, rows] = total(1 - y)
            keep_q[t, 0, rows] = total(y)
            keep_q[t, 1, rows] = total(2)
        send(24 + t, yq_out.at[t], yq_in.at[t], "pair")

    def x_base(t, a):
        return 12 + 6 * t + 3 * a

    ring = (("right", "left"), ("left", "right"))
    ahead = ((xr, xl), (xl, xr))

    def x_far(t, a):
        send(x_base(t, a), kvg_ref.at[t, a * NX + xf], x_in.at[t, a, 0], ring[t][0])

    def x_near(t, a):
        send(x_base(t, a) + 1, kvg_ref.at[t, a * NX + ahead[t][1]], x_in.at[t, a, 1], ring[t][1])

    def x_relay(t, a):
        arrived(x_base(t, a), x_in.at[t, a, 0])
        x_sum[t, a] = (wide(x_in[t, a, 0]) + wide(kvg_ref[t, a * NX + ahead[t][0]])).astype(BF)
        send(x_base(t, a) + 2, x_sum.at[t, a], x_in.at[t, a, 2], ring[t][0])

    def x_total(t, a):
        value = wide(kvg_ref[t, a * NX + x]) + wide(x_in[t, a, 1]) + wide(x_in[t, a, 2])
        return value * factor if t == 0 else value

    z_start(0)
    for t in range(2):
        x_far(t, 1 - y)
    z_relay(0)
    for t in range(2):
        x_relay(t, 1 - y)
        x_near(t, 1 - y)
    z_total(0, 1.0)
    z_start(1)
    for t in range(2):
        x_far(t, y)
    arrived(24, yq_in.at[0])
    attn[:, cols(0)] = by_y(keep_q[0, 0], yq_in[0])
    attn[:, cols(1)] = by_y(yq_in[0], keep_q[0, 0])
    attn[:, cols(2)] = keep_q[0, 1]
    load.wait()

    def project(n):
        return dot_nn(attn[...], w_ref[:, pl.ds(pl.multiple_of(n * 768, 128), 768)]).astype(BF)

    part[0] = project(core_other)
    send(28, part.at[0], core_in.at[0], "core")
    part[1] = project(core_head)
    send(29, part.at[1], core_in.at[1], "core")
    part[2] = project(other_head)
    arrived(28, core_in.at[0])
    pair_sum[...] = (wide(part[2]) + wide(core_in[0])).astype(BF)
    send(30, pair_sum.at[first], relay.at[0], "pair")
    send(31, pair_sum.at[second], relay.at[1], "back")
    z_relay(1)
    for t in range(2):
        arrived(x_base(t, 1 - y) + 1, x_in.at[t, 1 - y, 1])
        arrived(x_base(t, 1 - y) + 2, x_in.at[t, 1 - y, 2])
        yk_out[t] = x_total(t, 1 - y).astype(BF)
        send(26 + t, yk_out.at[t], yk_in.at[t], "pair")
    for t in range(2):
        x_relay(t, y)
        x_near(t, y)
    part[3] = project(head)
    arrived(30, relay.at[0])
    send(32, relay.at[0], far_in.at[first], "back")
    arrived(31, relay.at[1])
    send(33, relay.at[1], far_in.at[second], "pair")
    z_total(1, factor)
    for t in range(2):
        arrived(x_base(t, y) + 1, x_in.at[t, y, 1])
        arrived(x_base(t, y) + 2, x_in.at[t, y, 2])

    arrived(25, yq_in.at[1])
    gq_ref[:, cols(0)] = by_y(keep_q[1, 0], yq_in[1])
    gq_ref[:, cols(1)] = by_y(yq_in[1], keep_q[1, 0])
    gq_ref[:, cols(2)] = keep_q[1, 1]
    for t, (ref, text) in enumerate(((gk_ref, gtk_ref), (gv_ref, gtv_ref))):
        arrived(26 + t, yk_in.at[t])
        own = x_total(t, y)
        mine = own[0].astype(BF)
        other = yk_in[t, 0]
        both = (own[1] + wide(yk_in[t, 1])).astype(BF)
        for h, value in ((0, by_y(mine, other)), (1, by_y(other, mine)), (2, both)):
            ref[:, cols(h)] = value[0:TR]
            text[:, cols(h)] = value[TR:BR]
    arrived(29, core_in.at[1])
    arrived(32, far_in.at[first])
    arrived(33, far_in.at[second])
    out_ref[...] = (wide(part[3]) + wide(core_in[1]) + wide(far_in[...])).astype(BF)
    for copy in sent:
        copy.wait_send()


def store_kernel(*refs):
    count = len(refs) // 2
    sems = refs[-1]
    copies = [
        pltpu.make_async_copy(refs[n], refs[count + n], sems.at[n]) for n in range(count)
    ]
    for copy in copies:
        copy.start()
    for copy in copies:
        copy.wait()


def shards(
    queries,
    keys,
    values,
    text_keys,
    text_values,
    head_bias,
    out_weight,
    grad_out,
    clip_lengths,
    tile_mask,
    caption_order,
):
    vmem = pl.BlockSpec(memory_space=pltpu.VMEM)
    smem = pl.BlockSpec(memory_space=pltpu.SMEM)
    hbm = pl.BlockSpec(memory_space=pltpu.HBM)
    dma = pltpu.SemaphoreType.DMA
    qg_shape = (2, NZ, NH, TR, HS)
    kv_shape = (2, NY * NX, 2, BR, HS)
    out_cols = grad_out.shape[1]
    qg, kv = pl.pallas_call(
        gather_kernel,
        out_shape=(jax.ShapeDtypeStruct(qg_shape, BF), jax.ShapeDtypeStruct(kv_shape, BF)),
        in_specs=[hbm] * 7,
        out_specs=(hbm, hbm),
        scratch_shapes=[
            pltpu.VMEM(qg_shape, BF),
            pltpu.VMEM(kv_shape, BF),
            pltpu.VMEM((TR, NH * HS), BF),
            pltpu.VMEM((TR, NH * HS), BF),
            pltpu.VMEM((TR, NH * HS), BF),
            pltpu.VMEM((CR, NH * HS), BF),
            pltpu.VMEM((CR, NH * HS), BF),
            pltpu.VMEM((TR, out_cols), BF),
            pltpu.VMEM(out_weight.shape, BF),
            pltpu.VMEM((2, 2, BR, HS), BF),
            pltpu.VMEM((2, TR, HS), BF),
            pltpu.VMEM((4, TR, out_cols), BF),
            pltpu.VMEM((2, HALF, out_cols), BF),
            pltpu.VMEM((TR, NH * HS), F32),
            dma((42,)),
            dma((42,)),
            dma((13,)),
        ],
        compiler_params=pltpu.CompilerParams(
            collective_id=0, has_side_effects=True, vmem_limit_bytes=56 * 1024 * 1024
        ),
    )(queries, keys, values, text_keys, text_values, grad_out, out_weight)

    oq, kvg = pl.pallas_call(
        attend_kernel,
        out_shape=(jax.ShapeDtypeStruct(qg_shape, BF), jax.ShapeDtypeStruct(kv_shape, BF)),
        in_specs=[vmem] * 4 + [smem] * 2,
        out_specs=(vmem, vmem),
        scratch_shapes=[
            pltpu.VMEM((2, ROWS, 2 * HS), BF),
            pltpu.VMEM((2, ROWS, HS), BF),
            pltpu.VMEM((TR, 2 * HS), BF),
            pltpu.VMEM((TR, HS), F32),
            pltpu.VMEM((TR, HS), F32),
            pltpu.VMEM((2, HS, ROWS), F32),
            pltpu.VMEM((2, HS, ROWS), F32),
            pltpu.VMEM((HS, TR), BF),
            pltpu.VMEM((HS, TR), BF),
        ],
        compiler_params=pltpu.CompilerParams(vmem_limit_bytes=VMEM_LIMIT),
    )(
        qg,
        kv,
        tile_mask,
        caption_order.reshape(CLIPS, CAP),
        clip_lengths,
        head_bias,
    )

    token_shape = jax.ShapeDtypeStruct((TR, NH * HS), BF)
    text_shape = jax.ShapeDtypeStruct((CR, NH * HS), BF)
    result = (
        jax.ShapeDtypeStruct((TR, out_cols), BF),
        token_shape,
        token_shape,
        token_shape,
        text_shape,
        text_shape,
    )
    held = pl.pallas_call(
        reduce_kernel,
        out_shape=result,
        in_specs=[vmem, vmem, hbm],
        out_specs=(vmem,) * 6,
        scratch_shapes=[
            pltpu.VMEM((2, 6, NH, HALF, HS), BF),
            pltpu.VMEM((2, 2, NH, HALF, HS), BF),
            pltpu.VMEM((2, NY, 3, 2, BR, HS), BF),
            pltpu.VMEM((2, NY, 2, BR, HS), BF),
            pltpu.VMEM((2, TR, HS), BF),
            pltpu.VMEM((2, TR, HS), BF),
            pltpu.VMEM((2, 2, BR, HS), BF),
            pltpu.VMEM((2, 2, BR, HS), BF),
            pltpu.VMEM((2, 2, TR, HS), BF),
            pltpu.VMEM((TR, NH * HS), BF),
            pltpu.VMEM((4, TR, out_cols), BF),
            pltpu.VMEM((2, TR, out_cols), BF),
            pltpu.VMEM((TR, out_cols), BF),
            pltpu.VMEM((2, HALF, out_cols), BF),
            pltpu.VMEM((TR, out_cols), BF),
            pltpu.VMEM(out_weight.shape, BF),
            dma((34,)),
            dma((34,)),
            dma((1,)),
        ],
        compiler_params=pltpu.CompilerParams(
            collective_id=1, has_side_effects=True, vmem_limit_bytes=VMEM_LIMIT
        ),
    )(oq, kvg, out_weight)
    return pl.pallas_call(
        store_kernel,
        out_shape=result,
        in_specs=[vmem] * len(result),
        out_specs=(hbm,) * len(result),
        scratch_shapes=[dma((len(result),))],
    )(*held)


def solution(mesh):
    in_specs = (
        P("seq", "head"),
        P("seq", "head"),
        P("seq", "head"),
        P("seq", "head"),
        P("seq", "head"),
        P("head"),
        P("head", None),
        P("seq", "head"),
        P(),
        P(),
        P(),
    )
    out_specs = (P("seq", "head"),) * 6
    return jax.shard_map(shards, mesh=mesh, in_specs=in_specs, out_specs=out_specs, check_vma=False)
```

```python
import jax
import jax.numpy as jnp
from jax import lax
from jax.experimental import pallas as pl
from jax.experimental.pallas import tpu as pltpu
from jax.sharding import PartitionSpec as P

MESH = pl.DeviceIdType.MESH
BF = jnp.bfloat16
F32 = jnp.float32

NX, NZ, NY = 4, 4, 2
HS = 128
NH = 3
TR = 256
CR = 16
BR = TR + CR
HALF = TR // 2
CLIPS = 4
CAP = 128
TILE = 64
LAT = NY * NX * TR
ROWS = NY * NX * BR
MASKED = -32768.0
BLOCKS = NH * NZ
VMEM_LIMIT = 58 * 1024 * 1024


def place():
    seq = lax.axis_index("seq")
    head = lax.axis_index("head")
    y = seq // (NZ * NX)
    z = (seq // NX) % NZ
    x = seq % NX
    return seq, head, y, z, x


def peers(seq, head, y, z, x):
    def at(yy, zz, xx):
        return (yy * NZ + zz) * NX + xx

    other_head = (head + 2) % 4
    core_head = head + 1 - 2 * (head % 2)
    return {
        "pair": (at(1 - y, z, x), head),
        "back": (at(1 - y, z, x), other_head),
        "core": (seq, core_head),
        "right": (at(y, z, (x + 1) % NX), head),
        "left": (at(y, z, (x + NX - 1) % NX), head),
        "up": (at(y, (z + 1) % NZ, x), head),
        "down": (at(y, (z + NZ - 1) % NZ, x), head),
    }


def greet(peer):
    barrier = pltpu.get_barrier_semaphore()
    for device in peer.values():
        pl.semaphore_signal(barrier, inc=1, device_id=device, device_id_type=MESH)
    pl.semaphore_wait(barrier, len(peer))


def sender(peer, send_sem, recv_sem, sent):
    def send(n, src, dst, to):
        copy = pltpu.make_async_remote_copy(
            src_ref=src,
            dst_ref=dst,
            send_sem=send_sem.at[n],
            recv_sem=recv_sem.at[n],
            device_id=peer[to],
            device_id_type=MESH,
        )
        copy.start()
        sent.append(copy)

    def arrived(n, dst):
        pltpu.make_async_remote_copy(
            src_ref=dst,
            dst_ref=dst,
            send_sem=send_sem.at[n],
            recv_sem=recv_sem.at[n],
            device_id=peer["core"],
            device_id_type=MESH,
        ).wait_recv()

    return send, arrived


def dot_nt(a, b):
    return lax.dot_general(a, b, (((1,), (1,)), ((), ())), preferred_element_type=F32)


def dot_nn(a, b):
    return lax.dot_general(a, b, (((1,), (0,)), ((), ())), preferred_element_type=F32)


def fused_kernel(
    q_hbm,
    k_hbm,
    v_hbm,
    tk_hbm,
    tv_hbm,
    go_hbm,
    w_hbm,
    tile_hbm,
    order_hbm,
    len_ref,
    bias_ref,
    out_hbm,
    gq_hbm,
    gk_hbm,
    gv_hbm,
    gtk_hbm,
    gtv_hbm,
    q_ref,
    k_ref,
    v_ref,
    tk_ref,
    tv_ref,
    go_ref,
    w_ref,
    tile_ref,
    order_ref,
    out_ref,
    gq_ref,
    gk_ref,
    gv_ref,
    gtk_ref,
    gtv_ref,
    qg_ref,
    kv_ref,
    st_pair,
    q_pair,
    goall,
    go_relay,
    acc,
    kaug,
    qaug,
    weights,
    slopes,
    vtext,
    queries_t,
    grads_t,
    oacc,
    qacc,
    oq_ref,
    kvg_ref,
    z_in,
    z_sum,
    x_in,
    x_sum,
    yq_out,
    yq_in,
    yk_out,
    yk_in,
    keep_q,
    attn,
    part,
    core_in,
    pair_sum,
    out_relay,
    far_in,
    g_send,
    g_recv,
    r_send,
    r_recv,
    local_sem,
    store_sem,
):
    seq, head, y, z, x = place()
    peer = peers(seq, head, y, z, x)
    zu, zd, zf = (z + 1) % NZ, (z + NZ - 1) % NZ, (z + 2) % NZ
    xr, xl, xf = (x + 1) % NX, (x + NX - 1) % NX, (x + 2) % NX
    other_head = (head + 2) % 4
    core_head = head + 1 - 2 * (head % 2)
    core_other = core_head + 2 - 4 * (core_head // 2)
    first, second = pl.ds(0, HALF), pl.ds(HALF, HALF)
    sent = []
    send, arrived = sender(peer, g_send, g_recv, sent)
    rsend, rarrived = sender(peer, r_send, r_recv, sent)
    cols = lambda h: slice(h * HS, (h + 1) * HS)
    by_y = lambda a, b: jnp.where(y == 0, a, b)
    wide = lambda a: a.astype(F32)
    factor = HS ** (-0.5)
    log2e = 1.4426950408889634

    load = []
    for n, (src, dst) in enumerate(
        (
            (k_hbm, k_ref),
            (tk_hbm, tk_ref),
            (v_hbm, v_ref),
            (tv_hbm, tv_ref),
            (q_hbm, q_ref),
            (go_hbm, go_ref),
            (w_hbm, w_ref),
            (tile_hbm, tile_ref),
            (order_hbm, order_ref),
        )
    ):
        copy = pltpu.make_async_copy(src, dst, local_sem.at[n])
        copy.start()
        load.append(copy)

    greet(peer)


    def x_send(a, t, yy):
        c = yy * NX + x
        send(10 + 6 * a + 2 * t, kv_ref.at[t, c], kv_ref.at[t, c], ("right", "left")[t])
        send(11 + 6 * a + 2 * t, kv_ref.at[t, c], kv_ref.at[t, c], ("left", "right")[t])

    def x_forward(a, yy):
        base = 10 + 6 * a
        left, right = yy * NX + xl, yy * NX + xr
        arrived(base + 0, kv_ref.at[0, left])
        send(base + 4, kv_ref.at[0, left], kv_ref.at[0, left], "right")
        arrived(base + 2, kv_ref.at[1, right])
        send(base + 5, kv_ref.at[1, right], kv_ref.at[1, right], "left")

    def x_finish(a, yy):
        base = 10 + 6 * a
        arrived(base + 1, kv_ref.at[0, yy * NX + xr])
        arrived(base + 3, kv_ref.at[1, yy * NX + xl])
        arrived(base + 4, kv_ref.at[0, yy * NX + xf])
        arrived(base + 5, kv_ref.at[1, yy * NX + xf])

    def z_own(t):
        base = 22 + 10 * t
        send(base + 0, qg_ref.at[t, z, 2], qg_ref.at[t, z, 2], "up")
        send(base + 1, qg_ref.at[t, z, y], qg_ref.at[t, z, y], "down")
        send(base + 2, qg_ref.at[t, z, y], qg_ref.at[t, z, y], "up")
        send(base + 3, qg_ref.at[t, z, 2], qg_ref.at[t, z, 2], "down")

    def z_own_forward(t):
        base = 22 + 10 * t
        arrived(base + 0, qg_ref.at[t, zd, 2])
        send(base + 4, qg_ref.at[t, zd, 2], qg_ref.at[t, zd, 2], "up")
        arrived(base + 1, qg_ref.at[t, zu, y])
        send(base + 5, qg_ref.at[t, zu, y], qg_ref.at[t, zu, y], "down")

    def z_pair(t):
        base = 22 + 10 * t
        send(base + 6, qg_ref.at[t, z, 1 - y], qg_ref.at[t, z, 1 - y], "up")
        send(base + 7, qg_ref.at[t, z, 1 - y], qg_ref.at[t, z, 1 - y], "down")

    def z_pair_forward(t):
        base = 22 + 10 * t
        arrived(base + 6, qg_ref.at[t, zd, 1 - y])
        src = qg_ref.at[t, zd, 1 - y, first]
        send(base + 8, src, src, "up")
        arrived(base + 7, qg_ref.at[t, zu, 1 - y])
        src = qg_ref.at[t, zu, 1 - y, second]
        send(base + 9, src, src, "down")

    def z_own_finish(t):
        base = 22 + 10 * t
        arrived(base + 2, qg_ref.at[t, zd, y])
        arrived(base + 3, qg_ref.at[t, zu, 2])
        arrived(base + 4, qg_ref.at[t, zf, 2])
        arrived(base + 5, qg_ref.at[t, zf, y])

    def z_pair_finish(t):
        base = 22 + 10 * t
        arrived(base + 8, qg_ref.at[t, zf, 1 - y, first])
        arrived(base + 9, qg_ref.at[t, zf, 1 - y, second])

    def feature(n):
        return w_ref[:, pl.ds(pl.multiple_of(n * 768, 128), 768)]

    ends = [len_ref[0]]
    for c in range(1, CLIPS):
        ends.append(ends[-1] + len_ref[c])

    def clip_at(pos):
        total = 0
        for c in range(CLIPS - 1):
            total = total + jnp.where(pos >= ends[c], 1, 0)
        return total

    lane = lax.broadcasted_iota(jnp.int32, (1, HS), 1)
    tiles_here = (lane % 64) // 16 == z
    clip_lane = ((z + 1) % NZ) * 16
    bias_lane = clip_lane + CLIPS
    bias_ones = jnp.where((lane >= bias_lane) & (lane < bias_lane + 3), 1.0, 0.0)

    def kv_index(n):
        return ((y + n % 2) % NY) * NX + (x + n // 2) % NX

    def key_side():
        for n in range(NY * NX):
            pos = kv_index(n) // NX * (NZ * NX * TR) + z * (NX * TR) + kv_index(n) % NX * TR
            pos = pos + lax.broadcasted_iota(jnp.int32, (TR, HS), 0)
            hit = (tiles_here & (pos // TILE == lane)) | (clip_at(pos) == lane - clip_lane)
            aug = jnp.where(hit, 1.0, bias_ones).astype(BF)
            for s in range(2):
                kaug[s, n * TR : (n + 1) * TR, HS:] = aug
        row = lax.broadcasted_iota(jnp.int32, (NY * NX * CR, HS), 0)
        n = row // CR
        plane = ((y + n % 2) % NY) * NZ + z
        text_row = (plane * NX + (x + n // 2) % NX) * CR + row % CR
        aug = jnp.broadcast_to(bias_ones, text_row.shape)
        for c in range(CLIPS):
            listed = jnp.where(order_ref[c : c + 1, :] == text_row, 1.0, 0.0)
            found = jnp.max(listed, axis=1, keepdims=True)
            aug = jnp.where(lane == clip_lane + c, found, aug)
        for s in range(2):
            kaug[s, LAT:, HS:] = aug.astype(BF)

    log_len = [
        jnp.log(jnp.full((1, HS), len_ref[c] + CAP, jnp.int32).astype(F32)) for c in range(CLIPS)
    ]

    def query_side(n, carry):
        yq = jnp.where(n // NZ == 1, 1 - y, y)
        start = ((yq * NZ + n % NZ) * NX + x) * TR
        head_bias = bias_ref[jnp.where(n // NZ == 2, 2, y)]
        pos = start + lax.broadcasted_iota(jnp.int32, (TR, HS), 0)
        clip = clip_at(pos)
        offset = jnp.broadcast_to(log_len[CLIPS - 1], (TR, HS))
        for c in range(CLIPS - 2, -1, -1):
            offset = jnp.where(pos < ends[c], log_len[c], offset)
        total = (head_bias - offset) * (HS**0.5)
        hi = total.astype(BF).astype(F32)
        mid = (total - hi).astype(BF).astype(F32)
        low = total - hi - mid
        in_bias = jnp.where(lane == bias_lane, hi, jnp.where(lane == bias_lane + 1, mid, low))
        in_bias = jnp.where((lane >= bias_lane) & (lane < bias_lane + 3), in_bias, 0.0)
        in_clip = (lane >= clip_lane) & (lane < clip_lane + CLIPS) & (lane - clip_lane != clip)
        side = jnp.where(in_clip, MASKED, in_bias)
        for u in range(TR // TILE):
            tile = start // TILE + u
            off = (tile_ref[pl.ds(tile, 1), :] == 0) & (lane != tile) & tiles_here
            rows = slice(u * TILE, (u + 1) * TILE)
            qaug[n, rows, HS:] = jnp.where(off, MASKED, side[rows]).astype(BF)
        return carry

    def block_j(n):
        return jnp.where(n // NZ == 2, 2, jnp.where(n // NZ == 1, 1 - y, y))

    def take_queries(n):
        value = qg_ref[0, n % NZ, n // NZ if n // NZ == 2 else (y + n // NZ) % NY]
        qaug[n, :, 0:HS] = value
        queries_t[:, n * TR : (n + 1) * TR] = value.T

    def take_keys(r):
        for n in range(r, NY * NX, 2):
            for s in range(2):
                kaug[s, n * TR : (n + 1) * TR, 0:HS] = kv_ref[0, kv_index(n), s, 0:TR]
                kaug[s, LAT + n * CR : LAT + (n + 1) * CR, 0:HS] = kv_ref[0, kv_index(n), s, TR:BR]
                vtext[s, n * CR : (n + 1) * CR] = kv_ref[1, kv_index(n), s, TR:BR]

    def weigh(n, slot, first_row, count):
        scores = dot_nt(qaug[n], kaug[slot, first_row : first_row + count, :])
        e = jnp.exp2(jnp.minimum(scores * (factor * log2e), 115.0))
        rest = pl.reciprocal(1.0 + e, approx=True)
        sig = e * rest
        weight = sig.astype(BF)
        rows = pl.ds(pl.multiple_of(n * TR, TR), TR)
        weights[rows, first_row : first_row + count] = weight
        slopes[rows, first_row : first_row + count] = (sig * rest).astype(BF)
        return weight

    def forward(n, r, slot, text):
        total = None
        for d in range(NX):
            c = 2 * d + r
            weight = weigh(n, slot, c * TR, TR)
            share = dot_nn(weight, kv_ref[1, kv_index(c), slot, 0:TR])
            total = share if total is None else total + share
        if text:
            total = total + dot_nn(weigh(n, slot, LAT, NY * NX * CR), vtext[slot])
        if r == 0:
            oacc[n] = total
        else:
            oq_ref[0, n % NZ, block_j(n)] = (oacc[n] + total).astype(BF)

    def forward_blocks(low, high, r, text):
        def body(n, carry):
            forward(n, r, n // (2 * NZ), text)
            return carry

        lax.fori_loop(low, high, body, 0)

    def slope_blocks(first_row, count):
        def body(n, carry):
            slot = n // (2 * NZ)
            rows = pl.ds(pl.multiple_of(n * TR, TR), TR)
            slope = wide(slopes[rows, first_row : first_row + count])
            grads = qg_ref[1, n % NZ, block_j(n)]
            if first_row == LAT:
                vals = vtext[slot]
            else:
                c = first_row // TR
                vals = jnp.concatenate(
                    [kv_ref[1, kv_index(c + r), slot, 0:TR] for r in range(2)], axis=0
                )
            product = dot_nt(grads, vals)
            slope = (product * slope).astype(BF)
            slopes[rows, first_row : first_row + count] = slope
            share = dot_nn(slope, kaug[slot, first_row : first_row + count, 0:HS])
            if first_row == LAT:
                qacc[n] = share
            else:
                qacc[n] += share
            return carry

        lax.fori_loop(0, BLOCKS, body, 0)

    def key_grads(first_row, count):
        for s, (low, high) in enumerate(((0, 2 * NZ * TR), (2 * NZ * TR, BLOCKS * TR))):
            for t in range(2):
                left = (queries_t, grads_t)[t][:, low:high]
                right = (slopes, weights)[t][low:high, first_row : first_row + count]
                total = dot_nn(left, right).astype(BF)
                if first_row == LAT:
                    text_rows = total.T
                    for n in range(NY * NX):
                        kvg_ref[t, kv_index(n), s, TR:BR] = text_rows[n * CR : (n + 1) * CR]
                else:
                    for r in range(2):
                        n = first_row // TR + r
                        kvg_ref[t, kv_index(n), s, 0:TR] = total[:, r * TR : (r + 1) * TR].T


    def z_start(t):
        base = 6 * t
        rsend(base + 0, oq_ref.at[t, zf, :, first], z_in.at[t, 0], "up")
        rsend(base + 3, oq_ref.at[t, zf, :, second], z_in.at[t, 3], "down")
        rsend(base + 1, oq_ref.at[t, zd, :, first], z_in.at[t, 1], "down")
        rsend(base + 4, oq_ref.at[t, zu, :, second], z_in.at[t, 4], "up")

    def z_relay(t):
        base = 6 * t
        rarrived(base + 0, z_in.at[t, 0])
        z_sum[t, 0] = (wide(z_in[t, 0]) + wide(oq_ref[t, zu, :, first])).astype(BF)
        rsend(base + 2, z_sum.at[t, 0], z_in.at[t, 2], "up")
        rarrived(base + 3, z_in.at[t, 3])
        z_sum[t, 1] = (wide(z_in[t, 3]) + wide(oq_ref[t, zd, :, second])).astype(BF)
        rsend(base + 5, z_sum.at[t, 1], z_in.at[t, 5], "down")

    def z_total(t, scale):
        base = 6 * t
        for n in (1, 2, 4, 5):
            rarrived(base + n, z_in.at[t, n])
        for rows, one, two in ((first, 1, 2), (second, 4, 5)):

            def total(j):
                value = wide(oq_ref[t, z, j, rows]) + wide(z_in[t, one, j]) + wide(z_in[t, two, j])
                return (value * scale).astype(BF) if scale != 1.0 else value.astype(BF)

            yq_out[t, rows] = total(1 - y)
            keep_q[t, 0, rows] = total(y)
            keep_q[t, 1, rows] = total(2)
        rsend(24 + t, yq_out.at[t], yq_in.at[t], "pair")

    def x_base(t, a):
        return 12 + 6 * t + 3 * a

    ring = (("right", "left"), ("left", "right"))
    ahead = ((xr, xl), (xl, xr))
    plane = (y, 1 - y)

    def x_far(t, a):
        src = kvg_ref.at[t, plane[a] * NX + xf]
        rsend(x_base(t, a), src, x_in.at[t, a, 0], ring[t][0])

    def x_near(t, a):
        src = kvg_ref.at[t, plane[a] * NX + ahead[t][1]]
        rsend(x_base(t, a) + 1, src, x_in.at[t, a, 1], ring[t][1])

    def x_relay(t, a):
        rarrived(x_base(t, a), x_in.at[t, a, 0])
        mine = wide(kvg_ref[t, plane[a] * NX + ahead[t][0]])
        x_sum[t, a] = (wide(x_in[t, a, 0]) + mine).astype(BF)
        rsend(x_base(t, a) + 2, x_sum.at[t, a], x_in.at[t, a, 2], ring[t][0])

    def x_total(t, a):
        rarrived(x_base(t, a) + 1, x_in.at[t, a, 1])
        rarrived(x_base(t, a) + 2, x_in.at[t, a, 2])
        value = wide(kvg_ref[t, plane[a] * NX + x]) + wide(x_in[t, a, 1]) + wide(x_in[t, a, 2])
        return value * factor if t == 0 else value

    def project(n):
        return dot_nn(attn[...], feature(n)).astype(BF)

    send(0, go_hbm.at[first], go_relay.at[0], "pair")
    send(1, go_hbm.at[second], go_relay.at[1], "back")
    send(2, go_hbm, goall.at[head], "core")
    c = y * NX + x
    for t, (ref, text) in enumerate(((k_ref, tk_ref), (v_ref, tv_ref))):
        load[2 * t].wait()
        load[2 * t + 1].wait()
        kv_ref[t, c, 0, 0:TR] = by_y(ref[:, cols(0)], ref[:, cols(1)])
        kv_ref[t, c, 0, TR:BR] = by_y(text[:, cols(0)], text[:, cols(1)])
        kv_ref[t, c, 1, 0:TR] = ref[:, cols(2)]
        kv_ref[t, c, 1, TR:BR] = text[:, cols(2)]
        x_send(0, t, y)
        st_pair[t, 0, 0:TR] = by_y(ref[:, cols(1)], ref[:, cols(0)])
        st_pair[t, 0, TR:BR] = by_y(text[:, cols(1)], text[:, cols(0)])
        st_pair[t, 1, 0:TR] = ref[:, cols(2)]
        st_pair[t, 1, TR:BR] = text[:, cols(2)]
        send(7 + t, st_pair.at[t], kv_ref.at[t, c], "pair")
    load[4].wait()
    qg_ref[0, z, y] = by_y(q_ref[:, cols(0)], q_ref[:, cols(1)])
    qg_ref[0, z, 2] = q_ref[:, cols(2)]
    q_pair[0] = by_y(q_ref[:, cols(1)], q_ref[:, cols(0)])
    send(6, q_pair.at[0], qg_ref.at[0, z, y], "pair")
    z_own(0)
    load[5].wait()
    load[6].wait()
    acc[...] = dot_nt(go_ref[...], feature(head))
    load[7].wait()
    load[8].wait()
    key_side()
    lax.fori_loop(0, BLOCKS, query_side, 0)

    arrived(1, go_relay.at[1])
    send(4, go_relay.at[1], goall.at[other_head, second], "pair")
    z_own_forward(0)
    arrived(6, qg_ref.at[0, z, 1 - y])
    z_pair(0)
    arrived(0, go_relay.at[0])
    send(3, go_relay.at[0], goall.at[head, first], "back")
    x_forward(0, y)
    arrived(2, goall.at[core_head])
    acc[...] += dot_nt(goall[core_head], feature(core_head))
    z_own_finish(0)
    for n in (0, 1, 2, 3, 8, 9, 10, 11):
        take_queries(n)
    z_pair_forward(0)
    for t in range(2):
        arrived(7 + t, kv_ref.at[t, (1 - y) * NX + x])
        x_send(1, t, 1 - y)
    x_finish(0, y)
    take_keys(0)
    forward_blocks(0, NZ, 0, False)
    arrived(3, goall.at[other_head, first])
    arrived(4, goall.at[other_head, second])
    send(5, goall.at[other_head], goall.at[other_head], "core")
    acc[...] += dot_nt(goall[other_head], feature(other_head))
    forward_blocks(2 * NZ, 3 * NZ, 0, False)
    arrived(5, goall.at[core_other])
    grad = (acc[...] + dot_nt(goall[core_other], feature(core_other))).astype(BF)
    q_pair[1] = by_y(grad[:, cols(1)], grad[:, cols(0)])
    send(9, q_pair.at[1], qg_ref.at[1, z, y], "pair")
    qg_ref[1, z, y] = by_y(grad[:, cols(0)], grad[:, cols(1)])
    qg_ref[1, z, 2] = grad[:, cols(2)]
    z_own(1)
    x_forward(1, 1 - y)
    z_pair_finish(0)
    for n in range(NZ, 2 * NZ):
        take_queries(n)
    forward_blocks(NZ, 2 * NZ, 0, False)
    arrived(9, qg_ref.at[1, z, 1 - y])
    z_pair(1)
    z_own_forward(1)
    x_finish(1, 1 - y)
    take_keys(1)
    forward_blocks(0, NZ, 1, True)
    z_pair_forward(1)
    forward_blocks(NZ, 3 * NZ, 1, True)
    z_start(0)

    z_own_finish(1)
    z_pair_finish(1)
    for n in range(BLOCKS):
        j = 2 if n // NZ == 2 else (y + n // NZ) % NY
        grads_t[:, n * TR : (n + 1) * TR] = qg_ref[1, n % NZ, j].T
    slope_blocks(LAT, NY * NX * CR)
    key_grads(LAT, NY * NX * CR)
    pair_rows = 2 * TR

    slope_blocks(2 * pair_rows, pair_rows)
    z_relay(0)
    key_grads(2 * pair_rows, pair_rows)
    for a in (1, 0):
        for t in range(2):
            x_far(t, a)

    slope_blocks(1 * pair_rows, pair_rows)
    z_total(0, 1.0)
    key_grads(1 * pair_rows, pair_rows)
    for a in (1, 0):
        x_near(1, a)
        x_relay(0, a)

    rarrived(24, yq_in.at[0])
    attn[:, cols(0)] = by_y(keep_q[0, 0], yq_in[0])
    attn[:, cols(1)] = by_y(yq_in[0], keep_q[0, 0])
    attn[:, cols(2)] = keep_q[0, 1]
    part[0] = project(core_other)
    rsend(28, part.at[0], core_in.at[0], "core")
    part[1] = project(core_head)
    rsend(29, part.at[1], core_in.at[1], "core")
    part[2] = project(other_head)
    slope_blocks(3 * pair_rows, pair_rows)
    rarrived(28, core_in.at[0])
    pair_sum[...] = (wide(part[2]) + wide(core_in[0])).astype(BF)
    rsend(30, pair_sum.at[first], out_relay.at[0], "pair")
    rsend(31, pair_sum.at[second], out_relay.at[1], "back")
    key_grads(3 * pair_rows, pair_rows)
    for a in (1, 0):
        x_near(0, a)
        x_relay(1, a)

    slope_blocks(0, pair_rows)
    for n in range(BLOCKS):
        j = 2 if n // NZ == 2 else (y + n // NZ) % NY
        oq_ref[1, n % NZ, j] = qacc[n].astype(BF)
    z_start(1)
    key_grads(0, pair_rows)
    part[3] = project(head)
    rarrived(31, out_relay.at[1])
    rsend(33, out_relay.at[1], far_in.at[second], "pair")
    rarrived(30, out_relay.at[0])
    rsend(32, out_relay.at[0], far_in.at[first], "back")
    z_relay(1)
    for t in range(2):
        yk_out[t] = x_total(t, 1).astype(BF)
        rsend(26 + t, yk_out.at[t], yk_in.at[t], "pair")
    z_total(1, factor)

    stores = []

    def store(src, dst):
        copy = pltpu.make_async_copy(src, dst, store_sem.at[len(stores)])
        copy.start()
        stores.append(copy)

    results = ((gk_ref, gtk_ref, gk_hbm, gtk_hbm), (gv_ref, gtv_ref, gv_hbm, gtv_hbm))
    rarrived(29, core_in.at[1])
    rarrived(32, far_in.at[first])
    rarrived(33, far_in.at[second])
    out_ref[...] = (wide(part[3]) + wide(core_in[1]) + wide(far_in[...])).astype(BF)
    store(out_ref, out_hbm)
    for t, (ref, text, to, text_to) in enumerate(results):
        own = x_total(t, 0)
        rarrived(26 + t, yk_in.at[t])
        mine = own[0].astype(BF)
        other = yk_in[t, 0]
        both = (own[1] + wide(yk_in[t, 1])).astype(BF)
        for h, value in ((0, by_y(mine, other)), (1, by_y(other, mine)), (2, both)):
            ref[:, cols(h)] = value[0:TR]
            text[:, cols(h)] = value[TR:BR]
        store(ref, to)
        store(text, text_to)
    rarrived(25, yq_in.at[1])
    gq_ref[:, cols(0)] = by_y(keep_q[1, 0], yq_in[1])
    gq_ref[:, cols(1)] = by_y(yq_in[1], keep_q[1, 0])
    gq_ref[:, cols(2)] = keep_q[1, 1]
    store(gq_ref, gq_hbm)
    for copy in sent:
        copy.wait_send()
    for copy in stores:
        copy.wait()


def store_kernel(*refs):
    count = len(refs) // 2
    sems = refs[-1]
    copies = [
        pltpu.make_async_copy(refs[n], refs[count + n], sems.at[n]) for n in range(count)
    ]
    for copy in copies:
        copy.start()
    for copy in copies:
        copy.wait()


def shards(
    queries,
    keys,
    values,
    text_keys,
    text_values,
    head_bias,
    out_weight,
    grad_out,
    clip_lengths,
    tile_mask,
    caption_order,
):
    smem = pl.BlockSpec(memory_space=pltpu.SMEM)
    hbm = pl.BlockSpec(memory_space=pltpu.HBM)
    dma = pltpu.SemaphoreType.DMA
    qg_shape = (2, NZ, NH, TR, HS)
    kv_shape = (2, NY * NX, 2, BR, HS)
    out_cols = grad_out.shape[1]
    order = caption_order.reshape(CLIPS, CAP)
    token = pltpu.VMEM((TR, NH * HS), BF)
    text = pltpu.VMEM((CR, NH * HS), BF)
    wide_out = pltpu.VMEM((TR, out_cols), BF)
    halves = pltpu.VMEM((2, HALF, out_cols), BF)
    token_shape = jax.ShapeDtypeStruct((TR, NH * HS), BF)
    text_shape = jax.ShapeDtypeStruct((CR, NH * HS), BF)
    result = (
        jax.ShapeDtypeStruct((TR, out_cols), BF),
        token_shape,
        token_shape,
        token_shape,
        text_shape,
        text_shape,
    )
    held = pl.pallas_call(
        fused_kernel,
        out_shape=result,
        in_specs=[hbm] * 9 + [smem] * 2,
        out_specs=(hbm,) * len(result),
        scratch_shapes=[
            token,
            token,
            token,
            text,
            text,
            wide_out,
            pltpu.VMEM(out_weight.shape, BF),
            pltpu.VMEM(tile_mask.shape, jnp.int32),
            pltpu.VMEM(order.shape, jnp.int32),
            wide_out,
            token,
            token,
            token,
            text,
            text,
            pltpu.VMEM(qg_shape, BF),
            pltpu.VMEM(kv_shape, BF),
            pltpu.VMEM((2, 2, BR, HS), BF),
            pltpu.VMEM((2, TR, HS), BF),
            pltpu.VMEM((4, TR, out_cols), BF),
            halves,
            pltpu.VMEM((TR, NH * HS), F32),
            pltpu.VMEM((2, ROWS, 2 * HS), BF),
            pltpu.VMEM((BLOCKS, TR, 2 * HS), BF),
            pltpu.VMEM((BLOCKS * TR, ROWS), BF),
            pltpu.VMEM((BLOCKS * TR, ROWS), BF),
            pltpu.VMEM((2, NY * NX * CR, HS), BF),
            pltpu.VMEM((HS, BLOCKS * TR), BF),
            pltpu.VMEM((HS, BLOCKS * TR), BF),
            pltpu.VMEM((BLOCKS, TR, HS), F32),
            pltpu.VMEM((BLOCKS, TR, HS), F32),
            pltpu.VMEM(qg_shape, BF),
            pltpu.VMEM(kv_shape, BF),
            pltpu.VMEM((2, 6, NH, HALF, HS), BF),
            pltpu.VMEM((2, 2, NH, HALF, HS), BF),
            pltpu.VMEM((2, NY, 3, 2, BR, HS), BF),
            pltpu.VMEM((2, NY, 2, BR, HS), BF),
            pltpu.VMEM((2, TR, HS), BF),
            pltpu.VMEM((2, TR, HS), BF),
            pltpu.VMEM((2, 2, BR, HS), BF),
            pltpu.VMEM((2, 2, BR, HS), BF),
            pltpu.VMEM((2, 2, TR, HS), BF),
            token,
            pltpu.VMEM((4, TR, out_cols), BF),
            pltpu.VMEM((2, TR, out_cols), BF),
            wide_out,
            halves,
            wide_out,
            dma((42,)),
            dma((42,)),
            dma((34,)),
            dma((34,)),
            dma((9,)),
            dma((len(result),)),
        ],
        compiler_params=pltpu.CompilerParams(
            collective_id=0, has_side_effects=True, vmem_limit_bytes=VMEM_LIMIT
        ),
    )(
        queries,
        keys,
        values,
        text_keys,
        text_values,
        grad_out,
        out_weight,
        tile_mask,
        order,
        clip_lengths,
        head_bias,
    )
    return pl.pallas_call(
        store_kernel,
        out_shape=result,
        in_specs=[hbm] * len(result),
        out_specs=(hbm,) * len(result),
        scratch_shapes=[dma((len(result),))],
        compiler_params=pltpu.CompilerParams(vmem_limit_bytes=VMEM_LIMIT),
    )(*held)


def solution(mesh):
    in_specs = (
        P("seq", "head"),
        P("seq", "head"),
        P("seq", "head"),
        P("seq", "head"),
        P("seq", "head"),
        P("head"),
        P("head", None),
        P("seq", "head"),
        P(),
        P(),
        P(),
    )
    out_specs = (P("seq", "head"),) * 6
    return jax.shard_map(shards, mesh=mesh, in_specs=in_specs, out_specs=out_specs, check_vma=False)
```

```python
import jax
import jax.numpy as jnp
from jax import lax
from jax.experimental import pallas as pl
from jax.experimental.pallas import tpu as pltpu
from jax.sharding import PartitionSpec as P

MESH = pl.DeviceIdType.MESH
BF = jnp.bfloat16
F32 = jnp.float32

NX, NZ, NY = 4, 4, 2
HS = 128
NH = 3
TR = 256
CR = 16
BR = TR + CR
HALF = TR // 2
CLIPS = 4
CAP = 128
TILE = 64
LAT = NY * NX * TR
ROWS = NY * NX * BR
MASKED = -32768.0
BLOCKS = NH * NZ
VMEM_LIMIT = 58 * 1024 * 1024


def place():
    seq = lax.axis_index("seq")
    head = lax.axis_index("head")
    y = seq // (NZ * NX)
    z = (seq // NX) % NZ
    x = seq % NX
    return seq, head, y, z, x


def peers(seq, head, y, z, x):
    def at(yy, zz, xx):
        return (yy * NZ + zz) * NX + xx

    other_head = (head + 2) % 4
    core_head = head + 1 - 2 * (head % 2)
    return {
        "pair": (at(1 - y, z, x), head),
        "back": (at(1 - y, z, x), other_head),
        "core": (seq, core_head),
        "right": (at(y, z, (x + 1) % NX), head),
        "left": (at(y, z, (x + NX - 1) % NX), head),
        "up": (at(y, (z + 1) % NZ, x), head),
        "down": (at(y, (z + NZ - 1) % NZ, x), head),
    }


def greet(peer):
    barrier = pltpu.get_barrier_semaphore()
    for device in peer.values():
        pl.semaphore_signal(barrier, inc=1, device_id=device, device_id_type=MESH)
    pl.semaphore_wait(barrier, len(peer))


def sender(peer, send_sem, recv_sem, sent):
    def send(n, src, dst, to):
        copy = pltpu.make_async_remote_copy(
            src_ref=src,
            dst_ref=dst,
            send_sem=send_sem.at[n],
            recv_sem=recv_sem.at[n],
            device_id=peer[to],
            device_id_type=MESH,
        )
        copy.start()
        sent.append(copy)

    def arrived(n, dst):
        pltpu.make_async_remote_copy(
            src_ref=dst,
            dst_ref=dst,
            send_sem=send_sem.at[n],
            recv_sem=recv_sem.at[n],
            device_id=peer["core"],
            device_id_type=MESH,
        ).wait_recv()

    return send, arrived


def dot_nt(a, b):
    return lax.dot_general(a, b, (((1,), (1,)), ((), ())), preferred_element_type=F32)


def dot_nn(a, b):
    return lax.dot_general(a, b, (((1,), (0,)), ((), ())), preferred_element_type=F32)


def fused_kernel(
    q_hbm,
    k_hbm,
    v_hbm,
    tk_hbm,
    tv_hbm,
    go_hbm,
    w_hbm,
    tile_hbm,
    order_hbm,
    len_ref,
    bias_ref,
    out_hbm,
    gq_hbm,
    gk_hbm,
    gv_hbm,
    gtk_hbm,
    gtv_hbm,
    q_ref,
    k_ref,
    v_ref,
    tk_ref,
    tv_ref,
    go_ref,
    w_ref,
    tile_ref,
    order_ref,
    out_ref,
    gq_ref,
    gk_ref,
    gv_ref,
    gtk_ref,
    gtv_ref,
    qg_ref,
    kv_ref,
    st_pair,
    q_pair,
    goall,
    go_relay,
    acc,
    kaug,
    qaug,
    weights,
    slopes,
    vtext,
    queries_t,
    grads_t,
    oacc,
    qacc,
    oq_ref,
    kvg_ref,
    z_in,
    z_sum,
    x_in,
    x_sum,
    yq_out,
    yq_in,
    yk_out,
    yk_in,
    keep_q,
    attn,
    part,
    core_in,
    pair_sum,
    out_relay,
    far_in,
    g_send,
    g_recv,
    r_send,
    r_recv,
    local_sem,
    store_sem,
):
    seq, head, y, z, x = place()
    peer = peers(seq, head, y, z, x)
    zu, zd, zf = (z + 1) % NZ, (z + NZ - 1) % NZ, (z + 2) % NZ
    xr, xl, xf = (x + 1) % NX, (x + NX - 1) % NX, (x + 2) % NX
    other_head = (head + 2) % 4
    core_head = head + 1 - 2 * (head % 2)
    core_other = core_head + 2 - 4 * (core_head // 2)
    first, second = pl.ds(0, HALF), pl.ds(HALF, HALF)
    sent = []
    send, arrived = sender(peer, g_send, g_recv, sent)
    rsend, rarrived = sender(peer, r_send, r_recv, sent)
    cols = lambda h: slice(h * HS, (h + 1) * HS)
    by_y = lambda a, b: jnp.where(y == 0, a, b)
    wide = lambda a: a.astype(F32)
    factor = HS ** (-0.5)
    log2e = 1.4426950408889634

    load = []
    for n, (src, dst) in enumerate(
        (
            (k_hbm, k_ref),
            (tk_hbm, tk_ref),
            (v_hbm, v_ref),
            (tv_hbm, tv_ref),
            (q_hbm, q_ref),
            (go_hbm, go_ref),
            (w_hbm, w_ref),
            (tile_hbm, tile_ref),
            (order_hbm, order_ref),
        )
    ):
        copy = pltpu.make_async_copy(src, dst, local_sem.at[n])
        copy.start()
        load.append(copy)

    greet(peer)


    def x_send(a, t, yy):
        c = yy * NX + x
        send(10 + 6 * a + 2 * t, kv_ref.at[t, c], kv_ref.at[t, c], ("right", "left")[t])
        send(11 + 6 * a + 2 * t, kv_ref.at[t, c], kv_ref.at[t, c], ("left", "right")[t])

    def x_forward(a, yy):
        base = 10 + 6 * a
        left, right = yy * NX + xl, yy * NX + xr
        arrived(base + 0, kv_ref.at[0, left])
        send(base + 4, kv_ref.at[0, left], kv_ref.at[0, left], "right")
        arrived(base + 2, kv_ref.at[1, right])
        send(base + 5, kv_ref.at[1, right], kv_ref.at[1, right], "left")

    def x_near_finish(a, yy):
        base = 10 + 6 * a
        arrived(base + 1, kv_ref.at[0, yy * NX + xr])
        arrived(base + 3, kv_ref.at[1, yy * NX + xl])

    def x_far_finish(a, yy):
        base = 10 + 6 * a
        arrived(base + 4, kv_ref.at[0, yy * NX + xf])
        arrived(base + 5, kv_ref.at[1, yy * NX + xf])

    def z_own(t):
        base = 22 + 10 * t
        send(base + 0, qg_ref.at[t, z, 2], qg_ref.at[t, z, 2], "up")
        send(base + 1, qg_ref.at[t, z, y], qg_ref.at[t, z, y], "down")
        send(base + 2, qg_ref.at[t, z, y], qg_ref.at[t, z, y], "up")
        send(base + 3, qg_ref.at[t, z, 2], qg_ref.at[t, z, 2], "down")

    def z_own_forward(t):
        base = 22 + 10 * t
        arrived(base + 0, qg_ref.at[t, zd, 2])
        send(base + 4, qg_ref.at[t, zd, 2], qg_ref.at[t, zd, 2], "up")
        arrived(base + 1, qg_ref.at[t, zu, y])
        send(base + 5, qg_ref.at[t, zu, y], qg_ref.at[t, zu, y], "down")

    def z_pair(t):
        base = 22 + 10 * t
        send(base + 6, qg_ref.at[t, z, 1 - y], qg_ref.at[t, z, 1 - y], "up")
        send(base + 7, qg_ref.at[t, z, 1 - y], qg_ref.at[t, z, 1 - y], "down")

    def z_pair_forward(t):
        base = 22 + 10 * t
        arrived(base + 6, qg_ref.at[t, zd, 1 - y])
        src = qg_ref.at[t, zd, 1 - y, first]
        send(base + 8, src, src, "up")
        arrived(base + 7, qg_ref.at[t, zu, 1 - y])
        src = qg_ref.at[t, zu, 1 - y, second]
        send(base + 9, src, src, "down")

    def z_own_finish(t):
        base = 22 + 10 * t
        arrived(base + 2, qg_ref.at[t, zd, y])
        arrived(base + 3, qg_ref.at[t, zu, 2])
        arrived(base + 4, qg_ref.at[t, zf, 2])
        arrived(base + 5, qg_ref.at[t, zf, y])

    def z_pair_finish(t):
        base = 22 + 10 * t
        arrived(base + 8, qg_ref.at[t, zf, 1 - y, first])
        arrived(base + 9, qg_ref.at[t, zf, 1 - y, second])

    def feature(n):
        return w_ref[:, pl.ds(pl.multiple_of(n * 768, 128), 768)]

    ends = [len_ref[0]]
    for c in range(1, CLIPS):
        ends.append(ends[-1] + len_ref[c])

    def clip_at(pos):
        total = 0
        for c in range(CLIPS - 1):
            total = total + jnp.where(pos >= ends[c], 1, 0)
        return total

    lane = lax.broadcasted_iota(jnp.int32, (1, HS), 1)
    tiles_here = (lane % 64) // 16 == z
    clip_lane = ((z + 1) % NZ) * 16
    bias_lane = clip_lane + CLIPS
    bias_ones = jnp.where((lane >= bias_lane) & (lane < bias_lane + 3), 1.0, 0.0)

    def kv_index(n):
        return ((y + n % 2) % NY) * NX + (x + n // 2) % NX

    def key_side():
        for n in range(NY * NX):
            pos = kv_index(n) // NX * (NZ * NX * TR) + z * (NX * TR) + kv_index(n) % NX * TR
            pos = pos + lax.broadcasted_iota(jnp.int32, (TR, HS), 0)
            hit = (tiles_here & (pos // TILE == lane)) | (clip_at(pos) == lane - clip_lane)
            aug = jnp.where(hit, 1.0, bias_ones).astype(BF)
            for s in range(2):
                kaug[s, n * TR : (n + 1) * TR, HS:] = aug
        row = lax.broadcasted_iota(jnp.int32, (NY * NX * CR, HS), 0)
        n = row // CR
        plane = ((y + n % 2) % NY) * NZ + z
        text_row = (plane * NX + (x + n // 2) % NX) * CR + row % CR
        aug = jnp.broadcast_to(bias_ones, text_row.shape)
        for c in range(CLIPS):
            listed = jnp.where(order_ref[c : c + 1, :] == text_row, 1.0, 0.0)
            found = jnp.max(listed, axis=1, keepdims=True)
            aug = jnp.where(lane == clip_lane + c, found, aug)
        for s in range(2):
            kaug[s, LAT:, HS:] = aug.astype(BF)

    log_len = [
        jnp.log(jnp.full((1, HS), len_ref[c] + CAP, jnp.int32).astype(F32)) for c in range(CLIPS)
    ]

    def query_side(n, carry):
        yq = jnp.where(n // NZ == 1, 1 - y, y)
        start = ((yq * NZ + n % NZ) * NX + x) * TR
        head_bias = bias_ref[jnp.where(n // NZ == 2, 2, y)]
        pos = start + lax.broadcasted_iota(jnp.int32, (TR, HS), 0)
        clip = clip_at(pos)
        offset = jnp.broadcast_to(log_len[CLIPS - 1], (TR, HS))
        for c in range(CLIPS - 2, -1, -1):
            offset = jnp.where(pos < ends[c], log_len[c], offset)
        total = (head_bias - offset) * (HS**0.5)
        hi = total.astype(BF).astype(F32)
        mid = (total - hi).astype(BF).astype(F32)
        low = total - hi - mid
        in_bias = jnp.where(lane == bias_lane, hi, jnp.where(lane == bias_lane + 1, mid, low))
        in_bias = jnp.where((lane >= bias_lane) & (lane < bias_lane + 3), in_bias, 0.0)
        in_clip = (lane >= clip_lane) & (lane < clip_lane + CLIPS) & (lane - clip_lane != clip)
        side = jnp.where(in_clip, MASKED, in_bias)
        for u in range(TR // TILE):
            tile = start // TILE + u
            off = (tile_ref[pl.ds(tile, 1), :] == 0) & (lane != tile) & tiles_here
            rows = slice(u * TILE, (u + 1) * TILE)
            qaug[n, rows, HS:] = jnp.where(off, MASKED, side[rows]).astype(BF)
        return carry

    def block_j(n):
        return jnp.where(n // NZ == 2, 2, jnp.where(n // NZ == 1, 1 - y, y))

    def take_queries(n):
        value = qg_ref[0, n % NZ, n // NZ if n // NZ == 2 else (y + n // NZ) % NY]
        qaug[n, :, 0:HS] = value
        queries_t[:, n * TR : (n + 1) * TR] = value.T

    def take_key(n):
        for s in range(2):
            kaug[s, n * TR : (n + 1) * TR, 0:HS] = kv_ref[0, kv_index(n), s, 0:TR]
            kaug[s, LAT + n * CR : LAT + (n + 1) * CR, 0:HS] = kv_ref[0, kv_index(n), s, TR:BR]
            vtext[s, n * CR : (n + 1) * CR] = kv_ref[1, kv_index(n), s, TR:BR]

    def weigh(n, slot, first_row, count):
        scores = dot_nt(qaug[n], kaug[slot, first_row : first_row + count, :])
        e = jnp.exp2(jnp.minimum(scores * (factor * log2e), 115.0))
        rest = pl.reciprocal(1.0 + e, approx=True)
        sig = e * rest
        weight = sig.astype(BF)
        rows = pl.ds(pl.multiple_of(n * TR, TR), TR)
        weights[rows, first_row : first_row + count] = weight
        slopes[rows, first_row : first_row + count] = (sig * rest).astype(BF)
        return weight

    def per_plane(body):
        def step(zq, carry):
            for g in range(NH):
                body(g * NZ + zq, g // 2)
            return carry

        lax.fori_loop(0, NZ, step, 0)

    def forward(c, fresh=False):
        take_key(c)

        def body(n, slot):
            share = dot_nn(weigh(n, slot, c * TR, TR), kv_ref[1, kv_index(c), slot, 0:TR])
            if fresh:
                oacc[n] = share
            else:
                oacc[n] += share

        per_plane(body)

    def forward_text():
        def body(n, slot):
            share = dot_nn(weigh(n, slot, LAT, NY * NX * CR), vtext[slot])
            oq_ref[0, n % NZ, block_j(n)] = (oacc[n] + share).astype(BF)

        per_plane(body)

    def slope_blocks(first_row, count):
        def body(n, slot):
            rows = pl.ds(pl.multiple_of(n * TR, TR), TR)
            slope = wide(slopes[rows, first_row : first_row + count])
            grads = qg_ref[1, n % NZ, block_j(n)]
            if first_row == LAT:
                vals = vtext[slot]
            else:
                c = first_row // TR
                vals = jnp.concatenate(
                    [kv_ref[1, kv_index(c + r), slot, 0:TR] for r in range(2)], axis=0
                )
            product = dot_nt(grads, vals)
            slope = (product * slope).astype(BF)
            slopes[rows, first_row : first_row + count] = slope
            share = dot_nn(slope, kaug[slot, first_row : first_row + count, 0:HS])
            if first_row == LAT:
                qacc[n] = share
            else:
                qacc[n] += share

        per_plane(body)

    def key_grads(first_row, count):
        for s, (low, high) in enumerate(((0, 2 * NZ * TR), (2 * NZ * TR, BLOCKS * TR))):
            for t in range(2):
                left = (queries_t, grads_t)[t][:, low:high]
                right = (slopes, weights)[t][low:high, first_row : first_row + count]
                total = dot_nn(left, right).astype(BF)
                if first_row == LAT:
                    text_rows = total.T
                    for n in range(NY * NX):
                        kvg_ref[t, kv_index(n), s, TR:BR] = text_rows[n * CR : (n + 1) * CR]
                else:
                    for r in range(2):
                        n = first_row // TR + r
                        kvg_ref[t, kv_index(n), s, 0:TR] = total[:, r * TR : (r + 1) * TR].T


    def z_start(t):
        base = 6 * t
        rsend(base + 0, oq_ref.at[t, zf, :, first], z_in.at[t, 0], "up")
        rsend(base + 3, oq_ref.at[t, zf, :, second], z_in.at[t, 3], "down")
        rsend(base + 1, oq_ref.at[t, zd, :, first], z_in.at[t, 1], "down")
        rsend(base + 4, oq_ref.at[t, zu, :, second], z_in.at[t, 4], "up")

    def z_relay(t):
        base = 6 * t
        rarrived(base + 0, z_in.at[t, 0])
        z_sum[t, 0] = (wide(z_in[t, 0]) + wide(oq_ref[t, zu, :, first])).astype(BF)
        rsend(base + 2, z_sum.at[t, 0], z_in.at[t, 2], "up")
        rarrived(base + 3, z_in.at[t, 3])
        z_sum[t, 1] = (wide(z_in[t, 3]) + wide(oq_ref[t, zd, :, second])).astype(BF)
        rsend(base + 5, z_sum.at[t, 1], z_in.at[t, 5], "down")

    def z_total(t, scale):
        base = 6 * t
        for n in (1, 2, 4, 5):
            rarrived(base + n, z_in.at[t, n])
        for rows, one, two in ((first, 1, 2), (second, 4, 5)):

            def total(j):
                value = wide(oq_ref[t, z, j, rows]) + wide(z_in[t, one, j]) + wide(z_in[t, two, j])
                return (value * scale).astype(BF) if scale != 1.0 else value.astype(BF)

            yq_out[t, rows] = total(1 - y)
            keep_q[t, 0, rows] = total(y)
            keep_q[t, 1, rows] = total(2)
        rsend(24 + t, yq_out.at[t], yq_in.at[t], "pair")

    def x_base(t, a):
        return 12 + 6 * t + 3 * a

    ring = (("right", "left"), ("left", "right"))
    ahead = ((xr, xl), (xl, xr))
    plane = (y, 1 - y)

    def x_far(t, a):
        src = kvg_ref.at[t, plane[a] * NX + xf]
        rsend(x_base(t, a), src, x_in.at[t, a, 0], ring[t][0])

    def x_near(t, a):
        src = kvg_ref.at[t, plane[a] * NX + ahead[t][1]]
        rsend(x_base(t, a) + 1, src, x_in.at[t, a, 1], ring[t][1])

    def x_relay(t, a):
        rarrived(x_base(t, a), x_in.at[t, a, 0])
        mine = wide(kvg_ref[t, plane[a] * NX + ahead[t][0]])
        x_sum[t, a] = (wide(x_in[t, a, 0]) + mine).astype(BF)
        rsend(x_base(t, a) + 2, x_sum.at[t, a], x_in.at[t, a, 2], ring[t][0])

    def x_total(t, a):
        rarrived(x_base(t, a) + 1, x_in.at[t, a, 1])
        rarrived(x_base(t, a) + 2, x_in.at[t, a, 2])
        value = wide(kvg_ref[t, plane[a] * NX + x]) + wide(x_in[t, a, 1]) + wide(x_in[t, a, 2])
        return value * factor if t == 0 else value

    def project(n):
        return dot_nn(attn[...], feature(n)).astype(BF)

    send(1, go_hbm.at[second], go_relay.at[1], "back")
    load[4].wait()
    q_pair[0] = by_y(q_ref[:, cols(1)], q_ref[:, cols(0)])
    send(6, q_pair.at[0], qg_ref.at[0, z, y], "pair")
    qg_ref[0, z, y] = by_y(q_ref[:, cols(0)], q_ref[:, cols(1)])
    qg_ref[0, z, 2] = q_ref[:, cols(2)]
    z_own(0)
    c = y * NX + x
    for t, (ref, text) in enumerate(((k_ref, tk_ref), (v_ref, tv_ref))):
        load[2 * t].wait()
        load[2 * t + 1].wait()
        st_pair[t, 0, 0:TR] = by_y(ref[:, cols(1)], ref[:, cols(0)])
        st_pair[t, 0, TR:BR] = by_y(text[:, cols(1)], text[:, cols(0)])
        st_pair[t, 1, 0:TR] = ref[:, cols(2)]
        st_pair[t, 1, TR:BR] = text[:, cols(2)]
        send(7 + t, st_pair.at[t], kv_ref.at[t, c], "pair")
        kv_ref[t, c, 0, 0:TR] = by_y(ref[:, cols(0)], ref[:, cols(1)])
        kv_ref[t, c, 0, TR:BR] = by_y(text[:, cols(0)], text[:, cols(1)])
        kv_ref[t, c, 1, 0:TR] = ref[:, cols(2)]
        kv_ref[t, c, 1, TR:BR] = text[:, cols(2)]
        x_send(0, t, y)
    send(2, go_hbm, goall.at[head], "core")
    load[7].wait()
    load[8].wait()
    key_side()
    lax.fori_loop(0, BLOCKS, query_side, 0)
    z_own_forward(0)
    arrived(6, qg_ref.at[0, z, 1 - y])
    z_pair(0)
    load[5].wait()
    load[6].wait()
    acc[...] = dot_nt(go_ref[...], feature(head))
    x_forward(0, y)
    z_pair_forward(0)
    for t in range(2):
        arrived(7 + t, kv_ref.at[t, (1 - y) * NX + x])
        x_send(1, t, 1 - y)
    send(0, go_hbm.at[first], go_relay.at[0], "pair")
    z_own_finish(0)
    z_pair_finish(0)
    for n in range(BLOCKS):
        take_queries(n)
    forward(0, True)
    arrived(2, goall.at[core_head])
    acc[...] += dot_nt(goall[core_head], feature(core_head))
    forward(1)
    arrived(0, go_relay.at[0])
    send(3, go_relay.at[0], goall.at[head, first], "back")
    arrived(1, go_relay.at[1])
    send(4, go_relay.at[1], goall.at[other_head, second], "pair")
    x_near_finish(0, y)
    x_far_finish(0, y)
    forward(2)
    forward(6)
    x_forward(1, 1 - y)
    forward(4)
    arrived(3, goall.at[other_head, first])
    arrived(4, goall.at[other_head, second])
    send(5, goall.at[other_head], goall.at[other_head], "core")
    acc[...] += dot_nt(goall[other_head], feature(other_head))
    x_near_finish(1, 1 - y)
    forward(3)
    arrived(5, goall.at[core_other])
    grad = (acc[...] + dot_nt(goall[core_other], feature(core_other))).astype(BF)
    q_pair[1] = by_y(grad[:, cols(1)], grad[:, cols(0)])
    send(9, q_pair.at[1], qg_ref.at[1, z, y], "pair")
    qg_ref[1, z, y] = by_y(grad[:, cols(0)], grad[:, cols(1)])
    qg_ref[1, z, 2] = grad[:, cols(2)]
    z_own(1)
    forward(7)
    x_far_finish(1, 1 - y)
    forward(5)
    arrived(9, qg_ref.at[1, z, 1 - y])
    z_pair(1)
    z_own_forward(1)
    forward_text()
    z_start(0)
    z_pair_forward(1)

    z_own_finish(1)
    for n in (0, 1, 2, 3, 8, 9, 10, 11, 4, 5, 6, 7):
        if n == NZ:
            z_relay(0)
            z_pair_finish(1)
        j = 2 if n // NZ == 2 else (y + n // NZ) % NY
        grads_t[:, n * TR : (n + 1) * TR] = qg_ref[1, n % NZ, j].T
    slope_blocks(LAT, NY * NX * CR)
    key_grads(LAT, NY * NX * CR)
    pair_rows = 2 * TR

    slope_blocks(2 * pair_rows, pair_rows)
    z_total(0, 1.0)
    key_grads(2 * pair_rows, pair_rows)
    for a in (1, 0):
        for t in range(2):
            x_far(t, a)
    rarrived(24, yq_in.at[0])
    attn[:, cols(0)] = by_y(keep_q[0, 0], yq_in[0])
    attn[:, cols(1)] = by_y(yq_in[0], keep_q[0, 0])
    attn[:, cols(2)] = keep_q[0, 1]
    part[0] = project(core_other)
    rsend(28, part.at[0], core_in.at[0], "core")
    part[2] = project(other_head)
    part[1] = project(core_head)
    rarrived(28, core_in.at[0])
    pair_sum[...] = (wide(part[2]) + wide(core_in[0])).astype(BF)
    rsend(30, pair_sum.at[first], out_relay.at[0], "pair")
    rsend(31, pair_sum.at[second], out_relay.at[1], "back")
    rsend(29, part.at[1], core_in.at[1], "core")

    slope_blocks(1 * pair_rows, pair_rows)
    key_grads(1 * pair_rows, pair_rows)
    for a in (1, 0):
        x_near(1, a)
        x_relay(0, a)
    part[3] = project(head)

    slope_blocks(3 * pair_rows, pair_rows)
    key_grads(3 * pair_rows, pair_rows)
    for a in (1, 0):
        x_near(0, a)
        x_relay(1, a)
    rarrived(30, out_relay.at[0])
    rsend(32, out_relay.at[0], far_in.at[first], "back")
    rarrived(31, out_relay.at[1])
    rsend(33, out_relay.at[1], far_in.at[second], "pair")

    slope_blocks(0, pair_rows)
    for n in range(BLOCKS):
        j = 2 if n // NZ == 2 else (y + n // NZ) % NY
        oq_ref[1, n % NZ, j] = qacc[n].astype(BF)
    z_start(1)
    key_grads(0, pair_rows)
    z_relay(1)
    for t in range(2):
        yk_out[t] = x_total(t, 1).astype(BF)
        rsend(26 + t, yk_out.at[t], yk_in.at[t], "pair")
    z_total(1, factor)

    stores = []

    def store(src, dst):
        copy = pltpu.make_async_copy(src, dst, store_sem.at[len(stores)])
        copy.start()
        stores.append(copy)

    results = ((gk_ref, gtk_ref, gk_hbm, gtk_hbm), (gv_ref, gtv_ref, gv_hbm, gtv_hbm))
    rarrived(29, core_in.at[1])
    rarrived(32, far_in.at[first])
    rarrived(33, far_in.at[second])
    out_ref[...] = (wide(part[3]) + wide(core_in[1]) + wide(far_in[...])).astype(BF)
    store(out_ref, out_hbm)
    for t, (ref, text, to, text_to) in enumerate(results):
        own = x_total(t, 0)
        rarrived(26 + t, yk_in.at[t])
        mine = own[0].astype(BF)
        other = yk_in[t, 0]
        both = (own[1] + wide(yk_in[t, 1])).astype(BF)
        for h, value in ((0, by_y(mine, other)), (1, by_y(other, mine)), (2, both)):
            ref[:, cols(h)] = value[0:TR]
            text[:, cols(h)] = value[TR:BR]
        store(ref, to)
        store(text, text_to)
    rarrived(25, yq_in.at[1])
    gq_ref[:, cols(0)] = by_y(keep_q[1, 0], yq_in[1])
    gq_ref[:, cols(1)] = by_y(yq_in[1], keep_q[1, 0])
    gq_ref[:, cols(2)] = keep_q[1, 1]
    store(gq_ref, gq_hbm)
    for copy in sent:
        copy.wait_send()
    for copy in stores:
        copy.wait()


def store_kernel(*refs):
    count = (len(refs) - 2) // 3
    held, result, buffers = refs[:count], refs[count : 2 * count], refs[2 * count : 3 * count]
    load_sem, store_sem = refs[-2:]
    loads = [
        pltpu.make_async_copy(held[n], buffers[n], load_sem.at[n]) for n in range(count)
    ]
    stores = [
        pltpu.make_async_copy(buffers[n], result[n], store_sem.at[n]) for n in range(count)
    ]
    for copy in loads:
        copy.start()
    for load, copy in zip(loads, stores):
        load.wait()
        copy.start()
    for copy in stores:
        copy.wait()


def shards(
    queries,
    keys,
    values,
    text_keys,
    text_values,
    head_bias,
    out_weight,
    grad_out,
    clip_lengths,
    tile_mask,
    caption_order,
):
    smem = pl.BlockSpec(memory_space=pltpu.SMEM)
    hbm = pl.BlockSpec(memory_space=pltpu.HBM)
    dma = pltpu.SemaphoreType.DMA
    qg_shape = (2, NZ, NH, TR, HS)
    kv_shape = (2, NY * NX, 2, BR, HS)
    out_cols = grad_out.shape[1]
    order = caption_order.reshape(CLIPS, CAP)
    token = pltpu.VMEM((TR, NH * HS), BF)
    text = pltpu.VMEM((CR, NH * HS), BF)
    wide_out = pltpu.VMEM((TR, out_cols), BF)
    halves = pltpu.VMEM((2, HALF, out_cols), BF)
    token_shape = jax.ShapeDtypeStruct((TR, NH * HS), BF)
    text_shape = jax.ShapeDtypeStruct((CR, NH * HS), BF)
    result = (
        jax.ShapeDtypeStruct((TR, out_cols), BF),
        token_shape,
        token_shape,
        token_shape,
        text_shape,
        text_shape,
    )
    held = pl.pallas_call(
        fused_kernel,
        out_shape=result,
        in_specs=[hbm] * 9 + [smem] * 2,
        out_specs=(hbm,) * len(result),
        scratch_shapes=[
            token,
            token,
            token,
            text,
            text,
            wide_out,
            pltpu.VMEM(out_weight.shape, BF),
            pltpu.VMEM(tile_mask.shape, jnp.int32),
            pltpu.VMEM(order.shape, jnp.int32),
            wide_out,
            token,
            token,
            token,
            text,
            text,
            pltpu.VMEM(qg_shape, BF),
            pltpu.VMEM(kv_shape, BF),
            pltpu.VMEM((2, 2, BR, HS), BF),
            pltpu.VMEM((2, TR, HS), BF),
            pltpu.VMEM((4, TR, out_cols), BF),
            halves,
            pltpu.VMEM((TR, NH * HS), F32),
            pltpu.VMEM((2, ROWS, 2 * HS), BF),
            pltpu.VMEM((BLOCKS, TR, 2 * HS), BF),
            pltpu.VMEM((BLOCKS * TR, ROWS), BF),
            pltpu.VMEM((BLOCKS * TR, ROWS), BF),
            pltpu.VMEM((2, NY * NX * CR, HS), BF),
            pltpu.VMEM((HS, BLOCKS * TR), BF),
            pltpu.VMEM((HS, BLOCKS * TR), BF),
            pltpu.VMEM((BLOCKS, TR, HS), F32),
            pltpu.VMEM((BLOCKS, TR, HS), F32),
            pltpu.VMEM(qg_shape, BF),
            pltpu.VMEM(kv_shape, BF),
            pltpu.VMEM((2, 6, NH, HALF, HS), BF),
            pltpu.VMEM((2, 2, NH, HALF, HS), BF),
            pltpu.VMEM((2, NY, 3, 2, BR, HS), BF),
            pltpu.VMEM((2, NY, 2, BR, HS), BF),
            pltpu.VMEM((2, TR, HS), BF),
            pltpu.VMEM((2, TR, HS), BF),
            pltpu.VMEM((2, 2, BR, HS), BF),
            pltpu.VMEM((2, 2, BR, HS), BF),
            pltpu.VMEM((2, 2, TR, HS), BF),
            token,
            pltpu.VMEM((4, TR, out_cols), BF),
            pltpu.VMEM((2, TR, out_cols), BF),
            wide_out,
            halves,
            wide_out,
            dma((42,)),
            dma((42,)),
            dma((34,)),
            dma((34,)),
            dma((9,)),
            dma((len(result),)),
        ],
        compiler_params=pltpu.CompilerParams(
            collective_id=0, has_side_effects=True, vmem_limit_bytes=VMEM_LIMIT
        ),
    )(
        queries,
        keys,
        values,
        text_keys,
        text_values,
        grad_out,
        out_weight,
        tile_mask,
        order,
        clip_lengths,
        head_bias,
    )
    return pl.pallas_call(
        store_kernel,
        out_shape=result,
        in_specs=[hbm] * len(result),
        out_specs=(hbm,) * len(result),
        scratch_shapes=[pltpu.VMEM(array.shape, array.dtype) for array in result]
        + [dma((len(result),)), dma((len(result),))],
        compiler_params=pltpu.CompilerParams(vmem_limit_bytes=VMEM_LIMIT),
    )(*held)


def solution(mesh):
    in_specs = (
        P("seq", "head"),
        P("seq", "head"),
        P("seq", "head"),
        P("seq", "head"),
        P("seq", "head"),
        P("head"),
        P("head", None),
        P("seq", "head"),
        P(),
        P(),
        P(),
    )
    out_specs = (P("seq", "head"),) * 6
    return jax.shard_map(shards, mesh=mesh, in_specs=in_specs, out_specs=out_specs, check_vma=False)
```

```python
import jax
import jax.numpy as jnp
from jax import lax
from jax.experimental import pallas as pl
from jax.experimental.pallas import tpu as pltpu
from jax.sharding import PartitionSpec as P

MESH = pl.DeviceIdType.MESH
BF = jnp.bfloat16
F32 = jnp.float32

NX, NZ, NY = 4, 4, 2
HS = 128
NH = 3
TR = 256
CR = 16
BR = TR + CR
HALF = TR // 2
CLIPS = 4
CAP = 128
TILE = 64
LAT = NY * NX * TR
ROWS = NY * NX * BR
MASKED = -32768.0
BLOCKS = NH * NZ
VMEM_LIMIT = 58 * 1024 * 1024


def place():
    seq = lax.axis_index("seq")
    head = lax.axis_index("head")
    y = seq // (NZ * NX)
    z = (seq // NX) % NZ
    x = seq % NX
    return seq, head, y, z, x


def peers(seq, head, y, z, x):
    def at(yy, zz, xx):
        return (yy * NZ + zz) * NX + xx

    other_head = (head + 2) % 4
    core_head = head + 1 - 2 * (head % 2)
    return {
        "pair": (at(1 - y, z, x), head),
        "back": (at(1 - y, z, x), other_head),
        "core": (seq, core_head),
        "right": (at(y, z, (x + 1) % NX), head),
        "left": (at(y, z, (x + NX - 1) % NX), head),
        "up": (at(y, (z + 1) % NZ, x), head),
        "down": (at(y, (z + NZ - 1) % NZ, x), head),
    }


def greet(peer):
    barrier = pltpu.get_barrier_semaphore()
    for device in peer.values():
        pl.semaphore_signal(barrier, inc=1, device_id=device, device_id_type=MESH)
    pl.semaphore_wait(barrier, len(peer))


def sender(peer, send_sem, recv_sem, sent):
    def send(n, src, dst, to):
        copy = pltpu.make_async_remote_copy(
            src_ref=src,
            dst_ref=dst,
            send_sem=send_sem.at[n],
            recv_sem=recv_sem.at[n],
            device_id=peer[to],
            device_id_type=MESH,
        )
        copy.start()
        sent.append(copy)

    def arrived(n, dst):
        pltpu.make_async_remote_copy(
            src_ref=dst,
            dst_ref=dst,
            send_sem=send_sem.at[n],
            recv_sem=recv_sem.at[n],
            device_id=peer["core"],
            device_id_type=MESH,
        ).wait_recv()

    return send, arrived


def dot_nt(a, b):
    return lax.dot_general(a, b, (((1,), (1,)), ((), ())), preferred_element_type=F32)


def dot_nn(a, b):
    return lax.dot_general(a, b, (((1,), (0,)), ((), ())), preferred_element_type=F32)


def fused_kernel(
    q_hbm,
    k_hbm,
    v_hbm,
    tk_hbm,
    tv_hbm,
    go_hbm,
    w_hbm,
    tile_hbm,
    order_hbm,
    len_ref,
    bias_ref,
    out_hbm,
    gq_hbm,
    gk_hbm,
    gv_hbm,
    gtk_hbm,
    gtv_hbm,
    q_ref,
    k_ref,
    v_ref,
    tk_ref,
    tv_ref,
    go_ref,
    w_ref,
    tile_ref,
    order_ref,
    out_ref,
    gq_ref,
    gk_ref,
    gv_ref,
    gtk_ref,
    gtv_ref,
    qg_ref,
    kv_ref,
    st_pair,
    q_pair,
    goall,
    go_relay,
    acc,
    kaug,
    qaug,
    weights,
    slopes,
    vtext,
    queries_t,
    grads_t,
    oacc,
    qacc,
    oq_ref,
    kvg_ref,
    z_in,
    z_sum,
    x_in,
    x_sum,
    yq_out,
    yq_in,
    yk_out,
    yk_in,
    keep_q,
    attn,
    part,
    core_in,
    pair_sum,
    out_relay,
    far_in,
    g_send,
    g_recv,
    r_send,
    r_recv,
    local_sem,
    store_sem,
):
    seq, head, y, z, x = place()
    peer = peers(seq, head, y, z, x)
    zu, zd, zf = (z + 1) % NZ, (z + NZ - 1) % NZ, (z + 2) % NZ
    xr, xl, xf = (x + 1) % NX, (x + NX - 1) % NX, (x + 2) % NX
    other_head = (head + 2) % 4
    core_head = head + 1 - 2 * (head % 2)
    core_other = core_head + 2 - 4 * (core_head // 2)
    first, second = pl.ds(0, HALF), pl.ds(HALF, HALF)
    sent = []
    send, arrived = sender(peer, g_send, g_recv, sent)
    rsend, rarrived = sender(peer, r_send, r_recv, sent)
    cols = lambda h: slice(h * HS, (h + 1) * HS)
    by_y = lambda a, b: jnp.where(y == 0, a, b)
    wide = lambda a: a.astype(F32)
    factor = HS ** (-0.5)

    load = []
    for n, (src, dst) in enumerate(
        (
            (k_hbm, k_ref),
            (tk_hbm, tk_ref),
            (v_hbm, v_ref),
            (tv_hbm, tv_ref),
            (q_hbm, q_ref),
            (go_hbm, go_ref),
            (w_hbm, w_ref),
            (tile_hbm, tile_ref),
            (order_hbm, order_ref),
        )
    ):
        copy = pltpu.make_async_copy(src, dst, local_sem.at[n])
        copy.start()
        load.append(copy)

    greet(peer)


    def x_send(a, t, yy):
        c = yy * NX + x
        send(10 + 6 * a + 2 * t, kv_ref.at[t, c], kv_ref.at[t, c], ("right", "left")[t])
        send(11 + 6 * a + 2 * t, kv_ref.at[t, c], kv_ref.at[t, c], ("left", "right")[t])

    def x_forward(a, yy):
        base = 10 + 6 * a
        left, right = yy * NX + xl, yy * NX + xr
        arrived(base + 0, kv_ref.at[0, left])
        send(base + 4, kv_ref.at[0, left], kv_ref.at[0, left], "right")
        arrived(base + 2, kv_ref.at[1, right])
        send(base + 5, kv_ref.at[1, right], kv_ref.at[1, right], "left")

    def x_near_finish(a, yy):
        base = 10 + 6 * a
        arrived(base + 1, kv_ref.at[0, yy * NX + xr])
        arrived(base + 3, kv_ref.at[1, yy * NX + xl])

    def x_far_finish(a, yy):
        base = 10 + 6 * a
        arrived(base + 4, kv_ref.at[0, yy * NX + xf])
        arrived(base + 5, kv_ref.at[1, yy * NX + xf])

    def z_own(t):
        base = 22 + 10 * t
        send(base + 0, qg_ref.at[t, z, 2], qg_ref.at[t, z, 2], "up")
        send(base + 1, qg_ref.at[t, z, y], qg_ref.at[t, z, y], "down")
        send(base + 2, qg_ref.at[t, z, y], qg_ref.at[t, z, y], "up")
        send(base + 3, qg_ref.at[t, z, 2], qg_ref.at[t, z, 2], "down")

    def z_own_forward(t):
        base = 22 + 10 * t
        arrived(base + 0, qg_ref.at[t, zd, 2])
        send(base + 4, qg_ref.at[t, zd, 2], qg_ref.at[t, zd, 2], "up")
        arrived(base + 1, qg_ref.at[t, zu, y])
        send(base + 5, qg_ref.at[t, zu, y], qg_ref.at[t, zu, y], "down")

    def z_pair(t):
        base = 22 + 10 * t
        send(base + 6, qg_ref.at[t, z, 1 - y], qg_ref.at[t, z, 1 - y], "up")
        send(base + 7, qg_ref.at[t, z, 1 - y], qg_ref.at[t, z, 1 - y], "down")

    def z_pair_forward(t):
        base = 22 + 10 * t
        arrived(base + 6, qg_ref.at[t, zd, 1 - y])
        src = qg_ref.at[t, zd, 1 - y, first]
        send(base + 8, src, src, "up")
        arrived(base + 7, qg_ref.at[t, zu, 1 - y])
        src = qg_ref.at[t, zu, 1 - y, second]
        send(base + 9, src, src, "down")

    def z_own_finish(t):
        base = 22 + 10 * t
        arrived(base + 2, qg_ref.at[t, zd, y])
        arrived(base + 3, qg_ref.at[t, zu, 2])
        arrived(base + 4, qg_ref.at[t, zf, 2])
        arrived(base + 5, qg_ref.at[t, zf, y])

    def z_pair_finish(t):
        base = 22 + 10 * t
        arrived(base + 8, qg_ref.at[t, zf, 1 - y, first])
        arrived(base + 9, qg_ref.at[t, zf, 1 - y, second])

    def feature(n):
        return w_ref[:, pl.ds(pl.multiple_of(n * 768, 128), 768)]

    ends = [len_ref[0]]
    for c in range(1, CLIPS):
        ends.append(ends[-1] + len_ref[c])

    def clip_at(pos):
        total = 0
        for c in range(CLIPS - 1):
            total = total + jnp.where(pos >= ends[c], 1, 0)
        return total

    lane = lax.broadcasted_iota(jnp.int32, (1, HS), 1)
    tiles_here = (lane % 64) // 16 == z
    clip_lane = ((z + 1) % NZ) * 16
    bias_lane = clip_lane + CLIPS
    bias_ones = jnp.where((lane >= bias_lane) & (lane < bias_lane + 3), 1.0, 0.0)

    def kv_index(n):
        return ((y + n % 2) % NY) * NX + (x + n // 2) % NX

    def key_side():
        for n in range(NY * NX):
            pos = kv_index(n) // NX * (NZ * NX * TR) + z * (NX * TR) + kv_index(n) % NX * TR
            pos = pos + lax.broadcasted_iota(jnp.int32, (TR, HS), 0)
            hit = (tiles_here & (pos // TILE == lane)) | (clip_at(pos) == lane - clip_lane)
            aug = jnp.where(hit, 1.0, bias_ones).astype(BF)
            for s in range(2):
                kaug[s, n * TR : (n + 1) * TR, HS:] = aug
        row = lax.broadcasted_iota(jnp.int32, (NY * NX * CR, HS), 0)
        n = row // CR
        plane = ((y + n % 2) % NY) * NZ + z
        text_row = (plane * NX + (x + n // 2) % NX) * CR + row % CR
        aug = jnp.broadcast_to(bias_ones, text_row.shape)
        for c in range(CLIPS):
            listed = jnp.where(order_ref[c : c + 1, :] == text_row, 1.0, 0.0)
            found = jnp.max(listed, axis=1, keepdims=True)
            aug = jnp.where(lane == clip_lane + c, found, aug)
        for s in range(2):
            kaug[s, LAT:, HS:] = aug.astype(BF)

    log_len = [
        jnp.log(jnp.full((1, HS), len_ref[c] + CAP, jnp.int32).astype(F32)) for c in range(CLIPS)
    ]

    def query_side(n, carry):
        yq = jnp.where(n // NZ == 1, 1 - y, y)
        start = ((yq * NZ + n % NZ) * NX + x) * TR
        head_bias = bias_ref[jnp.where(n // NZ == 2, 2, y)]
        pos = start + lax.broadcasted_iota(jnp.int32, (TR, HS), 0)
        clip = clip_at(pos)
        offset = jnp.broadcast_to(log_len[CLIPS - 1], (TR, HS))
        for c in range(CLIPS - 2, -1, -1):
            offset = jnp.where(pos < ends[c], log_len[c], offset)
        total = (head_bias - offset) * (HS**0.5)
        hi = total.astype(BF).astype(F32)
        mid = (total - hi).astype(BF).astype(F32)
        low = total - hi - mid
        in_bias = jnp.where(lane == bias_lane, hi, jnp.where(lane == bias_lane + 1, mid, low))
        in_bias = jnp.where((lane >= bias_lane) & (lane < bias_lane + 3), in_bias, 0.0)
        in_clip = (lane >= clip_lane) & (lane < clip_lane + CLIPS) & (lane - clip_lane != clip)
        side = jnp.where(in_clip, MASKED, in_bias)
        for u in range(TR // TILE):
            tile = start // TILE + u
            off = (tile_ref[pl.ds(tile, 1), :] == 0) & (lane != tile) & tiles_here
            rows = slice(u * TILE, (u + 1) * TILE)
            qaug[n, rows, HS:] = jnp.where(off, MASKED, side[rows]).astype(BF)
        return carry

    def block_j(n):
        return jnp.where(n // NZ == 2, 2, jnp.where(n // NZ == 1, 1 - y, y))

    def take_queries(n):
        value = qg_ref[0, n % NZ, n // NZ if n // NZ == 2 else (y + n // NZ) % NY]
        qaug[n, :, 0:HS] = value
        queries_t[:, n * TR : (n + 1) * TR] = value.T

    def take_key(n):
        for s in range(2):
            kaug[s, n * TR : (n + 1) * TR, 0:HS] = kv_ref[0, kv_index(n), s, 0:TR]
            kaug[s, LAT + n * CR : LAT + (n + 1) * CR, 0:HS] = kv_ref[0, kv_index(n), s, TR:BR]
            vtext[s, n * CR : (n + 1) * CR] = kv_ref[1, kv_index(n), s, TR:BR]

    def weigh(n, slot, first_row, count):
        scores = dot_nt(qaug[n], kaug[slot, first_row : first_row + count, :])
        half = jnp.tanh(scores * (0.5 * factor))
        twice = 1.0 + half
        weight = twice.astype(BF)
        rows = pl.ds(pl.multiple_of(n * TR, TR), TR)
        weights[rows, first_row : first_row + count] = weight
        slopes[rows, first_row : first_row + count] = (twice * (1.0 - half)).astype(BF)
        return weight

    def per_plane(body):
        def step(zq, carry):
            for g in range(NH):
                body(g * NZ + zq, g // 2)
            return carry

        lax.fori_loop(0, NZ, step, 0)

    def forward(c, fresh=False):
        take_key(c)

        def body(n, slot):
            share = dot_nn(weigh(n, slot, c * TR, TR), kv_ref[1, kv_index(c), slot, 0:TR])
            if fresh:
                oacc[n] = share
            else:
                oacc[n] += share

        per_plane(body)

    def forward_text():
        def body(n, slot):
            share = dot_nn(weigh(n, slot, LAT, NY * NX * CR), vtext[slot])
            oq_ref[0, n % NZ, block_j(n)] = ((oacc[n] + share) * 0.5).astype(BF)

        per_plane(body)

    def slope_blocks(first_row, count):
        def body(n, slot):
            rows = pl.ds(pl.multiple_of(n * TR, TR), TR)
            slope = wide(slopes[rows, first_row : first_row + count])
            grads = qg_ref[1, n % NZ, block_j(n)]
            if first_row == LAT:
                vals = vtext[slot]
            else:
                c = first_row // TR
                vals = jnp.concatenate(
                    [kv_ref[1, kv_index(c + r), slot, 0:TR] for r in range(2)], axis=0
                )
            product = dot_nt(grads, vals)
            slope = (product * slope).astype(BF)
            slopes[rows, first_row : first_row + count] = slope
            share = dot_nn(slope, kaug[slot, first_row : first_row + count, 0:HS])
            if first_row == LAT:
                qacc[n] = share
            else:
                qacc[n] += share

        per_plane(body)

    def key_grads(first_row, count):
        for s, (low, high) in enumerate(((0, 2 * NZ * TR), (2 * NZ * TR, BLOCKS * TR))):
            for t in range(2):
                left = (queries_t, grads_t)[t][:, low:high]
                right = (slopes, weights)[t][low:high, first_row : first_row + count]
                total = (dot_nn(left, right) * (0.25, 0.5)[t]).astype(BF)
                if first_row == LAT:
                    text_rows = total.T
                    for n in range(NY * NX):
                        kvg_ref[t, kv_index(n), s, TR:BR] = text_rows[n * CR : (n + 1) * CR]
                else:
                    for r in range(2):
                        n = first_row // TR + r
                        kvg_ref[t, kv_index(n), s, 0:TR] = total[:, r * TR : (r + 1) * TR].T


    def z_start(t):
        base = 6 * t
        rsend(base + 0, oq_ref.at[t, zf, :, first], z_in.at[t, 0], "up")
        rsend(base + 3, oq_ref.at[t, zf, :, second], z_in.at[t, 3], "down")
        rsend(base + 1, oq_ref.at[t, zd, :, first], z_in.at[t, 1], "down")
        rsend(base + 4, oq_ref.at[t, zu, :, second], z_in.at[t, 4], "up")

    def z_relay(t):
        base = 6 * t
        rarrived(base + 0, z_in.at[t, 0])
        z_sum[t, 0] = (wide(z_in[t, 0]) + wide(oq_ref[t, zu, :, first])).astype(BF)
        rsend(base + 2, z_sum.at[t, 0], z_in.at[t, 2], "up")
        rarrived(base + 3, z_in.at[t, 3])
        z_sum[t, 1] = (wide(z_in[t, 3]) + wide(oq_ref[t, zd, :, second])).astype(BF)
        rsend(base + 5, z_sum.at[t, 1], z_in.at[t, 5], "down")

    def z_total(t, scale):
        base = 6 * t
        for n in (1, 2, 4, 5):
            rarrived(base + n, z_in.at[t, n])
        for rows, one, two in ((first, 1, 2), (second, 4, 5)):

            def total(j):
                value = wide(oq_ref[t, z, j, rows]) + wide(z_in[t, one, j]) + wide(z_in[t, two, j])
                return (value * scale).astype(BF) if scale != 1.0 else value.astype(BF)

            yq_out[t, rows] = total(1 - y)
            keep_q[t, 0, rows] = total(y)
            keep_q[t, 1, rows] = total(2)
        rsend(24 + t, yq_out.at[t], yq_in.at[t], "pair")

    def x_base(t, a):
        return 12 + 6 * t + 3 * a

    ring = (("right", "left"), ("left", "right"))
    ahead = ((xr, xl), (xl, xr))
    plane = (y, 1 - y)

    def x_far(t, a):
        src = kvg_ref.at[t, plane[a] * NX + xf]
        rsend(x_base(t, a), src, x_in.at[t, a, 0], ring[t][0])

    def x_near(t, a):
        src = kvg_ref.at[t, plane[a] * NX + ahead[t][1]]
        rsend(x_base(t, a) + 1, src, x_in.at[t, a, 1], ring[t][1])

    def x_relay(t, a):
        rarrived(x_base(t, a), x_in.at[t, a, 0])
        mine = wide(kvg_ref[t, plane[a] * NX + ahead[t][0]])
        x_sum[t, a] = (wide(x_in[t, a, 0]) + mine).astype(BF)
        rsend(x_base(t, a) + 2, x_sum.at[t, a], x_in.at[t, a, 2], ring[t][0])

    def x_total(t, a):
        rarrived(x_base(t, a) + 1, x_in.at[t, a, 1])
        rarrived(x_base(t, a) + 2, x_in.at[t, a, 2])
        value = wide(kvg_ref[t, plane[a] * NX + x]) + wide(x_in[t, a, 1]) + wide(x_in[t, a, 2])
        return value * factor if t == 0 else value

    def project(n):
        return dot_nn(attn[...], feature(n)).astype(BF)

    send(1, go_hbm.at[second], go_relay.at[1], "back")
    load[4].wait()
    q_pair[0] = by_y(q_ref[:, cols(1)], q_ref[:, cols(0)])
    send(6, q_pair.at[0], qg_ref.at[0, z, y], "pair")
    qg_ref[0, z, y] = by_y(q_ref[:, cols(0)], q_ref[:, cols(1)])
    qg_ref[0, z, 2] = q_ref[:, cols(2)]
    z_own(0)
    c = y * NX + x
    for t, (ref, text) in enumerate(((k_ref, tk_ref), (v_ref, tv_ref))):
        load[2 * t].wait()
        load[2 * t + 1].wait()
        st_pair[t, 0, 0:TR] = by_y(ref[:, cols(1)], ref[:, cols(0)])
        st_pair[t, 0, TR:BR] = by_y(text[:, cols(1)], text[:, cols(0)])
        st_pair[t, 1, 0:TR] = ref[:, cols(2)]
        st_pair[t, 1, TR:BR] = text[:, cols(2)]
        send(7 + t, st_pair.at[t], kv_ref.at[t, c], "pair")
        kv_ref[t, c, 0, 0:TR] = by_y(ref[:, cols(0)], ref[:, cols(1)])
        kv_ref[t, c, 0, TR:BR] = by_y(text[:, cols(0)], text[:, cols(1)])
        kv_ref[t, c, 1, 0:TR] = ref[:, cols(2)]
        kv_ref[t, c, 1, TR:BR] = text[:, cols(2)]
        x_send(0, t, y)
    send(2, go_hbm, goall.at[head], "core")
    load[7].wait()
    load[8].wait()
    key_side()
    lax.fori_loop(0, BLOCKS, query_side, 0)
    z_own_forward(0)
    arrived(6, qg_ref.at[0, z, 1 - y])
    z_pair(0)
    load[5].wait()
    load[6].wait()
    acc[...] = dot_nt(go_ref[...], feature(head))
    x_forward(0, y)
    z_pair_forward(0)
    for t in range(2):
        arrived(7 + t, kv_ref.at[t, (1 - y) * NX + x])
        x_send(1, t, 1 - y)
    send(0, go_hbm.at[first], go_relay.at[0], "pair")
    z_own_finish(0)
    z_pair_finish(0)
    for n in range(BLOCKS):
        take_queries(n)
    forward(0, True)
    arrived(2, goall.at[core_head])
    acc[...] += dot_nt(goall[core_head], feature(core_head))
    forward(1)
    arrived(0, go_relay.at[0])
    send(3, go_relay.at[0], goall.at[head, first], "back")
    arrived(1, go_relay.at[1])
    send(4, go_relay.at[1], goall.at[other_head, second], "pair")
    x_near_finish(0, y)
    x_far_finish(0, y)
    forward(2)
    forward(6)
    x_forward(1, 1 - y)
    forward(4)
    arrived(3, goall.at[other_head, first])
    arrived(4, goall.at[other_head, second])
    send(5, goall.at[other_head], goall.at[other_head], "core")
    acc[...] += dot_nt(goall[other_head], feature(other_head))
    x_near_finish(1, 1 - y)
    forward(3)
    arrived(5, goall.at[core_other])
    grad = (acc[...] + dot_nt(goall[core_other], feature(core_other))).astype(BF)
    q_pair[1] = by_y(grad[:, cols(1)], grad[:, cols(0)])
    send(9, q_pair.at[1], qg_ref.at[1, z, y], "pair")
    qg_ref[1, z, y] = by_y(grad[:, cols(0)], grad[:, cols(1)])
    qg_ref[1, z, 2] = grad[:, cols(2)]
    z_own(1)
    forward(7)
    x_far_finish(1, 1 - y)
    forward(5)
    arrived(9, qg_ref.at[1, z, 1 - y])
    z_pair(1)
    z_own_forward(1)
    forward_text()
    z_start(0)
    z_pair_forward(1)

    z_own_finish(1)
    for n in (0, 1, 2, 3, 8, 9, 10, 11, 4, 5, 6, 7):
        if n == NZ:
            z_relay(0)
            z_pair_finish(1)
        j = 2 if n // NZ == 2 else (y + n // NZ) % NY
        grads_t[:, n * TR : (n + 1) * TR] = qg_ref[1, n % NZ, j].T
    slope_blocks(LAT, NY * NX * CR)
    key_grads(LAT, NY * NX * CR)
    pair_rows = 2 * TR

    slope_blocks(2 * pair_rows, pair_rows)
    z_total(0, 1.0)
    key_grads(2 * pair_rows, pair_rows)
    for a in (1, 0):
        for t in range(2):
            x_far(t, a)
    rarrived(24, yq_in.at[0])
    attn[:, cols(0)] = by_y(keep_q[0, 0], yq_in[0])
    attn[:, cols(1)] = by_y(yq_in[0], keep_q[0, 0])
    attn[:, cols(2)] = keep_q[0, 1]
    part[0] = project(core_other)
    rsend(28, part.at[0], core_in.at[0], "core")
    part[2] = project(other_head)
    part[1] = project(core_head)
    rarrived(28, core_in.at[0])
    pair_sum[...] = (wide(part[2]) + wide(core_in[0])).astype(BF)
    rsend(30, pair_sum.at[first], out_relay.at[0], "pair")
    rsend(31, pair_sum.at[second], out_relay.at[1], "back")
    rsend(29, part.at[1], core_in.at[1], "core")

    slope_blocks(1 * pair_rows, pair_rows)
    key_grads(1 * pair_rows, pair_rows)
    for a in (1, 0):
        x_near(1, a)
        x_relay(0, a)
    part[3] = project(head)

    slope_blocks(3 * pair_rows, pair_rows)
    key_grads(3 * pair_rows, pair_rows)
    for a in (1, 0):
        x_near(0, a)
        x_relay(1, a)
    rarrived(30, out_relay.at[0])
    rsend(32, out_relay.at[0], far_in.at[first], "back")
    rarrived(31, out_relay.at[1])
    rsend(33, out_relay.at[1], far_in.at[second], "pair")

    slope_blocks(0, pair_rows)
    for n in range(BLOCKS):
        j = 2 if n // NZ == 2 else (y + n // NZ) % NY
        oq_ref[1, n % NZ, j] = (qacc[n] * 0.25).astype(BF)
    z_start(1)
    key_grads(0, pair_rows)
    z_relay(1)
    for t in range(2):
        yk_out[t] = x_total(t, 1).astype(BF)
        rsend(26 + t, yk_out.at[t], yk_in.at[t], "pair")
    z_total(1, factor)

    stores = []

    def store(src, dst):
        copy = pltpu.make_async_copy(src, dst, store_sem.at[len(stores)])
        copy.start()
        stores.append(copy)

    results = ((gk_ref, gtk_ref, gk_hbm, gtk_hbm), (gv_ref, gtv_ref, gv_hbm, gtv_hbm))
    rarrived(29, core_in.at[1])
    rarrived(32, far_in.at[first])
    rarrived(33, far_in.at[second])
    out_ref[...] = (wide(part[3]) + wide(core_in[1]) + wide(far_in[...])).astype(BF)
    store(out_ref, out_hbm)
    for t, (ref, text, to, text_to) in enumerate(results):
        own = x_total(t, 0)
        rarrived(26 + t, yk_in.at[t])
        mine = own[0].astype(BF)
        other = yk_in[t, 0]
        both = (own[1] + wide(yk_in[t, 1])).astype(BF)
        for h, value in ((0, by_y(mine, other)), (1, by_y(other, mine)), (2, both)):
            ref[:, cols(h)] = value[0:TR]
            text[:, cols(h)] = value[TR:BR]
        store(ref, to)
        store(text, text_to)
    rarrived(25, yq_in.at[1])
    gq_ref[:, cols(0)] = by_y(keep_q[1, 0], yq_in[1])
    gq_ref[:, cols(1)] = by_y(yq_in[1], keep_q[1, 0])
    gq_ref[:, cols(2)] = keep_q[1, 1]
    store(gq_ref, gq_hbm)
    for copy in sent:
        copy.wait_send()
    for copy in stores:
        copy.wait()


def store_kernel(*refs):
    count = (len(refs) - 2) // 3
    held, result, buffers = refs[:count], refs[count : 2 * count], refs[2 * count : 3 * count]
    load_sem, store_sem = refs[-2:]
    loads = [
        pltpu.make_async_copy(held[n], buffers[n], load_sem.at[n]) for n in range(count)
    ]
    stores = [
        pltpu.make_async_copy(buffers[n], result[n], store_sem.at[n]) for n in range(count)
    ]
    for copy in loads:
        copy.start()
    for load, copy in zip(loads, stores):
        load.wait()
        copy.start()
    for copy in stores:
        copy.wait()


def shards(
    queries,
    keys,
    values,
    text_keys,
    text_values,
    head_bias,
    out_weight,
    grad_out,
    clip_lengths,
    tile_mask,
    caption_order,
):
    smem = pl.BlockSpec(memory_space=pltpu.SMEM)
    hbm = pl.BlockSpec(memory_space=pltpu.HBM)
    dma = pltpu.SemaphoreType.DMA
    qg_shape = (2, NZ, NH, TR, HS)
    kv_shape = (2, NY * NX, 2, BR, HS)
    out_cols = grad_out.shape[1]
    order = caption_order.reshape(CLIPS, CAP)
    token = pltpu.VMEM((TR, NH * HS), BF)
    text = pltpu.VMEM((CR, NH * HS), BF)
    wide_out = pltpu.VMEM((TR, out_cols), BF)
    halves = pltpu.VMEM((2, HALF, out_cols), BF)
    token_shape = jax.ShapeDtypeStruct((TR, NH * HS), BF)
    text_shape = jax.ShapeDtypeStruct((CR, NH * HS), BF)
    result = (
        jax.ShapeDtypeStruct((TR, out_cols), BF),
        token_shape,
        token_shape,
        token_shape,
        text_shape,
        text_shape,
    )
    held = pl.pallas_call(
        fused_kernel,
        out_shape=result,
        in_specs=[hbm] * 9 + [smem] * 2,
        out_specs=(hbm,) * len(result),
        scratch_shapes=[
            token,
            token,
            token,
            text,
            text,
            wide_out,
            pltpu.VMEM(out_weight.shape, BF),
            pltpu.VMEM(tile_mask.shape, jnp.int32),
            pltpu.VMEM(order.shape, jnp.int32),
            wide_out,
            token,
            token,
            token,
            text,
            text,
            pltpu.VMEM(qg_shape, BF),
            pltpu.VMEM(kv_shape, BF),
            pltpu.VMEM((2, 2, BR, HS), BF),
            pltpu.VMEM((2, TR, HS), BF),
            pltpu.VMEM((4, TR, out_cols), BF),
            halves,
            pltpu.VMEM((TR, NH * HS), F32),
            pltpu.VMEM((2, ROWS, 2 * HS), BF),
            pltpu.VMEM((BLOCKS, TR, 2 * HS), BF),
            pltpu.VMEM((BLOCKS * TR, ROWS), BF),
            pltpu.VMEM((BLOCKS * TR, ROWS), BF),
            pltpu.VMEM((2, NY * NX * CR, HS), BF),
            pltpu.VMEM((HS, BLOCKS * TR), BF),
            pltpu.VMEM((HS, BLOCKS * TR), BF),
            pltpu.VMEM((BLOCKS, TR, HS), F32),
            pltpu.VMEM((BLOCKS, TR, HS), F32),
            pltpu.VMEM(qg_shape, BF),
            pltpu.VMEM(kv_shape, BF),
            pltpu.VMEM((2, 6, NH, HALF, HS), BF),
            pltpu.VMEM((2, 2, NH, HALF, HS), BF),
            pltpu.VMEM((2, NY, 3, 2, BR, HS), BF),
            pltpu.VMEM((2, NY, 2, BR, HS), BF),
            pltpu.VMEM((2, TR, HS), BF),
            pltpu.VMEM((2, TR, HS), BF),
            pltpu.VMEM((2, 2, BR, HS), BF),
            pltpu.VMEM((2, 2, BR, HS), BF),
            pltpu.VMEM((2, 2, TR, HS), BF),
            token,
            pltpu.VMEM((4, TR, out_cols), BF),
            pltpu.VMEM((2, TR, out_cols), BF),
            wide_out,
            halves,
            wide_out,
            dma((42,)),
            dma((42,)),
            dma((34,)),
            dma((34,)),
            dma((9,)),
            dma((len(result),)),
        ],
        compiler_params=pltpu.CompilerParams(
            collective_id=0, has_side_effects=True, vmem_limit_bytes=VMEM_LIMIT
        ),
    )(
        queries,
        keys,
        values,
        text_keys,
        text_values,
        grad_out,
        out_weight,
        tile_mask,
        order,
        clip_lengths,
        head_bias,
    )
    return pl.pallas_call(
        store_kernel,
        out_shape=result,
        in_specs=[hbm] * len(result),
        out_specs=(hbm,) * len(result),
        scratch_shapes=[pltpu.VMEM(array.shape, array.dtype) for array in result]
        + [dma((len(result),)), dma((len(result),))],
        compiler_params=pltpu.CompilerParams(vmem_limit_bytes=VMEM_LIMIT),
    )(*held)


def solution(mesh):
    in_specs = (
        P("seq", "head"),
        P("seq", "head"),
        P("seq", "head"),
        P("seq", "head"),
        P("seq", "head"),
        P("head"),
        P("head", None),
        P("seq", "head"),
        P(),
        P(),
        P(),
    )
    out_specs = (P("seq", "head"),) * 6
    return jax.shard_map(shards, mesh=mesh, in_specs=in_specs, out_specs=out_specs, check_vma=False)
```

```python
import jax
import jax.numpy as jnp
from jax import lax
from jax.experimental import pallas as pl
from jax.experimental.pallas import tpu as pltpu
from jax.sharding import PartitionSpec as P

MESH = pl.DeviceIdType.MESH
BF = jnp.bfloat16
F32 = jnp.float32

NX, NZ, NY = 4, 4, 2
HS = 128
NH = 3
TR = 256
CR = 16
BR = TR + CR
HALF = TR // 2
CLIPS = 4
CAP = 128
TILE = 64
LAT = NY * NX * TR
ROWS = NY * NX * BR
MASKED = -32768.0
BLOCKS = NH * NZ
SIDE = NX * TR
TEXT = NY * NX * CR
VMEM_LIMIT = 58 * 1024 * 1024


def place():
    seq = lax.axis_index("seq")
    head = lax.axis_index("head")
    y = seq // (NZ * NX)
    z = (seq // NX) % NZ
    x = seq % NX
    return seq, head, y, z, x


def peers(seq, head, y, z, x):
    def at(yy, zz, xx):
        return (yy * NZ + zz) * NX + xx

    other_head = (head + 2) % 4
    core_head = head + 1 - 2 * (head % 2)
    return {
        "pair": (at(1 - y, z, x), head),
        "back": (at(1 - y, z, x), other_head),
        "core": (seq, core_head),
        "right": (at(y, z, (x + 1) % NX), head),
        "left": (at(y, z, (x + NX - 1) % NX), head),
        "up": (at(y, (z + 1) % NZ, x), head),
        "down": (at(y, (z + NZ - 1) % NZ, x), head),
    }


def greet(peer):
    barrier = pltpu.get_barrier_semaphore()
    for device in peer.values():
        pl.semaphore_signal(barrier, inc=1, device_id=device, device_id_type=MESH)
    pl.semaphore_wait(barrier, len(peer))


def sender(peer, send_sem, recv_sem, sent):
    def send(n, src, dst, to):
        copy = pltpu.make_async_remote_copy(
            src_ref=src,
            dst_ref=dst,
            send_sem=send_sem.at[n],
            recv_sem=recv_sem.at[n],
            device_id=peer[to],
            device_id_type=MESH,
        )
        copy.start()
        sent.append(copy)

    def arrived(n, dst):
        pltpu.make_async_remote_copy(
            src_ref=dst,
            dst_ref=dst,
            send_sem=send_sem.at[n],
            recv_sem=recv_sem.at[n],
            device_id=peer["core"],
            device_id_type=MESH,
        ).wait_recv()

    return send, arrived


def dot_nt(a, b):
    return lax.dot_general(a, b, (((1,), (1,)), ((), ())), preferred_element_type=F32)


def dot_nn(a, b):
    return lax.dot_general(a, b, (((1,), (0,)), ((), ())), preferred_element_type=F32)


def fused_kernel(
    q_hbm,
    k_hbm,
    v_hbm,
    tk_hbm,
    tv_hbm,
    go_hbm,
    w_hbm,
    tile_hbm,
    order_hbm,
    len_ref,
    bias_ref,
    out_hbm,
    gq_hbm,
    gk_hbm,
    gv_hbm,
    gtk_hbm,
    gtv_hbm,
    q_ref,
    k_ref,
    v_ref,
    tk_ref,
    tv_ref,
    go_ref,
    w_ref,
    tile_ref,
    order_ref,
    out_ref,
    gq_ref,
    gk_ref,
    gv_ref,
    gtk_ref,
    gtv_ref,
    qg_ref,
    kv_ref,
    st_pair,
    q_pair,
    goall,
    go_relay,
    acc,
    kaug,
    kaug_own,
    ktext,
    vals_own,
    vtext,
    qaug,
    gsel,
    weights,
    slopes,
    weights_own,
    slopes_own,
    queries_t,
    grads_t,
    oacc,
    qacc,
    oq_ref,
    kvg_ref,
    z_in,
    z_sum,
    x_in,
    x_sum,
    yq_out,
    yq_in,
    yk_out,
    yk_in,
    keep_q,
    attn,
    part,
    core_in,
    pair_sum,
    out_relay,
    far_in,
    g_send,
    g_recv,
    r_send,
    r_recv,
    local_sem,
    store_sem,
):
    seq, head, y, z, x = place()
    peer = peers(seq, head, y, z, x)
    zu, zd, zf = (z + 1) % NZ, (z + NZ - 1) % NZ, (z + 2) % NZ
    xr, xl, xf = (x + 1) % NX, (x + NX - 1) % NX, (x + 2) % NX
    other_head = (head + 2) % 4
    core_head = head + 1 - 2 * (head % 2)
    core_other = core_head + 2 - 4 * (core_head // 2)
    first, second = pl.ds(0, HALF), pl.ds(HALF, HALF)
    sent = []
    send, arrived = sender(peer, g_send, g_recv, sent)
    rsend, rarrived = sender(peer, r_send, r_recv, sent)
    cols = lambda h: slice(h * HS, (h + 1) * HS)
    by_y = lambda a, b: jnp.where(y == 0, a, b)
    wide = lambda a: a.astype(F32)
    factor = HS ** (-0.5)

    load = []
    for n, (src, dst) in enumerate(
        (
            (k_hbm, k_ref),
            (tk_hbm, tk_ref),
            (v_hbm, v_ref),
            (tv_hbm, tv_ref),
            (q_hbm, q_ref),
            (go_hbm, go_ref),
            (w_hbm, w_ref),
            (tile_hbm, tile_ref),
            (order_hbm, order_ref),
        )
    ):
        copy = pltpu.make_async_copy(src, dst, local_sem.at[n])
        copy.start()
        load.append(copy)

    greet(peer)


    def x_send(a, t, yy):
        c = yy * NX + x
        send(10 + 6 * a + 2 * t, kv_ref.at[t, c], kv_ref.at[t, c], ("right", "left")[t])
        send(11 + 6 * a + 2 * t, kv_ref.at[t, c], kv_ref.at[t, c], ("left", "right")[t])

    def x_forward(a, yy):
        base = 10 + 6 * a
        left, right = yy * NX + xl, yy * NX + xr
        arrived(base + 0, kv_ref.at[0, left])
        send(base + 4, kv_ref.at[0, left], kv_ref.at[0, left], "right")
        arrived(base + 2, kv_ref.at[1, right])
        send(base + 5, kv_ref.at[1, right], kv_ref.at[1, right], "left")

    def x_near_finish(a, yy):
        base = 10 + 6 * a
        arrived(base + 1, kv_ref.at[0, yy * NX + xr])
        arrived(base + 3, kv_ref.at[1, yy * NX + xl])

    def x_far_finish(a, yy):
        base = 10 + 6 * a
        arrived(base + 4, kv_ref.at[0, yy * NX + xf])
        arrived(base + 5, kv_ref.at[1, yy * NX + xf])

    def z_own(t):
        base = 22 + 10 * t
        send(base + 0, qg_ref.at[t, z, 2], qg_ref.at[t, z, 2], "up")
        send(base + 1, qg_ref.at[t, z, y], qg_ref.at[t, z, y], "down")
        send(base + 2, qg_ref.at[t, z, y], qg_ref.at[t, z, y], "up")
        send(base + 3, qg_ref.at[t, z, 2], qg_ref.at[t, z, 2], "down")

    def z_own_forward(t):
        base = 22 + 10 * t
        arrived(base + 0, qg_ref.at[t, zd, 2])
        send(base + 4, qg_ref.at[t, zd, 2], qg_ref.at[t, zd, 2], "up")
        arrived(base + 1, qg_ref.at[t, zu, y])
        send(base + 5, qg_ref.at[t, zu, y], qg_ref.at[t, zu, y], "down")

    def z_pair(t):
        base = 22 + 10 * t
        send(base + 6, qg_ref.at[t, z, 1 - y], qg_ref.at[t, z, 1 - y], "up")
        send(base + 7, qg_ref.at[t, z, 1 - y], qg_ref.at[t, z, 1 - y], "down")

    def z_pair_forward(t):
        base = 22 + 10 * t
        arrived(base + 6, qg_ref.at[t, zd, 1 - y])
        src = qg_ref.at[t, zd, 1 - y, first]
        send(base + 8, src, src, "up")
        arrived(base + 7, qg_ref.at[t, zu, 1 - y])
        src = qg_ref.at[t, zu, 1 - y, second]
        send(base + 9, src, src, "down")

    def z_own_finish(t):
        base = 22 + 10 * t
        arrived(base + 2, qg_ref.at[t, zd, y])
        arrived(base + 3, qg_ref.at[t, zu, 2])
        arrived(base + 4, qg_ref.at[t, zf, 2])
        arrived(base + 5, qg_ref.at[t, zf, y])

    def z_pair_finish(t):
        base = 22 + 10 * t
        arrived(base + 8, qg_ref.at[t, zf, 1 - y, first])
        arrived(base + 9, qg_ref.at[t, zf, 1 - y, second])

    def feature(n):
        return w_ref[:, pl.ds(pl.multiple_of(n * 768, 128), 768)]

    half_rows = NZ * NX * TR
    ends = [len_ref[0]]
    for c in range(1, CLIPS):
        ends.append(ends[-1] + len_ref[c])
    long_start = 0
    for c in range(1, CLIPS):
        long_start = jnp.where(len_ref[c] == half_rows, ends[c - 1], long_start)

    def clip_at(pos):
        total = 0
        for c in range(CLIPS - 1):
            total = total + jnp.where(pos >= ends[c], 1, 0)
        return total

    row_index = lax.broadcasted_iota(jnp.int32, (TR, HS), 0)

    def chunk_rows(zz, xx):
        return (zz * NX + xx) * TR + row_index

    def own_is_long(zz, xx):
        t = chunk_rows(zz, xx)
        return jnp.where(y == 0, t - long_start, long_start - 1 - t) >= 0

    def by_side(mask, mine, other):
        mine, other = wide(mine), wide(other)
        return jnp.where(mask, mine, other).astype(BF), jnp.where(mask, other, mine).astype(BF)

    lane = lax.broadcasted_iota(jnp.int32, (1, HS), 1)
    tiles_here = (lane % 64) // 16 == z
    clip_lane = ((z + 1) % NZ) * 16
    bias_lane = clip_lane + CLIPS
    bias_ones = jnp.where((lane >= bias_lane) & (lane < bias_lane + 3), 1.0, 0.0)

    def kv_index(n):
        return ((y + n % 2) % NY) * NX + (x + n // 2) % NX

    def key_columns(pos):
        hit = (tiles_here & ((pos >> 6) == lane)) | (clip_at(pos) == lane - clip_lane)
        return jnp.where(hit, 1.0, bias_ones).astype(BF)

    def key_side():
        for d in range(NX):
            t = chunk_rows(z, (x + d) % NX)
            low = key_columns(t)
            high = key_columns(t + half_rows)
            for r in range(2):
                n = 2 * d + r
                plane_zero = (y + r) % NY == 0
                kaug[n * TR : (n + 1) * TR, HS:] = jnp.where(plane_zero, low, high)
            for side, value in enumerate(by_side(t >= long_start, low, high)):
                kaug_own[side, d * TR : (d + 1) * TR, HS:] = value
        row = lax.broadcasted_iota(jnp.int32, (TEXT, HS), 0)
        n = row // CR
        plane = ((y + n % 2) % NY) * NZ + z
        text_row = (plane * NX + (x + n // 2) % NX) * CR + row % CR
        aug = jnp.broadcast_to(bias_ones, text_row.shape)
        for c in range(CLIPS):
            listed = jnp.where(order_ref[c : c + 1, :] == text_row, 1.0, 0.0)
            found = jnp.max(listed, axis=1, keepdims=True)
            aug = jnp.where(lane == clip_lane + c, found, aug)
        for s in range(2):
            ktext[s, :, HS:] = aug.astype(BF)

    log_len = [
        jnp.log(jnp.full((1, HS), len_ref[c] + CAP, jnp.int32).astype(F32)) for c in range(CLIPS)
    ]

    def query_side(n, carry):
        g, zq = n // NZ, n % NZ
        t = chunk_rows(zq, x)
        in_high = jnp.where(g == 0, long_start - 1 - t, t - long_start)
        in_high = jnp.where(g == 2, 2 * y - 1, in_high) >= 0
        pos = t + jnp.where(in_high, half_rows, 0)
        head_bias = bias_ref[jnp.where(g == 2, 2, y)]
        clip = clip_at(pos)
        offset = jnp.broadcast_to(log_len[CLIPS - 1], (TR, HS))
        for c in range(CLIPS - 2, -1, -1):
            offset = jnp.where(pos < ends[c], log_len[c], offset)
        total = (head_bias - offset) * (HS**0.5)
        hi = total.astype(BF).astype(F32)
        mid = (total - hi).astype(BF).astype(F32)
        low = total - hi - mid
        in_bias = jnp.where(lane == bias_lane, hi, jnp.where(lane == bias_lane + 1, mid, low))
        in_bias = jnp.where((lane >= bias_lane) & (lane < bias_lane + 3), in_bias, 0.0)
        in_clip = (lane >= clip_lane) & (lane < clip_lane + CLIPS) & (lane - clip_lane != clip)
        side = jnp.where(in_clip, MASKED, in_bias)
        for u in range(TR // TILE):
            rows = slice(u * TILE, (u + 1) * TILE)
            tile = (zq * NX + x) * (TR // TILE) + u
            off = []
            for p in range(NY):
                at = tile + p * (half_rows // TILE)
                mask_row = tile_ref[pl.ds(at, 1), :]
                off.append(jnp.where((mask_row == 0) & (lane != at) & tiles_here, 1.0, 0.0))
            masked = jnp.where(in_high[rows], off[1], off[0]) > 0.5
            qaug[n, rows, HS:] = jnp.where(masked, MASKED, side[rows]).astype(BF)
        return carry

    def keep_query(n, value):
        qaug[n, :, 0:HS] = value
        queries_t[:, n * TR : (n + 1) * TR] = value.T

    def keep_grad(n, value):
        gsel[n] = value
        grads_t[:, n * TR : (n + 1) * TR] = value.T

    def take_own(t, keep):
        for zq in range(NZ):
            mask = own_is_long(zq, x)
            sides = by_side(mask, qg_ref[t, zq, y], qg_ref[t, zq, 1 - y])
            for g in range(2):
                keep(g * NZ + zq, sides[g])

    def take_shared(t, keep):
        for zq in range(NZ):
            keep(2 * NZ + zq, qg_ref[t, zq, 2])

    def take_key(n):
        kaug[n * TR : (n + 1) * TR, 0:HS] = kv_ref[0, kv_index(n), 1, 0:TR]
        for s in range(2):
            ktext[s, n * CR : (n + 1) * CR, 0:HS] = kv_ref[0, kv_index(n), s, TR:BR]
            vtext[s, n * CR : (n + 1) * CR] = kv_ref[1, kv_index(n), s, TR:BR]

    def take_key_own(d):
        mask = own_is_long(z, (x + d) % NX)
        mine, other = kv_index(2 * d), kv_index(2 * d + 1)
        rows = slice(d * TR, (d + 1) * TR)
        for side, value in enumerate(by_side(mask, kv_ref[0, mine, 0, 0:TR], kv_ref[0, other, 0, 0:TR])):
            kaug_own[side, rows, 0:HS] = value
        for side, value in enumerate(by_side(mask, kv_ref[1, mine, 0, 0:TR], kv_ref[1, other, 0, 0:TR])):
            vals_own[side, rows, :] = value

    def weigh(n, keys, weight_ref, slope_ref, rows, columns):
        scores = dot_nt(qaug[n], keys)
        half = jnp.tanh(scores * (0.5 * factor))
        twice = 1.0 + half
        weight = twice.astype(BF)
        weight_ref[rows, columns] = weight
        slope_ref[rows, columns] = (twice * (1.0 - half)).astype(BF)
        return weight

    def block_rows(n):
        return pl.ds(pl.multiple_of(n * TR, TR), TR)

    def forward(n, fresh=False):
        take_key(n)
        columns = slice(n * TR, (n + 1) * TR)

        def step(half, carry):
            for u in range(2):
                zq = 2 * half + u
                block = 2 * NZ + zq
                weight = weigh(block, kaug[columns, :], weights, slopes, block_rows(zq), columns)
                share = dot_nn(weight, kv_ref[1, kv_index(n), 1, 0:TR])
                if fresh:
                    oacc[block] = share
                else:
                    oacc[block] += share
            return carry

        lax.fori_loop(0, NZ // 2, step, 0)

    def forward_own(d, fresh=False):
        take_key_own(d)
        columns = slice(d * TR, (d + 1) * TR)

        def step(zq, carry):
            for g in range(2):
                block = g * NZ + zq
                keys = kaug_own[g, columns, :]
                weight = weigh(block, keys, weights_own, slopes_own, block_rows(block), columns)
                share = dot_nn(weight, vals_own[g, columns, :])
                if fresh:
                    oacc[block] = share
                else:
                    oacc[block] += share
            return carry

        lax.fori_loop(0, NZ, step, 0)

    own_text = slice(SIDE, SIDE + TEXT)
    shared_text = slice(LAT, LAT + TEXT)

    def forward_text(zq):
        totals = []
        for g in range(NH):
            block = g * NZ + zq
            if g == 2:
                weight = weigh(block, ktext[1], weights, slopes, block_rows(zq), shared_text)
            else:
                weight = weigh(block, ktext[0], weights_own, slopes_own, block_rows(block), own_text)
            totals.append((oacc[block] + dot_nn(weight, vtext[g // 2])) * 0.5)
        mine, other = by_side(own_is_long(zq, x), totals[0], totals[1])
        oq_ref[0, zq, y] = mine
        oq_ref[0, zq, 1 - y] = other
        oq_ref[0, zq, 2] = totals[2].astype(BF)

    def slope_step(block, slope_ref, rows, columns, vals, keys, fresh):
        slope = (dot_nt(gsel[block], vals) * wide(slope_ref[rows, columns])).astype(BF)
        slope_ref[rows, columns] = slope
        share = dot_nn(slope, keys)
        if fresh:
            qacc[block] = share
        else:
            qacc[block] += share

    def slope_shared(d):
        columns = slice(d * 2 * TR, (d + 1) * 2 * TR)

        def step(zq, carry):
            vals = jnp.concatenate(
                [kv_ref[1, kv_index(2 * d + r), 1, 0:TR] for r in range(2)], axis=0
            )
            keys = kaug[columns, 0:HS]
            slope_step(2 * NZ + zq, slopes, block_rows(zq), columns, vals, keys, False)
            return carry

        lax.fori_loop(0, NZ, step, 0)

    def slope_shared_text():
        def step(zq, carry):
            rows = block_rows(zq)
            slope_step(2 * NZ + zq, slopes, rows, shared_text, vtext[1], ktext[1, :, 0:HS], True)
            return carry

        lax.fori_loop(0, NZ, step, 0)

    def slope_own_row(d, zq):
        columns = slice(d * TR, (d + 1) * TR)
        for g in range(2):
            block = g * NZ + zq
            vals, keys = vals_own[g, columns, :], kaug_own[g, columns, 0:HS]
            slope_step(block, slopes_own, block_rows(block), columns, vals, keys, False)

    def slope_own(d):
        def step(half, carry):
            for u in range(2):
                slope_own_row(d, 2 * half + u)
            return carry

        lax.fori_loop(0, NZ // 2, step, 0)

    def slope_own_text():
        def step(half, carry):
            for u in range(2):
                for g in range(2):
                    block = g * NZ + 2 * half + u
                    rows = block_rows(block)
                    slope_step(block, slopes_own, rows, own_text, vtext[0], ktext[0, :, 0:HS], True)
            return carry

        lax.fori_loop(0, NZ // 2, step, 0)

    def finish_dq(zq):
        mine, other = by_side(own_is_long(zq, x), qacc[zq] * 0.25, qacc[NZ + zq] * 0.25)
        oq_ref[1, zq, y] = mine
        oq_ref[1, zq, 1 - y] = other
        oq_ref[1, zq, 2] = (qacc[2 * NZ + zq] * 0.25).astype(BF)

    left_of = (queries_t, grads_t)
    scale_of = (0.25, 0.5)

    def key_grads_shared(d):
        for t in range(2):
            right = (slopes, weights)[t][:, d * 2 * TR : (d + 1) * 2 * TR]
            total = (dot_nn(left_of[t][:, 2 * NZ * TR :], right) * scale_of[t]).astype(BF)
            for r in range(2):
                kvg_ref[t, kv_index(2 * d + r), 1, 0:TR] = total[:, r * TR : (r + 1) * TR].T

    def key_grads_own(d):
        mask = own_is_long(z, (x + d) % NX)
        for t in range(2):
            sides = []
            for g in range(2):
                rows = slice(g * SIDE, (g + 1) * SIDE)
                right = (slopes_own, weights_own)[t][rows, d * TR : (d + 1) * TR]
                total = dot_nn(left_of[t][:, rows], right) * scale_of[t]
                sides.append(total.astype(BF).T)
            mine, other = by_side(mask, sides[0], sides[1])
            kvg_ref[t, kv_index(2 * d), 0, 0:TR] = mine
            kvg_ref[t, kv_index(2 * d + 1), 0, 0:TR] = other

    def key_grads_text(s):
        for t in range(2):
            if s == 0:
                left = left_of[t][:, 0 : 2 * NZ * TR]
                right = (slopes_own, weights_own)[t][:, own_text]
            else:
                left = left_of[t][:, 2 * NZ * TR :]
                right = (slopes, weights)[t][:, shared_text]
            text_rows = (dot_nn(left, right) * scale_of[t]).astype(BF).T
            for n in range(NY * NX):
                kvg_ref[t, kv_index(n), s, TR:BR] = text_rows[n * CR : (n + 1) * CR]


    def z_far(t):
        rsend(6 * t + 0, oq_ref.at[t, zf, :, first], z_in.at[t, 0], "up")
        rsend(6 * t + 3, oq_ref.at[t, zf, :, second], z_in.at[t, 3], "down")

    def z_near(t):
        rsend(6 * t + 1, oq_ref.at[t, zd, :, first], z_in.at[t, 1], "down")
        rsend(6 * t + 4, oq_ref.at[t, zu, :, second], z_in.at[t, 4], "up")

    def z_relay(t):
        base = 6 * t
        rarrived(base + 0, z_in.at[t, 0])
        z_sum[t, 0] = (wide(z_in[t, 0]) + wide(oq_ref[t, zu, :, first])).astype(BF)
        rsend(base + 2, z_sum.at[t, 0], z_in.at[t, 2], "up")
        rarrived(base + 3, z_in.at[t, 3])
        z_sum[t, 1] = (wide(z_in[t, 3]) + wide(oq_ref[t, zd, :, second])).astype(BF)
        rsend(base + 5, z_sum.at[t, 1], z_in.at[t, 5], "down")

    def z_total(t, scale):
        base = 6 * t
        for n in (1, 2, 4, 5):
            rarrived(base + n, z_in.at[t, n])
        for rows, one, two in ((first, 1, 2), (second, 4, 5)):

            def total(j):
                value = wide(oq_ref[t, z, j, rows]) + wide(z_in[t, one, j]) + wide(z_in[t, two, j])
                return (value * scale).astype(BF) if scale != 1.0 else value.astype(BF)

            yq_out[t, rows] = total(1 - y)
            keep_q[t, 0, rows] = total(y)
            keep_q[t, 1, rows] = total(2)
        rsend(24 + t, yq_out.at[t], yq_in.at[t], "pair")

    def x_base(t, a):
        return 12 + 6 * t + 3 * a

    ring = (("right", "left"), ("left", "right"))
    ahead = ((xr, xl), (xl, xr))
    plane = (y, 1 - y)

    def x_far(t, a):
        src = kvg_ref.at[t, plane[a] * NX + xf]
        rsend(x_base(t, a), src, x_in.at[t, a, 0], ring[t][0])

    def x_near(t, a):
        src = kvg_ref.at[t, plane[a] * NX + ahead[t][1]]
        rsend(x_base(t, a) + 1, src, x_in.at[t, a, 1], ring[t][1])

    def x_relay(t, a):
        rarrived(x_base(t, a), x_in.at[t, a, 0])
        mine = wide(kvg_ref[t, plane[a] * NX + ahead[t][0]])
        x_sum[t, a] = (wide(x_in[t, a, 0]) + mine).astype(BF)
        rsend(x_base(t, a) + 2, x_sum.at[t, a], x_in.at[t, a, 2], ring[t][0])

    def x_total(t, a):
        rarrived(x_base(t, a) + 1, x_in.at[t, a, 1])
        rarrived(x_base(t, a) + 2, x_in.at[t, a, 2])
        value = wide(kvg_ref[t, plane[a] * NX + x]) + wide(x_in[t, a, 1]) + wide(x_in[t, a, 2])
        return value * factor if t == 0 else value

    def project(n):
        return dot_nn(attn[...], feature(n)).astype(BF)

    send(1, go_hbm.at[second], go_relay.at[1], "back")
    load[4].wait()
    q_pair[0] = by_y(q_ref[:, cols(1)], q_ref[:, cols(0)])
    send(6, q_pair.at[0], qg_ref.at[0, z, y], "pair")
    qg_ref[0, z, y] = by_y(q_ref[:, cols(0)], q_ref[:, cols(1)])
    qg_ref[0, z, 2] = q_ref[:, cols(2)]
    z_own(0)
    c = y * NX + x
    for t, (ref, text) in enumerate(((k_ref, tk_ref), (v_ref, tv_ref))):
        load[2 * t].wait()
        load[2 * t + 1].wait()
        st_pair[t, 0, 0:TR] = by_y(ref[:, cols(1)], ref[:, cols(0)])
        st_pair[t, 0, TR:BR] = by_y(text[:, cols(1)], text[:, cols(0)])
        st_pair[t, 1, 0:TR] = ref[:, cols(2)]
        st_pair[t, 1, TR:BR] = text[:, cols(2)]
        send(7 + t, st_pair.at[t], kv_ref.at[t, c], "pair")
        kv_ref[t, c, 0, 0:TR] = by_y(ref[:, cols(0)], ref[:, cols(1)])
        kv_ref[t, c, 0, TR:BR] = by_y(text[:, cols(0)], text[:, cols(1)])
        kv_ref[t, c, 1, 0:TR] = ref[:, cols(2)]
        kv_ref[t, c, 1, TR:BR] = text[:, cols(2)]
        x_send(0, t, y)
    send(2, go_hbm, goall.at[head], "core")
    load[7].wait()
    load[8].wait()
    key_side()
    lax.fori_loop(0, BLOCKS, query_side, 0)
    z_own_forward(0)
    arrived(6, qg_ref.at[0, z, 1 - y])
    z_pair(0)
    load[5].wait()
    load[6].wait()
    acc[...] = dot_nt(go_ref[...], feature(head))
    x_forward(0, y)
    z_pair_forward(0)
    for t in range(2):
        arrived(7 + t, kv_ref.at[t, (1 - y) * NX + x])
        x_send(1, t, 1 - y)
    send(0, go_hbm.at[first], go_relay.at[0], "pair")
    z_own_finish(0)
    z_pair_finish(0)
    take_shared(0, keep_query)
    take_own(0, keep_query)
    forward(0, True)
    arrived(2, goall.at[core_head])
    acc[...] += dot_nt(goall[core_head], feature(core_head))
    forward(1)
    forward_own(0, True)
    arrived(0, go_relay.at[0])
    send(3, go_relay.at[0], goall.at[head, first], "back")
    arrived(1, go_relay.at[1])
    send(4, go_relay.at[1], goall.at[other_head, second], "pair")
    x_near_finish(0, y)
    x_far_finish(0, y)
    forward(2)
    forward(6)
    x_forward(1, 1 - y)
    forward(4)
    arrived(3, goall.at[other_head, first])
    arrived(4, goall.at[other_head, second])
    send(5, goall.at[other_head], goall.at[other_head], "core")
    acc[...] += dot_nt(goall[other_head], feature(other_head))
    x_near_finish(1, 1 - y)
    forward(3)
    forward_own(1)
    arrived(5, goall.at[core_other])
    grad = (acc[...] + dot_nt(goall[core_other], feature(core_other))).astype(BF)
    q_pair[1] = by_y(grad[:, cols(1)], grad[:, cols(0)])
    send(9, q_pair.at[1], qg_ref.at[1, z, y], "pair")
    qg_ref[1, z, y] = by_y(grad[:, cols(0)], grad[:, cols(1)])
    qg_ref[1, z, 2] = grad[:, cols(2)]
    z_own(1)
    forward(7)
    forward_own(3)
    arrived(9, qg_ref.at[1, z, 1 - y])
    z_pair(1)
    z_own_forward(1)
    x_far_finish(1, 1 - y)
    forward(5)
    forward_own(2)
    forward_text(zf)
    z_far(0)
    forward_text(zu)
    forward_text(zd)
    z_near(0)
    forward_text(z)
    z_pair_forward(1)

    z_own_finish(1)
    take_shared(1, keep_grad)
    slope_shared_text()
    z_relay(0)
    for d in (2, 1):
        slope_shared(d)
    z_pair_finish(1)
    take_own(1, keep_grad)
    slope_own_text()
    for s in range(2):
        key_grads_text(s)
    slope_own(2)
    key_grads_own(2)
    key_grads_shared(2)
    for a in (1, 0):
        for t in range(2):
            x_far(t, a)
    z_total(0, 1.0)
    for d in (3, 0):
        slope_shared(d)
    slope_own(1)
    rarrived(24, yq_in.at[0])
    attn[:, cols(0)] = by_y(keep_q[0, 0], yq_in[0])
    attn[:, cols(1)] = by_y(yq_in[0], keep_q[0, 0])
    attn[:, cols(2)] = keep_q[0, 1]
    part[0] = project(core_other)
    rsend(28, part.at[0], core_in.at[0], "core")
    part[2] = project(other_head)
    key_grads_own(1)
    key_grads_shared(1)
    rarrived(28, core_in.at[0])
    pair_sum[...] = (wide(part[2]) + wide(core_in[0])).astype(BF)
    rsend(30, pair_sum.at[first], out_relay.at[0], "pair")
    rsend(31, pair_sum.at[second], out_relay.at[1], "back")
    for a in (1, 0):
        x_near(1, a)
        x_relay(0, a)
    part[1] = project(core_head)
    rsend(29, part.at[1], core_in.at[1], "core")

    slope_own(3)
    key_grads_own(3)
    key_grads_shared(3)
    for a in (1, 0):
        x_near(0, a)
        x_relay(1, a)
    part[3] = project(head)
    for zq in (zf, zu, zd, z):
        slope_own_row(0, zq)
        finish_dq(zq)
        if zq is zf:
            z_far(1)
        elif zq is zd:
            z_near(1)
    rarrived(30, out_relay.at[0])
    rsend(32, out_relay.at[0], far_in.at[first], "back")
    rarrived(31, out_relay.at[1])
    rsend(33, out_relay.at[1], far_in.at[second], "pair")
    z_relay(1)
    key_grads_own(0)
    key_grads_shared(0)
    for t in range(2):
        yk_out[t] = x_total(t, 1).astype(BF)
        rsend(26 + t, yk_out.at[t], yk_in.at[t], "pair")
    z_total(1, factor)

    stores = []

    def store(src, dst):
        copy = pltpu.make_async_copy(src, dst, store_sem.at[len(stores)])
        copy.start()
        stores.append(copy)

    results = ((gk_ref, gtk_ref, gk_hbm, gtk_hbm), (gv_ref, gtv_ref, gv_hbm, gtv_hbm))
    rarrived(29, core_in.at[1])
    rarrived(32, far_in.at[first])
    rarrived(33, far_in.at[second])
    out_ref[...] = (wide(part[3]) + wide(core_in[1]) + wide(far_in[...])).astype(BF)
    store(out_ref, out_hbm)
    for t, (ref, text, to, text_to) in enumerate(results):
        own = x_total(t, 0)
        rarrived(26 + t, yk_in.at[t])
        mine = own[0].astype(BF)
        other = yk_in[t, 0]
        both = (own[1] + wide(yk_in[t, 1])).astype(BF)
        for h, value in ((0, by_y(mine, other)), (1, by_y(other, mine)), (2, both)):
            ref[:, cols(h)] = value[0:TR]
            text[:, cols(h)] = value[TR:BR]
        store(ref, to)
        store(text, text_to)
    rarrived(25, yq_in.at[1])
    gq_ref[:, cols(0)] = by_y(keep_q[1, 0], yq_in[1])
    gq_ref[:, cols(1)] = by_y(yq_in[1], keep_q[1, 0])
    gq_ref[:, cols(2)] = keep_q[1, 1]
    store(gq_ref, gq_hbm)
    for copy in sent:
        copy.wait_send()
    for copy in stores:
        copy.wait()


def store_kernel(*refs):
    count = (len(refs) - 2) // 3
    held, result, buffers = refs[:count], refs[count : 2 * count], refs[2 * count : 3 * count]
    load_sem, store_sem = refs[-2:]
    loads = [
        pltpu.make_async_copy(held[n], buffers[n], load_sem.at[n]) for n in range(count)
    ]
    stores = [
        pltpu.make_async_copy(buffers[n], result[n], store_sem.at[n]) for n in range(count)
    ]
    for copy in loads:
        copy.start()
    for load, copy in zip(loads, stores):
        load.wait()
        copy.start()
    for copy in stores:
        copy.wait()


def shards(
    queries,
    keys,
    values,
    text_keys,
    text_values,
    head_bias,
    out_weight,
    grad_out,
    clip_lengths,
    tile_mask,
    caption_order,
):
    smem = pl.BlockSpec(memory_space=pltpu.SMEM)
    hbm = pl.BlockSpec(memory_space=pltpu.HBM)
    dma = pltpu.SemaphoreType.DMA
    qg_shape = (2, NZ, NH, TR, HS)
    kv_shape = (2, NY * NX, 2, BR, HS)
    out_cols = grad_out.shape[1]
    order = caption_order.reshape(CLIPS, CAP)
    token = pltpu.VMEM((TR, NH * HS), BF)
    text = pltpu.VMEM((CR, NH * HS), BF)
    wide_out = pltpu.VMEM((TR, out_cols), BF)
    halves = pltpu.VMEM((2, HALF, out_cols), BF)
    token_shape = jax.ShapeDtypeStruct((TR, NH * HS), BF)
    text_shape = jax.ShapeDtypeStruct((CR, NH * HS), BF)
    result = (
        jax.ShapeDtypeStruct((TR, out_cols), BF),
        token_shape,
        token_shape,
        token_shape,
        text_shape,
        text_shape,
    )
    held = pl.pallas_call(
        fused_kernel,
        out_shape=result,
        in_specs=[hbm] * 9 + [smem] * 2,
        out_specs=(hbm,) * len(result),
        scratch_shapes=[
            token,
            token,
            token,
            text,
            text,
            wide_out,
            pltpu.VMEM(out_weight.shape, BF),
            pltpu.VMEM(tile_mask.shape, jnp.int32),
            pltpu.VMEM(order.shape, jnp.int32),
            wide_out,
            token,
            token,
            token,
            text,
            text,
            pltpu.VMEM(qg_shape, BF),
            pltpu.VMEM(kv_shape, BF),
            pltpu.VMEM((2, 2, BR, HS), BF),
            pltpu.VMEM((2, TR, HS), BF),
            pltpu.VMEM((4, TR, out_cols), BF),
            halves,
            pltpu.VMEM((TR, NH * HS), F32),
            pltpu.VMEM((LAT, 2 * HS), BF),
            pltpu.VMEM((2, SIDE, 2 * HS), BF),
            pltpu.VMEM((2, TEXT, 2 * HS), BF),
            pltpu.VMEM((2, SIDE, HS), BF),
            pltpu.VMEM((2, TEXT, HS), BF),
            pltpu.VMEM((BLOCKS, TR, 2 * HS), BF),
            pltpu.VMEM((BLOCKS, TR, HS), BF),
            pltpu.VMEM((NZ * TR, LAT + TEXT), BF),
            pltpu.VMEM((NZ * TR, LAT + TEXT), BF),
            pltpu.VMEM((2 * NZ * TR, SIDE + TEXT), BF),
            pltpu.VMEM((2 * NZ * TR, SIDE + TEXT), BF),
            pltpu.VMEM((HS, BLOCKS * TR), BF),
            pltpu.VMEM((HS, BLOCKS * TR), BF),
            pltpu.VMEM((BLOCKS, TR, HS), F32),
            pltpu.VMEM((BLOCKS, TR, HS), F32),
            pltpu.VMEM(qg_shape, BF),
            pltpu.VMEM(kv_shape, BF),
            pltpu.VMEM((2, 6, NH, HALF, HS), BF),
            pltpu.VMEM((2, 2, NH, HALF, HS), BF),
            pltpu.VMEM((2, NY, 3, 2, BR, HS), BF),
            pltpu.VMEM((2, NY, 2, BR, HS), BF),
            pltpu.VMEM((2, TR, HS), BF),
            pltpu.VMEM((2, TR, HS), BF),
            pltpu.VMEM((2, 2, BR, HS), BF),
            pltpu.VMEM((2, 2, BR, HS), BF),
            pltpu.VMEM((2, 2, TR, HS), BF),
            token,
            pltpu.VMEM((4, TR, out_cols), BF),
            pltpu.VMEM((2, TR, out_cols), BF),
            wide_out,
            halves,
            wide_out,
            dma((42,)),
            dma((42,)),
            dma((34,)),
            dma((34,)),
            dma((9,)),
            dma((len(result),)),
        ],
        compiler_params=pltpu.CompilerParams(
            collective_id=0, has_side_effects=True, vmem_limit_bytes=VMEM_LIMIT
        ),
    )(
        queries,
        keys,
        values,
        text_keys,
        text_values,
        grad_out,
        out_weight,
        tile_mask,
        order,
        clip_lengths,
        head_bias,
    )
    return pl.pallas_call(
        store_kernel,
        out_shape=result,
        in_specs=[hbm] * len(result),
        out_specs=(hbm,) * len(result),
        scratch_shapes=[pltpu.VMEM(array.shape, array.dtype) for array in result]
        + [dma((len(result),)), dma((len(result),))],
        compiler_params=pltpu.CompilerParams(vmem_limit_bytes=VMEM_LIMIT),
    )(*held)


def solution(mesh):
    in_specs = (
        P("seq", "head"),
        P("seq", "head"),
        P("seq", "head"),
        P("seq", "head"),
        P("seq", "head"),
        P("head"),
        P("head", None),
        P("seq", "head"),
        P(),
        P(),
        P(),
    )
    out_specs = (P("seq", "head"),) * 6
    return jax.shard_map(shards, mesh=mesh, in_specs=in_specs, out_specs=out_specs, check_vma=False)
```

```python
import jax
import jax.numpy as jnp
from jax import lax
from jax.experimental import pallas as pl
from jax.experimental.pallas import tpu as pltpu
from jax.sharding import PartitionSpec as P

MESH = pl.DeviceIdType.MESH
BF = jnp.bfloat16
F32 = jnp.float32

NX, NZ, NY = 4, 4, 2
HS = 128
NH = 3
TR = 256
CR = 16
BR = TR + CR
HALF = TR // 2
CLIPS = 4
CAP = 128
TILE = 64
LAT = NY * NX * TR
ROWS = NY * NX * BR
MASKED = -32768.0
BLOCKS = NH * NZ
SIDE = NX * TR
TEXT = NY * NX * CR
VMEM_LIMIT = 58 * 1024 * 1024


def place():
    seq = lax.axis_index("seq")
    head = lax.axis_index("head")
    y = seq // (NZ * NX)
    z = (seq // NX) % NZ
    x = seq % NX
    return seq, head, y, z, x


def peers(seq, head, y, z, x):
    def at(yy, zz, xx):
        return (yy * NZ + zz) * NX + xx

    other_head = (head + 2) % 4
    core_head = head + 1 - 2 * (head % 2)
    return {
        "pair": (at(1 - y, z, x), head),
        "back": (at(1 - y, z, x), other_head),
        "core": (seq, core_head),
        "right": (at(y, z, (x + 1) % NX), head),
        "left": (at(y, z, (x + NX - 1) % NX), head),
        "up": (at(y, (z + 1) % NZ, x), head),
        "down": (at(y, (z + NZ - 1) % NZ, x), head),
    }


def greet(peer):
    barrier = pltpu.get_barrier_semaphore()
    for device in peer.values():
        pl.semaphore_signal(barrier, inc=1, device_id=device, device_id_type=MESH)
    pl.semaphore_wait(barrier, len(peer))


def sender(peer, send_sem, recv_sem, sent):
    def send(n, src, dst, to):
        copy = pltpu.make_async_remote_copy(
            src_ref=src,
            dst_ref=dst,
            send_sem=send_sem.at[n],
            recv_sem=recv_sem.at[n],
            device_id=peer[to],
            device_id_type=MESH,
        )
        copy.start()
        sent.append(copy)

    def arrived(n, dst):
        pltpu.make_async_remote_copy(
            src_ref=dst,
            dst_ref=dst,
            send_sem=send_sem.at[n],
            recv_sem=recv_sem.at[n],
            device_id=peer["core"],
            device_id_type=MESH,
        ).wait_recv()

    return send, arrived


def dot_nt(a, b):
    return lax.dot_general(a, b, (((1,), (1,)), ((), ())), preferred_element_type=F32)


def dot_nn(a, b):
    return lax.dot_general(a, b, (((1,), (0,)), ((), ())), preferred_element_type=F32)


def fused_kernel(
    q_hbm,
    k_hbm,
    v_hbm,
    tk_hbm,
    tv_hbm,
    go_hbm,
    w_hbm,
    tile_hbm,
    order_hbm,
    len_ref,
    bias_ref,
    out_hbm,
    gq_hbm,
    gk_hbm,
    gv_hbm,
    gtk_hbm,
    gtv_hbm,
    q_ref,
    k_ref,
    v_ref,
    tk_ref,
    tv_ref,
    go_ref,
    w_ref,
    tile_ref,
    order_ref,
    out_ref,
    gq_ref,
    gk_ref,
    gv_ref,
    gtk_ref,
    gtv_ref,
    qg_ref,
    kv_ref,
    st_pair,
    q_pair,
    goall,
    go_relay,
    acc,
    kaug,
    kaug_own,
    ktext,
    vals_own,
    vals,
    qaug,
    gsel,
    weights,
    slopes,
    weights_own,
    slopes_own,
    queries_t,
    grads_t,
    oacc,
    qacc,
    oq_ref,
    kvg_ref,
    z_in,
    z_sum,
    x_in,
    x_sum,
    yq_out,
    yq_in,
    yk_out,
    yk_in,
    keep_q,
    attn,
    part,
    core_in,
    pair_sum,
    out_relay,
    far_in,
    g_send,
    g_recv,
    r_send,
    r_recv,
    local_sem,
    store_sem,
):
    seq, head, y, z, x = place()
    peer = peers(seq, head, y, z, x)
    zu, zd, zf = (z + 1) % NZ, (z + NZ - 1) % NZ, (z + 2) % NZ
    xr, xl, xf = (x + 1) % NX, (x + NX - 1) % NX, (x + 2) % NX
    other_head = (head + 2) % 4
    core_head = head + 1 - 2 * (head % 2)
    core_other = core_head + 2 - 4 * (core_head // 2)
    first, second = pl.ds(0, HALF), pl.ds(HALF, HALF)
    sent = []
    send, arrived = sender(peer, g_send, g_recv, sent)
    rsend, rarrived = sender(peer, r_send, r_recv, sent)
    cols = lambda h: slice(h * HS, (h + 1) * HS)
    by_y = lambda a, b: jnp.where(y == 0, a, b)
    wide = lambda a: a.astype(F32)
    factor = HS ** (-0.5)

    load = []
    for n, (src, dst) in enumerate(
        (
            (k_hbm, k_ref),
            (tk_hbm, tk_ref),
            (v_hbm, v_ref),
            (tv_hbm, tv_ref),
            (q_hbm, q_ref),
            (go_hbm, go_ref),
            (w_hbm, w_ref),
            (tile_hbm, tile_ref),
            (order_hbm, order_ref),
        )
    ):
        copy = pltpu.make_async_copy(src, dst, local_sem.at[n])
        copy.start()
        load.append(copy)

    greet(peer)


    def x_send(a, t, yy):
        c = yy * NX + x
        send(10 + 6 * a + 2 * t, kv_ref.at[t, c], kv_ref.at[t, c], ("right", "left")[t])
        send(11 + 6 * a + 2 * t, kv_ref.at[t, c], kv_ref.at[t, c], ("left", "right")[t])

    def x_forward(a, t, yy):
        base = 10 + 6 * a
        source = yy * NX + (xl, xr)[t]
        arrived(base + 2 * t, kv_ref.at[t, source])
        send(base + 4 + t, kv_ref.at[t, source], kv_ref.at[t, source], ("right", "left")[t])

    def x_near_finish(a, t, yy):
        arrived(10 + 6 * a + 1 + 2 * t, kv_ref.at[t, yy * NX + (xr, xl)[t]])

    def x_far_finish(a, t, yy):
        arrived(10 + 6 * a + 4 + t, kv_ref.at[t, yy * NX + xf])

    def z_own(t):
        base = 22 + 10 * t
        send(base + 0, qg_ref.at[t, z, 2], qg_ref.at[t, z, 2], "up")
        send(base + 1, qg_ref.at[t, z, y], qg_ref.at[t, z, y], "down")
        send(base + 2, qg_ref.at[t, z, y], qg_ref.at[t, z, y], "up")
        send(base + 3, qg_ref.at[t, z, 2], qg_ref.at[t, z, 2], "down")

    def z_own_forward(t):
        base = 22 + 10 * t
        arrived(base + 0, qg_ref.at[t, zd, 2])
        send(base + 4, qg_ref.at[t, zd, 2], qg_ref.at[t, zd, 2], "up")
        arrived(base + 1, qg_ref.at[t, zu, y])
        send(base + 5, qg_ref.at[t, zu, y], qg_ref.at[t, zu, y], "down")

    def z_pair(t):
        base = 22 + 10 * t
        send(base + 6, qg_ref.at[t, z, 1 - y], qg_ref.at[t, z, 1 - y], "up")
        send(base + 7, qg_ref.at[t, z, 1 - y], qg_ref.at[t, z, 1 - y], "down")

    def z_pair_forward(t):
        base = 22 + 10 * t
        arrived(base + 6, qg_ref.at[t, zd, 1 - y])
        src = qg_ref.at[t, zd, 1 - y, first]
        send(base + 8, src, src, "up")
        arrived(base + 7, qg_ref.at[t, zu, 1 - y])
        src = qg_ref.at[t, zu, 1 - y, second]
        send(base + 9, src, src, "down")

    def z_own_finish(t):
        base = 22 + 10 * t
        arrived(base + 2, qg_ref.at[t, zd, y])
        arrived(base + 3, qg_ref.at[t, zu, 2])
        arrived(base + 4, qg_ref.at[t, zf, 2])
        arrived(base + 5, qg_ref.at[t, zf, y])

    def z_pair_finish(t):
        base = 22 + 10 * t
        arrived(base + 8, qg_ref.at[t, zf, 1 - y, first])
        arrived(base + 9, qg_ref.at[t, zf, 1 - y, second])

    def feature(n):
        return w_ref[:, pl.ds(pl.multiple_of(n * 768, 128), 768)]

    half_rows = NZ * NX * TR
    ends = [len_ref[0]]
    for c in range(1, CLIPS):
        ends.append(ends[-1] + len_ref[c])
    long_start = 0
    for c in range(1, CLIPS):
        long_start = jnp.where(len_ref[c] == half_rows, ends[c - 1], long_start)

    def clip_at(pos):
        total = 0
        for c in range(CLIPS - 1):
            total = total + jnp.where(pos >= ends[c], 1, 0)
        return total

    row_index = lax.broadcasted_iota(jnp.int32, (TR, HS), 0)

    def chunk_rows(zz, xx):
        return (zz * NX + xx) * TR + row_index

    def own_is_long(zz, xx):
        t = chunk_rows(zz, xx)
        return jnp.where(y == 0, t - long_start, long_start - 1 - t) >= 0

    def by_side(mask, mine, other):
        mine, other = wide(mine), wide(other)
        return jnp.where(mask, mine, other).astype(BF), jnp.where(mask, other, mine).astype(BF)

    lane = lax.broadcasted_iota(jnp.int32, (1, HS), 1)
    tiles_here = (lane % 64) // 16 == z
    clip_lane = ((z + 1) % NZ) * 16
    bias_lane = clip_lane + CLIPS
    bias_ones = jnp.where((lane >= bias_lane) & (lane < bias_lane + 3), 1.0, 0.0)

    def kv_index(n):
        return ((y + n % 2) % NY) * NX + (x + n // 2) % NX

    def key_columns(pos):
        hit = (tiles_here & ((pos >> 6) == lane)) | (clip_at(pos) == lane - clip_lane)
        return jnp.where(hit, 1.0, bias_ones).astype(BF)

    def key_side():
        for d in range(NX):
            t = chunk_rows(z, (x + d) % NX)
            low = key_columns(t)
            high = key_columns(t + half_rows)
            for r in range(2):
                n = 2 * d + r
                plane_zero = (y + r) % NY == 0
                kaug[n * TR : (n + 1) * TR, HS:] = jnp.where(plane_zero, low, high)
            for side, value in enumerate(by_side(t >= long_start, low, high)):
                kaug_own[side, d * TR : (d + 1) * TR, HS:] = value
        row = lax.broadcasted_iota(jnp.int32, (TEXT, HS), 0)
        n = row // CR
        plane = ((y + n % 2) % NY) * NZ + z
        text_row = (plane * NX + (x + n // 2) % NX) * CR + row % CR
        aug = jnp.broadcast_to(bias_ones, text_row.shape)
        for c in range(CLIPS):
            listed = jnp.where(order_ref[c : c + 1, :] == text_row, 1.0, 0.0)
            found = jnp.max(listed, axis=1, keepdims=True)
            aug = jnp.where(lane == clip_lane + c, found, aug)
        for s in range(2):
            ktext[s, :, HS:] = aug.astype(BF)

    log_len = [
        jnp.log(jnp.full((1, HS), len_ref[c] + CAP, jnp.int32).astype(F32)) for c in range(CLIPS)
    ]

    def query_side(n, carry):
        g, zq = n // NZ, n % NZ
        t = chunk_rows(zq, x)
        in_high = jnp.where(g == 0, long_start - 1 - t, t - long_start)
        in_high = jnp.where(g == 2, 2 * y - 1, in_high) >= 0
        pos = t + jnp.where(in_high, half_rows, 0)
        head_bias = bias_ref[jnp.where(g == 2, 2, y)]
        clip = clip_at(pos)
        offset = jnp.broadcast_to(log_len[CLIPS - 1], (TR, HS))
        for c in range(CLIPS - 2, -1, -1):
            offset = jnp.where(pos < ends[c], log_len[c], offset)
        total = (head_bias - offset) * (HS**0.5)
        hi = total.astype(BF).astype(F32)
        mid = (total - hi).astype(BF).astype(F32)
        low = total - hi - mid
        in_bias = jnp.where(lane == bias_lane, hi, jnp.where(lane == bias_lane + 1, mid, low))
        in_bias = jnp.where((lane >= bias_lane) & (lane < bias_lane + 3), in_bias, 0.0)
        in_clip = (lane >= clip_lane) & (lane < clip_lane + CLIPS) & (lane - clip_lane != clip)
        side = jnp.where(in_clip, MASKED, in_bias)
        for u in range(TR // TILE):
            rows = slice(u * TILE, (u + 1) * TILE)
            tile = (zq * NX + x) * (TR // TILE) + u
            off = []
            for p in range(NY):
                at = tile + p * (half_rows // TILE)
                mask_row = tile_ref[pl.ds(at, 1), :]
                off.append(jnp.where((mask_row == 0) & (lane != at) & tiles_here, 1.0, 0.0))
            masked = jnp.where(in_high[rows], off[1], off[0]) > 0.5
            qaug[n, rows, HS:] = jnp.where(masked, MASKED, side[rows]).astype(BF)
        return carry

    def keep_query(n, value):
        qaug[n, :, 0:HS] = value
        queries_t[:, n * TR : (n + 1) * TR] = value.T

    def keep_grad(n, value):
        gsel[n] = value
        grads_t[:, n * TR : (n + 1) * TR] = value.T

    def take_own(t, keep):
        for zq in range(NZ):
            mask = own_is_long(zq, x)
            sides = by_side(mask, qg_ref[t, zq, y], qg_ref[t, zq, 1 - y])
            for g in range(2):
                keep(g * NZ + zq, sides[g])

    def take_shared(t, keep):
        for zq in range(NZ):
            keep(2 * NZ + zq, qg_ref[t, zq, 2])

    def take_key(n):
        kaug[n * TR : (n + 1) * TR, 0:HS] = kv_ref[0, kv_index(n), 1, 0:TR]
        for s in range(2):
            ktext[s, n * CR : (n + 1) * CR, 0:HS] = kv_ref[0, kv_index(n), s, TR:BR]

    def take_value(n):
        vals[n * TR : (n + 1) * TR] = kv_ref[1, kv_index(n), 1, 0:TR]
        vals[LAT + n * CR : LAT + (n + 1) * CR] = kv_ref[1, kv_index(n), 1, TR:BR]
        for g in range(2):
            rows = slice(SIDE + n * CR, SIDE + (n + 1) * CR)
            vals_own[g, rows] = kv_ref[1, kv_index(n), 0, TR:BR]

    def take_sides(t, d, ref, lanes):
        mask = own_is_long(z, (x + d) % NX)
        mine, other = kv_index(2 * d), kv_index(2 * d + 1)
        sides = by_side(mask, kv_ref[t, mine, 0, 0:TR], kv_ref[t, other, 0, 0:TR])
        for side, value in enumerate(sides):
            ref[side, d * TR : (d + 1) * TR, lanes] = value

    def weigh(n, keys, weight_ref, slope_ref, rows, columns):
        scores = dot_nt(qaug[n], keys)
        half = jnp.tanh(scores * (0.5 * factor))
        twice = 1.0 + half
        weight = twice.astype(BF)
        weight_ref[rows, columns] = weight
        slope_ref[rows, columns] = (twice * (1.0 - half)).astype(BF)
        return weight

    def block_rows(n):
        return pl.ds(pl.multiple_of(n * TR, TR), TR)

    def score(n):
        take_key(n)
        columns = slice(n * TR, (n + 1) * TR)

        def step(half, carry):
            for u in range(2):
                zq = 2 * half + u
                rows = block_rows(zq)
                weigh(2 * NZ + zq, kaug[columns, :], weights, slopes, rows, columns)
            return carry

        lax.fori_loop(0, NZ // 2, step, 0)

    def score_own(d):
        take_sides(0, d, kaug_own, slice(0, HS))
        columns = slice(d * TR, (d + 1) * TR)

        def step(zq, carry):
            for g in range(2):
                block = g * NZ + zq
                keys = kaug_own[g, columns, :]
                weigh(block, keys, weights_own, slopes_own, block_rows(block), columns)
            return carry

        lax.fori_loop(0, NZ, step, 0)

    own_text = slice(SIDE, SIDE + TEXT)
    shared_text = slice(LAT, LAT + TEXT)

    def score_text():
        def step(zq, carry):
            for g in range(NH):
                block = g * NZ + zq
                if g == 2:
                    weigh(block, ktext[1], weights, slopes, block_rows(zq), shared_text)
                else:
                    weigh(block, ktext[0], weights_own, slopes_own, block_rows(block), own_text)
            return carry

        lax.fori_loop(0, NZ, step, 0)

    def mix(block, low, high):
        g, zq = block
        if g == 2:
            columns = slice(low * 2 * TR, high * 2 * TR)
            return dot_nn(weights[block_rows(zq), columns], vals[columns, :])
        columns = slice(low * TR, high * TR)
        return dot_nn(weights_own[block_rows(g * NZ + zq), columns], vals_own[g, columns, :])

    def mix_near():
        def step(zq, carry):
            for g in range(NH):
                oacc[g * NZ + zq] = mix((g, zq), 0, 2) + mix((g, zq), 3, 4)
            return carry

        lax.fori_loop(0, NZ, step, 0)

    def mix_far(zq):
        totals = []
        for g in range(NH):
            if g == 2:
                text = dot_nn(weights[block_rows(zq), shared_text], vals[LAT:, :])
            else:
                rows = block_rows(g * NZ + zq)
                text = dot_nn(weights_own[rows, own_text], vals_own[g, SIDE:, :])
            totals.append((oacc[g * NZ + zq] + mix((g, zq), 2, 3) + text) * 0.5)
        mine, other = by_side(own_is_long(zq, x), totals[0], totals[1])
        oq_ref[0, zq, y] = mine
        oq_ref[0, zq, 1 - y] = other
        oq_ref[0, zq, 2] = totals[2].astype(BF)

    def slope_step(block, slope_ref, rows, columns, values, keys, fresh):
        slope = (dot_nt(gsel[block], values) * wide(slope_ref[rows, columns])).astype(BF)
        slope_ref[rows, columns] = slope
        share = dot_nn(slope, keys)
        if fresh:
            qacc[block] = share
        else:
            qacc[block] += share

    def slope_shared(n, fresh=False):
        columns = slice(n * TR, (n + 1) * TR)

        def step(half, carry):
            for u in range(2):
                zq = 2 * half + u
                keys = kaug[columns, 0:HS]
                rows = block_rows(zq)
                slope_step(2 * NZ + zq, slopes, rows, columns, vals[columns, :], keys, fresh)
            return carry

        lax.fori_loop(0, NZ // 2, step, 0)

    def slope_shared_text():
        def step(half, carry):
            for u in range(2):
                zq = 2 * half + u
                keys = ktext[1, :, 0:HS]
                rows = block_rows(zq)
                slope_step(2 * NZ + zq, slopes, rows, shared_text, vals[LAT:, :], keys, False)
            return carry

        lax.fori_loop(0, NZ // 2, step, 0)

    def slope_own_row(d, zq):
        columns = slice(d * TR, (d + 1) * TR)
        for g in range(2):
            block = g * NZ + zq
            side_vals, keys = vals_own[g, columns, :], kaug_own[g, columns, 0:HS]
            slope_step(block, slopes_own, block_rows(block), columns, side_vals, keys, False)

    def slope_own(d):
        def step(half, carry):
            for u in range(2):
                slope_own_row(d, 2 * half + u)
            return carry

        lax.fori_loop(0, NZ // 2, step, 0)

    def slope_own_text():
        def step(half, carry):
            for u in range(2):
                for g in range(2):
                    block = g * NZ + 2 * half + u
                    rows = block_rows(block)
                    keys = ktext[0, :, 0:HS]
                    slope_step(block, slopes_own, rows, own_text, vals_own[g, SIDE:, :], keys, True)
            return carry

        lax.fori_loop(0, NZ // 2, step, 0)

    def finish_dq(zq):
        mine, other = by_side(own_is_long(zq, x), qacc[zq] * 0.25, qacc[NZ + zq] * 0.25)
        oq_ref[1, zq, y] = mine
        oq_ref[1, zq, 1 - y] = other
        oq_ref[1, zq, 2] = (qacc[2 * NZ + zq] * 0.25).astype(BF)

    left_of = (queries_t, grads_t)
    scale_of = (0.25, 0.5)

    def key_grads_shared(d):
        for t in range(2):
            right = (slopes, weights)[t][:, d * 2 * TR : (d + 1) * 2 * TR]
            total = (dot_nn(left_of[t][:, 2 * NZ * TR :], right) * scale_of[t]).astype(BF)
            for r in range(2):
                kvg_ref[t, kv_index(2 * d + r), 1, 0:TR] = total[:, r * TR : (r + 1) * TR].T

    def key_grads_own(d):
        mask = own_is_long(z, (x + d) % NX)
        for t in range(2):
            sides = []
            for g in range(2):
                rows = slice(g * SIDE, (g + 1) * SIDE)
                right = (slopes_own, weights_own)[t][rows, d * TR : (d + 1) * TR]
                total = dot_nn(left_of[t][:, rows], right) * scale_of[t]
                sides.append(total.astype(BF).T)
            mine, other = by_side(mask, sides[0], sides[1])
            kvg_ref[t, kv_index(2 * d), 0, 0:TR] = mine
            kvg_ref[t, kv_index(2 * d + 1), 0, 0:TR] = other

    def key_grads_text(s):
        for t in range(2):
            if s == 0:
                left = left_of[t][:, 0 : 2 * NZ * TR]
                right = (slopes_own, weights_own)[t][:, own_text]
            else:
                left = left_of[t][:, 2 * NZ * TR :]
                right = (slopes, weights)[t][:, shared_text]
            text_rows = (dot_nn(left, right) * scale_of[t]).astype(BF).T
            for n in range(NY * NX):
                kvg_ref[t, kv_index(n), s, TR:BR] = text_rows[n * CR : (n + 1) * CR]


    def z_far(t):
        rsend(6 * t + 0, oq_ref.at[t, zf, :, first], z_in.at[t, 0], "up")
        rsend(6 * t + 3, oq_ref.at[t, zf, :, second], z_in.at[t, 3], "down")

    def z_near(t):
        rsend(6 * t + 1, oq_ref.at[t, zd, :, first], z_in.at[t, 1], "down")
        rsend(6 * t + 4, oq_ref.at[t, zu, :, second], z_in.at[t, 4], "up")

    def z_relay(t):
        base = 6 * t
        rarrived(base + 0, z_in.at[t, 0])
        z_sum[t, 0] = (wide(z_in[t, 0]) + wide(oq_ref[t, zu, :, first])).astype(BF)
        rsend(base + 2, z_sum.at[t, 0], z_in.at[t, 2], "up")
        rarrived(base + 3, z_in.at[t, 3])
        z_sum[t, 1] = (wide(z_in[t, 3]) + wide(oq_ref[t, zd, :, second])).astype(BF)
        rsend(base + 5, z_sum.at[t, 1], z_in.at[t, 5], "down")

    def z_total(t, scale):
        base = 6 * t
        for n in (1, 2, 4, 5):
            rarrived(base + n, z_in.at[t, n])
        for rows, one, two in ((first, 1, 2), (second, 4, 5)):

            def total(j):
                value = wide(oq_ref[t, z, j, rows]) + wide(z_in[t, one, j]) + wide(z_in[t, two, j])
                return (value * scale).astype(BF) if scale != 1.0 else value.astype(BF)

            yq_out[t, rows] = total(1 - y)
            keep_q[t, 0, rows] = total(y)
            keep_q[t, 1, rows] = total(2)
        rsend(24 + t, yq_out.at[t], yq_in.at[t], "pair")

    def x_base(t, a):
        return 12 + 6 * t + 3 * a

    ring = (("right", "left"), ("left", "right"))
    ahead = ((xr, xl), (xl, xr))
    plane = (y, 1 - y)

    def x_far(t, a):
        src = kvg_ref.at[t, plane[a] * NX + xf]
        rsend(x_base(t, a), src, x_in.at[t, a, 0], ring[t][0])

    def x_near(t, a):
        src = kvg_ref.at[t, plane[a] * NX + ahead[t][1]]
        rsend(x_base(t, a) + 1, src, x_in.at[t, a, 1], ring[t][1])

    def x_relay(t, a):
        rarrived(x_base(t, a), x_in.at[t, a, 0])
        mine = wide(kvg_ref[t, plane[a] * NX + ahead[t][0]])
        x_sum[t, a] = (wide(x_in[t, a, 0]) + mine).astype(BF)
        rsend(x_base(t, a) + 2, x_sum.at[t, a], x_in.at[t, a, 2], ring[t][0])

    def x_total(t, a):
        rarrived(x_base(t, a) + 1, x_in.at[t, a, 1])
        rarrived(x_base(t, a) + 2, x_in.at[t, a, 2])
        value = wide(kvg_ref[t, plane[a] * NX + x]) + wide(x_in[t, a, 1]) + wide(x_in[t, a, 2])
        return value * factor if t == 0 else value

    def project(n):
        return dot_nn(attn[...], feature(n)).astype(BF)

    send(1, go_hbm.at[second], go_relay.at[1], "back")
    load[4].wait()
    q_pair[0] = by_y(q_ref[:, cols(1)], q_ref[:, cols(0)])
    send(6, q_pair.at[0], qg_ref.at[0, z, y], "pair")
    qg_ref[0, z, y] = by_y(q_ref[:, cols(0)], q_ref[:, cols(1)])
    qg_ref[0, z, 2] = q_ref[:, cols(2)]
    z_own(0)
    c = y * NX + x
    pair_y = 1 - y
    for t, (ref, text) in enumerate(((k_ref, tk_ref), (v_ref, tv_ref))):
        load[2 * t].wait()
        load[2 * t + 1].wait()
        st_pair[t, 0, 0:TR] = by_y(ref[:, cols(1)], ref[:, cols(0)])
        st_pair[t, 0, TR:BR] = by_y(text[:, cols(1)], text[:, cols(0)])
        st_pair[t, 1, 0:TR] = ref[:, cols(2)]
        st_pair[t, 1, TR:BR] = text[:, cols(2)]
        if t == 0:
            send(7, st_pair.at[0], kv_ref.at[0, c], "pair")
            send(0, go_hbm.at[first], go_relay.at[0], "pair")
        kv_ref[t, c, 0, 0:TR] = by_y(ref[:, cols(0)], ref[:, cols(1)])
        kv_ref[t, c, 0, TR:BR] = by_y(text[:, cols(0)], text[:, cols(1)])
        kv_ref[t, c, 1, 0:TR] = ref[:, cols(2)]
        kv_ref[t, c, 1, TR:BR] = text[:, cols(2)]
        x_send(0, t, y)
    send(2, go_hbm, goall.at[head], "core")
    load[7].wait()
    load[8].wait()
    key_side()
    lax.fori_loop(0, BLOCKS, query_side, 0)
    arrived(1, go_relay.at[1])
    send(4, go_relay.at[1], goall.at[other_head, second], "pair")
    z_own_forward(0)
    arrived(6, qg_ref.at[0, z, 1 - y])
    z_pair(0)
    arrived(7, kv_ref.at[0, pair_y * NX + x])
    x_send(1, 0, pair_y)
    load[5].wait()
    load[6].wait()
    acc[...] = dot_nt(go_ref[...], feature(head))
    x_forward(0, 0, y)
    x_forward(0, 1, y)
    z_pair_forward(0)
    z_own_finish(0)
    take_shared(0, keep_query)
    score(0)
    score(1)
    z_pair_finish(0)
    take_own(0, keep_query)
    arrived(0, go_relay.at[0])
    send(3, go_relay.at[0], goall.at[head, first], "back")
    send(8, st_pair.at[1], kv_ref.at[1, c], "pair")
    x_forward(1, 0, pair_y)
    score_own(0)
    arrived(2, goall.at[core_head])
    acc[...] += dot_nt(goall[core_head], feature(core_head))
    x_near_finish(0, 0, y)
    x_far_finish(0, 0, y)
    score(2)
    score(6)
    score(4)
    arrived(3, goall.at[other_head, first])
    arrived(4, goall.at[other_head, second])
    send(5, goall.at[other_head], goall.at[other_head], "core")
    acc[...] += dot_nt(goall[other_head], feature(other_head))
    x_near_finish(1, 0, pair_y)
    score(3)
    score_own(1)
    arrived(5, goall.at[core_other])
    grad = (acc[...] + dot_nt(goall[core_other], feature(core_other))).astype(BF)
    q_pair[1] = by_y(grad[:, cols(1)], grad[:, cols(0)])
    send(9, q_pair.at[1], qg_ref.at[1, z, y], "pair")
    qg_ref[1, z, y] = by_y(grad[:, cols(0)], grad[:, cols(1)])
    qg_ref[1, z, 2] = grad[:, cols(2)]
    z_own(1)
    arrived(8, kv_ref.at[1, pair_y * NX + x])
    x_send(1, 1, pair_y)
    score(7)
    score_own(3)
    arrived(9, qg_ref.at[1, z, 1 - y])
    z_pair(1)
    z_own_forward(1)
    x_far_finish(1, 0, pair_y)
    score(5)
    score_own(2)
    x_forward(1, 1, pair_y)
    z_pair_forward(1)
    score_text()
    x_near_finish(0, 1, y)
    x_far_finish(0, 1, y)
    for n in (0, 2, 6, 4, 1):
        take_value(n)
    take_sides(1, 0, vals_own, slice(0, HS))

    z_own_finish(1)
    take_shared(1, keep_grad)
    slope_shared(0, True)
    for n in (2, 6, 4):
        slope_shared(n)
    x_near_finish(1, 1, pair_y)
    for n in (3, 7):
        take_value(n)
    for d in (1, 3):
        take_sides(1, d, vals_own, slice(0, HS))
    mix_near()
    x_far_finish(1, 1, pair_y)
    take_value(5)
    take_sides(1, 2, vals_own, slice(0, HS))
    mix_far(zf)
    z_far(0)
    mix_far(zu)
    mix_far(zd)
    z_near(0)
    mix_far(z)
    z_pair_finish(1)
    take_own(1, keep_grad)
    slope_shared_text()
    slope_own_text()
    z_relay(0)
    for s in range(2):
        key_grads_text(s)
    slope_shared(5)
    slope_own(2)
    key_grads_own(2)
    key_grads_shared(2)
    for a in (1, 0):
        for t in range(2):
            x_far(t, a)
    slope_shared(3)
    slope_own(1)
    z_total(0, 1.0)
    slope_shared(7)
    slope_shared(1)
    rarrived(24, yq_in.at[0])
    attn[:, cols(0)] = by_y(keep_q[0, 0], yq_in[0])
    attn[:, cols(1)] = by_y(yq_in[0], keep_q[0, 0])
    attn[:, cols(2)] = keep_q[0, 1]
    part[0] = project(core_other)
    rsend(28, part.at[0], core_in.at[0], "core")
    part[2] = project(other_head)
    key_grads_own(1)
    key_grads_shared(1)
    rarrived(28, core_in.at[0])
    pair_sum[...] = (wide(part[2]) + wide(core_in[0])).astype(BF)
    rsend(30, pair_sum.at[first], out_relay.at[0], "pair")
    rsend(31, pair_sum.at[second], out_relay.at[1], "back")
    for a in (1, 0):
        x_near(1, a)
        x_relay(0, a)
    part[1] = project(core_head)
    rsend(29, part.at[1], core_in.at[1], "core")

    slope_own(3)
    key_grads_own(3)
    key_grads_shared(3)
    for a in (1, 0):
        x_near(0, a)
        x_relay(1, a)
    part[3] = project(head)
    for zq in (zf, zu, zd, z):
        slope_own_row(0, zq)
        finish_dq(zq)
        if zq is zf:
            z_far(1)
        elif zq is zd:
            z_near(1)
    rarrived(30, out_relay.at[0])
    rsend(32, out_relay.at[0], far_in.at[first], "back")
    rarrived(31, out_relay.at[1])
    rsend(33, out_relay.at[1], far_in.at[second], "pair")
    z_relay(1)
    key_grads_own(0)
    key_grads_shared(0)
    for t in range(2):
        yk_out[t] = x_total(t, 1).astype(BF)
        rsend(26 + t, yk_out.at[t], yk_in.at[t], "pair")
    z_total(1, factor)

    stores = []

    def store(src, dst):
        copy = pltpu.make_async_copy(src, dst, store_sem.at[len(stores)])
        copy.start()
        stores.append(copy)

    results = ((gk_ref, gtk_ref, gk_hbm, gtk_hbm), (gv_ref, gtv_ref, gv_hbm, gtv_hbm))
    rarrived(29, core_in.at[1])
    rarrived(32, far_in.at[first])
    rarrived(33, far_in.at[second])
    out_ref[...] = (wide(part[3]) + wide(core_in[1]) + wide(far_in[...])).astype(BF)
    store(out_ref, out_hbm)
    for t, (ref, text, to, text_to) in enumerate(results):
        own = x_total(t, 0)
        rarrived(26 + t, yk_in.at[t])
        mine = own[0].astype(BF)
        other = yk_in[t, 0]
        both = (own[1] + wide(yk_in[t, 1])).astype(BF)
        for h, value in ((0, by_y(mine, other)), (1, by_y(other, mine)), (2, both)):
            ref[:, cols(h)] = value[0:TR]
            text[:, cols(h)] = value[TR:BR]
        store(ref, to)
        store(text, text_to)
    rarrived(25, yq_in.at[1])
    gq_ref[:, cols(0)] = by_y(keep_q[1, 0], yq_in[1])
    gq_ref[:, cols(1)] = by_y(yq_in[1], keep_q[1, 0])
    gq_ref[:, cols(2)] = keep_q[1, 1]
    store(gq_ref, gq_hbm)
    for copy in sent:
        copy.wait_send()
    for copy in stores:
        copy.wait()


def store_kernel(*refs):
    count = (len(refs) - 2) // 3
    held, result, buffers = refs[:count], refs[count : 2 * count], refs[2 * count : 3 * count]
    load_sem, store_sem = refs[-2:]
    loads = [
        pltpu.make_async_copy(held[n], buffers[n], load_sem.at[n]) for n in range(count)
    ]
    stores = [
        pltpu.make_async_copy(buffers[n], result[n], store_sem.at[n]) for n in range(count)
    ]
    for copy in loads:
        copy.start()
    for load, copy in zip(loads, stores):
        load.wait()
        copy.start()
    for copy in stores:
        copy.wait()


def shards(
    queries,
    keys,
    values,
    text_keys,
    text_values,
    head_bias,
    out_weight,
    grad_out,
    clip_lengths,
    tile_mask,
    caption_order,
):
    smem = pl.BlockSpec(memory_space=pltpu.SMEM)
    hbm = pl.BlockSpec(memory_space=pltpu.HBM)
    dma = pltpu.SemaphoreType.DMA
    qg_shape = (2, NZ, NH, TR, HS)
    kv_shape = (2, NY * NX, 2, BR, HS)
    out_cols = grad_out.shape[1]
    order = caption_order.reshape(CLIPS, CAP)
    token = pltpu.VMEM((TR, NH * HS), BF)
    text = pltpu.VMEM((CR, NH * HS), BF)
    wide_out = pltpu.VMEM((TR, out_cols), BF)
    halves = pltpu.VMEM((2, HALF, out_cols), BF)
    token_shape = jax.ShapeDtypeStruct((TR, NH * HS), BF)
    text_shape = jax.ShapeDtypeStruct((CR, NH * HS), BF)
    result = (
        jax.ShapeDtypeStruct((TR, out_cols), BF),
        token_shape,
        token_shape,
        token_shape,
        text_shape,
        text_shape,
    )
    held = pl.pallas_call(
        fused_kernel,
        out_shape=result,
        in_specs=[hbm] * 9 + [smem] * 2,
        out_specs=(hbm,) * len(result),
        scratch_shapes=[
            token,
            token,
            token,
            text,
            text,
            wide_out,
            pltpu.VMEM(out_weight.shape, BF),
            pltpu.VMEM(tile_mask.shape, jnp.int32),
            pltpu.VMEM(order.shape, jnp.int32),
            wide_out,
            token,
            token,
            token,
            text,
            text,
            pltpu.VMEM(qg_shape, BF),
            pltpu.VMEM(kv_shape, BF),
            pltpu.VMEM((2, 2, BR, HS), BF),
            pltpu.VMEM((2, TR, HS), BF),
            pltpu.VMEM((4, TR, out_cols), BF),
            halves,
            pltpu.VMEM((TR, NH * HS), F32),
            pltpu.VMEM((LAT, 2 * HS), BF),
            pltpu.VMEM((2, SIDE, 2 * HS), BF),
            pltpu.VMEM((2, TEXT, 2 * HS), BF),
            pltpu.VMEM((2, SIDE + TEXT, HS), BF),
            pltpu.VMEM((LAT + TEXT, HS), BF),
            pltpu.VMEM((BLOCKS, TR, 2 * HS), BF),
            pltpu.VMEM((BLOCKS, TR, HS), BF),
            pltpu.VMEM((NZ * TR, LAT + TEXT), BF),
            pltpu.VMEM((NZ * TR, LAT + TEXT), BF),
            pltpu.VMEM((2 * NZ * TR, SIDE + TEXT), BF),
            pltpu.VMEM((2 * NZ * TR, SIDE + TEXT), BF),
            pltpu.VMEM((HS, BLOCKS * TR), BF),
            pltpu.VMEM((HS, BLOCKS * TR), BF),
            pltpu.VMEM((BLOCKS, TR, HS), F32),
            pltpu.VMEM((BLOCKS, TR, HS), F32),
            pltpu.VMEM(qg_shape, BF),
            pltpu.VMEM(kv_shape, BF),
            pltpu.VMEM((2, 6, NH, HALF, HS), BF),
            pltpu.VMEM((2, 2, NH, HALF, HS), BF),
            pltpu.VMEM((2, NY, 3, 2, BR, HS), BF),
            pltpu.VMEM((2, NY, 2, BR, HS), BF),
            pltpu.VMEM((2, TR, HS), BF),
            pltpu.VMEM((2, TR, HS), BF),
            pltpu.VMEM((2, 2, BR, HS), BF),
            pltpu.VMEM((2, 2, BR, HS), BF),
            pltpu.VMEM((2, 2, TR, HS), BF),
            token,
            pltpu.VMEM((4, TR, out_cols), BF),
            pltpu.VMEM((2, TR, out_cols), BF),
            wide_out,
            halves,
            wide_out,
            dma((42,)),
            dma((42,)),
            dma((34,)),
            dma((34,)),
            dma((9,)),
            dma((len(result),)),
        ],
        compiler_params=pltpu.CompilerParams(
            collective_id=0, has_side_effects=True, vmem_limit_bytes=VMEM_LIMIT
        ),
    )(
        queries,
        keys,
        values,
        text_keys,
        text_values,
        grad_out,
        out_weight,
        tile_mask,
        order,
        clip_lengths,
        head_bias,
    )
    return pl.pallas_call(
        store_kernel,
        out_shape=result,
        in_specs=[hbm] * len(result),
        out_specs=(hbm,) * len(result),
        scratch_shapes=[pltpu.VMEM(array.shape, array.dtype) for array in result]
        + [dma((len(result),)), dma((len(result),))],
        compiler_params=pltpu.CompilerParams(vmem_limit_bytes=VMEM_LIMIT),
    )(*held)


def solution(mesh):
    in_specs = (
        P("seq", "head"),
        P("seq", "head"),
        P("seq", "head"),
        P("seq", "head"),
        P("seq", "head"),
        P("head"),
        P("head", None),
        P("seq", "head"),
        P(),
        P(),
        P(),
    )
    out_specs = (P("seq", "head"),) * 6
    return jax.shard_map(shards, mesh=mesh, in_specs=in_specs, out_specs=out_specs, check_vma=False)
```

```python
import jax
import jax.numpy as jnp
from jax import lax
from jax.experimental import pallas as pl
from jax.experimental.pallas import tpu as pltpu
from jax.sharding import PartitionSpec as P

MESH = pl.DeviceIdType.MESH
BF = jnp.bfloat16
F32 = jnp.float32

NX, NZ, NY = 4, 4, 2
HS = 128
NH = 3
TR = 256
CR = 16
BR = TR + CR
HALF = TR // 2
CLIPS = 4
CAP = 128
TILE = 64
LAT = NY * NX * TR
ROWS = NY * NX * BR
MASKED = -32768.0
BLOCKS = NH * NZ
SIDE = NX * TR
TEXT = NY * NX * CR
VMEM_LIMIT = 58 * 1024 * 1024


def place():
    seq = lax.axis_index("seq")
    head = lax.axis_index("head")
    y = seq // (NZ * NX)
    z = (seq // NX) % NZ
    x = seq % NX
    return seq, head, y, z, x


def peers(seq, head, y, z, x):
    def at(yy, zz, xx):
        return (yy * NZ + zz) * NX + xx

    other_head = (head + 2) % 4
    core_head = head + 1 - 2 * (head % 2)
    return {
        "pair": (at(1 - y, z, x), head),
        "back": (at(1 - y, z, x), other_head),
        "core": (seq, core_head),
        "right": (at(y, z, (x + 1) % NX), head),
        "left": (at(y, z, (x + NX - 1) % NX), head),
        "up": (at(y, (z + 1) % NZ, x), head),
        "down": (at(y, (z + NZ - 1) % NZ, x), head),
    }


def greet(peer):
    barrier = pltpu.get_barrier_semaphore()
    for device in peer.values():
        pl.semaphore_signal(barrier, inc=1, device_id=device, device_id_type=MESH)
    pl.semaphore_wait(barrier, len(peer))


def sender(peer, send_sem, recv_sem, sent):
    def send(n, src, dst, to):
        copy = pltpu.make_async_remote_copy(
            src_ref=src,
            dst_ref=dst,
            send_sem=send_sem.at[n],
            recv_sem=recv_sem.at[n],
            device_id=peer[to],
            device_id_type=MESH,
        )
        copy.start()
        sent.append(copy)

    def arrived(n, dst):
        pltpu.make_async_remote_copy(
            src_ref=dst,
            dst_ref=dst,
            send_sem=send_sem.at[n],
            recv_sem=recv_sem.at[n],
            device_id=peer["core"],
            device_id_type=MESH,
        ).wait_recv()

    return send, arrived


def dot_nt(a, b):
    return lax.dot_general(a, b, (((1,), (1,)), ((), ())), preferred_element_type=F32)


def dot_nn(a, b):
    return lax.dot_general(a, b, (((1,), (0,)), ((), ())), preferred_element_type=F32)


def fused_kernel(
    q_hbm,
    k_hbm,
    v_hbm,
    tk_hbm,
    tv_hbm,
    go_hbm,
    w_hbm,
    tile_hbm,
    order_hbm,
    len_ref,
    bias_ref,
    out_hbm,
    gq_hbm,
    gk_hbm,
    gv_hbm,
    gtk_hbm,
    gtv_hbm,
    q_ref,
    k_ref,
    v_ref,
    tk_ref,
    tv_ref,
    go_ref,
    w_ref,
    tile_ref,
    order_ref,
    out_ref,
    gq_ref,
    gk_ref,
    gv_ref,
    gtk_ref,
    gtv_ref,
    qg_ref,
    kv_ref,
    st_pair,
    q_pair,
    goall,
    go_relay,
    acc,
    kaug,
    kaug_own,
    ktext,
    vals_own,
    vals,
    qaug,
    gsel,
    weights,
    slopes,
    weights_own,
    slopes_own,
    queries_t,
    grads_t,
    oacc,
    qacc,
    oq_ref,
    kvg_ref,
    z_in,
    z_sum,
    x_in,
    x_sum,
    yq_out,
    yq_in,
    yk_out,
    yk_in,
    keep_q,
    attn,
    part,
    core_in,
    pair_sum,
    out_relay,
    far_in,
    g_send,
    g_recv,
    r_send,
    r_recv,
    local_sem,
    store_sem,
):
    seq, head, y, z, x = place()
    peer = peers(seq, head, y, z, x)
    zu, zd, zf = (z + 1) % NZ, (z + NZ - 1) % NZ, (z + 2) % NZ
    xr, xl, xf = (x + 1) % NX, (x + NX - 1) % NX, (x + 2) % NX
    other_head = (head + 2) % 4
    core_head = head + 1 - 2 * (head % 2)
    core_other = core_head + 2 - 4 * (core_head // 2)
    first, second = pl.ds(0, HALF), pl.ds(HALF, HALF)
    sent = []
    send, arrived = sender(peer, g_send, g_recv, sent)
    rsend, rarrived = sender(peer, r_send, r_recv, sent)
    cols = lambda h: slice(h * HS, (h + 1) * HS)
    by_y = lambda a, b: jnp.where(y == 0, a, b)
    wide = lambda a: a.astype(F32)
    factor = HS ** (-0.5)

    load = []
    for n, (src, dst) in enumerate(
        (
            (k_hbm, k_ref),
            (tk_hbm, tk_ref),
            (v_hbm, v_ref),
            (tv_hbm, tv_ref),
            (q_hbm, q_ref),
            (go_hbm, go_ref),
            (w_hbm, w_ref),
            (tile_hbm, tile_ref),
            (order_hbm, order_ref),
        )
    ):
        copy = pltpu.make_async_copy(src, dst, local_sem.at[n])
        copy.start()
        load.append(copy)

    greet(peer)


    def x_send(a, t, yy):
        c = yy * NX + x
        send(10 + 6 * a + 2 * t, kv_ref.at[t, c], kv_ref.at[t, c], ("right", "left")[t])
        send(11 + 6 * a + 2 * t, kv_ref.at[t, c], kv_ref.at[t, c], ("left", "right")[t])

    def x_forward(a, t, yy):
        base = 10 + 6 * a
        source = yy * NX + (xl, xr)[t]
        arrived(base + 2 * t, kv_ref.at[t, source])
        send(base + 4 + t, kv_ref.at[t, source], kv_ref.at[t, source], ("right", "left")[t])

    def x_near_finish(a, t, yy):
        arrived(10 + 6 * a + 1 + 2 * t, kv_ref.at[t, yy * NX + (xr, xl)[t]])

    def x_far_finish(a, t, yy):
        arrived(10 + 6 * a + 4 + t, kv_ref.at[t, yy * NX + xf])

    def z_own(t):
        base = 22 + 10 * t
        send(base + 0, qg_ref.at[t, z, 2], qg_ref.at[t, z, 2], "up")
        send(base + 1, qg_ref.at[t, z, y], qg_ref.at[t, z, y], "down")
        send(base + 2, qg_ref.at[t, z, y], qg_ref.at[t, z, y], "up")
        send(base + 3, qg_ref.at[t, z, 2], qg_ref.at[t, z, 2], "down")

    def z_own_forward(t):
        base = 22 + 10 * t
        arrived(base + 0, qg_ref.at[t, zd, 2])
        send(base + 4, qg_ref.at[t, zd, 2], qg_ref.at[t, zd, 2], "up")
        arrived(base + 1, qg_ref.at[t, zu, y])
        send(base + 5, qg_ref.at[t, zu, y], qg_ref.at[t, zu, y], "down")

    def z_pair(t):
        base = 22 + 10 * t
        send(base + 6, qg_ref.at[t, z, 1 - y], qg_ref.at[t, z, 1 - y], "up")
        send(base + 7, qg_ref.at[t, z, 1 - y], qg_ref.at[t, z, 1 - y], "down")

    def z_pair_forward(t):
        base = 22 + 10 * t
        arrived(base + 6, qg_ref.at[t, zd, 1 - y])
        src = qg_ref.at[t, zd, 1 - y, first]
        send(base + 8, src, src, "up")
        arrived(base + 7, qg_ref.at[t, zu, 1 - y])
        src = qg_ref.at[t, zu, 1 - y, second]
        send(base + 9, src, src, "down")

    def z_own_finish(t):
        base = 22 + 10 * t
        arrived(base + 2, qg_ref.at[t, zd, y])
        arrived(base + 3, qg_ref.at[t, zu, 2])
        arrived(base + 4, qg_ref.at[t, zf, 2])
        arrived(base + 5, qg_ref.at[t, zf, y])

    def z_pair_finish(t):
        base = 22 + 10 * t
        arrived(base + 8, qg_ref.at[t, zf, 1 - y, first])
        arrived(base + 9, qg_ref.at[t, zf, 1 - y, second])

    def feature(n):
        return w_ref[:, pl.ds(pl.multiple_of(n * 768, 128), 768)]

    half_rows = NZ * NX * TR
    ends = [len_ref[0]]
    for c in range(1, CLIPS):
        ends.append(ends[-1] + len_ref[c])
    long_start = 0
    for c in range(1, CLIPS):
        long_start = jnp.where(len_ref[c] == half_rows, ends[c - 1], long_start)

    def clip_at(pos):
        total = 0
        for c in range(CLIPS - 1):
            total = total + jnp.where(pos >= ends[c], 1, 0)
        return total

    row_index = lax.broadcasted_iota(jnp.int32, (TR, HS), 0)

    def chunk_rows(zz, xx):
        return (zz * NX + xx) * TR + row_index

    def own_is_long(zz, xx):
        t = chunk_rows(zz, xx)
        return jnp.where(y == 0, t - long_start, long_start - 1 - t) >= 0

    def by_side(mask, mine, other):
        mine, other = wide(mine), wide(other)
        return jnp.where(mask, mine, other).astype(BF), jnp.where(mask, other, mine).astype(BF)

    lane = lax.broadcasted_iota(jnp.int32, (1, HS), 1)
    tiles_here = (lane % 64) // 16 == z
    clip_lane = ((z + 1) % NZ) * 16
    bias_lane = clip_lane + CLIPS
    bias_ones = jnp.where((lane >= bias_lane) & (lane < bias_lane + 3), 1.0, 0.0)

    def kv_index(n):
        return ((y + n % 2) % NY) * NX + (x + n // 2) % NX

    def key_columns(pos):
        hit = (tiles_here & ((pos >> 6) == lane)) | (clip_at(pos) == lane - clip_lane)
        return jnp.where(hit, 1.0, bias_ones).astype(BF)

    def key_side():
        for d in range(NX):
            t = chunk_rows(z, (x + d) % NX)
            low = key_columns(t)
            high = key_columns(t + half_rows)
            for r in range(2):
                n = 2 * d + r
                plane_zero = (y + r) % NY == 0
                kaug[n * TR : (n + 1) * TR, HS:] = jnp.where(plane_zero, low, high)
            for side, value in enumerate(by_side(t >= long_start, low, high)):
                kaug_own[side, d * TR : (d + 1) * TR, HS:] = value
        row = lax.broadcasted_iota(jnp.int32, (TEXT, HS), 0)
        n = row // CR
        plane = ((y + n % 2) % NY) * NZ + z
        text_row = (plane * NX + (x + n // 2) % NX) * CR + row % CR
        aug = jnp.broadcast_to(bias_ones, text_row.shape)
        for c in range(CLIPS):
            listed = jnp.where(order_ref[c : c + 1, :] == text_row, 1.0, 0.0)
            found = jnp.max(listed, axis=1, keepdims=True)
            aug = jnp.where(lane == clip_lane + c, found, aug)
        for s in range(2):
            ktext[s, :, HS:] = aug.astype(BF)

    log_len = [
        jnp.log(jnp.full((1, HS), len_ref[c] + CAP, jnp.int32).astype(F32)) for c in range(CLIPS)
    ]

    def query_side(n, carry):
        g, zq = n // NZ, n % NZ
        t = chunk_rows(zq, x)
        in_high = jnp.where(g == 0, long_start - 1 - t, t - long_start)
        in_high = jnp.where(g == 2, 2 * y - 1, in_high) >= 0
        pos = t + jnp.where(in_high, half_rows, 0)
        head_bias = bias_ref[jnp.where(g == 2, 2, y)]
        clip = clip_at(pos)
        offset = jnp.broadcast_to(log_len[CLIPS - 1], (TR, HS))
        for c in range(CLIPS - 2, -1, -1):
            offset = jnp.where(pos < ends[c], log_len[c], offset)
        total = (head_bias - offset) * (HS**0.5)
        hi = total.astype(BF).astype(F32)
        mid = (total - hi).astype(BF).astype(F32)
        low = total - hi - mid
        in_bias = jnp.where(lane == bias_lane, hi, jnp.where(lane == bias_lane + 1, mid, low))
        in_bias = jnp.where((lane >= bias_lane) & (lane < bias_lane + 3), in_bias, 0.0)
        in_clip = (lane >= clip_lane) & (lane < clip_lane + CLIPS) & (lane - clip_lane != clip)
        side = jnp.where(in_clip, MASKED, in_bias)
        for u in range(TR // TILE):
            rows = slice(u * TILE, (u + 1) * TILE)
            tile = (zq * NX + x) * (TR // TILE) + u
            off = []
            for p in range(NY):
                at = tile + p * (half_rows // TILE)
                mask_row = tile_ref[pl.ds(at, 1), :]
                off.append(jnp.where((mask_row == 0) & (lane != at) & tiles_here, 1.0, 0.0))
            masked = jnp.where(in_high[rows], off[1], off[0]) > 0.5
            qaug[n, rows, HS:] = jnp.where(masked, MASKED, side[rows]).astype(BF)
        return carry

    def keep_query(n, value):
        qaug[n, :, 0:HS] = value
        queries_t[:, n * TR : (n + 1) * TR] = value.T

    def keep_grad(n, value):
        gsel[n] = value
        grads_t[:, n * TR : (n + 1) * TR] = value.T

    def take_own(t, keep):
        for zq in range(NZ):
            mask = own_is_long(zq, x)
            sides = by_side(mask, qg_ref[t, zq, y], qg_ref[t, zq, 1 - y])
            for g in range(2):
                keep(g * NZ + zq, sides[g])

    def take_shared(t, keep):
        for zq in range(NZ):
            keep(2 * NZ + zq, qg_ref[t, zq, 2])

    def take_key(n):
        kaug[n * TR : (n + 1) * TR, 0:HS] = kv_ref[0, kv_index(n), 1, 0:TR]
        for s in range(2):
            ktext[s, n * CR : (n + 1) * CR, 0:HS] = kv_ref[0, kv_index(n), s, TR:BR]

    def take_value(n):
        vals[n * TR : (n + 1) * TR] = kv_ref[1, kv_index(n), 1, 0:TR]
        vals[LAT + n * CR : LAT + (n + 1) * CR] = kv_ref[1, kv_index(n), 1, TR:BR]
        for g in range(2):
            rows = slice(SIDE + n * CR, SIDE + (n + 1) * CR)
            vals_own[g, rows] = kv_ref[1, kv_index(n), 0, TR:BR]

    def take_sides(t, d, ref, lanes):
        mask = own_is_long(z, (x + d) % NX)
        mine, other = kv_index(2 * d), kv_index(2 * d + 1)
        sides = by_side(mask, kv_ref[t, mine, 0, 0:TR], kv_ref[t, other, 0, 0:TR])
        for side, value in enumerate(sides):
            ref[side, d * TR : (d + 1) * TR, lanes] = value

    def weigh(n, keys, weight_ref, slope_ref, rows, columns):
        scores = dot_nt(qaug[n], keys)
        half = jnp.tanh(scores * (0.5 * factor))
        twice = 1.0 + half
        weight = twice.astype(BF)
        weight_ref[rows, columns] = weight
        slope_ref[rows, columns] = (twice * (1.0 - half)).astype(BF)
        return weight

    def block_rows(n):
        return pl.ds(pl.multiple_of(n * TR, TR), TR)

    def score(n):
        take_key(n)
        columns = slice(n * TR, (n + 1) * TR)

        def step(half, carry):
            for u in range(2):
                zq = 2 * half + u
                rows = block_rows(zq)
                weigh(2 * NZ + zq, kaug[columns, :], weights, slopes, rows, columns)
            return carry

        lax.fori_loop(0, NZ // 2, step, 0)

    def score_own(d):
        take_sides(0, d, kaug_own, slice(0, HS))
        columns = slice(d * TR, (d + 1) * TR)

        def step(zq, carry):
            for g in range(2):
                block = g * NZ + zq
                keys = kaug_own[g, columns, :]
                weigh(block, keys, weights_own, slopes_own, block_rows(block), columns)
            return carry

        lax.fori_loop(0, NZ, step, 0)

    own_text = slice(SIDE, SIDE + TEXT)
    shared_text = slice(LAT, LAT + TEXT)

    def score_text():
        def step(zq, carry):
            for g in range(NH):
                block = g * NZ + zq
                if g == 2:
                    weigh(block, ktext[1], weights, slopes, block_rows(zq), shared_text)
                else:
                    weigh(block, ktext[0], weights_own, slopes_own, block_rows(block), own_text)
            return carry

        lax.fori_loop(0, NZ, step, 0)

    def mix(block, low, high):
        g, zq = block
        if g == 2:
            columns = slice(low * 2 * TR, high * 2 * TR)
            return dot_nn(weights[block_rows(zq), columns], vals[columns, :])
        columns = slice(low * TR, high * TR)
        return dot_nn(weights_own[block_rows(g * NZ + zq), columns], vals_own[g, columns, :])

    def mix_near():
        def step(zq, carry):
            for g in range(NH):
                oacc[g * NZ + zq] = mix((g, zq), 0, 2) + mix((g, zq), 3, 4)
            return carry

        lax.fori_loop(0, NZ, step, 0)

    def mix_far(zq):
        totals = []
        for g in range(NH):
            if g == 2:
                text = dot_nn(weights[block_rows(zq), shared_text], vals[LAT:, :])
            else:
                rows = block_rows(g * NZ + zq)
                text = dot_nn(weights_own[rows, own_text], vals_own[g, SIDE:, :])
            totals.append((oacc[g * NZ + zq] + mix((g, zq), 2, 3) + text) * 0.5)
        mine, other = by_side(own_is_long(zq, x), totals[0], totals[1])
        oq_ref[0, zq, y] = mine
        oq_ref[0, zq, 1 - y] = other
        oq_ref[0, zq, 2] = totals[2].astype(BF)

    def slope_step(block, slope_ref, rows, columns, values, keys, fresh):
        slope = (dot_nt(gsel[block], values) * wide(slope_ref[rows, columns])).astype(BF)
        slope_ref[rows, columns] = slope
        share = dot_nn(slope, keys)
        if fresh:
            qacc[block] = share
        else:
            qacc[block] += share

    def slope_shared(n, fresh=False):
        columns = slice(n * TR, (n + 1) * TR)

        def step(half, carry):
            for u in range(2):
                zq = 2 * half + u
                keys = kaug[columns, 0:HS]
                rows = block_rows(zq)
                slope_step(2 * NZ + zq, slopes, rows, columns, vals[columns, :], keys, fresh)
            return carry

        lax.fori_loop(0, NZ // 2, step, 0)

    def slope_shared_text():
        def step(half, carry):
            for u in range(2):
                zq = 2 * half + u
                keys = ktext[1, :, 0:HS]
                rows = block_rows(zq)
                slope_step(2 * NZ + zq, slopes, rows, shared_text, vals[LAT:, :], keys, False)
            return carry

        lax.fori_loop(0, NZ // 2, step, 0)

    def slope_own_row(d, zq):
        columns = slice(d * TR, (d + 1) * TR)
        for g in range(2):
            block = g * NZ + zq
            side_vals, keys = vals_own[g, columns, :], kaug_own[g, columns, 0:HS]
            slope_step(block, slopes_own, block_rows(block), columns, side_vals, keys, False)

    def slope_own(d):
        def step(half, carry):
            for u in range(2):
                slope_own_row(d, 2 * half + u)
            return carry

        lax.fori_loop(0, NZ // 2, step, 0)

    def slope_own_text():
        def step(half, carry):
            for u in range(2):
                for g in range(2):
                    block = g * NZ + 2 * half + u
                    rows = block_rows(block)
                    keys = ktext[0, :, 0:HS]
                    slope_step(block, slopes_own, rows, own_text, vals_own[g, SIDE:, :], keys, True)
            return carry

        lax.fori_loop(0, NZ // 2, step, 0)

    def finish_dq(zq):
        mine, other = by_side(own_is_long(zq, x), qacc[zq] * 0.25, qacc[NZ + zq] * 0.25)
        oq_ref[1, zq, y] = mine
        oq_ref[1, zq, 1 - y] = other
        oq_ref[1, zq, 2] = (qacc[2 * NZ + zq] * 0.25).astype(BF)

    left_of = (queries_t, grads_t)
    scale_of = (0.25, 0.5)

    def key_grads_shared(t, d):
        right = (slopes, weights)[t][:, d * 2 * TR : (d + 1) * 2 * TR]
        total = (dot_nn(left_of[t][:, 2 * NZ * TR :], right) * scale_of[t]).astype(BF)
        for r in range(2):
            kvg_ref[t, kv_index(2 * d + r), 1, 0:TR] = total[:, r * TR : (r + 1) * TR].T

    def key_grads_own(t, d):
        sides = []
        for g in range(2):
            rows = slice(g * SIDE, (g + 1) * SIDE)
            right = (slopes_own, weights_own)[t][rows, d * TR : (d + 1) * TR]
            total = dot_nn(left_of[t][:, rows], right) * scale_of[t]
            sides.append(total.astype(BF).T)
        mine, other = by_side(own_is_long(z, (x + d) % NX), sides[0], sides[1])
        kvg_ref[t, kv_index(2 * d), 0, 0:TR] = mine
        kvg_ref[t, kv_index(2 * d + 1), 0, 0:TR] = other

    def key_grads_text(t, s):
        if s == 0:
            left = left_of[t][:, 0 : 2 * NZ * TR]
            right = (slopes_own, weights_own)[t][:, own_text]
        else:
            left = left_of[t][:, 2 * NZ * TR :]
            right = (slopes, weights)[t][:, shared_text]
        text_rows = (dot_nn(left, right) * scale_of[t]).astype(BF).T
        for n in range(NY * NX):
            kvg_ref[t, kv_index(n), s, TR:BR] = text_rows[n * CR : (n + 1) * CR]


    def z_far(t):
        rsend(6 * t + 0, oq_ref.at[t, zf, :, first], z_in.at[t, 0], "up")
        rsend(6 * t + 3, oq_ref.at[t, zf, :, second], z_in.at[t, 3], "down")

    def z_near(t):
        rsend(6 * t + 1, oq_ref.at[t, zd, :, first], z_in.at[t, 1], "down")
        rsend(6 * t + 4, oq_ref.at[t, zu, :, second], z_in.at[t, 4], "up")

    def z_relay(t):
        base = 6 * t
        rarrived(base + 0, z_in.at[t, 0])
        z_sum[t, 0] = (wide(z_in[t, 0]) + wide(oq_ref[t, zu, :, first])).astype(BF)
        rsend(base + 2, z_sum.at[t, 0], z_in.at[t, 2], "up")
        rarrived(base + 3, z_in.at[t, 3])
        z_sum[t, 1] = (wide(z_in[t, 3]) + wide(oq_ref[t, zd, :, second])).astype(BF)
        rsend(base + 5, z_sum.at[t, 1], z_in.at[t, 5], "down")

    def z_total(t, scale):
        base = 6 * t
        for n in (1, 2, 4, 5):
            rarrived(base + n, z_in.at[t, n])
        for rows, one, two in ((first, 1, 2), (second, 4, 5)):

            def total(j):
                value = wide(oq_ref[t, z, j, rows]) + wide(z_in[t, one, j]) + wide(z_in[t, two, j])
                return (value * scale).astype(BF) if scale != 1.0 else value.astype(BF)

            yq_out[t, rows] = total(1 - y)
            keep_q[t, 0, rows] = total(y)
            keep_q[t, 1, rows] = total(2)
        rsend(24 + t, yq_out.at[t], yq_in.at[t], "pair")

    def x_base(t, a):
        return 12 + 6 * t + 3 * a

    ring = (("right", "left"), ("left", "right"))
    ahead = ((xr, xl), (xl, xr))
    plane = (y, 1 - y)

    def x_far(t):
        for a in (1, 0):
            src = kvg_ref.at[t, plane[a] * NX + xf]
            rsend(x_base(t, a), src, x_in.at[t, a, 0], ring[a][0])

    def x_near(t):
        for a in (1, 0):
            src = kvg_ref.at[t, plane[a] * NX + ahead[a][1]]
            rsend(x_base(t, a) + 1, src, x_in.at[t, a, 1], ring[a][1])

    def x_relay(t):
        for a in (1, 0):
            rarrived(x_base(t, a), x_in.at[t, a, 0])
            mine = wide(kvg_ref[t, plane[a] * NX + ahead[a][0]])
            x_sum[t, a] = (wide(x_in[t, a, 0]) + mine).astype(BF)
            rsend(x_base(t, a) + 2, x_sum.at[t, a], x_in.at[t, a, 2], ring[a][0])

    def to_pair(t):
        yk_out[t] = x_total(t, 1).astype(BF)
        rsend(26 + t, yk_out.at[t], yk_in.at[t], "pair")

    def x_total(t, a):
        rarrived(x_base(t, a) + 1, x_in.at[t, a, 1])
        rarrived(x_base(t, a) + 2, x_in.at[t, a, 2])
        value = wide(kvg_ref[t, plane[a] * NX + x]) + wide(x_in[t, a, 1]) + wide(x_in[t, a, 2])
        return value * factor if t == 0 else value

    def project(n):
        return dot_nn(attn[...], feature(n)).astype(BF)

    send(1, go_hbm.at[second], go_relay.at[1], "back")
    load[4].wait()
    q_pair[0] = by_y(q_ref[:, cols(1)], q_ref[:, cols(0)])
    send(6, q_pair.at[0], qg_ref.at[0, z, y], "pair")
    qg_ref[0, z, y] = by_y(q_ref[:, cols(0)], q_ref[:, cols(1)])
    qg_ref[0, z, 2] = q_ref[:, cols(2)]
    z_own(0)
    c = y * NX + x
    pair_y = 1 - y
    for t, (ref, text) in enumerate(((k_ref, tk_ref), (v_ref, tv_ref))):
        load[2 * t].wait()
        load[2 * t + 1].wait()
        st_pair[t, 0, 0:TR] = by_y(ref[:, cols(1)], ref[:, cols(0)])
        st_pair[t, 0, TR:BR] = by_y(text[:, cols(1)], text[:, cols(0)])
        st_pair[t, 1, 0:TR] = ref[:, cols(2)]
        st_pair[t, 1, TR:BR] = text[:, cols(2)]
        if t == 0:
            send(7, st_pair.at[0], kv_ref.at[0, c], "pair")
            send(0, go_hbm.at[first], go_relay.at[0], "pair")
        kv_ref[t, c, 0, 0:TR] = by_y(ref[:, cols(0)], ref[:, cols(1)])
        kv_ref[t, c, 0, TR:BR] = by_y(text[:, cols(0)], text[:, cols(1)])
        kv_ref[t, c, 1, 0:TR] = ref[:, cols(2)]
        kv_ref[t, c, 1, TR:BR] = text[:, cols(2)]
        x_send(0, t, y)
    send(2, go_hbm, goall.at[head], "core")
    load[7].wait()
    load[8].wait()
    key_side()
    lax.fori_loop(0, BLOCKS, query_side, 0)
    arrived(1, go_relay.at[1])
    send(4, go_relay.at[1], goall.at[other_head, second], "pair")
    z_own_forward(0)
    arrived(6, qg_ref.at[0, z, 1 - y])
    z_pair(0)
    arrived(7, kv_ref.at[0, pair_y * NX + x])
    x_send(1, 0, pair_y)
    load[5].wait()
    load[6].wait()
    acc[...] = dot_nt(go_ref[...], feature(head))
    x_forward(0, 0, y)
    x_forward(0, 1, y)
    z_pair_forward(0)
    z_own_finish(0)
    take_shared(0, keep_query)
    score(0)
    score(1)
    z_pair_finish(0)
    take_own(0, keep_query)
    arrived(0, go_relay.at[0])
    send(3, go_relay.at[0], goall.at[head, first], "back")
    send(8, st_pair.at[1], kv_ref.at[1, c], "pair")
    x_forward(1, 0, pair_y)
    score_own(0)
    arrived(2, goall.at[core_head])
    acc[...] += dot_nt(goall[core_head], feature(core_head))
    x_near_finish(0, 0, y)
    x_far_finish(0, 0, y)
    score(2)
    score(6)
    score(4)
    arrived(3, goall.at[other_head, first])
    arrived(4, goall.at[other_head, second])
    send(5, goall.at[other_head], goall.at[other_head], "core")
    acc[...] += dot_nt(goall[other_head], feature(other_head))
    x_near_finish(1, 0, pair_y)
    score(3)
    score_own(1)
    arrived(5, goall.at[core_other])
    grad = (acc[...] + dot_nt(goall[core_other], feature(core_other))).astype(BF)
    q_pair[1] = by_y(grad[:, cols(1)], grad[:, cols(0)])
    send(9, q_pair.at[1], qg_ref.at[1, z, y], "pair")
    qg_ref[1, z, y] = by_y(grad[:, cols(0)], grad[:, cols(1)])
    qg_ref[1, z, 2] = grad[:, cols(2)]
    z_own(1)
    arrived(8, kv_ref.at[1, pair_y * NX + x])
    x_send(1, 1, pair_y)
    score(7)
    score_own(3)
    arrived(9, qg_ref.at[1, z, 1 - y])
    z_pair(1)
    z_own_forward(1)
    x_far_finish(1, 0, pair_y)
    score(5)
    score_own(2)
    x_forward(1, 1, pair_y)
    z_pair_forward(1)
    score_text()
    x_near_finish(0, 1, y)
    x_far_finish(0, 1, y)
    for n in (0, 2, 6, 4, 1):
        take_value(n)
    take_sides(1, 0, vals_own, slice(0, HS))

    z_own_finish(1)
    take_shared(1, keep_grad)
    key_grads_text(1, 1)
    for d in (2, 3, 1):
        key_grads_shared(1, d)
    z_pair_finish(1)
    take_own(1, keep_grad)
    key_grads_text(1, 0)
    key_grads_own(1, 2)
    x_far(1)
    x_near_finish(1, 1, pair_y)
    for n in (3, 7):
        take_value(n)
    for d in (1, 3):
        take_sides(1, d, vals_own, slice(0, HS))
    mix_near()
    x_far_finish(1, 1, pair_y)
    take_value(5)
    take_sides(1, 2, vals_own, slice(0, HS))
    mix_far(zf)
    z_far(0)
    mix_far(zu)
    mix_far(zd)
    z_near(0)
    mix_far(z)
    key_grads_own(1, 3)
    key_grads_own(1, 1)
    x_relay(1)
    x_near(1)
    slope_shared(4, True)
    slope_shared(5)
    slope_shared_text()
    slope_own_text()
    z_relay(0)
    slope_own(2)
    for part_of in range(2):
        key_grads_text(0, part_of)
    key_grads_own(0, 2)
    key_grads_shared(0, 2)
    x_far(0)
    key_grads_shared(1, 0)
    key_grads_own(1, 0)
    z_total(0, 1.0)
    to_pair(1)
    for n in (2, 3):
        slope_shared(n)
    slope_own(1)
    rarrived(24, yq_in.at[0])
    attn[:, cols(0)] = by_y(keep_q[0, 0], yq_in[0])
    attn[:, cols(1)] = by_y(yq_in[0], keep_q[0, 0])
    attn[:, cols(2)] = keep_q[0, 1]
    part[0] = project(core_other)
    rsend(28, part.at[0], core_in.at[0], "core")
    part[2] = project(other_head)
    for n in (6, 7):
        slope_shared(n)
    slope_own(3)
    rarrived(28, core_in.at[0])
    pair_sum[...] = (wide(part[2]) + wide(core_in[0])).astype(BF)
    rsend(30, pair_sum.at[first], out_relay.at[0], "pair")
    rsend(31, pair_sum.at[second], out_relay.at[1], "back")
    for d in (1, 3):
        key_grads_own(0, d)
        key_grads_shared(0, d)
    x_relay(0)
    x_near(0)
    part[1] = project(core_head)
    rsend(29, part.at[1], core_in.at[1], "core")
    for n in (0, 1):
        slope_shared(n)
    for zq in (zf, zu, zd, z):
        slope_own_row(0, zq)
        finish_dq(zq)
        if zq is zf:
            z_far(1)
        elif zq is zd:
            z_near(1)
    rarrived(30, out_relay.at[0])
    rsend(32, out_relay.at[0], far_in.at[first], "back")
    rarrived(31, out_relay.at[1])
    rsend(33, out_relay.at[1], far_in.at[second], "pair")
    key_grads_own(0, 0)
    key_grads_shared(0, 0)
    z_relay(1)
    part[3] = project(head)
    to_pair(0)
    z_total(1, factor)

    stores = []

    def store(src, dst):
        copy = pltpu.make_async_copy(src, dst, store_sem.at[len(stores)])
        copy.start()
        stores.append(copy)

    results = ((gk_ref, gtk_ref, gk_hbm, gtk_hbm), (gv_ref, gtv_ref, gv_hbm, gtv_hbm))
    rarrived(29, core_in.at[1])
    rarrived(32, far_in.at[first])
    rarrived(33, far_in.at[second])
    out_ref[...] = (wide(part[3]) + wide(core_in[1]) + wide(far_in[...])).astype(BF)
    store(out_ref, out_hbm)
    for t, (ref, text, to, text_to) in enumerate(results):
        own = x_total(t, 0)
        rarrived(26 + t, yk_in.at[t])
        mine = own[0].astype(BF)
        other = yk_in[t, 0]
        both = (own[1] + wide(yk_in[t, 1])).astype(BF)
        for h, value in ((0, by_y(mine, other)), (1, by_y(other, mine)), (2, both)):
            ref[:, cols(h)] = value[0:TR]
            text[:, cols(h)] = value[TR:BR]
        store(ref, to)
        store(text, text_to)
    rarrived(25, yq_in.at[1])
    gq_ref[:, cols(0)] = by_y(keep_q[1, 0], yq_in[1])
    gq_ref[:, cols(1)] = by_y(yq_in[1], keep_q[1, 0])
    gq_ref[:, cols(2)] = keep_q[1, 1]
    store(gq_ref, gq_hbm)
    for copy in sent:
        copy.wait_send()
    for copy in stores:
        copy.wait()


def store_kernel(*refs):
    count = (len(refs) - 2) // 3
    held, result, buffers = refs[:count], refs[count : 2 * count], refs[2 * count : 3 * count]
    load_sem, store_sem = refs[-2:]
    loads = [
        pltpu.make_async_copy(held[n], buffers[n], load_sem.at[n]) for n in range(count)
    ]
    stores = [
        pltpu.make_async_copy(buffers[n], result[n], store_sem.at[n]) for n in range(count)
    ]
    for copy in loads:
        copy.start()
    for load, copy in zip(loads, stores):
        load.wait()
        copy.start()
    for copy in stores:
        copy.wait()


def shards(
    queries,
    keys,
    values,
    text_keys,
    text_values,
    head_bias,
    out_weight,
    grad_out,
    clip_lengths,
    tile_mask,
    caption_order,
):
    smem = pl.BlockSpec(memory_space=pltpu.SMEM)
    hbm = pl.BlockSpec(memory_space=pltpu.HBM)
    dma = pltpu.SemaphoreType.DMA
    qg_shape = (2, NZ, NH, TR, HS)
    kv_shape = (2, NY * NX, 2, BR, HS)
    out_cols = grad_out.shape[1]
    order = caption_order.reshape(CLIPS, CAP)
    token = pltpu.VMEM((TR, NH * HS), BF)
    text = pltpu.VMEM((CR, NH * HS), BF)
    wide_out = pltpu.VMEM((TR, out_cols), BF)
    halves = pltpu.VMEM((2, HALF, out_cols), BF)
    token_shape = jax.ShapeDtypeStruct((TR, NH * HS), BF)
    text_shape = jax.ShapeDtypeStruct((CR, NH * HS), BF)
    result = (
        jax.ShapeDtypeStruct((TR, out_cols), BF),
        token_shape,
        token_shape,
        token_shape,
        text_shape,
        text_shape,
    )
    held = pl.pallas_call(
        fused_kernel,
        out_shape=result,
        in_specs=[hbm] * 9 + [smem] * 2,
        out_specs=(hbm,) * len(result),
        scratch_shapes=[
            token,
            token,
            token,
            text,
            text,
            wide_out,
            pltpu.VMEM(out_weight.shape, BF),
            pltpu.VMEM(tile_mask.shape, jnp.int32),
            pltpu.VMEM(order.shape, jnp.int32),
            wide_out,
            token,
            token,
            token,
            text,
            text,
            pltpu.VMEM(qg_shape, BF),
            pltpu.VMEM(kv_shape, BF),
            pltpu.VMEM((2, 2, BR, HS), BF),
            pltpu.VMEM((2, TR, HS), BF),
            pltpu.VMEM((4, TR, out_cols), BF),
            halves,
            pltpu.VMEM((TR, NH * HS), F32),
            pltpu.VMEM((LAT, 2 * HS), BF),
            pltpu.VMEM((2, SIDE, 2 * HS), BF),
            pltpu.VMEM((2, TEXT, 2 * HS), BF),
            pltpu.VMEM((2, SIDE + TEXT, HS), BF),
            pltpu.VMEM((LAT + TEXT, HS), BF),
            pltpu.VMEM((BLOCKS, TR, 2 * HS), BF),
            pltpu.VMEM((BLOCKS, TR, HS), BF),
            pltpu.VMEM((NZ * TR, LAT + TEXT), BF),
            pltpu.VMEM((NZ * TR, LAT + TEXT), BF),
            pltpu.VMEM((2 * NZ * TR, SIDE + TEXT), BF),
            pltpu.VMEM((2 * NZ * TR, SIDE + TEXT), BF),
            pltpu.VMEM((HS, BLOCKS * TR), BF),
            pltpu.VMEM((HS, BLOCKS * TR), BF),
            pltpu.VMEM((BLOCKS, TR, HS), F32),
            pltpu.VMEM((BLOCKS, TR, HS), F32),
            pltpu.VMEM(qg_shape, BF),
            pltpu.VMEM(kv_shape, BF),
            pltpu.VMEM((2, 6, NH, HALF, HS), BF),
            pltpu.VMEM((2, 2, NH, HALF, HS), BF),
            pltpu.VMEM((2, NY, 3, 2, BR, HS), BF),
            pltpu.VMEM((2, NY, 2, BR, HS), BF),
            pltpu.VMEM((2, TR, HS), BF),
            pltpu.VMEM((2, TR, HS), BF),
            pltpu.VMEM((2, 2, BR, HS), BF),
            pltpu.VMEM((2, 2, BR, HS), BF),
            pltpu.VMEM((2, 2, TR, HS), BF),
            token,
            pltpu.VMEM((4, TR, out_cols), BF),
            pltpu.VMEM((2, TR, out_cols), BF),
            wide_out,
            halves,
            wide_out,
            dma((42,)),
            dma((42,)),
            dma((34,)),
            dma((34,)),
            dma((9,)),
            dma((len(result),)),
        ],
        compiler_params=pltpu.CompilerParams(
            collective_id=0, has_side_effects=True, vmem_limit_bytes=VMEM_LIMIT
        ),
    )(
        queries,
        keys,
        values,
        text_keys,
        text_values,
        grad_out,
        out_weight,
        tile_mask,
        order,
        clip_lengths,
        head_bias,
    )
    return pl.pallas_call(
        store_kernel,
        out_shape=result,
        in_specs=[hbm] * len(result),
        out_specs=(hbm,) * len(result),
        scratch_shapes=[pltpu.VMEM(array.shape, array.dtype) for array in result]
        + [dma((len(result),)), dma((len(result),))],
        compiler_params=pltpu.CompilerParams(vmem_limit_bytes=VMEM_LIMIT),
    )(*held)


def solution(mesh):
    in_specs = (
        P("seq", "head"),
        P("seq", "head"),
        P("seq", "head"),
        P("seq", "head"),
        P("seq", "head"),
        P("head"),
        P("head", None),
        P("seq", "head"),
        P(),
        P(),
        P(),
    )
    out_specs = (P("seq", "head"),) * 6
    return jax.shard_map(shards, mesh=mesh, in_specs=in_specs, out_specs=out_specs, check_vma=False)
```

```python
import jax
import jax.numpy as jnp
from jax import lax
from jax.experimental import pallas as pl
from jax.experimental.pallas import tpu as pltpu
from jax.sharding import PartitionSpec as P

MESH = pl.DeviceIdType.MESH
BF = jnp.bfloat16
F32 = jnp.float32

NX, NZ, NY = 4, 4, 2
HS = 128
NH = 3
TR = 256
CR = 16
BR = TR + CR
HALF = TR // 2
CLIPS = 4
CAP = 128
TILE = 64
MASKED = -32768.0
BLOCKS = NH * NZ
SIDE = NX * TR
SHARED_TEXT = BR
SHARED = BR + CR
CHUNK = BR + BR
TEXT = NY * NX * CR
VMEM_LIMIT = 58 * 1024 * 1024


def place():
    seq = lax.axis_index("seq")
    head = lax.axis_index("head")
    y = seq // (NZ * NX)
    z = (seq // NX) % NZ
    x = seq % NX
    return seq, head, y, z, x


def peers(seq, head, y, z, x):
    def at(yy, zz, xx):
        return (yy * NZ + zz) * NX + xx

    other_head = (head + 2) % 4
    core_head = head + 1 - 2 * (head % 2)
    return {
        "pair": (at(1 - y, z, x), head),
        "back": (at(1 - y, z, x), other_head),
        "core": (seq, core_head),
        "right": (at(y, z, (x + 1) % NX), head),
        "left": (at(y, z, (x + NX - 1) % NX), head),
        "up": (at(y, (z + 1) % NZ, x), head),
        "down": (at(y, (z + NZ - 1) % NZ, x), head),
    }


def greet(peer):
    barrier = pltpu.get_barrier_semaphore()
    for device in peer.values():
        pl.semaphore_signal(barrier, inc=1, device_id=device, device_id_type=MESH)
    pl.semaphore_wait(barrier, len(peer))


def sender(peer, send_sem, recv_sem, sent):
    def send(n, src, dst, to):
        copy = pltpu.make_async_remote_copy(
            src_ref=src,
            dst_ref=dst,
            send_sem=send_sem.at[n],
            recv_sem=recv_sem.at[n],
            device_id=peer[to],
            device_id_type=MESH,
        )
        copy.start()
        sent.append(copy)

    def arrived(n, dst):
        pltpu.make_async_remote_copy(
            src_ref=dst,
            dst_ref=dst,
            send_sem=send_sem.at[n],
            recv_sem=recv_sem.at[n],
            device_id=peer["core"],
            device_id_type=MESH,
        ).wait_recv()

    return send, arrived


def dot_nt(a, b):
    return lax.dot_general(a, b, (((1,), (1,)), ((), ())), preferred_element_type=F32)


def dot_nn(a, b):
    return lax.dot_general(a, b, (((1,), (0,)), ((), ())), preferred_element_type=F32)


def fused_kernel(
    q_hbm,
    k_hbm,
    v_hbm,
    tk_hbm,
    tv_hbm,
    go_hbm,
    w_hbm,
    tile_hbm,
    order_hbm,
    len_ref,
    bias_ref,
    out_hbm,
    gq_hbm,
    gk_hbm,
    gv_hbm,
    gtk_hbm,
    gtv_hbm,
    q_ref,
    k_ref,
    v_ref,
    tk_ref,
    tv_ref,
    go_ref,
    w_ref,
    tile_ref,
    order_ref,
    out_ref,
    gq_ref,
    gk_ref,
    gv_ref,
    gtk_ref,
    gtv_ref,
    qg_ref,
    kv_ref,
    st_pair,
    pair_out,
    pair_in,
    goall,
    go_relay,
    acc,
    kaug,
    vals,
    qaug,
    gsel,
    weights,
    slopes,
    queries_t,
    grads_t,
    oacc,
    qacc,
    oq_ref,
    kvg_ref,
    z_in,
    z_sum,
    x_in,
    x_sum,
    yq_out,
    yq_in,
    yk_out,
    yk_in,
    keep_q,
    attn,
    part,
    core_in,
    pair_sum,
    out_relay,
    far_in,
    g_send,
    g_recv,
    r_send,
    r_recv,
    local_sem,
    store_sem,
):
    seq, head, y, z, x = place()
    peer = peers(seq, head, y, z, x)
    zu, zd, zf = (z + 1) % NZ, (z + NZ - 1) % NZ, (z + 2) % NZ
    xr, xl, xf = (x + 1) % NX, (x + NX - 1) % NX, (x + 2) % NX
    other_head = (head + 2) % 4
    core_head = head + 1 - 2 * (head % 2)
    core_other = core_head + 2 - 4 * (core_head // 2)
    first, second = pl.ds(0, HALF), pl.ds(HALF, HALF)
    sent = []
    send, arrived = sender(peer, g_send, g_recv, sent)
    rsend, rarrived = sender(peer, r_send, r_recv, sent)
    cols = lambda h: slice(h * HS, (h + 1) * HS)
    by_y = lambda a, b: jnp.where(y == 0, a, b)
    wide = lambda a: a.astype(F32)
    factor = HS ** (-0.5)

    load = []
    for n, (src, dst) in enumerate(
        (
            (k_hbm, k_ref),
            (tk_hbm, tk_ref),
            (v_hbm, v_ref),
            (tv_hbm, tv_ref),
            (q_hbm, q_ref),
            (go_hbm, go_ref),
            (w_hbm, w_ref),
            (tile_hbm, tile_ref),
            (order_hbm, order_ref),
        )
    ):
        copy = pltpu.make_async_copy(src, dst, local_sem.at[n])
        copy.start()
        load.append(copy)

    greet(peer)


    def chunk_of(a, t, index):
        return kv_ref.at[t, index, pl.ds(0, (SHARED, CHUNK)[a])]

    def x_send(a, t, yy):
        chunk = chunk_of(a, t, yy * NX + x)
        send(10 + 6 * a + 2 * t, chunk, chunk, ("right", "left")[t])
        send(11 + 6 * a + 2 * t, chunk, chunk, ("left", "right")[t])

    def x_forward(a, t, yy):
        base = 10 + 6 * a
        chunk = chunk_of(a, t, yy * NX + (xl, xr)[t])
        arrived(base + 2 * t, chunk)
        send(base + 4 + t, chunk, chunk, ("right", "left")[t])

    def x_near_finish(a, t, yy):
        arrived(10 + 6 * a + 1 + 2 * t, chunk_of(a, t, yy * NX + (xr, xl)[t]))

    def x_far_finish(a, t, yy):
        arrived(10 + 6 * a + 4 + t, chunk_of(a, t, yy * NX + xf))

    def z_pair(t):
        base = 22 + 10 * t
        send(base + 0, qg_ref.at[t, z, 2], qg_ref.at[t, z, 2], "up")
        send(base + 1, qg_ref.at[t, z, 1 - y], qg_ref.at[t, z, 1 - y], "down")
        send(base + 2, qg_ref.at[t, z, 1 - y], qg_ref.at[t, z, 1 - y], "up")
        send(base + 3, qg_ref.at[t, z, 2], qg_ref.at[t, z, 2], "down")

    def z_pair_forward(t):
        base = 22 + 10 * t
        arrived(base + 0, qg_ref.at[t, zd, 2])
        send(base + 4, qg_ref.at[t, zd, 2], qg_ref.at[t, zd, 2], "up")
        arrived(base + 1, qg_ref.at[t, zu, 1 - y])
        send(base + 5, qg_ref.at[t, zu, 1 - y], qg_ref.at[t, zu, 1 - y], "down")

    def z_own(t):
        base = 22 + 10 * t
        send(base + 6, qg_ref.at[t, z, y], qg_ref.at[t, z, y], "up")
        send(base + 7, qg_ref.at[t, z, y], qg_ref.at[t, z, y], "down")

    def z_own_forward(t):
        base = 22 + 10 * t
        arrived(base + 6, qg_ref.at[t, zd, y])
        src = qg_ref.at[t, zd, y, first]
        send(base + 8, src, src, "up")
        arrived(base + 7, qg_ref.at[t, zu, y])
        src = qg_ref.at[t, zu, y, second]
        send(base + 9, src, src, "down")

    def z_pair_finish(t):
        base = 22 + 10 * t
        arrived(base + 2, qg_ref.at[t, zd, 1 - y])
        arrived(base + 3, qg_ref.at[t, zu, 2])
        arrived(base + 4, qg_ref.at[t, zf, 2])
        arrived(base + 5, qg_ref.at[t, zf, 1 - y])

    def z_own_finish(t):
        base = 22 + 10 * t
        arrived(base + 8, qg_ref.at[t, zf, y, first])
        arrived(base + 9, qg_ref.at[t, zf, y, second])

    def pair_rows(t, shared):
        arrived((6, 9)[t], pair_in.at[t])
        qg_ref[t, z, 1 - y] = pair_in[t, 0]
        mask = chunk_rows(z, x) >= long_start
        qg_ref[t, z, 2] = by_side(mask, shared, pair_in[t, 1])[0]

    def pair_keys(t, ref):
        index = (1 - y) * NX + x
        arrived(7 + t, kv_ref.at[t, index])
        mask = chunk_rows(z, x) >= long_start
        rows = pl.ds(SHARED, TR)
        kv_ref[t, index, rows] = by_side(mask, ref[:, cols(2)], kv_ref[t, index, rows])[0]
        x_send(1, t, 1 - y)

    def feature(n):
        return w_ref[:, pl.ds(pl.multiple_of(n * 768, 128), 768)]

    half_rows = NZ * NX * TR
    ends = [len_ref[0]]
    for c in range(1, CLIPS):
        ends.append(ends[-1] + len_ref[c])
    long_start = 0
    for c in range(1, CLIPS):
        long_start = jnp.where(len_ref[c] == half_rows, ends[c - 1], long_start)

    def clip_at(pos):
        total = 0
        for c in range(CLIPS - 1):
            total = total + jnp.where(pos >= ends[c], 1, 0)
        return total

    row_index = lax.broadcasted_iota(jnp.int32, (TR, HS), 0)

    def chunk_rows(zz, xx):
        return (zz * NX + xx) * TR + row_index

    def own_is_long(zz, xx):
        t = chunk_rows(zz, xx)
        return jnp.where(y == 0, t - long_start, long_start - 1 - t) >= 0

    def by_side(mask, mine, other):
        mine, other = wide(mine), wide(other)
        return jnp.where(mask, mine, other).astype(BF), jnp.where(mask, other, mine).astype(BF)

    lane = lax.broadcasted_iota(jnp.int32, (1, HS), 1)
    tiles_here = (lane % 64) // 16 == z
    clip_lane = ((z + 1) % NZ) * 16
    bias_lane = clip_lane + CLIPS
    bias_ones = jnp.where((lane >= bias_lane) & (lane < bias_lane + 3), 1.0, 0.0)

    def kv_index(n):
        return ((y + n % 2) % NY) * NX + (x + n // 2) % NX

    def key_columns(pos):
        hit = (tiles_here & ((pos >> 6) == lane)) | (clip_at(pos) == lane - clip_lane)
        return jnp.where(hit, 1.0, bias_ones).astype(BF)

    def key_side():
        for d in range(NX):
            t = chunk_rows(z, (x + d) % NX)
            rows = slice(d * TR, (d + 1) * TR)
            sides = by_side(t >= long_start, key_columns(t), key_columns(t + half_rows))
            for side, value in enumerate(sides + (by_y(*sides),)):
                kaug[side, rows, HS:] = value
        row = lax.broadcasted_iota(jnp.int32, (TEXT, HS), 0)
        n = row // CR
        plane = ((y + n % 2) % NY) * NZ + z
        text_row = (plane * NX + (x + n // 2) % NX) * CR + row % CR
        aug = jnp.broadcast_to(bias_ones, text_row.shape)
        for c in range(CLIPS):
            listed = jnp.where(order_ref[c : c + 1, :] == text_row, 1.0, 0.0)
            found = jnp.max(listed, axis=1, keepdims=True)
            aug = jnp.where(lane == clip_lane + c, found, aug)
        for g in range(NH):
            kaug[g, SIDE:, HS:] = aug.astype(BF)

    log_len = [
        jnp.log(jnp.full((1, HS), len_ref[c] + CAP, jnp.int32).astype(F32)) for c in range(CLIPS)
    ]

    def query_side(n, carry):
        g, zq = n // NZ, n % NZ
        t = chunk_rows(zq, x)
        side = jnp.where(g == 2, y, g)
        in_high = jnp.where(side == 0, long_start - 1 - t, t - long_start) >= 0
        pos = t + jnp.where(in_high, half_rows, 0)
        head_bias = bias_ref[jnp.where(g == 2, 2, y)]
        clip = clip_at(pos)
        offset = jnp.broadcast_to(log_len[CLIPS - 1], (TR, HS))
        for c in range(CLIPS - 2, -1, -1):
            offset = jnp.where(pos < ends[c], log_len[c], offset)
        total = (head_bias - offset) * (HS**0.5)
        hi = total.astype(BF).astype(F32)
        mid = (total - hi).astype(BF).astype(F32)
        low = total - hi - mid
        in_bias = jnp.where(lane == bias_lane, hi, jnp.where(lane == bias_lane + 1, mid, low))
        in_bias = jnp.where((lane >= bias_lane) & (lane < bias_lane + 3), in_bias, 0.0)
        in_clip = (lane >= clip_lane) & (lane < clip_lane + CLIPS) & (lane - clip_lane != clip)
        side = jnp.where(in_clip, MASKED, in_bias)
        for u in range(TR // TILE):
            rows = slice(u * TILE, (u + 1) * TILE)
            tile = (zq * NX + x) * (TR // TILE) + u
            off = []
            for p in range(NY):
                at = tile + p * (half_rows // TILE)
                mask_row = tile_ref[pl.ds(at, 1), :]
                off.append(jnp.where((mask_row == 0) & (lane != at) & tiles_here, 1.0, 0.0))
            masked = jnp.where(in_high[rows], off[1], off[0]) > 0.5
            qaug[n, rows, HS:] = jnp.where(masked, MASKED, side[rows]).astype(BF)
        return carry

    def keep_query(n, value):
        qaug[n, :, 0:HS] = value
        queries_t[:, n * TR : (n + 1) * TR] = value.T

    def keep_grad(n, value):
        gsel[n] = value
        grads_t[:, n * TR : (n + 1) * TR] = value.T

    def take_rows(t, keep):
        for zq in range(NZ):
            mask = own_is_long(zq, x)
            sides = by_side(mask, qg_ref[t, zq, y], qg_ref[t, zq, 1 - y])
            for g, value in enumerate(sides + (qg_ref[t, zq, 2],)):
                keep(g * NZ + zq, value)

    def take_column(t, d):
        lanes = slice(0, HS)
        ref = (kaug, vals)[t]
        mask = own_is_long(z, (x + d) % NX)
        mine, other = kv_index(2 * d), kv_index(2 * d + 1)
        sides = by_side(mask, kv_ref[t, mine, 0:TR], kv_ref[t, other, 0:TR])
        for g, value in enumerate(sides + (kv_ref[t, other, SHARED:CHUNK],)):
            ref[g, d * TR : (d + 1) * TR, lanes] = value
        for r in range(2):
            index = kv_index(2 * d + r)
            rows = slice(SIDE + (2 * d + r) * CR, SIDE + (2 * d + r + 1) * CR)
            for g in range(NH):
                low = SHARED_TEXT if g == 2 else TR
                ref[g, rows, lanes] = kv_ref[t, index, low : low + CR]

    def block_rows(n):
        return pl.ds(pl.multiple_of(n * TR, TR), TR)

    def weigh(block, columns):
        scores = dot_nt(qaug[block], kaug[block // NZ, columns, :])
        half = jnp.tanh(scores * (0.5 * factor))
        twice = 1.0 + half
        weights[block_rows(block), columns] = twice.astype(BF)
        slopes[block_rows(block), columns] = (twice * (1.0 - half)).astype(BF)

    def every_block(body):
        def step(zq, carry):
            for g in range(NH):
                body(g * NZ + zq)
            return carry

        lax.fori_loop(0, NZ, step, 0)

    def column(d):
        return slice(d * TR, (d + 1) * TR)

    text_columns = slice(SIDE, SIDE + TEXT)

    def score(d):
        take_column(0, d)
        every_block(lambda block: weigh(block, column(d)))

    def score_text():
        every_block(lambda block: weigh(block, text_columns))

    def mix(block, columns):
        return dot_nn(weights[block_rows(block), columns], vals[block // NZ, columns, :])

    def mix_near():
        def body(block):
            oacc[block] = mix(block, slice(0, 2 * TR)) + mix(block, column(3))

        every_block(body)

    def mix_far(zq):
        totals = []
        for g in range(NH):
            block = g * NZ + zq
            total = oacc[block] + mix(block, column(2)) + mix(block, text_columns)
            totals.append(total * 0.5)
        mine, other = by_side(own_is_long(zq, x), totals[0], totals[1])
        oq_ref[0, zq, y] = mine
        oq_ref[0, zq, 1 - y] = other
        oq_ref[0, zq, 2] = totals[2].astype(BF)

    def slope_step(block, columns, fresh=False):
        rows, g = block_rows(block), block // NZ
        slope = (dot_nt(gsel[block], vals[g, columns, :]) * wide(slopes[rows, columns])).astype(BF)
        slopes[rows, columns] = slope
        share = dot_nn(slope, kaug[g, columns, 0:HS])
        if fresh:
            qacc[block] = share
        else:
            qacc[block] += share

    def slope(d):
        every_block(lambda block: slope_step(block, column(d)))

    def slope_text():
        every_block(lambda block: slope_step(block, text_columns, True))

    def slope_row(d, zq):
        for g in range(NH):
            slope_step(g * NZ + zq, column(d))

    def finish_dq(zq):
        mine, other = by_side(own_is_long(zq, x), qacc[zq] * 0.25, qacc[NZ + zq] * 0.25)
        oq_ref[1, zq, y] = mine
        oq_ref[1, zq, 1 - y] = other
        oq_ref[1, zq, 2] = (qacc[2 * NZ + zq] * 0.25).astype(BF)

    left_of = (queries_t, grads_t)
    scale_of = (0.25, 0.5)

    def key_grads(t, d):
        sides = []
        for g in range(NH):
            rows = slice(g * SIDE, (g + 1) * SIDE)
            total = dot_nn(left_of[t][:, rows], (slopes, weights)[t][rows, column(d)])
            sides.append((total * scale_of[t]).astype(BF).T)
        mine, other = by_side(own_is_long(z, (x + d) % NX), sides[0], sides[1])
        kvg_ref[t, kv_index(2 * d), 0:TR] = mine
        kvg_ref[t, kv_index(2 * d + 1), 0:TR] = other
        kvg_ref[t, kv_index(2 * d + 1), SHARED:CHUNK] = sides[2]

    def key_grads_text(t):
        for low, high, at in ((0, 2 * SIDE, TR), (2 * SIDE, 3 * SIDE, SHARED_TEXT)):
            right = (slopes, weights)[t][low:high, text_columns]
            text_rows = (dot_nn(left_of[t][:, low:high], right) * scale_of[t]).astype(BF).T
            for n in range(NY * NX):
                kvg_ref[t, kv_index(n), at : at + CR] = text_rows[n * CR : (n + 1) * CR]


    def z_far(t):
        rsend(6 * t + 0, oq_ref.at[t, zf, :, first], z_in.at[t, 0], "up")
        rsend(6 * t + 3, oq_ref.at[t, zf, :, second], z_in.at[t, 3], "down")

    def z_near(t):
        rsend(6 * t + 1, oq_ref.at[t, zd, :, first], z_in.at[t, 1], "down")
        rsend(6 * t + 4, oq_ref.at[t, zu, :, second], z_in.at[t, 4], "up")

    def z_relay(t):
        base = 6 * t
        rarrived(base + 0, z_in.at[t, 0])
        z_sum[t, 0] = (wide(z_in[t, 0]) + wide(oq_ref[t, zu, :, first])).astype(BF)
        rsend(base + 2, z_sum.at[t, 0], z_in.at[t, 2], "up")
        rarrived(base + 3, z_in.at[t, 3])
        z_sum[t, 1] = (wide(z_in[t, 3]) + wide(oq_ref[t, zd, :, second])).astype(BF)
        rsend(base + 5, z_sum.at[t, 1], z_in.at[t, 5], "down")

    def z_total(t, scale):
        base = 6 * t
        for n in (1, 2, 4, 5):
            rarrived(base + n, z_in.at[t, n])
        for rows, one, two in ((first, 1, 2), (second, 4, 5)):

            def total(j):
                value = wide(oq_ref[t, z, j, rows]) + wide(z_in[t, one, j]) + wide(z_in[t, two, j])
                return (value * scale).astype(BF) if scale != 1.0 else value.astype(BF)

            yq_out[t, 0, rows] = total(1 - y)
            yq_out[t, 1, rows] = total(2)
            keep_q[t, rows] = total(y)
        rsend(24 + t, yq_out.at[t], yq_in.at[t], "pair")

    def x_base(t, a):
        return 12 + 6 * t + 3 * a

    ring = (("right", "left"), ("left", "right"))
    ahead = ((xr, xl), (xl, xr))
    plane = (y, 1 - y)

    def sums_of(a):
        return pl.ds(0, (SHARED, CHUNK)[a])

    def x_far(t):
        for a in (1, 0):
            src = kvg_ref.at[t, plane[a] * NX + xf, sums_of(a)]
            rsend(x_base(t, a), src, x_in.at[t, a, 0, sums_of(a)], ring[a][0])

    def x_near(t):
        for a in (1, 0):
            src = kvg_ref.at[t, plane[a] * NX + ahead[a][1], sums_of(a)]
            rsend(x_base(t, a) + 1, src, x_in.at[t, a, 1, sums_of(a)], ring[a][1])

    def x_relay(t):
        for a in (1, 0):
            rows = sums_of(a)
            rarrived(x_base(t, a), x_in.at[t, a, 0, rows])
            mine = wide(kvg_ref[t, plane[a] * NX + ahead[a][0], rows])
            x_sum[t, a, rows] = (wide(x_in[t, a, 0, rows]) + mine).astype(BF)
            rsend(x_base(t, a) + 2, x_sum.at[t, a, rows], x_in.at[t, a, 2, rows], ring[a][0])

    def to_pair(t):
        yk_out[t] = x_total(t, 1).astype(BF)
        rsend(26 + t, yk_out.at[t], yk_in.at[t], "pair")

    def x_total(t, a):
        rows = sums_of(a)
        rarrived(x_base(t, a) + 1, x_in.at[t, a, 1, rows])
        rarrived(x_base(t, a) + 2, x_in.at[t, a, 2, rows])
        value = wide(kvg_ref[t, plane[a] * NX + x, rows])
        value = value + wide(x_in[t, a, 1, rows]) + wide(x_in[t, a, 2, rows])
        return value * factor if t == 0 else value

    def take_attn(t, ref):
        rarrived(24 + t, yq_in.at[t])
        ref[:, cols(0)] = by_y(keep_q[t], yq_in[t, 0])
        ref[:, cols(1)] = by_y(yq_in[t, 0], keep_q[t])
        mask = chunk_rows(z, x) >= long_start
        ref[:, cols(2)] = by_side(mask, yq_out[t, 1], yq_in[t, 1])[0]

    def project(n):
        return dot_nn(attn[...], feature(n)).astype(BF)

    send(1, go_hbm.at[second], go_relay.at[1], "back")
    load[4].wait()
    pair_out[0, 0] = by_y(q_ref[:, cols(1)], q_ref[:, cols(0)])
    pair_out[0, 1] = q_ref[:, cols(2)]
    send(6, pair_out.at[0], pair_in.at[0], "pair")
    qg_ref[0, z, y] = by_y(q_ref[:, cols(0)], q_ref[:, cols(1)])
    z_own(0)
    c = y * NX + x
    pair_y = 1 - y
    for t, (ref, text) in enumerate(((k_ref, tk_ref), (v_ref, tv_ref))):
        load[2 * t].wait()
        load[2 * t + 1].wait()
        st_pair[t, 0:TR] = by_y(ref[:, cols(1)], ref[:, cols(0)])
        st_pair[t, TR:BR] = by_y(text[:, cols(1)], text[:, cols(0)])
        st_pair[t, SHARED_TEXT:SHARED] = text[:, cols(2)]
        st_pair[t, SHARED:CHUNK] = ref[:, cols(2)]
        if t == 0:
            send(7, st_pair.at[0], kv_ref.at[0, c], "pair")
            send(0, go_hbm.at[first], go_relay.at[0], "pair")
        kv_ref[t, c, 0:TR] = by_y(ref[:, cols(0)], ref[:, cols(1)])
        kv_ref[t, c, TR:BR] = by_y(text[:, cols(0)], text[:, cols(1)])
        kv_ref[t, c, SHARED_TEXT:SHARED] = text[:, cols(2)]
        x_send(0, t, y)
    send(2, go_hbm, goall.at[head], "core")
    load[7].wait()
    load[8].wait()
    key_side()
    pair_rows(0, q_ref[:, cols(2)])
    z_pair(0)
    lax.fori_loop(0, BLOCKS, query_side, 0)
    arrived(1, go_relay.at[1])
    send(4, go_relay.at[1], goall.at[other_head, second], "pair")
    z_own_forward(0)
    pair_keys(0, k_ref)
    load[5].wait()
    load[6].wait()
    acc[...] = dot_nt(go_ref[...], feature(head))
    x_forward(0, 0, y)
    x_forward(0, 1, y)
    z_pair_forward(0)
    z_own_finish(0)
    z_pair_finish(0)
    take_rows(0, keep_query)
    arrived(0, go_relay.at[0])
    send(3, go_relay.at[0], goall.at[head, first], "back")
    send(8, st_pair.at[1], kv_ref.at[1, c], "pair")
    x_forward(1, 0, pair_y)
    score(0)
    arrived(2, goall.at[core_head])
    acc[...] += dot_nt(goall[core_head], feature(core_head))
    x_near_finish(0, 0, y)
    x_near_finish(1, 0, pair_y)
    score(1)
    arrived(3, goall.at[other_head, first])
    arrived(4, goall.at[other_head, second])
    send(5, goall.at[other_head], goall.at[other_head], "core")
    acc[...] += dot_nt(goall[other_head], feature(other_head))
    score(3)
    arrived(5, goall.at[core_other])
    grad = (acc[...] + dot_nt(goall[core_other], feature(core_other))).astype(BF)
    pair_out[1, 0] = by_y(grad[:, cols(1)], grad[:, cols(0)])
    pair_out[1, 1] = grad[:, cols(2)]
    send(9, pair_out.at[1], pair_in.at[1], "pair")
    qg_ref[1, z, y] = by_y(grad[:, cols(0)], grad[:, cols(1)])
    z_own(1)
    pair_keys(1, v_ref)
    x_far_finish(0, 0, y)
    x_far_finish(1, 0, pair_y)
    score(2)
    pair_rows(1, pair_out[1, 1])
    z_pair(1)
    z_own_forward(1)
    score_text()
    x_forward(1, 1, pair_y)
    z_pair_forward(1)
    x_near_finish(0, 1, y)
    x_far_finish(0, 1, y)
    take_column(1, 0)

    z_own_finish(1)
    z_pair_finish(1)
    take_rows(1, keep_grad)
    key_grads_text(1)
    key_grads(1, 2)
    x_far(1)
    x_near_finish(1, 1, pair_y)
    take_column(1, 1)
    take_column(1, 3)
    mix_near()
    x_far_finish(1, 1, pair_y)
    take_column(1, 2)
    mix_far(zf)
    z_far(0)
    mix_far(zu)
    mix_far(zd)
    z_near(0)
    mix_far(z)
    key_grads(1, 3)
    key_grads(1, 1)
    x_relay(1)
    x_near(1)
    slope_text()
    z_relay(0)
    slope(2)
    key_grads_text(0)
    key_grads(0, 2)
    x_far(0)
    key_grads(1, 0)
    z_total(0, 1.0)
    to_pair(1)
    slope(1)
    take_attn(0, attn)
    part[0] = project(core_other)
    rsend(28, part.at[0], core_in.at[0], "core")
    part[2] = project(other_head)
    slope(3)
    rarrived(28, core_in.at[0])
    pair_sum[...] = (wide(part[2]) + wide(core_in[0])).astype(BF)
    rsend(30, pair_sum.at[first], out_relay.at[0], "pair")
    rsend(31, pair_sum.at[second], out_relay.at[1], "back")
    key_grads(0, 1)
    key_grads(0, 3)
    x_relay(0)
    x_near(0)
    part[1] = project(core_head)
    rsend(29, part.at[1], core_in.at[1], "core")
    for zq in (zf, zu, zd, z):
        slope_row(0, zq)
        finish_dq(zq)
        if zq is zf:
            z_far(1)
        elif zq is zd:
            z_near(1)
    key_grads(0, 0)
    rarrived(30, out_relay.at[0])
    rsend(32, out_relay.at[0], far_in.at[first], "back")
    rarrived(31, out_relay.at[1])
    rsend(33, out_relay.at[1], far_in.at[second], "pair")
    z_relay(1)
    part[3] = project(head)
    to_pair(0)
    z_total(1, factor)

    stores = []

    def store(src, dst):
        copy = pltpu.make_async_copy(src, dst, store_sem.at[len(stores)])
        copy.start()
        stores.append(copy)

    results = ((gk_ref, gtk_ref, gk_hbm, gtk_hbm), (gv_ref, gtv_ref, gv_hbm, gtv_hbm))
    rarrived(29, core_in.at[1])
    rarrived(32, far_in.at[first])
    rarrived(33, far_in.at[second])
    out_ref[...] = (wide(part[3]) + wide(core_in[1]) + wide(far_in[...])).astype(BF)
    store(out_ref, out_hbm)
    for t, (ref, text, to, text_to) in enumerate(results):
        own = x_total(t, 0)
        rarrived(26 + t, yk_in.at[t])
        mine, other = own[0:BR].astype(BF), yk_in[t, 0:BR]
        mask = chunk_rows(z, x) >= long_start
        both = by_side(mask, yk_out[t, SHARED:CHUNK], yk_in[t, SHARED:CHUNK])[0]
        for h, value in ((0, by_y(mine, other)), (1, by_y(other, mine))):
            ref[:, cols(h)] = value[0:TR]
            text[:, cols(h)] = value[TR:BR]
        ref[:, cols(2)] = both
        text[:, cols(2)] = (own[BR:SHARED] + wide(yk_in[t, SHARED_TEXT:SHARED])).astype(BF)
        store(ref, to)
        store(text, text_to)
    take_attn(1, gq_ref)
    store(gq_ref, gq_hbm)
    for copy in sent:
        copy.wait_send()
    for copy in stores:
        copy.wait()


def store_kernel(*refs):
    count = (len(refs) - 2) // 3
    held, result, buffers = refs[:count], refs[count : 2 * count], refs[2 * count : 3 * count]
    load_sem, store_sem = refs[-2:]
    loads = [
        pltpu.make_async_copy(held[n], buffers[n], load_sem.at[n]) for n in range(count)
    ]
    stores = [
        pltpu.make_async_copy(buffers[n], result[n], store_sem.at[n]) for n in range(count)
    ]
    for copy in loads:
        copy.start()
    for load, copy in zip(loads, stores):
        load.wait()
        copy.start()
    for copy in stores:
        copy.wait()


def shards(
    queries,
    keys,
    values,
    text_keys,
    text_values,
    head_bias,
    out_weight,
    grad_out,
    clip_lengths,
    tile_mask,
    caption_order,
):
    smem = pl.BlockSpec(memory_space=pltpu.SMEM)
    hbm = pl.BlockSpec(memory_space=pltpu.HBM)
    dma = pltpu.SemaphoreType.DMA
    qg_shape = (2, NZ, NH, TR, HS)
    kv_shape = (2, NY * NX, CHUNK, HS)
    out_cols = grad_out.shape[1]
    order = caption_order.reshape(CLIPS, CAP)
    token = pltpu.VMEM((TR, NH * HS), BF)
    text = pltpu.VMEM((CR, NH * HS), BF)
    wide_out = pltpu.VMEM((TR, out_cols), BF)
    halves = pltpu.VMEM((2, HALF, out_cols), BF)
    token_shape = jax.ShapeDtypeStruct((TR, NH * HS), BF)
    text_shape = jax.ShapeDtypeStruct((CR, NH * HS), BF)
    result = (
        jax.ShapeDtypeStruct((TR, out_cols), BF),
        token_shape,
        token_shape,
        token_shape,
        text_shape,
        text_shape,
    )
    held = pl.pallas_call(
        fused_kernel,
        out_shape=result,
        in_specs=[hbm] * 9 + [smem] * 2,
        out_specs=(hbm,) * len(result),
        scratch_shapes=[
            token,
            token,
            token,
            text,
            text,
            wide_out,
            pltpu.VMEM(out_weight.shape, BF),
            pltpu.VMEM(tile_mask.shape, jnp.int32),
            pltpu.VMEM(order.shape, jnp.int32),
            wide_out,
            token,
            token,
            token,
            text,
            text,
            pltpu.VMEM(qg_shape, BF),
            pltpu.VMEM(kv_shape, BF),
            pltpu.VMEM((2, CHUNK, HS), BF),
            pltpu.VMEM((2, 2, TR, HS), BF),
            pltpu.VMEM((2, 2, TR, HS), BF),
            pltpu.VMEM((4, TR, out_cols), BF),
            halves,
            pltpu.VMEM((TR, NH * HS), F32),
            pltpu.VMEM((NH, SIDE + TEXT, 2 * HS), BF),
            pltpu.VMEM((NH, SIDE + TEXT, HS), BF),
            pltpu.VMEM((BLOCKS, TR, 2 * HS), BF),
            pltpu.VMEM((BLOCKS, TR, HS), BF),
            pltpu.VMEM((BLOCKS * TR, SIDE + TEXT), BF),
            pltpu.VMEM((BLOCKS * TR, SIDE + TEXT), BF),
            pltpu.VMEM((HS, BLOCKS * TR), BF),
            pltpu.VMEM((HS, BLOCKS * TR), BF),
            pltpu.VMEM((BLOCKS, TR, HS), F32),
            pltpu.VMEM((BLOCKS, TR, HS), F32),
            pltpu.VMEM(qg_shape, BF),
            pltpu.VMEM(kv_shape, BF),
            pltpu.VMEM((2, 6, NH, HALF, HS), BF),
            pltpu.VMEM((2, 2, NH, HALF, HS), BF),
            pltpu.VMEM((2, NY, 3, CHUNK, HS), BF),
            pltpu.VMEM((2, NY, CHUNK, HS), BF),
            pltpu.VMEM((2, 2, TR, HS), BF),
            pltpu.VMEM((2, 2, TR, HS), BF),
            pltpu.VMEM((2, CHUNK, HS), BF),
            pltpu.VMEM((2, CHUNK, HS), BF),
            pltpu.VMEM((2, TR, HS), BF),
            token,
            pltpu.VMEM((4, TR, out_cols), BF),
            pltpu.VMEM((2, TR, out_cols), BF),
            wide_out,
            halves,
            wide_out,
            dma((42,)),
            dma((42,)),
            dma((34,)),
            dma((34,)),
            dma((9,)),
            dma((len(result),)),
        ],
        compiler_params=pltpu.CompilerParams(
            collective_id=0, has_side_effects=True, vmem_limit_bytes=VMEM_LIMIT
        ),
    )(
        queries,
        keys,
        values,
        text_keys,
        text_values,
        grad_out,
        out_weight,
        tile_mask,
        order,
        clip_lengths,
        head_bias,
    )
    return pl.pallas_call(
        store_kernel,
        out_shape=result,
        in_specs=[hbm] * len(result),
        out_specs=(hbm,) * len(result),
        scratch_shapes=[pltpu.VMEM(array.shape, array.dtype) for array in result]
        + [dma((len(result),)), dma((len(result),))],
        compiler_params=pltpu.CompilerParams(vmem_limit_bytes=VMEM_LIMIT),
    )(*held)


def solution(mesh):
    in_specs = (
        P("seq", "head"),
        P("seq", "head"),
        P("seq", "head"),
        P("seq", "head"),
        P("seq", "head"),
        P("head"),
        P("head", None),
        P("seq", "head"),
        P(),
        P(),
        P(),
    )
    out_specs = (P("seq", "head"),) * 6
    return jax.shard_map(shards, mesh=mesh, in_specs=in_specs, out_specs=out_specs, check_vma=False)
```

```python
import jax
import jax.numpy as jnp
from jax import lax
from jax.experimental import pallas as pl
from jax.experimental.pallas import tpu as pltpu
from jax.sharding import PartitionSpec as P

MESH = pl.DeviceIdType.MESH
BF = jnp.bfloat16
F32 = jnp.float32

NX, NZ, NY = 4, 4, 2
HS = 128
NH = 3
TR = 256
CR = 16
BR = TR + CR
HALF = TR // 2
CLIPS = 4
CAP = 128
TILE = 64
MASKED = -32768.0
BLOCKS = NH * NZ
SIDE = NX * TR
SHARED_TEXT = BR
SHARED = BR + CR
CHUNK = BR + BR
TEXT = NY * NX * CR
VMEM_LIMIT = 58 * 1024 * 1024


def place():
    seq = lax.axis_index("seq")
    head = lax.axis_index("head")
    y = seq // (NZ * NX)
    z = (seq // NX) % NZ
    x = seq % NX
    return seq, head, y, z, x


def peers(seq, head, y, z, x):
    def at(yy, zz, xx):
        return (yy * NZ + zz) * NX + xx

    other_head = (head + 2) % 4
    core_head = head + 1 - 2 * (head % 2)
    return {
        "pair": (at(1 - y, z, x), head),
        "back": (at(1 - y, z, x), other_head),
        "core": (seq, core_head),
        "right": (at(y, z, (x + 1) % NX), head),
        "left": (at(y, z, (x + NX - 1) % NX), head),
        "up": (at(y, (z + 1) % NZ, x), head),
        "down": (at(y, (z + NZ - 1) % NZ, x), head),
    }


def greet(peer):
    barrier = pltpu.get_barrier_semaphore()
    for device in peer.values():
        pl.semaphore_signal(barrier, inc=1, device_id=device, device_id_type=MESH)
    pl.semaphore_wait(barrier, len(peer))


def sender(peer, send_sem, recv_sem, sent):
    def send(n, src, dst, to):
        copy = pltpu.make_async_remote_copy(
            src_ref=src,
            dst_ref=dst,
            send_sem=send_sem.at[n],
            recv_sem=recv_sem.at[n],
            device_id=peer[to],
            device_id_type=MESH,
        )
        copy.start()
        sent.append(copy)

    def arrived(n, dst):
        pltpu.make_async_remote_copy(
            src_ref=dst,
            dst_ref=dst,
            send_sem=send_sem.at[n],
            recv_sem=recv_sem.at[n],
            device_id=peer["core"],
            device_id_type=MESH,
        ).wait_recv()

    return send, arrived


def dot_nt(a, b):
    return lax.dot_general(a, b, (((1,), (1,)), ((), ())), preferred_element_type=F32)


def dot_nn(a, b):
    return lax.dot_general(a, b, (((1,), (0,)), ((), ())), preferred_element_type=F32)


def fused_kernel(
    q_hbm,
    k_hbm,
    v_hbm,
    tk_hbm,
    tv_hbm,
    go_hbm,
    w_hbm,
    tile_hbm,
    order_hbm,
    len_ref,
    bias_ref,
    out_hbm,
    gq_hbm,
    gk_hbm,
    gv_hbm,
    gtk_hbm,
    gtv_hbm,
    q_ref,
    k_ref,
    v_ref,
    tk_ref,
    tv_ref,
    go_ref,
    w_ref,
    tile_ref,
    order_ref,
    out_ref,
    gq_ref,
    gk_ref,
    gv_ref,
    gtk_ref,
    gtv_ref,
    qg_ref,
    kv_ref,
    st_pair,
    pair_out,
    pair_in,
    goall,
    go_relay,
    acc,
    kaug,
    vals,
    qaug,
    gsel,
    weights,
    slopes,
    queries_t,
    grads_t,
    oacc,
    qacc,
    oq_ref,
    kvg_ref,
    z_in,
    z_sum,
    x_in,
    x_sum,
    yq_out,
    yq_in,
    yk_out,
    yk_in,
    keep_q,
    attn,
    part,
    core_in,
    pair_sum,
    out_relay,
    far_in,
    g_send,
    g_recv,
    r_send,
    r_recv,
    local_sem,
    store_sem,
):
    seq, head, y, z, x = place()
    peer = peers(seq, head, y, z, x)
    zu, zd, zf = (z + 1) % NZ, (z + NZ - 1) % NZ, (z + 2) % NZ
    xr, xl, xf = (x + 1) % NX, (x + NX - 1) % NX, (x + 2) % NX
    other_head = (head + 2) % 4
    core_head = head + 1 - 2 * (head % 2)
    core_other = core_head + 2 - 4 * (core_head // 2)
    first, second = pl.ds(0, HALF), pl.ds(HALF, HALF)
    sent = []
    send, arrived = sender(peer, g_send, g_recv, sent)
    rsend, rarrived = sender(peer, r_send, r_recv, sent)
    cols = lambda h: slice(h * HS, (h + 1) * HS)
    by_y = lambda a, b: jnp.where(y == 0, a, b)
    wide = lambda a: a.astype(F32)
    factor = HS ** (-0.5)

    load = []
    for n, (src, dst) in enumerate(
        (
            (k_hbm, k_ref),
            (tk_hbm, tk_ref),
            (v_hbm, v_ref),
            (tv_hbm, tv_ref),
            (q_hbm, q_ref),
            (go_hbm, go_ref),
            (w_hbm, w_ref),
            (tile_hbm, tile_ref),
            (order_hbm, order_ref),
        )
    ):
        copy = pltpu.make_async_copy(src, dst, local_sem.at[n])
        copy.start()
        load.append(copy)

    greet(peer)


    def chunk_of(a, t, index):
        return kv_ref.at[t, index, pl.ds(0, (SHARED, CHUNK)[a])]

    def x_send(a, t, yy):
        chunk = chunk_of(a, t, yy * NX + x)
        send(10 + 6 * a + 2 * t, chunk, chunk, ("right", "left")[t])
        send(11 + 6 * a + 2 * t, chunk, chunk, ("left", "right")[t])

    def x_forward(a, t, yy):
        base = 10 + 6 * a
        chunk = chunk_of(a, t, yy * NX + (xl, xr)[t])
        arrived(base + 2 * t, chunk)
        send(base + 4 + t, chunk, chunk, ("right", "left")[t])

    def x_near_finish(a, t, yy):
        arrived(10 + 6 * a + 1 + 2 * t, chunk_of(a, t, yy * NX + (xr, xl)[t]))

    def x_far_finish(a, t, yy):
        arrived(10 + 6 * a + 4 + t, chunk_of(a, t, yy * NX + xf))

    def z_pair(t):
        base = 22 + 10 * t
        send(base + 0, qg_ref.at[t, z, 2], qg_ref.at[t, z, 2], "up")
        send(base + 1, qg_ref.at[t, z, 1 - y], qg_ref.at[t, z, 1 - y], "down")
        send(base + 2, qg_ref.at[t, z, 1 - y], qg_ref.at[t, z, 1 - y], "up")
        send(base + 3, qg_ref.at[t, z, 2], qg_ref.at[t, z, 2], "down")

    def z_pair_forward(t):
        base = 22 + 10 * t
        arrived(base + 0, qg_ref.at[t, zd, 2])
        send(base + 4, qg_ref.at[t, zd, 2], qg_ref.at[t, zd, 2], "up")
        arrived(base + 1, qg_ref.at[t, zu, 1 - y])
        send(base + 5, qg_ref.at[t, zu, 1 - y], qg_ref.at[t, zu, 1 - y], "down")

    def z_own(t):
        base = 22 + 10 * t
        send(base + 6, qg_ref.at[t, z, y], qg_ref.at[t, z, y], "up")
        send(base + 7, qg_ref.at[t, z, y], qg_ref.at[t, z, y], "down")

    def z_own_forward(t):
        base = 22 + 10 * t
        arrived(base + 6, qg_ref.at[t, zd, y])
        src = qg_ref.at[t, zd, y, first]
        send(base + 8, src, src, "up")
        arrived(base + 7, qg_ref.at[t, zu, y])
        src = qg_ref.at[t, zu, y, second]
        send(base + 9, src, src, "down")

    def z_pair_finish(t):
        base = 22 + 10 * t
        arrived(base + 2, qg_ref.at[t, zd, 1 - y])
        arrived(base + 3, qg_ref.at[t, zu, 2])
        arrived(base + 4, qg_ref.at[t, zf, 2])
        arrived(base + 5, qg_ref.at[t, zf, 1 - y])

    def z_own_finish(t):
        base = 22 + 10 * t
        arrived(base + 8, qg_ref.at[t, zf, y, first])
        arrived(base + 9, qg_ref.at[t, zf, y, second])

    def pair_rows(t, shared):
        arrived((6, 9)[t], pair_in.at[t])
        qg_ref[t, z, 1 - y] = pair_in[t, 0]
        mask = chunk_rows(z, x) >= long_start
        qg_ref[t, z, 2] = by_side(mask, shared, pair_in[t, 1])[0]

    def pair_keys(t, ref):
        index = (1 - y) * NX + x
        arrived(7 + t, kv_ref.at[t, index])
        mask = chunk_rows(z, x) >= long_start
        rows = pl.ds(SHARED, TR)
        kv_ref[t, index, rows] = by_side(mask, ref[:, cols(2)], kv_ref[t, index, rows])[0]
        x_send(1, t, 1 - y)

    def feature(n):
        return w_ref[:, pl.ds(pl.multiple_of(n * 768, 128), 768)]

    half_rows = NZ * NX * TR
    ends = [len_ref[0]]
    for c in range(1, CLIPS):
        ends.append(ends[-1] + len_ref[c])
    long_start = 0
    for c in range(1, CLIPS):
        long_start = jnp.where(len_ref[c] == half_rows, ends[c - 1], long_start)

    def clip_at(pos):
        total = 0
        for c in range(CLIPS - 1):
            total = total + jnp.where(pos >= ends[c], 1, 0)
        return total

    row_index = lax.broadcasted_iota(jnp.int32, (TR, HS), 0)

    def chunk_rows(zz, xx):
        return (zz * NX + xx) * TR + row_index

    def own_is_long(zz, xx):
        t = chunk_rows(zz, xx)
        return jnp.where(y == 0, t - long_start, long_start - 1 - t) >= 0

    def by_side(mask, mine, other):
        mine, other = wide(mine), wide(other)
        return jnp.where(mask, mine, other).astype(BF), jnp.where(mask, other, mine).astype(BF)

    lane = lax.broadcasted_iota(jnp.int32, (1, HS), 1)
    tiles_here = (lane % 64) // 16 == z
    clip_lane = ((z + 1) % NZ) * 16
    bias_lane = clip_lane + CLIPS
    bias_ones = jnp.where((lane >= bias_lane) & (lane < bias_lane + 3), 1.0, 0.0)

    def kv_index(n):
        return ((y + n % 2) % NY) * NX + (x + n // 2) % NX

    def key_columns(pos):
        hit = (tiles_here & ((pos >> 6) == lane)) | (clip_at(pos) == lane - clip_lane)
        return jnp.where(hit, 1.0, bias_ones).astype(BF)

    def key_side():
        for d in range(NX):
            t = chunk_rows(z, (x + d) % NX)
            rows = slice(d * TR, (d + 1) * TR)
            sides = by_side(t >= long_start, key_columns(t), key_columns(t + half_rows))
            for side, value in enumerate(sides + (by_y(*sides),)):
                kaug[side, rows, HS:] = value
        row = lax.broadcasted_iota(jnp.int32, (TEXT, HS), 0)
        n = row // CR
        plane = ((y + n % 2) % NY) * NZ + z
        text_row = (plane * NX + (x + n // 2) % NX) * CR + row % CR
        aug = jnp.broadcast_to(bias_ones, text_row.shape)
        for c in range(CLIPS):
            listed = jnp.where(order_ref[c : c + 1, :] == text_row, 1.0, 0.0)
            found = jnp.max(listed, axis=1, keepdims=True)
            aug = jnp.where(lane == clip_lane + c, found, aug)
        for g in range(NH):
            kaug[g, SIDE:, HS:] = aug.astype(BF)

    log_len = [
        jnp.log(jnp.full((1, HS), len_ref[c] + CAP, jnp.int32).astype(F32)) for c in range(CLIPS)
    ]

    def query_side(n, carry):
        g, zq = n // NZ, n % NZ
        t = chunk_rows(zq, x)
        side = jnp.where(g == 2, y, g)
        in_high = jnp.where(side == 0, long_start - 1 - t, t - long_start) >= 0
        pos = t + jnp.where(in_high, half_rows, 0)
        head_bias = bias_ref[jnp.where(g == 2, 2, y)]
        clip = clip_at(pos)
        offset = jnp.broadcast_to(log_len[CLIPS - 1], (TR, HS))
        for c in range(CLIPS - 2, -1, -1):
            offset = jnp.where(pos < ends[c], log_len[c], offset)
        total = (head_bias - offset) * (HS**0.5)
        hi = total.astype(BF).astype(F32)
        mid = (total - hi).astype(BF).astype(F32)
        low = total - hi - mid
        in_bias = jnp.where(lane == bias_lane, hi, jnp.where(lane == bias_lane + 1, mid, low))
        in_bias = jnp.where((lane >= bias_lane) & (lane < bias_lane + 3), in_bias, 0.0)
        in_clip = (lane >= clip_lane) & (lane < clip_lane + CLIPS) & (lane - clip_lane != clip)
        side = jnp.where(in_clip, MASKED, in_bias)
        for u in range(TR // TILE):
            rows = slice(u * TILE, (u + 1) * TILE)
            tile = (zq * NX + x) * (TR // TILE) + u
            off = []
            for p in range(NY):
                at = tile + p * (half_rows // TILE)
                mask_row = tile_ref[pl.ds(at, 1), :]
                off.append(jnp.where((mask_row == 0) & (lane != at) & tiles_here, 1.0, 0.0))
            masked = jnp.where(in_high[rows], off[1], off[0]) > 0.5
            qaug[n, rows, HS:] = jnp.where(masked, MASKED, side[rows]).astype(BF)
        return carry

    def keep_query(n, value):
        qaug[n, :, 0:HS] = value
        queries_t[:, n * TR : (n + 1) * TR] = value.T

    def keep_grad(n, value):
        gsel[n] = value
        grads_t[:, n * TR : (n + 1) * TR] = value.T

    def take_rows(t, keep):
        for zq in range(NZ):
            mask = own_is_long(zq, x)
            sides = by_side(mask, qg_ref[t, zq, y], qg_ref[t, zq, 1 - y])
            for g, value in enumerate(sides + (qg_ref[t, zq, 2],)):
                keep(g * NZ + zq, value)

    def take_column(t, d):
        lanes = slice(0, HS)
        ref = (kaug, vals)[t]
        mask = own_is_long(z, (x + d) % NX)
        mine, other = kv_index(2 * d), kv_index(2 * d + 1)
        sides = by_side(mask, kv_ref[t, mine, 0:TR], kv_ref[t, other, 0:TR])
        for g, value in enumerate(sides + (kv_ref[t, other, SHARED:CHUNK],)):
            ref[g, d * TR : (d + 1) * TR, lanes] = value
        for r in range(2):
            index = kv_index(2 * d + r)
            rows = slice(SIDE + (2 * d + r) * CR, SIDE + (2 * d + r + 1) * CR)
            for g in range(NH):
                low = SHARED_TEXT if g == 2 else TR
                ref[g, rows, lanes] = kv_ref[t, index, low : low + CR]

    def block_rows(n):
        return pl.ds(pl.multiple_of(n * TR, TR), TR)

    def weigh(block, columns):
        scores = dot_nt(qaug[block], kaug[block // NZ, columns, :])
        half = jnp.tanh(scores * (0.5 * factor))
        twice = 1.0 + half
        weights[block_rows(block), columns] = twice.astype(BF)
        slopes[block_rows(block), columns] = (twice * (1.0 - half)).astype(BF)

    def every_block(body):
        def step(zq, carry):
            for g in range(NH):
                body(g * NZ + zq)
            return carry

        lax.fori_loop(0, NZ, step, 0)

    def column(d):
        return slice(d * TR, (d + 1) * TR)

    text_columns = slice(SIDE, SIDE + TEXT)

    def score(d):
        take_column(0, d)
        every_block(lambda block: weigh(block, column(d)))

    def score_text():
        every_block(lambda block: weigh(block, text_columns))

    def mix(block, columns):
        return dot_nn(weights[block_rows(block), columns], vals[block // NZ, columns, :])

    def mix_near():
        def body(block):
            oacc[block] = mix(block, slice(0, 2 * TR)) + mix(block, column(3))

        every_block(body)

    def mix_far(zq):
        totals = []
        for g in range(NH):
            block = g * NZ + zq
            total = oacc[block] + mix(block, column(2)) + mix(block, text_columns)
            totals.append(total * 0.5)
        mine, other = by_side(own_is_long(zq, x), totals[0], totals[1])
        oq_ref[0, zq, y] = mine
        oq_ref[0, zq, 1 - y] = other
        oq_ref[0, zq, 2] = totals[2].astype(BF)

    def slope_step(block, columns, fresh=False):
        rows, g = block_rows(block), block // NZ
        slope = (dot_nt(gsel[block], vals[g, columns, :]) * wide(slopes[rows, columns])).astype(BF)
        slopes[rows, columns] = slope
        share = dot_nn(slope, kaug[g, columns, 0:HS])
        if fresh:
            qacc[block] = share
        else:
            qacc[block] += share

    def slope(d):
        every_block(lambda block: slope_step(block, column(d)))

    def slope_text():
        every_block(lambda block: slope_step(block, text_columns, True))

    def slope_row(d, zq):
        for g in range(NH):
            slope_step(g * NZ + zq, column(d))

    def finish_dq(zq):
        mine, other = by_side(own_is_long(zq, x), qacc[zq] * 0.25, qacc[NZ + zq] * 0.25)
        oq_ref[1, zq, y] = mine
        oq_ref[1, zq, 1 - y] = other
        oq_ref[1, zq, 2] = (qacc[2 * NZ + zq] * 0.25).astype(BF)

    left_of = (queries_t, grads_t)
    scale_of = (0.25, 0.5)

    def key_grads(t, d):
        sides = []
        for g in range(NH):
            rows = slice(g * SIDE, (g + 1) * SIDE)
            total = dot_nn(left_of[t][:, rows], (slopes, weights)[t][rows, column(d)])
            sides.append((total * scale_of[t]).astype(BF).T)
        mine, other = by_side(own_is_long(z, (x + d) % NX), sides[0], sides[1])
        kvg_ref[t, kv_index(2 * d), 0:TR] = mine
        kvg_ref[t, kv_index(2 * d + 1), 0:TR] = other
        kvg_ref[t, kv_index(2 * d + 1), SHARED:CHUNK] = sides[2]

    def key_grads_text(t):
        for low, high, at in ((0, 2 * SIDE, TR), (2 * SIDE, 3 * SIDE, SHARED_TEXT)):
            right = (slopes, weights)[t][low:high, text_columns]
            text_rows = (dot_nn(left_of[t][:, low:high], right) * scale_of[t]).astype(BF).T
            for n in range(NY * NX):
                kvg_ref[t, kv_index(n), at : at + CR] = text_rows[n * CR : (n + 1) * CR]


    def z_far(t):
        rsend(6 * t + 0, oq_ref.at[t, zf, :, first], z_in.at[t, 0], "up")
        rsend(6 * t + 3, oq_ref.at[t, zf, :, second], z_in.at[t, 3], "down")

    def z_near(t):
        rsend(6 * t + 1, oq_ref.at[t, zd, :, first], z_in.at[t, 1], "down")
        rsend(6 * t + 4, oq_ref.at[t, zu, :, second], z_in.at[t, 4], "up")

    def z_relay(t):
        base = 6 * t
        rarrived(base + 0, z_in.at[t, 0])
        z_sum[t, 0] = (wide(z_in[t, 0]) + wide(oq_ref[t, zu, :, first])).astype(BF)
        rsend(base + 2, z_sum.at[t, 0], z_in.at[t, 2], "up")
        rarrived(base + 3, z_in.at[t, 3])
        z_sum[t, 1] = (wide(z_in[t, 3]) + wide(oq_ref[t, zd, :, second])).astype(BF)
        rsend(base + 5, z_sum.at[t, 1], z_in.at[t, 5], "down")

    def z_total(t, scale):
        base = 6 * t
        for n in (1, 2, 4, 5):
            rarrived(base + n, z_in.at[t, n])
        for rows, one, two in ((first, 1, 2), (second, 4, 5)):

            def total(j):
                value = wide(oq_ref[t, z, j, rows]) + wide(z_in[t, one, j]) + wide(z_in[t, two, j])
                return (value * scale).astype(BF) if scale != 1.0 else value.astype(BF)

            yq_out[t, 0, rows] = total(1 - y)
            yq_out[t, 1, rows] = total(2)
            keep_q[t, rows] = total(y)
        rsend(24 + t, yq_out.at[t], yq_in.at[t], "pair")

    def x_base(t, a):
        return 12 + 6 * t + 3 * a

    ring = (("right", "left"), ("left", "right"))
    ahead = ((xr, xl), (xl, xr))
    plane = (y, 1 - y)

    def sums_of(a):
        return pl.ds(0, (SHARED, CHUNK)[a])

    def x_far(t):
        for a in (1, 0):
            src = kvg_ref.at[t, plane[a] * NX + xf, sums_of(a)]
            rsend(x_base(t, a), src, x_in.at[t, a, 0, sums_of(a)], ring[a][0])

    def x_near(t):
        for a in (1, 0):
            src = kvg_ref.at[t, plane[a] * NX + ahead[a][1], sums_of(a)]
            rsend(x_base(t, a) + 1, src, x_in.at[t, a, 1, sums_of(a)], ring[a][1])

    def x_relay(t):
        for a in (1, 0):
            rows = sums_of(a)
            rarrived(x_base(t, a), x_in.at[t, a, 0, rows])
            mine = wide(kvg_ref[t, plane[a] * NX + ahead[a][0], rows])
            x_sum[t, a, rows] = (wide(x_in[t, a, 0, rows]) + mine).astype(BF)
            rsend(x_base(t, a) + 2, x_sum.at[t, a, rows], x_in.at[t, a, 2, rows], ring[a][0])

    def to_pair(t):
        yk_out[t] = x_total(t, 1).astype(BF)
        rsend(26 + t, yk_out.at[t], yk_in.at[t], "pair")

    def x_total(t, a):
        rows = sums_of(a)
        rarrived(x_base(t, a) + 1, x_in.at[t, a, 1, rows])
        rarrived(x_base(t, a) + 2, x_in.at[t, a, 2, rows])
        value = wide(kvg_ref[t, plane[a] * NX + x, rows])
        value = value + wide(x_in[t, a, 1, rows]) + wide(x_in[t, a, 2, rows])
        return value * factor if t == 0 else value

    def take_attn(t, ref):
        rarrived(24 + t, yq_in.at[t])
        ref[:, cols(0)] = by_y(keep_q[t], yq_in[t, 0])
        ref[:, cols(1)] = by_y(yq_in[t, 0], keep_q[t])
        mask = chunk_rows(z, x) >= long_start
        ref[:, cols(2)] = by_side(mask, yq_out[t, 1], yq_in[t, 1])[0]

    def project(n):
        return dot_nn(attn[...], feature(n)).astype(BF)

    send(1, go_hbm.at[second], go_relay.at[1], "back")
    load[4].wait()
    pair_out[0, 0] = by_y(q_ref[:, cols(1)], q_ref[:, cols(0)])
    pair_out[0, 1] = q_ref[:, cols(2)]
    send(6, pair_out.at[0], pair_in.at[0], "pair")
    qg_ref[0, z, y] = by_y(q_ref[:, cols(0)], q_ref[:, cols(1)])
    z_own(0)
    c = y * NX + x
    pair_y = 1 - y
    for t, (ref, text) in enumerate(((k_ref, tk_ref), (v_ref, tv_ref))):
        load[2 * t].wait()
        load[2 * t + 1].wait()
        st_pair[t, 0:TR] = by_y(ref[:, cols(1)], ref[:, cols(0)])
        st_pair[t, TR:BR] = by_y(text[:, cols(1)], text[:, cols(0)])
        st_pair[t, SHARED_TEXT:SHARED] = text[:, cols(2)]
        st_pair[t, SHARED:CHUNK] = ref[:, cols(2)]
        if t == 0:
            send(7, st_pair.at[0], kv_ref.at[0, c], "pair")
        kv_ref[t, c, 0:TR] = by_y(ref[:, cols(0)], ref[:, cols(1)])
        kv_ref[t, c, TR:BR] = by_y(text[:, cols(0)], text[:, cols(1)])
        kv_ref[t, c, SHARED_TEXT:SHARED] = text[:, cols(2)]
        x_send(0, t, y)
    send(2, go_hbm, goall.at[head], "core")
    load[7].wait()
    load[8].wait()
    key_side()
    pair_rows(0, q_ref[:, cols(2)])
    z_pair(0)
    send(0, go_hbm.at[first], go_relay.at[0], "pair")
    lax.fori_loop(0, BLOCKS, query_side, 0)
    z_own_forward(0)
    pair_keys(0, k_ref)
    load[5].wait()
    load[6].wait()
    acc[...] = dot_nt(go_ref[...], feature(head))
    x_forward(0, 0, y)
    x_forward(0, 1, y)
    z_pair_forward(0)
    z_own_finish(0)
    z_pair_finish(0)
    take_rows(0, keep_query)
    arrived(0, go_relay.at[0])
    send(3, go_relay.at[0], goall.at[head, first], "back")
    arrived(1, go_relay.at[1])
    send(4, go_relay.at[1], goall.at[other_head, second], "pair")
    send(8, st_pair.at[1], kv_ref.at[1, c], "pair")
    x_forward(1, 0, pair_y)
    score(0)
    arrived(2, goall.at[core_head])
    acc[...] += dot_nt(goall[core_head], feature(core_head))
    x_near_finish(0, 0, y)
    x_near_finish(1, 0, pair_y)
    score(1)
    score(3)
    arrived(3, goall.at[other_head, first])
    arrived(4, goall.at[other_head, second])
    send(5, goall.at[other_head], goall.at[other_head], "core")
    acc[...] += dot_nt(goall[other_head], feature(other_head))
    pair_keys(1, v_ref)
    arrived(5, goall.at[core_other])
    grad = (acc[...] + dot_nt(goall[core_other], feature(core_other))).astype(BF)
    pair_out[1, 0] = by_y(grad[:, cols(1)], grad[:, cols(0)])
    pair_out[1, 1] = grad[:, cols(2)]
    send(9, pair_out.at[1], pair_in.at[1], "pair")
    qg_ref[1, z, y] = by_y(grad[:, cols(0)], grad[:, cols(1)])
    z_own(1)
    x_far_finish(0, 0, y)
    x_far_finish(1, 0, pair_y)
    score(2)
    x_forward(1, 1, pair_y)
    pair_rows(1, pair_out[1, 1])
    z_pair(1)
    z_own_forward(1)
    score_text()
    x_near_finish(0, 1, y)
    x_far_finish(0, 1, y)
    take_column(1, 0)
    x_near_finish(1, 1, pair_y)
    take_column(1, 1)
    take_column(1, 3)
    mix_near()
    z_pair_forward(1)
    x_far_finish(1, 1, pair_y)
    take_column(1, 2)
    mix_far(zf)
    z_far(0)
    mix_far(zu)
    mix_far(zd)
    z_near(0)
    mix_far(z)

    z_own_finish(1)
    z_pair_finish(1)
    take_rows(1, keep_grad)
    key_grads_text(1)
    key_grads(1, 2)
    x_far(1)
    z_relay(0)
    key_grads(1, 3)
    key_grads(1, 1)
    x_near(1)
    slope_text()
    slope(2)
    x_relay(1)
    z_total(0, 1.0)
    key_grads_text(0)
    key_grads(0, 2)
    x_far(0)
    slope(1)
    take_attn(0, attn)
    part[0] = project(core_other)
    rsend(28, part.at[0], core_in.at[0], "core")
    part[2] = project(other_head)
    slope(3)
    rarrived(28, core_in.at[0])
    pair_sum[...] = (wide(part[2]) + wide(core_in[0])).astype(BF)
    rsend(30, pair_sum.at[first], out_relay.at[0], "pair")
    rsend(31, pair_sum.at[second], out_relay.at[1], "back")
    key_grads(0, 1)
    key_grads(0, 3)
    x_relay(0)
    x_near(0)
    for zq in (zf, zu, zd, z):
        slope_row(0, zq)
        finish_dq(zq)
        if zq is zf:
            z_far(1)
        elif zq is zd:
            z_near(1)
    key_grads(1, 0)
    to_pair(1)
    rarrived(30, out_relay.at[0])
    rsend(32, out_relay.at[0], far_in.at[first], "back")
    rarrived(31, out_relay.at[1])
    rsend(33, out_relay.at[1], far_in.at[second], "pair")
    z_relay(1)
    key_grads(0, 0)
    part[1] = project(core_head)
    rsend(29, part.at[1], core_in.at[1], "core")
    part[3] = project(head)
    to_pair(0)
    z_total(1, factor)

    stores = []

    def store(src, dst):
        copy = pltpu.make_async_copy(src, dst, store_sem.at[len(stores)])
        copy.start()
        stores.append(copy)

    results = ((gk_ref, gtk_ref, gk_hbm, gtk_hbm), (gv_ref, gtv_ref, gv_hbm, gtv_hbm))
    rarrived(29, core_in.at[1])
    rarrived(32, far_in.at[first])
    rarrived(33, far_in.at[second])
    out_ref[...] = (wide(part[3]) + wide(core_in[1]) + wide(far_in[...])).astype(BF)
    store(out_ref, out_hbm)
    for t, (ref, text, to, text_to) in enumerate(results):
        own = x_total(t, 0)
        rarrived(26 + t, yk_in.at[t])
        mine, other = own[0:BR].astype(BF), yk_in[t, 0:BR]
        mask = chunk_rows(z, x) >= long_start
        both = by_side(mask, yk_out[t, SHARED:CHUNK], yk_in[t, SHARED:CHUNK])[0]
        for h, value in ((0, by_y(mine, other)), (1, by_y(other, mine))):
            ref[:, cols(h)] = value[0:TR]
            text[:, cols(h)] = value[TR:BR]
        ref[:, cols(2)] = both
        text[:, cols(2)] = (own[BR:SHARED] + wide(yk_in[t, SHARED_TEXT:SHARED])).astype(BF)
        store(ref, to)
        store(text, text_to)
    take_attn(1, gq_ref)
    store(gq_ref, gq_hbm)
    for copy in sent:
        copy.wait_send()
    for copy in stores:
        copy.wait()


def store_kernel(*refs):
    count = (len(refs) - 2) // 3
    held, result, buffers = refs[:count], refs[count : 2 * count], refs[2 * count : 3 * count]
    load_sem, store_sem = refs[-2:]
    loads = [
        pltpu.make_async_copy(held[n], buffers[n], load_sem.at[n]) for n in range(count)
    ]
    stores = [
        pltpu.make_async_copy(buffers[n], result[n], store_sem.at[n]) for n in range(count)
    ]
    for copy in loads:
        copy.start()
    for load, copy in zip(loads, stores):
        load.wait()
        copy.start()
    for copy in stores:
        copy.wait()


def shards(
    queries,
    keys,
    values,
    text_keys,
    text_values,
    head_bias,
    out_weight,
    grad_out,
    clip_lengths,
    tile_mask,
    caption_order,
):
    smem = pl.BlockSpec(memory_space=pltpu.SMEM)
    hbm = pl.BlockSpec(memory_space=pltpu.HBM)
    dma = pltpu.SemaphoreType.DMA
    qg_shape = (2, NZ, NH, TR, HS)
    kv_shape = (2, NY * NX, CHUNK, HS)
    out_cols = grad_out.shape[1]
    order = caption_order.reshape(CLIPS, CAP)
    token = pltpu.VMEM((TR, NH * HS), BF)
    text = pltpu.VMEM((CR, NH * HS), BF)
    wide_out = pltpu.VMEM((TR, out_cols), BF)
    halves = pltpu.VMEM((2, HALF, out_cols), BF)
    token_shape = jax.ShapeDtypeStruct((TR, NH * HS), BF)
    text_shape = jax.ShapeDtypeStruct((CR, NH * HS), BF)
    result = (
        jax.ShapeDtypeStruct((TR, out_cols), BF),
        token_shape,
        token_shape,
        token_shape,
        text_shape,
        text_shape,
    )
    held = pl.pallas_call(
        fused_kernel,
        out_shape=result,
        in_specs=[hbm] * 9 + [smem] * 2,
        out_specs=(hbm,) * len(result),
        scratch_shapes=[
            token,
            token,
            token,
            text,
            text,
            wide_out,
            pltpu.VMEM(out_weight.shape, BF),
            pltpu.VMEM(tile_mask.shape, jnp.int32),
            pltpu.VMEM(order.shape, jnp.int32),
            wide_out,
            token,
            token,
            token,
            text,
            text,
            pltpu.VMEM(qg_shape, BF),
            pltpu.VMEM(kv_shape, BF),
            pltpu.VMEM((2, CHUNK, HS), BF),
            pltpu.VMEM((2, 2, TR, HS), BF),
            pltpu.VMEM((2, 2, TR, HS), BF),
            pltpu.VMEM((4, TR, out_cols), BF),
            halves,
            pltpu.VMEM((TR, NH * HS), F32),
            pltpu.VMEM((NH, SIDE + TEXT, 2 * HS), BF),
            pltpu.VMEM((NH, SIDE + TEXT, HS), BF),
            pltpu.VMEM((BLOCKS, TR, 2 * HS), BF),
            pltpu.VMEM((BLOCKS, TR, HS), BF),
            pltpu.VMEM((BLOCKS * TR, SIDE + TEXT), BF),
            pltpu.VMEM((BLOCKS * TR, SIDE + TEXT), BF),
            pltpu.VMEM((HS, BLOCKS * TR), BF),
            pltpu.VMEM((HS, BLOCKS * TR), BF),
            pltpu.VMEM((BLOCKS, TR, HS), F32),
            pltpu.VMEM((BLOCKS, TR, HS), F32),
            pltpu.VMEM(qg_shape, BF),
            pltpu.VMEM(kv_shape, BF),
            pltpu.VMEM((2, 6, NH, HALF, HS), BF),
            pltpu.VMEM((2, 2, NH, HALF, HS), BF),
            pltpu.VMEM((2, NY, 3, CHUNK, HS), BF),
            pltpu.VMEM((2, NY, CHUNK, HS), BF),
            pltpu.VMEM((2, 2, TR, HS), BF),
            pltpu.VMEM((2, 2, TR, HS), BF),
            pltpu.VMEM((2, CHUNK, HS), BF),
            pltpu.VMEM((2, CHUNK, HS), BF),
            pltpu.VMEM((2, TR, HS), BF),
            token,
            pltpu.VMEM((4, TR, out_cols), BF),
            pltpu.VMEM((2, TR, out_cols), BF),
            wide_out,
            halves,
            wide_out,
            dma((42,)),
            dma((42,)),
            dma((34,)),
            dma((34,)),
            dma((9,)),
            dma((len(result),)),
        ],
        compiler_params=pltpu.CompilerParams(
            collective_id=0, has_side_effects=True, vmem_limit_bytes=VMEM_LIMIT
        ),
    )(
        queries,
        keys,
        values,
        text_keys,
        text_values,
        grad_out,
        out_weight,
        tile_mask,
        order,
        clip_lengths,
        head_bias,
    )
    return pl.pallas_call(
        store_kernel,
        out_shape=result,
        in_specs=[hbm] * len(result),
        out_specs=(hbm,) * len(result),
        scratch_shapes=[pltpu.VMEM(array.shape, array.dtype) for array in result]
        + [dma((len(result),)), dma((len(result),))],
        compiler_params=pltpu.CompilerParams(vmem_limit_bytes=VMEM_LIMIT),
    )(*held)


def solution(mesh):
    in_specs = (
        P("seq", "head"),
        P("seq", "head"),
        P("seq", "head"),
        P("seq", "head"),
        P("seq", "head"),
        P("head"),
        P("head", None),
        P("seq", "head"),
        P(),
        P(),
        P(),
    )
    out_specs = (P("seq", "head"),) * 6
    return jax.shard_map(shards, mesh=mesh, in_specs=in_specs, out_specs=out_specs, check_vma=False)
```

```python
import jax
import jax.numpy as jnp
from jax import lax
from jax.experimental import pallas as pl
from jax.experimental.pallas import tpu as pltpu
from jax.sharding import PartitionSpec as P

MESH = pl.DeviceIdType.MESH
BF = jnp.bfloat16
F32 = jnp.float32

NX, NZ, NY = 4, 4, 2
HS = 128
NH = 3
TR = 256
CR = 16
BR = TR + CR
HALF = TR // 2
CLIPS = 4
CAP = 128
TILE = 64
MASKED = -32768.0
BLOCKS = NH * NZ
SIDE = NX * TR
SHARED_TEXT = BR
SHARED = BR + CR
CHUNK = BR + BR
TEXT = NY * NX * CR
VMEM_LIMIT = 58 * 1024 * 1024


def place():
    seq = lax.axis_index("seq")
    head = lax.axis_index("head")
    y = seq // (NZ * NX)
    z = (seq // NX) % NZ
    x = seq % NX
    return seq, head, y, z, x


def peers(seq, head, y, z, x):
    def at(yy, zz, xx):
        return (yy * NZ + zz) * NX + xx

    other_head = (head + 2) % 4
    core_head = head + 1 - 2 * (head % 2)
    return {
        "pair": (at(1 - y, z, x), head),
        "back": (at(1 - y, z, x), other_head),
        "core": (seq, core_head),
        "right": (at(y, z, (x + 1) % NX), head),
        "left": (at(y, z, (x + NX - 1) % NX), head),
        "up": (at(y, (z + 1) % NZ, x), head),
        "down": (at(y, (z + NZ - 1) % NZ, x), head),
    }


def greet(peer):
    barrier = pltpu.get_barrier_semaphore()
    for device in peer.values():
        pl.semaphore_signal(barrier, inc=1, device_id=device, device_id_type=MESH)
    pl.semaphore_wait(barrier, len(peer))


def sender(peer, send_sem, recv_sem, sent):
    def send(n, src, dst, to):
        copy = pltpu.make_async_remote_copy(
            src_ref=src,
            dst_ref=dst,
            send_sem=send_sem.at[n],
            recv_sem=recv_sem.at[n],
            device_id=peer[to],
            device_id_type=MESH,
        )
        copy.start()
        sent.append(copy)

    def arrived(n, dst):
        pltpu.make_async_remote_copy(
            src_ref=dst,
            dst_ref=dst,
            send_sem=send_sem.at[n],
            recv_sem=recv_sem.at[n],
            device_id=peer["core"],
            device_id_type=MESH,
        ).wait_recv()

    return send, arrived


def dot_nt(a, b):
    return lax.dot_general(a, b, (((1,), (1,)), ((), ())), preferred_element_type=F32)


def dot_nn(a, b):
    return lax.dot_general(a, b, (((1,), (0,)), ((), ())), preferred_element_type=F32)


def fused_kernel(
    q_hbm,
    k_hbm,
    v_hbm,
    tk_hbm,
    tv_hbm,
    go_hbm,
    w_hbm,
    tile_hbm,
    order_hbm,
    len_ref,
    bias_ref,
    out_hbm,
    gq_hbm,
    gk_hbm,
    gv_hbm,
    gtk_hbm,
    gtv_hbm,
    q_ref,
    k_ref,
    v_ref,
    tk_ref,
    tv_ref,
    go_ref,
    w_ref,
    tile_ref,
    order_ref,
    out_ref,
    gq_ref,
    gk_ref,
    gv_ref,
    gtk_ref,
    gtv_ref,
    qg_ref,
    kv_ref,
    st_pair,
    pair_out,
    pair_in,
    goall,
    go_relay,
    acc,
    kaug,
    vals,
    qaug,
    gsel,
    weights,
    slopes,
    queries_t,
    grads_t,
    oacc,
    qacc,
    oq_ref,
    kvg_ref,
    z_in,
    z_sum,
    x_in,
    x_sum,
    yq_out,
    yq_in,
    yk_out,
    yk_in,
    keep_q,
    attn,
    part,
    core_in,
    pair_sum,
    out_relay,
    far_in,
    g_send,
    g_recv,
    r_send,
    r_recv,
    local_sem,
    store_sem,
):
    seq, head, y, z, x = place()
    peer = peers(seq, head, y, z, x)
    zu, zd, zf = (z + 1) % NZ, (z + NZ - 1) % NZ, (z + 2) % NZ
    xr, xl, xf = (x + 1) % NX, (x + NX - 1) % NX, (x + 2) % NX
    other_head = (head + 2) % 4
    core_head = head + 1 - 2 * (head % 2)
    core_other = core_head + 2 - 4 * (core_head // 2)
    first, second = pl.ds(0, HALF), pl.ds(HALF, HALF)
    sent = []
    send, arrived = sender(peer, g_send, g_recv, sent)
    rsend, rarrived = sender(peer, r_send, r_recv, sent)
    cols = lambda h: slice(h * HS, (h + 1) * HS)
    by_y = lambda a, b: jnp.where(y == 0, a, b)
    wide = lambda a: a.astype(F32)
    factor = HS ** (-0.5)

    load = []
    for n, (src, dst) in enumerate(
        (
            (k_hbm, k_ref),
            (tk_hbm, tk_ref),
            (v_hbm, v_ref),
            (tv_hbm, tv_ref),
            (q_hbm, q_ref),
            (go_hbm, go_ref),
            (w_hbm, w_ref),
            (tile_hbm, tile_ref),
            (order_hbm, order_ref),
        )
    ):
        copy = pltpu.make_async_copy(src, dst, local_sem.at[n])
        copy.start()
        load.append(copy)

    greet(peer)


    def chunk_of(a, t, index):
        return kv_ref.at[t, index, pl.ds(0, (SHARED, CHUNK)[a])]

    def x_send(a, t, yy):
        chunk = chunk_of(a, t, yy * NX + x)
        send(10 + 6 * a + 2 * t, chunk, chunk, ("right", "left")[t])
        send(11 + 6 * a + 2 * t, chunk, chunk, ("left", "right")[t])

    def x_forward(a, t, yy):
        base = 10 + 6 * a
        chunk = chunk_of(a, t, yy * NX + (xl, xr)[t])
        arrived(base + 2 * t, chunk)
        send(base + 4 + t, chunk, chunk, ("right", "left")[t])

    def x_near_finish(a, t, yy):
        arrived(10 + 6 * a + 1 + 2 * t, chunk_of(a, t, yy * NX + (xr, xl)[t]))

    def x_far_finish(a, t, yy):
        arrived(10 + 6 * a + 4 + t, chunk_of(a, t, yy * NX + xf))

    def z_pair(t):
        base = 22 + 10 * t
        send(base + 0, qg_ref.at[t, z, 2], qg_ref.at[t, z, 2], "up")
        send(base + 1, qg_ref.at[t, z, 1 - y], qg_ref.at[t, z, 1 - y], "down")
        send(base + 2, qg_ref.at[t, z, 1 - y], qg_ref.at[t, z, 1 - y], "up")
        send(base + 3, qg_ref.at[t, z, 2], qg_ref.at[t, z, 2], "down")

    def z_pair_forward(t):
        base = 22 + 10 * t
        arrived(base + 0, qg_ref.at[t, zd, 2])
        send(base + 4, qg_ref.at[t, zd, 2], qg_ref.at[t, zd, 2], "up")
        arrived(base + 1, qg_ref.at[t, zu, 1 - y])
        send(base + 5, qg_ref.at[t, zu, 1 - y], qg_ref.at[t, zu, 1 - y], "down")

    def z_own(t):
        base = 22 + 10 * t
        send(base + 6, qg_ref.at[t, z, y], qg_ref.at[t, z, y], "up")
        send(base + 7, qg_ref.at[t, z, y], qg_ref.at[t, z, y], "down")

    def z_own_forward(t):
        base = 22 + 10 * t
        arrived(base + 6, qg_ref.at[t, zd, y])
        src = qg_ref.at[t, zd, y, first]
        send(base + 8, src, src, "up")
        arrived(base + 7, qg_ref.at[t, zu, y])
        src = qg_ref.at[t, zu, y, second]
        send(base + 9, src, src, "down")

    def z_pair_finish(t):
        base = 22 + 10 * t
        arrived(base + 2, qg_ref.at[t, zd, 1 - y])
        arrived(base + 3, qg_ref.at[t, zu, 2])
        arrived(base + 4, qg_ref.at[t, zf, 2])
        arrived(base + 5, qg_ref.at[t, zf, 1 - y])

    def z_own_finish(t):
        base = 22 + 10 * t
        arrived(base + 8, qg_ref.at[t, zf, y, first])
        arrived(base + 9, qg_ref.at[t, zf, y, second])

    def pair_rows(t, shared):
        arrived((6, 9)[t], pair_in.at[t])
        qg_ref[t, z, 1 - y] = pair_in[t, 0]
        mask = chunk_rows(z, x) >= long_start
        qg_ref[t, z, 2] = by_side(mask, shared, pair_in[t, 1])[0]

    def pair_keys(t, ref):
        index = (1 - y) * NX + x
        arrived(7 + t, kv_ref.at[t, index])
        mask = chunk_rows(z, x) >= long_start
        rows = pl.ds(SHARED, TR)
        kv_ref[t, index, rows] = by_side(mask, ref[:, cols(2)], kv_ref[t, index, rows])[0]
        x_send(1, t, 1 - y)

    def feature(n):
        return w_ref[:, pl.ds(pl.multiple_of(n * 768, 128), 768)]

    half_rows = NZ * NX * TR
    ends = [len_ref[0]]
    for c in range(1, CLIPS):
        ends.append(ends[-1] + len_ref[c])
    long_start = 0
    for c in range(1, CLIPS):
        long_start = jnp.where(len_ref[c] == half_rows, ends[c - 1], long_start)

    def clip_at(pos):
        total = 0
        for c in range(CLIPS - 1):
            total = total + jnp.where(pos >= ends[c], 1, 0)
        return total

    row_index = lax.broadcasted_iota(jnp.int32, (TR, HS), 0)

    def chunk_rows(zz, xx):
        return (zz * NX + xx) * TR + row_index

    def own_is_long(zz, xx):
        t = chunk_rows(zz, xx)
        return jnp.where(y == 0, t - long_start, long_start - 1 - t) >= 0

    def by_side(mask, mine, other):
        mine, other = wide(mine), wide(other)
        return jnp.where(mask, mine, other).astype(BF), jnp.where(mask, other, mine).astype(BF)

    lane = lax.broadcasted_iota(jnp.int32, (1, HS), 1)
    tiles_here = (lane % 64) // 16 == z
    clip_lane = ((z + 1) % NZ) * 16
    bias_lane = clip_lane + CLIPS
    bias_ones = jnp.where((lane >= bias_lane) & (lane < bias_lane + 3), 1.0, 0.0)

    def kv_index(n):
        return ((y + n % 2) % NY) * NX + (x + n // 2) % NX

    def key_columns(pos):
        hit = (tiles_here & ((pos >> 6) == lane)) | (clip_at(pos) == lane - clip_lane)
        return jnp.where(hit, 1.0, bias_ones).astype(BF)

    def key_side():
        for d in range(NX):
            t = chunk_rows(z, (x + d) % NX)
            rows = slice(d * TR, (d + 1) * TR)
            sides = by_side(t >= long_start, key_columns(t), key_columns(t + half_rows))
            for side, value in enumerate(sides + (by_y(*sides),)):
                kaug[side, rows, HS:] = value
        row = lax.broadcasted_iota(jnp.int32, (TEXT, HS), 0)
        n = row // CR
        plane = ((y + n % 2) % NY) * NZ + z
        text_row = (plane * NX + (x + n // 2) % NX) * CR + row % CR
        aug = jnp.broadcast_to(bias_ones, text_row.shape)
        for c in range(CLIPS):
            listed = jnp.where(order_ref[c : c + 1, :] == text_row, 1.0, 0.0)
            found = jnp.max(listed, axis=1, keepdims=True)
            aug = jnp.where(lane == clip_lane + c, found, aug)
        for g in range(NH):
            kaug[g, SIDE:, HS:] = aug.astype(BF)

    log_len = [
        jnp.log(jnp.full((1, HS), len_ref[c] + CAP, jnp.int32).astype(F32)) for c in range(CLIPS)
    ]

    def query_side(n, carry):
        g, zq = n // NZ, n % NZ
        t = chunk_rows(zq, x)
        side = jnp.where(g == 2, y, g)
        in_high = jnp.where(side == 0, long_start - 1 - t, t - long_start) >= 0
        pos = t + jnp.where(in_high, half_rows, 0)
        head_bias = bias_ref[jnp.where(g == 2, 2, y)]
        clip = clip_at(pos)
        offset = jnp.broadcast_to(log_len[CLIPS - 1], (TR, HS))
        for c in range(CLIPS - 2, -1, -1):
            offset = jnp.where(pos < ends[c], log_len[c], offset)
        total = (head_bias - offset) * (HS**0.5)
        hi = total.astype(BF).astype(F32)
        mid = (total - hi).astype(BF).astype(F32)
        low = total - hi - mid
        in_bias = jnp.where(lane == bias_lane, hi, jnp.where(lane == bias_lane + 1, mid, low))
        in_bias = jnp.where((lane >= bias_lane) & (lane < bias_lane + 3), in_bias, 0.0)
        in_clip = (lane >= clip_lane) & (lane < clip_lane + CLIPS) & (lane - clip_lane != clip)
        side = jnp.where(in_clip, MASKED, in_bias)
        for u in range(TR // TILE):
            rows = slice(u * TILE, (u + 1) * TILE)
            tile = (zq * NX + x) * (TR // TILE) + u
            off = []
            for p in range(NY):
                at = tile + p * (half_rows // TILE)
                mask_row = tile_ref[pl.ds(at, 1), :]
                off.append(jnp.where((mask_row == 0) & (lane != at) & tiles_here, 1.0, 0.0))
            masked = jnp.where(in_high[rows], off[1], off[0]) > 0.5
            qaug[n, rows, HS:] = jnp.where(masked, MASKED, side[rows]).astype(BF)
        return carry

    def keep_query(n, value):
        qaug[n, :, 0:HS] = value
        queries_t[:, n * TR : (n + 1) * TR] = value.T

    def keep_grad(n, value):
        gsel[n] = value
        grads_t[:, n * TR : (n + 1) * TR] = value.T

    def take_rows(t, keep):
        for zq in range(NZ):
            mask = own_is_long(zq, x)
            sides = by_side(mask, qg_ref[t, zq, y], qg_ref[t, zq, 1 - y])
            for g, value in enumerate(sides + (qg_ref[t, zq, 2],)):
                keep(g * NZ + zq, value)

    def take_column(t, d):
        lanes = slice(0, HS)
        ref = (kaug, vals)[t]
        mask = own_is_long(z, (x + d) % NX)
        mine, other = kv_index(2 * d), kv_index(2 * d + 1)
        sides = by_side(mask, kv_ref[t, mine, 0:TR], kv_ref[t, other, 0:TR])
        for g, value in enumerate(sides + (kv_ref[t, other, SHARED:CHUNK],)):
            ref[g, d * TR : (d + 1) * TR, lanes] = value
        for r in range(2):
            index = kv_index(2 * d + r)
            rows = slice(SIDE + (2 * d + r) * CR, SIDE + (2 * d + r + 1) * CR)
            for g in range(NH):
                low = SHARED_TEXT if g == 2 else TR
                ref[g, rows, lanes] = kv_ref[t, index, low : low + CR]

    def block_rows(n):
        return pl.ds(pl.multiple_of(n * TR, TR), TR)

    def weigh(block, columns):
        scores = dot_nt(qaug[block], kaug[block // NZ, columns, :])
        half = jnp.tanh(scores * (0.5 * factor))
        twice = 1.0 + half
        weights[block_rows(block), columns] = twice.astype(BF)
        slopes[block_rows(block), columns] = (twice * (1.0 - half)).astype(BF)

    def every_block(body):
        def step(zq, carry):
            for g in range(NH):
                body(g * NZ + zq)
            return carry

        lax.fori_loop(0, NZ, step, 0)

    def column(d):
        return slice(d * TR, (d + 1) * TR)

    text_columns = slice(SIDE, SIDE + TEXT)

    def score(d):
        take_column(0, d)
        every_block(lambda block: weigh(block, column(d)))

    def score_text():
        every_block(lambda block: weigh(block, text_columns))

    def mix(block, columns):
        return dot_nn(weights[block_rows(block), columns], vals[block // NZ, columns, :])

    def mix_near():
        def body(block):
            oacc[block] = mix(block, slice(0, 2 * TR)) + mix(block, column(3))

        every_block(body)

    def mix_far(zq):
        totals = []
        for g in range(NH):
            block = g * NZ + zq
            total = oacc[block] + mix(block, column(2)) + mix(block, text_columns)
            totals.append(total * 0.5)
        mine, other = by_side(own_is_long(zq, x), totals[0], totals[1])
        oq_ref[0, zq, y] = mine
        oq_ref[0, zq, 1 - y] = other
        oq_ref[0, zq, 2] = totals[2].astype(BF)

    def slope_step(block, columns, fresh=False):
        rows, g = block_rows(block), block // NZ
        slope = (dot_nt(gsel[block], vals[g, columns, :]) * wide(slopes[rows, columns])).astype(BF)
        slopes[rows, columns] = slope
        share = dot_nn(slope, kaug[g, columns, 0:HS])
        if fresh:
            qacc[block] = share
        else:
            qacc[block] += share

    def slope(d):
        every_block(lambda block: slope_step(block, column(d)))

    def slope_text():
        every_block(lambda block: slope_step(block, text_columns, True))

    def slope_row(d, zq):
        for g in range(NH):
            slope_step(g * NZ + zq, column(d))

    def finish_dq(zq):
        mine, other = by_side(own_is_long(zq, x), qacc[zq] * 0.25, qacc[NZ + zq] * 0.25)
        oq_ref[1, zq, y] = mine
        oq_ref[1, zq, 1 - y] = other
        oq_ref[1, zq, 2] = (qacc[2 * NZ + zq] * 0.25).astype(BF)

    left_of = (queries_t, grads_t)
    scale_of = (0.25, 0.5)

    def key_grads(t, d):
        sides = []
        for g in range(NH):
            rows = slice(g * SIDE, (g + 1) * SIDE)
            total = dot_nn(left_of[t][:, rows], (slopes, weights)[t][rows, column(d)])
            sides.append((total * scale_of[t]).astype(BF).T)
        mine, other = by_side(own_is_long(z, (x + d) % NX), sides[0], sides[1])
        kvg_ref[t, kv_index(2 * d), 0:TR] = mine
        kvg_ref[t, kv_index(2 * d + 1), 0:TR] = other
        kvg_ref[t, kv_index(2 * d + 1), SHARED:CHUNK] = sides[2]

    def key_grads_text(t):
        for low, high, at in ((0, 2 * SIDE, TR), (2 * SIDE, 3 * SIDE, SHARED_TEXT)):
            right = (slopes, weights)[t][low:high, text_columns]
            text_rows = (dot_nn(left_of[t][:, low:high], right) * scale_of[t]).astype(BF).T
            for n in range(NY * NX):
                kvg_ref[t, kv_index(n), at : at + CR] = text_rows[n * CR : (n + 1) * CR]


    def z_far(t):
        rsend(6 * t + 0, oq_ref.at[t, zf, :, first], z_in.at[t, 0], "up")
        rsend(6 * t + 3, oq_ref.at[t, zf, :, second], z_in.at[t, 3], "down")

    def z_near(t):
        rsend(6 * t + 1, oq_ref.at[t, zd, :, first], z_in.at[t, 1], "down")
        rsend(6 * t + 4, oq_ref.at[t, zu, :, second], z_in.at[t, 4], "up")

    def z_relay(t):
        base = 6 * t
        rarrived(base + 0, z_in.at[t, 0])
        z_sum[t, 0] = (wide(z_in[t, 0]) + wide(oq_ref[t, zu, :, first])).astype(BF)
        rsend(base + 2, z_sum.at[t, 0], z_in.at[t, 2], "up")
        rarrived(base + 3, z_in.at[t, 3])
        z_sum[t, 1] = (wide(z_in[t, 3]) + wide(oq_ref[t, zd, :, second])).astype(BF)
        rsend(base + 5, z_sum.at[t, 1], z_in.at[t, 5], "down")

    def z_total(t, scale):
        base = 6 * t
        for n in (1, 2, 4, 5):
            rarrived(base + n, z_in.at[t, n])
        for rows, one, two in ((first, 1, 2), (second, 4, 5)):

            def total(j):
                value = wide(oq_ref[t, z, j, rows]) + wide(z_in[t, one, j]) + wide(z_in[t, two, j])
                return (value * scale).astype(BF) if scale != 1.0 else value.astype(BF)

            yq_out[t, 0, rows] = total(1 - y)
            yq_out[t, 1, rows] = total(2)
            keep_q[t, rows] = total(y)
        rsend(24 + t, yq_out.at[t], yq_in.at[t], "pair")

    def x_base(t, a):
        return 12 + 6 * t + 3 * a

    ring = (("right", "left"), ("left", "right"))
    ahead = ((xr, xl), (xl, xr))
    plane = (y, 1 - y)

    def sums_of(a):
        return pl.ds(0, (SHARED, CHUNK)[a])

    def x_far(t):
        for a in (1, 0):
            src = kvg_ref.at[t, plane[a] * NX + xf, sums_of(a)]
            rsend(x_base(t, a), src, x_in.at[t, a, 0, sums_of(a)], ring[a][0])

    def x_near(t):
        for a in (1, 0):
            src = kvg_ref.at[t, plane[a] * NX + ahead[a][1], sums_of(a)]
            rsend(x_base(t, a) + 1, src, x_in.at[t, a, 1, sums_of(a)], ring[a][1])

    def x_relay(t):
        for a in (1, 0):
            rows = sums_of(a)
            rarrived(x_base(t, a), x_in.at[t, a, 0, rows])
            mine = wide(kvg_ref[t, plane[a] * NX + ahead[a][0], rows])
            x_sum[t, a, rows] = (wide(x_in[t, a, 0, rows]) + mine).astype(BF)
            rsend(x_base(t, a) + 2, x_sum.at[t, a, rows], x_in.at[t, a, 2, rows], ring[a][0])

    def to_pair(t):
        yk_out[t] = x_total(t, 1).astype(BF)
        rsend(26 + t, yk_out.at[t], yk_in.at[t], "pair")

    def x_total(t, a):
        rows = sums_of(a)
        rarrived(x_base(t, a) + 1, x_in.at[t, a, 1, rows])
        rarrived(x_base(t, a) + 2, x_in.at[t, a, 2, rows])
        value = wide(kvg_ref[t, plane[a] * NX + x, rows])
        value = value + wide(x_in[t, a, 1, rows]) + wide(x_in[t, a, 2, rows])
        return value * factor if t == 0 else value

    def take_attn(t, ref):
        rarrived(24 + t, yq_in.at[t])
        ref[:, cols(0)] = by_y(keep_q[t], yq_in[t, 0])
        ref[:, cols(1)] = by_y(yq_in[t, 0], keep_q[t])
        mask = chunk_rows(z, x) >= long_start
        ref[:, cols(2)] = by_side(mask, yq_out[t, 1], yq_in[t, 1])[0]

    def project(n):
        return dot_nn(attn[...], feature(n)).astype(BF)

    send(1, go_hbm.at[second], go_relay.at[1], "back")
    load[4].wait()
    pair_out[0, 0] = by_y(q_ref[:, cols(1)], q_ref[:, cols(0)])
    pair_out[0, 1] = q_ref[:, cols(2)]
    send(6, pair_out.at[0], pair_in.at[0], "pair")
    qg_ref[0, z, y] = by_y(q_ref[:, cols(0)], q_ref[:, cols(1)])
    z_own(0)
    c = y * NX + x
    pair_y = 1 - y
    for t, (ref, text) in enumerate(((k_ref, tk_ref), (v_ref, tv_ref))):
        load[2 * t].wait()
        load[2 * t + 1].wait()
        st_pair[t, 0:TR] = by_y(ref[:, cols(1)], ref[:, cols(0)])
        st_pair[t, TR:BR] = by_y(text[:, cols(1)], text[:, cols(0)])
        st_pair[t, SHARED_TEXT:SHARED] = text[:, cols(2)]
        st_pair[t, SHARED:CHUNK] = ref[:, cols(2)]
        if t == 0:
            send(7, st_pair.at[0], kv_ref.at[0, c], "pair")
        kv_ref[t, c, 0:TR] = by_y(ref[:, cols(0)], ref[:, cols(1)])
        kv_ref[t, c, TR:BR] = by_y(text[:, cols(0)], text[:, cols(1)])
        kv_ref[t, c, SHARED_TEXT:SHARED] = text[:, cols(2)]
        x_send(0, t, y)
    send(2, go_hbm, goall.at[head], "core")
    load[7].wait()
    load[8].wait()
    key_side()
    send(0, go_hbm.at[first], go_relay.at[0], "pair")
    pair_rows(0, q_ref[:, cols(2)])
    z_pair(0)
    lax.fori_loop(0, BLOCKS, query_side, 0)
    z_own_forward(0)
    pair_keys(0, k_ref)
    load[5].wait()
    load[6].wait()
    acc[...] = dot_nt(go_ref[...], feature(head))
    x_forward(0, 0, y)
    x_forward(0, 1, y)
    z_pair_forward(0)
    z_own_finish(0)
    z_pair_finish(0)
    take_rows(0, keep_query)
    arrived(0, go_relay.at[0])
    send(3, go_relay.at[0], goall.at[head, first], "back")
    arrived(1, go_relay.at[1])
    send(4, go_relay.at[1], goall.at[other_head, second], "pair")
    x_forward(1, 0, pair_y)
    score(0)
    arrived(2, goall.at[core_head])
    acc[...] += dot_nt(goall[core_head], feature(core_head))
    x_near_finish(0, 0, y)
    x_near_finish(1, 0, pair_y)
    score(1)
    send(8, st_pair.at[1], kv_ref.at[1, c], "pair")
    score(3)
    arrived(3, goall.at[other_head, first])
    arrived(4, goall.at[other_head, second])
    send(5, goall.at[other_head], goall.at[other_head], "core")
    acc[...] += dot_nt(goall[other_head], feature(other_head))
    arrived(5, goall.at[core_other])
    grad = (acc[...] + dot_nt(goall[core_other], feature(core_other))).astype(BF)
    pair_out[1, 0] = by_y(grad[:, cols(1)], grad[:, cols(0)])
    pair_out[1, 1] = grad[:, cols(2)]
    send(9, pair_out.at[1], pair_in.at[1], "pair")
    qg_ref[1, z, y] = by_y(grad[:, cols(0)], grad[:, cols(1)])
    z_own(1)
    x_far_finish(0, 0, y)
    x_far_finish(1, 0, pair_y)
    score(2)
    pair_keys(1, v_ref)
    score_text()
    pair_rows(1, pair_out[1, 1])
    z_pair(1)
    z_own_forward(1)
    x_near_finish(0, 1, y)
    x_far_finish(0, 1, y)
    take_column(1, 0)
    x_forward(1, 1, pair_y)
    x_near_finish(1, 1, pair_y)
    take_column(1, 1)
    take_column(1, 3)
    mix_near()
    z_pair_forward(1)
    x_far_finish(1, 1, pair_y)
    take_column(1, 2)
    mix_far(zf)
    z_far(0)
    mix_far(zu)
    mix_far(zd)
    z_near(0)
    mix_far(z)

    z_own_finish(1)
    z_pair_finish(1)
    take_rows(1, keep_grad)
    key_grads_text(1)
    key_grads(1, 2)
    x_far(1)
    z_relay(0)
    key_grads(1, 3)
    key_grads(1, 1)
    x_near(1)
    slope_text()
    slope(2)
    x_relay(1)
    z_total(0, 1.0)
    key_grads_text(0)
    key_grads(0, 2)
    x_far(0)
    slope(1)
    take_attn(0, attn)
    part[0] = project(core_other)
    rsend(28, part.at[0], core_in.at[0], "core")
    part[2] = project(other_head)
    key_grads(1, 0)
    to_pair(1)
    slope(3)
    rarrived(28, core_in.at[0])
    pair_sum[...] = (wide(part[2]) + wide(core_in[0])).astype(BF)
    rsend(30, pair_sum.at[first], out_relay.at[0], "pair")
    rsend(31, pair_sum.at[second], out_relay.at[1], "back")
    key_grads(0, 1)
    key_grads(0, 3)
    x_relay(0)
    x_near(0)
    for zq in (zf, zu, zd, z):
        slope_row(0, zq)
        finish_dq(zq)
        if zq is zf:
            z_far(1)
        elif zq is zd:
            z_near(1)
    part[1] = project(core_head)
    rsend(29, part.at[1], core_in.at[1], "core")
    part[3] = project(head)
    rarrived(30, out_relay.at[0])
    rsend(32, out_relay.at[0], far_in.at[first], "back")
    rarrived(31, out_relay.at[1])
    rsend(33, out_relay.at[1], far_in.at[second], "pair")
    z_relay(1)
    key_grads(0, 0)
    to_pair(0)
    z_total(1, factor)

    stores = []

    def store(src, dst):
        copy = pltpu.make_async_copy(src, dst, store_sem.at[len(stores)])
        copy.start()
        stores.append(copy)

    results = ((gk_ref, gtk_ref, gk_hbm, gtk_hbm), (gv_ref, gtv_ref, gv_hbm, gtv_hbm))
    rarrived(29, core_in.at[1])
    rarrived(32, far_in.at[first])
    rarrived(33, far_in.at[second])
    out_ref[...] = (wide(part[3]) + wide(core_in[1]) + wide(far_in[...])).astype(BF)
    store(out_ref, out_hbm)
    for t, (ref, text, to, text_to) in enumerate(results):
        own = x_total(t, 0)
        rarrived(26 + t, yk_in.at[t])
        mine, other = own[0:BR].astype(BF), yk_in[t, 0:BR]
        mask = chunk_rows(z, x) >= long_start
        both = by_side(mask, yk_out[t, SHARED:CHUNK], yk_in[t, SHARED:CHUNK])[0]
        for h, value in ((0, by_y(mine, other)), (1, by_y(other, mine))):
            ref[:, cols(h)] = value[0:TR]
            text[:, cols(h)] = value[TR:BR]
        ref[:, cols(2)] = both
        text[:, cols(2)] = (own[BR:SHARED] + wide(yk_in[t, SHARED_TEXT:SHARED])).astype(BF)
        store(ref, to)
        store(text, text_to)
    take_attn(1, gq_ref)
    store(gq_ref, gq_hbm)
    for copy in sent:
        copy.wait_send()
    for copy in stores:
        copy.wait()


def store_kernel(*refs):
    count = (len(refs) - 2) // 3
    held, result, buffers = refs[:count], refs[count : 2 * count], refs[2 * count : 3 * count]
    load_sem, store_sem = refs[-2:]
    loads = [
        pltpu.make_async_copy(held[n], buffers[n], load_sem.at[n]) for n in range(count)
    ]
    stores = [
        pltpu.make_async_copy(buffers[n], result[n], store_sem.at[n]) for n in range(count)
    ]
    for copy in loads:
        copy.start()
    for load, copy in zip(loads, stores):
        load.wait()
        copy.start()
    for copy in stores:
        copy.wait()


def shards(
    queries,
    keys,
    values,
    text_keys,
    text_values,
    head_bias,
    out_weight,
    grad_out,
    clip_lengths,
    tile_mask,
    caption_order,
):
    smem = pl.BlockSpec(memory_space=pltpu.SMEM)
    hbm = pl.BlockSpec(memory_space=pltpu.HBM)
    dma = pltpu.SemaphoreType.DMA
    qg_shape = (2, NZ, NH, TR, HS)
    kv_shape = (2, NY * NX, CHUNK, HS)
    out_cols = grad_out.shape[1]
    order = caption_order.reshape(CLIPS, CAP)
    token = pltpu.VMEM((TR, NH * HS), BF)
    text = pltpu.VMEM((CR, NH * HS), BF)
    wide_out = pltpu.VMEM((TR, out_cols), BF)
    halves = pltpu.VMEM((2, HALF, out_cols), BF)
    token_shape = jax.ShapeDtypeStruct((TR, NH * HS), BF)
    text_shape = jax.ShapeDtypeStruct((CR, NH * HS), BF)
    result = (
        jax.ShapeDtypeStruct((TR, out_cols), BF),
        token_shape,
        token_shape,
        token_shape,
        text_shape,
        text_shape,
    )
    held = pl.pallas_call(
        fused_kernel,
        out_shape=result,
        in_specs=[hbm] * 9 + [smem] * 2,
        out_specs=(hbm,) * len(result),
        scratch_shapes=[
            token,
            token,
            token,
            text,
            text,
            wide_out,
            pltpu.VMEM(out_weight.shape, BF),
            pltpu.VMEM(tile_mask.shape, jnp.int32),
            pltpu.VMEM(order.shape, jnp.int32),
            wide_out,
            token,
            token,
            token,
            text,
            text,
            pltpu.VMEM(qg_shape, BF),
            pltpu.VMEM(kv_shape, BF),
            pltpu.VMEM((2, CHUNK, HS), BF),
            pltpu.VMEM((2, 2, TR, HS), BF),
            pltpu.VMEM((2, 2, TR, HS), BF),
            pltpu.VMEM((4, TR, out_cols), BF),
            halves,
            pltpu.VMEM((TR, NH * HS), F32),
            pltpu.VMEM((NH, SIDE + TEXT, 2 * HS), BF),
            pltpu.VMEM((NH, SIDE + TEXT, HS), BF),
            pltpu.VMEM((BLOCKS, TR, 2 * HS), BF),
            pltpu.VMEM((BLOCKS, TR, HS), BF),
            pltpu.VMEM((BLOCKS * TR, SIDE + TEXT), BF),
            pltpu.VMEM((BLOCKS * TR, SIDE + TEXT), BF),
            pltpu.VMEM((HS, BLOCKS * TR), BF),
            pltpu.VMEM((HS, BLOCKS * TR), BF),
            pltpu.VMEM((BLOCKS, TR, HS), F32),
            pltpu.VMEM((BLOCKS, TR, HS), F32),
            pltpu.VMEM(qg_shape, BF),
            pltpu.VMEM(kv_shape, BF),
            pltpu.VMEM((2, 6, NH, HALF, HS), BF),
            pltpu.VMEM((2, 2, NH, HALF, HS), BF),
            pltpu.VMEM((2, NY, 3, CHUNK, HS), BF),
            pltpu.VMEM((2, NY, CHUNK, HS), BF),
            pltpu.VMEM((2, 2, TR, HS), BF),
            pltpu.VMEM((2, 2, TR, HS), BF),
            pltpu.VMEM((2, CHUNK, HS), BF),
            pltpu.VMEM((2, CHUNK, HS), BF),
            pltpu.VMEM((2, TR, HS), BF),
            token,
            pltpu.VMEM((4, TR, out_cols), BF),
            pltpu.VMEM((2, TR, out_cols), BF),
            wide_out,
            halves,
            wide_out,
            dma((42,)),
            dma((42,)),
            dma((34,)),
            dma((34,)),
            dma((9,)),
            dma((len(result),)),
        ],
        compiler_params=pltpu.CompilerParams(
            collective_id=0, has_side_effects=True, vmem_limit_bytes=VMEM_LIMIT
        ),
    )(
        queries,
        keys,
        values,
        text_keys,
        text_values,
        grad_out,
        out_weight,
        tile_mask,
        order,
        clip_lengths,
        head_bias,
    )
    return pl.pallas_call(
        store_kernel,
        out_shape=result,
        in_specs=[hbm] * len(result),
        out_specs=(hbm,) * len(result),
        scratch_shapes=[pltpu.VMEM(array.shape, array.dtype) for array in result]
        + [dma((len(result),)), dma((len(result),))],
        compiler_params=pltpu.CompilerParams(vmem_limit_bytes=VMEM_LIMIT),
    )(*held)


def solution(mesh):
    in_specs = (
        P("seq", "head"),
        P("seq", "head"),
        P("seq", "head"),
        P("seq", "head"),
        P("seq", "head"),
        P("head"),
        P("head", None),
        P("seq", "head"),
        P(),
        P(),
        P(),
    )
    out_specs = (P("seq", "head"),) * 6
    return jax.shard_map(shards, mesh=mesh, in_specs=in_specs, out_specs=out_specs, check_vma=False)
```

```python
import jax
import jax.numpy as jnp
from jax import lax
from jax.experimental import pallas as pl
from jax.experimental.pallas import tpu as pltpu
from jax.sharding import PartitionSpec as P

MESH = pl.DeviceIdType.MESH
BF = jnp.bfloat16
F32 = jnp.float32

NX, NZ, NY = 4, 4, 2
HS = 128
NH = 3
TR = 256
CR = 16
BR = TR + CR
HALF = TR // 2
CLIPS = 4
CAP = 128
TILE = 64
MASKED = -32768.0
BLOCKS = NH * NZ
SIDE = NX * TR
SHARED_TEXT = BR
SHARED = BR + CR
CHUNK = BR + BR
TEXT = NY * NX * CR
VMEM_LIMIT = 58 * 1024 * 1024


def place():
    seq = lax.axis_index("seq")
    head = lax.axis_index("head")
    y = seq // (NZ * NX)
    z = (seq // NX) % NZ
    x = seq % NX
    return seq, head, y, z, x


def peers(seq, head, y, z, x):
    def at(yy, zz, xx):
        return (yy * NZ + zz) * NX + xx

    other_head = (head + 2) % 4
    core_head = head + 1 - 2 * (head % 2)
    return {
        "pair": (at(1 - y, z, x), head),
        "back": (at(1 - y, z, x), other_head),
        "core": (seq, core_head),
        "right": (at(y, z, (x + 1) % NX), head),
        "left": (at(y, z, (x + NX - 1) % NX), head),
        "up": (at(y, (z + 1) % NZ, x), head),
        "down": (at(y, (z + NZ - 1) % NZ, x), head),
    }


def greet(peer):
    barrier = pltpu.get_barrier_semaphore()
    for device in peer.values():
        pl.semaphore_signal(barrier, inc=1, device_id=device, device_id_type=MESH)
    pl.semaphore_wait(barrier, len(peer))


def sender(peer, send_sem, recv_sem, sent):
    def send(n, src, dst, to):
        copy = pltpu.make_async_remote_copy(
            src_ref=src,
            dst_ref=dst,
            send_sem=send_sem.at[n],
            recv_sem=recv_sem.at[n],
            device_id=peer[to],
            device_id_type=MESH,
        )
        copy.start()
        sent.append(copy)

    def arrived(n, dst):
        pltpu.make_async_remote_copy(
            src_ref=dst,
            dst_ref=dst,
            send_sem=send_sem.at[n],
            recv_sem=recv_sem.at[n],
            device_id=peer["core"],
            device_id_type=MESH,
        ).wait_recv()

    return send, arrived


def dot_nt(a, b):
    return lax.dot_general(a, b, (((1,), (1,)), ((), ())), preferred_element_type=F32)


def dot_nn(a, b):
    return lax.dot_general(a, b, (((1,), (0,)), ((), ())), preferred_element_type=F32)


def fused_kernel(
    q_hbm,
    k_hbm,
    v_hbm,
    tk_hbm,
    tv_hbm,
    go_hbm,
    w_hbm,
    tile_hbm,
    order_hbm,
    len_ref,
    bias_ref,
    out_hbm,
    gq_hbm,
    gk_hbm,
    gv_hbm,
    gtk_hbm,
    gtv_hbm,
    q_ref,
    k_ref,
    v_ref,
    tk_ref,
    tv_ref,
    go_ref,
    w_ref,
    tile_ref,
    order_ref,
    out_ref,
    gq_ref,
    gk_ref,
    gv_ref,
    gtk_ref,
    gtv_ref,
    qg_ref,
    kv_ref,
    st_pair,
    pair_out,
    pair_in,
    goall,
    go_relay,
    acc,
    kaug,
    vals,
    qaug,
    gsel,
    weights,
    slopes,
    queries_t,
    grads_t,
    oacc,
    qacc,
    oq_ref,
    kvg_ref,
    z_in,
    z_sum,
    x_in,
    x_sum,
    yq_out,
    yq_in,
    yk_out,
    yk_in,
    keep_q,
    attn,
    part,
    core_in,
    pair_sum,
    out_relay,
    far_in,
    g_send,
    g_recv,
    r_send,
    r_recv,
    local_sem,
    store_sem,
):
    seq, head, y, z, x = place()
    peer = peers(seq, head, y, z, x)
    zu, zd, zf = (z + 1) % NZ, (z + NZ - 1) % NZ, (z + 2) % NZ
    xr, xl, xf = (x + 1) % NX, (x + NX - 1) % NX, (x + 2) % NX
    other_head = (head + 2) % 4
    core_head = head + 1 - 2 * (head % 2)
    core_other = core_head + 2 - 4 * (core_head // 2)
    first, second = pl.ds(0, HALF), pl.ds(HALF, HALF)
    sent = []
    send, arrived = sender(peer, g_send, g_recv, sent)
    rsend, rarrived = sender(peer, r_send, r_recv, sent)
    cols = lambda h: slice(h * HS, (h + 1) * HS)
    by_y = lambda a, b: jnp.where(y == 0, a, b)
    wide = lambda a: a.astype(F32)
    factor = HS ** (-0.5)

    load = []
    for n, (src, dst) in enumerate(
        (
            (k_hbm, k_ref),
            (tk_hbm, tk_ref),
            (v_hbm, v_ref),
            (tv_hbm, tv_ref),
            (q_hbm, q_ref),
            (go_hbm, go_ref),
            (w_hbm, w_ref),
            (tile_hbm, tile_ref),
            (order_hbm, order_ref),
        )
    ):
        copy = pltpu.make_async_copy(src, dst, local_sem.at[n])
        copy.start()
        load.append(copy)

    greet(peer)


    def chunk_of(a, t, index):
        return kv_ref.at[t, index, pl.ds(0, (SHARED, CHUNK)[a])]

    def x_send(a, t, yy):
        chunk = chunk_of(a, t, yy * NX + x)
        send(10 + 6 * a + 2 * t, chunk, chunk, ("right", "left")[t])
        send(11 + 6 * a + 2 * t, chunk, chunk, ("left", "right")[t])

    def x_forward(a, t, yy):
        base = 10 + 6 * a
        chunk = chunk_of(a, t, yy * NX + (xl, xr)[t])
        arrived(base + 2 * t, chunk)
        send(base + 4 + t, chunk, chunk, ("right", "left")[t])

    def x_near_finish(a, t, yy):
        arrived(10 + 6 * a + 1 + 2 * t, chunk_of(a, t, yy * NX + (xr, xl)[t]))

    def x_far_finish(a, t, yy):
        arrived(10 + 6 * a + 4 + t, chunk_of(a, t, yy * NX + xf))

    def z_pair(t):
        base = 22 + 10 * t
        send(base + 0, qg_ref.at[t, z, 2], qg_ref.at[t, z, 2], "up")
        send(base + 1, qg_ref.at[t, z, 1 - y], qg_ref.at[t, z, 1 - y], "down")
        send(base + 2, qg_ref.at[t, z, 1 - y], qg_ref.at[t, z, 1 - y], "up")
        send(base + 3, qg_ref.at[t, z, 2], qg_ref.at[t, z, 2], "down")

    def z_pair_forward(t):
        base = 22 + 10 * t
        arrived(base + 0, qg_ref.at[t, zd, 2])
        send(base + 4, qg_ref.at[t, zd, 2], qg_ref.at[t, zd, 2], "up")
        arrived(base + 1, qg_ref.at[t, zu, 1 - y])
        send(base + 5, qg_ref.at[t, zu, 1 - y], qg_ref.at[t, zu, 1 - y], "down")

    def z_own(t):
        base = 22 + 10 * t
        send(base + 6, qg_ref.at[t, z, y], qg_ref.at[t, z, y], "up")
        send(base + 7, qg_ref.at[t, z, y], qg_ref.at[t, z, y], "down")

    def z_own_forward(t):
        base = 22 + 10 * t
        arrived(base + 6, qg_ref.at[t, zd, y])
        src = qg_ref.at[t, zd, y, first]
        send(base + 8, src, src, "up")
        arrived(base + 7, qg_ref.at[t, zu, y])
        src = qg_ref.at[t, zu, y, second]
        send(base + 9, src, src, "down")

    def z_pair_finish(t):
        base = 22 + 10 * t
        arrived(base + 2, qg_ref.at[t, zd, 1 - y])
        arrived(base + 3, qg_ref.at[t, zu, 2])
        arrived(base + 4, qg_ref.at[t, zf, 2])
        arrived(base + 5, qg_ref.at[t, zf, 1 - y])

    def z_own_finish(t):
        base = 22 + 10 * t
        arrived(base + 8, qg_ref.at[t, zf, y, first])
        arrived(base + 9, qg_ref.at[t, zf, y, second])

    def pair_rows(t, shared):
        arrived((6, 9)[t], pair_in.at[t])
        qg_ref[t, z, 1 - y] = pair_in[t, 0]
        mask = chunk_rows(z, x) >= long_start
        qg_ref[t, z, 2] = by_side(mask, shared, pair_in[t, 1])[0]

    def pair_keys(t, ref):
        index = (1 - y) * NX + x
        arrived(7 + t, kv_ref.at[t, index])
        mask = chunk_rows(z, x) >= long_start
        rows = pl.ds(SHARED, TR)
        kv_ref[t, index, rows] = by_side(mask, ref[:, cols(2)], kv_ref[t, index, rows])[0]
        x_send(1, t, 1 - y)

    def feature(n):
        return w_ref[:, pl.ds(pl.multiple_of(n * 768, 128), 768)]

    half_rows = NZ * NX * TR
    ends = [len_ref[0]]
    for c in range(1, CLIPS):
        ends.append(ends[-1] + len_ref[c])
    long_start = 0
    for c in range(1, CLIPS):
        long_start = jnp.where(len_ref[c] == half_rows, ends[c - 1], long_start)

    def clip_at(pos):
        total = 0
        for c in range(CLIPS - 1):
            total = total + jnp.where(pos >= ends[c], 1, 0)
        return total

    row_index = lax.broadcasted_iota(jnp.int32, (TR, HS), 0)

    def chunk_rows(zz, xx):
        return (zz * NX + xx) * TR + row_index

    def own_is_long(zz, xx):
        t = chunk_rows(zz, xx)
        return jnp.where(y == 0, t - long_start, long_start - 1 - t) >= 0

    def by_side(mask, mine, other):
        mine, other = wide(mine), wide(other)
        return jnp.where(mask, mine, other).astype(BF), jnp.where(mask, other, mine).astype(BF)

    lane = lax.broadcasted_iota(jnp.int32, (1, HS), 1)
    tiles_here = (lane % 64) // 16 == z
    clip_lane = ((z + 1) % NZ) * 16
    bias_lane = clip_lane + CLIPS
    bias_ones = jnp.where((lane >= bias_lane) & (lane < bias_lane + 3), 1.0, 0.0)

    def kv_index(n):
        return ((y + n % 2) % NY) * NX + (x + n // 2) % NX

    def key_columns(pos):
        hit = (tiles_here & ((pos >> 6) == lane)) | (clip_at(pos) == lane - clip_lane)
        return jnp.where(hit, 1.0, bias_ones).astype(BF)

    def key_side():
        for d in range(NX):
            t = chunk_rows(z, (x + d) % NX)
            rows = slice(d * TR, (d + 1) * TR)
            sides = by_side(t >= long_start, key_columns(t), key_columns(t + half_rows))
            for side, value in enumerate(sides + (by_y(*sides),)):
                kaug[side, rows, HS:] = value
        row = lax.broadcasted_iota(jnp.int32, (TEXT, HS), 0)
        n = row // CR
        plane = ((y + n % 2) % NY) * NZ + z
        text_row = (plane * NX + (x + n // 2) % NX) * CR + row % CR
        aug = jnp.broadcast_to(bias_ones, text_row.shape)
        for c in range(CLIPS):
            listed = jnp.where(order_ref[c : c + 1, :] == text_row, 1.0, 0.0)
            found = jnp.max(listed, axis=1, keepdims=True)
            aug = jnp.where(lane == clip_lane + c, found, aug)
        for g in range(NH):
            kaug[g, SIDE:, HS:] = aug.astype(BF)

    log_len = [
        jnp.log(jnp.full((1, HS), len_ref[c] + CAP, jnp.int32).astype(F32)) for c in range(CLIPS)
    ]

    def query_side(n, carry):
        g, zq = n // NZ, n % NZ
        t = chunk_rows(zq, x)
        side = jnp.where(g == 2, y, g)
        in_high = jnp.where(side == 0, long_start - 1 - t, t - long_start) >= 0
        pos = t + jnp.where(in_high, half_rows, 0)
        head_bias = bias_ref[jnp.where(g == 2, 2, y)]
        clip = clip_at(pos)
        offset = jnp.broadcast_to(log_len[CLIPS - 1], (TR, HS))
        for c in range(CLIPS - 2, -1, -1):
            offset = jnp.where(pos < ends[c], log_len[c], offset)
        total = (head_bias - offset) * (HS**0.5)
        hi = total.astype(BF).astype(F32)
        mid = (total - hi).astype(BF).astype(F32)
        low = total - hi - mid
        in_bias = jnp.where(lane == bias_lane, hi, jnp.where(lane == bias_lane + 1, mid, low))
        in_bias = jnp.where((lane >= bias_lane) & (lane < bias_lane + 3), in_bias, 0.0)
        in_clip = (lane >= clip_lane) & (lane < clip_lane + CLIPS) & (lane - clip_lane != clip)
        side = jnp.where(in_clip, MASKED, in_bias)
        for u in range(TR // TILE):
            rows = slice(u * TILE, (u + 1) * TILE)
            tile = (zq * NX + x) * (TR // TILE) + u
            off = []
            for p in range(NY):
                at = tile + p * (half_rows // TILE)
                mask_row = tile_ref[pl.ds(at, 1), :]
                off.append(jnp.where((mask_row == 0) & (lane != at) & tiles_here, 1.0, 0.0))
            masked = jnp.where(in_high[rows], off[1], off[0]) > 0.5
            qaug[n, rows, HS:] = jnp.where(masked, MASKED, side[rows]).astype(BF)
        return carry

    def keep_query(n, value):
        qaug[n, :, 0:HS] = value
        queries_t[:, n * TR : (n + 1) * TR] = value.T

    def keep_grad(n, value):
        gsel[n] = value
        grads_t[:, n * TR : (n + 1) * TR] = value.T

    def take_rows(t, keep):
        for zq in range(NZ):
            mask = own_is_long(zq, x)
            sides = by_side(mask, qg_ref[t, zq, y], qg_ref[t, zq, 1 - y])
            for g, value in enumerate(sides + (qg_ref[t, zq, 2],)):
                keep(g * NZ + zq, value)

    def take_column(t, d):
        lanes = slice(0, HS)
        ref = (kaug, vals)[t]
        mask = own_is_long(z, (x + d) % NX)
        mine, other = kv_index(2 * d), kv_index(2 * d + 1)
        sides = by_side(mask, kv_ref[t, mine, 0:TR], kv_ref[t, other, 0:TR])
        for g, value in enumerate(sides + (kv_ref[t, other, SHARED:CHUNK],)):
            ref[g, d * TR : (d + 1) * TR, lanes] = value
        for r in range(2):
            index = kv_index(2 * d + r)
            rows = slice(SIDE + (2 * d + r) * CR, SIDE + (2 * d + r + 1) * CR)
            for g in range(NH):
                low = SHARED_TEXT if g == 2 else TR
                ref[g, rows, lanes] = kv_ref[t, index, low : low + CR]

    def block_rows(n):
        return pl.ds(pl.multiple_of(n * TR, TR), TR)

    def weigh(block, columns):
        scores = dot_nt(qaug[block], kaug[block // NZ, columns, :])
        half = jnp.tanh(scores * (0.5 * factor))
        twice = 1.0 + half
        weights[block_rows(block), columns] = twice.astype(BF)
        slopes[block_rows(block), columns] = (twice * (1.0 - half)).astype(BF)

    def every_block(body):
        def step(zq, carry):
            for g in range(NH):
                body(g * NZ + zq)
            return carry

        lax.fori_loop(0, NZ, step, 0)

    def column(d):
        return slice(d * TR, (d + 1) * TR)

    text_columns = slice(SIDE, SIDE + TEXT)

    def score(d):
        take_column(0, d)
        every_block(lambda block: weigh(block, column(d)))

    def score_text():
        every_block(lambda block: weigh(block, text_columns))

    def mix(block, columns):
        return dot_nn(weights[block_rows(block), columns], vals[block // NZ, columns, :])

    def mix_near():
        def body(block):
            oacc[block] = mix(block, slice(0, 2 * TR)) + mix(block, column(3))

        every_block(body)

    def mix_far(zq):
        totals = []
        for g in range(NH):
            block = g * NZ + zq
            total = oacc[block] + mix(block, column(2)) + mix(block, text_columns)
            totals.append(total * 0.5)
        mine, other = by_side(own_is_long(zq, x), totals[0], totals[1])
        oq_ref[0, zq, y] = mine
        oq_ref[0, zq, 1 - y] = other
        oq_ref[0, zq, 2] = totals[2].astype(BF)

    def slope_step(block, columns, fresh=False):
        rows, g = block_rows(block), block // NZ
        slope = (dot_nt(gsel[block], vals[g, columns, :]) * wide(slopes[rows, columns])).astype(BF)
        slopes[rows, columns] = slope
        share = dot_nn(slope, kaug[g, columns, 0:HS])
        if fresh:
            qacc[block] = share
        else:
            qacc[block] += share

    def slope(d):
        every_block(lambda block: slope_step(block, column(d)))

    def slope_text():
        every_block(lambda block: slope_step(block, text_columns, True))

    def slope_row(d, zq):
        for g in range(NH):
            slope_step(g * NZ + zq, column(d))

    def finish_dq(zq):
        mine, other = by_side(own_is_long(zq, x), qacc[zq] * 0.25, qacc[NZ + zq] * 0.25)
        oq_ref[1, zq, y] = mine
        oq_ref[1, zq, 1 - y] = other
        oq_ref[1, zq, 2] = (qacc[2 * NZ + zq] * 0.25).astype(BF)

    left_of = (queries_t, grads_t)
    scale_of = (0.25, 0.5)

    def key_grads(t, d):
        sides = []
        for g in range(NH):
            rows = slice(g * SIDE, (g + 1) * SIDE)
            total = dot_nn(left_of[t][:, rows], (slopes, weights)[t][rows, column(d)])
            sides.append((total * scale_of[t]).astype(BF).T)
        mine, other = by_side(own_is_long(z, (x + d) % NX), sides[0], sides[1])
        kvg_ref[t, kv_index(2 * d), 0:TR] = mine
        kvg_ref[t, kv_index(2 * d + 1), 0:TR] = other
        kvg_ref[t, kv_index(2 * d + 1), SHARED:CHUNK] = sides[2]

    def key_grads_text(t):
        for low, high, at in ((0, 2 * SIDE, TR), (2 * SIDE, 3 * SIDE, SHARED_TEXT)):
            right = (slopes, weights)[t][low:high, text_columns]
            text_rows = (dot_nn(left_of[t][:, low:high], right) * scale_of[t]).astype(BF).T
            for n in range(NY * NX):
                kvg_ref[t, kv_index(n), at : at + CR] = text_rows[n * CR : (n + 1) * CR]


    def z_far(t):
        rsend(6 * t + 0, oq_ref.at[t, zf, :, first], z_in.at[t, 0], "up")
        rsend(6 * t + 3, oq_ref.at[t, zf, :, second], z_in.at[t, 3], "down")

    def z_near(t):
        rsend(6 * t + 1, oq_ref.at[t, zd, :, first], z_in.at[t, 1], "down")
        rsend(6 * t + 4, oq_ref.at[t, zu, :, second], z_in.at[t, 4], "up")

    def z_relay(t):
        base = 6 * t
        rarrived(base + 0, z_in.at[t, 0])
        z_sum[t, 0] = (wide(z_in[t, 0]) + wide(oq_ref[t, zu, :, first])).astype(BF)
        rsend(base + 2, z_sum.at[t, 0], z_in.at[t, 2], "up")
        rarrived(base + 3, z_in.at[t, 3])
        z_sum[t, 1] = (wide(z_in[t, 3]) + wide(oq_ref[t, zd, :, second])).astype(BF)
        rsend(base + 5, z_sum.at[t, 1], z_in.at[t, 5], "down")

    def z_total(t, scale):
        base = 6 * t
        for n in (1, 2, 4, 5):
            rarrived(base + n, z_in.at[t, n])
        for rows, one, two in ((first, 1, 2), (second, 4, 5)):

            def total(j):
                value = wide(oq_ref[t, z, j, rows]) + wide(z_in[t, one, j]) + wide(z_in[t, two, j])
                return (value * scale).astype(BF) if scale != 1.0 else value.astype(BF)

            yq_out[t, 0, rows] = total(1 - y)
            yq_out[t, 1, rows] = total(2)
            keep_q[t, rows] = total(y)
        rsend(24 + t, yq_out.at[t], yq_in.at[t], "pair")

    def x_base(t, a):
        return 12 + 6 * t + 3 * a

    ring = (("right", "left"), ("left", "right"))
    ahead = ((xr, xl), (xl, xr))
    plane = (y, 1 - y)

    def sums_of(a):
        return pl.ds(0, (SHARED, CHUNK)[a])

    def x_far(t):
        for a in (1, 0):
            src = kvg_ref.at[t, plane[a] * NX + xf, sums_of(a)]
            rsend(x_base(t, a), src, x_in.at[t, a, 0, sums_of(a)], ring[a][0])

    def x_near(t):
        for a in (1, 0):
            src = kvg_ref.at[t, plane[a] * NX + ahead[a][1], sums_of(a)]
            rsend(x_base(t, a) + 1, src, x_in.at[t, a, 1, sums_of(a)], ring[a][1])

    def x_relay(t):
        for a in (1, 0):
            rows = sums_of(a)
            rarrived(x_base(t, a), x_in.at[t, a, 0, rows])
            mine = wide(kvg_ref[t, plane[a] * NX + ahead[a][0], rows])
            x_sum[t, a, rows] = (wide(x_in[t, a, 0, rows]) + mine).astype(BF)
            rsend(x_base(t, a) + 2, x_sum.at[t, a, rows], x_in.at[t, a, 2, rows], ring[a][0])

    def to_pair(t):
        yk_out[t] = x_total(t, 1).astype(BF)
        rsend(26 + t, yk_out.at[t], yk_in.at[t], "pair")

    def x_total(t, a):
        rows = sums_of(a)
        rarrived(x_base(t, a) + 1, x_in.at[t, a, 1, rows])
        rarrived(x_base(t, a) + 2, x_in.at[t, a, 2, rows])
        value = wide(kvg_ref[t, plane[a] * NX + x, rows])
        value = value + wide(x_in[t, a, 1, rows]) + wide(x_in[t, a, 2, rows])
        return value * factor if t == 0 else value

    def take_attn(t, ref):
        rarrived(24 + t, yq_in.at[t])
        ref[:, cols(0)] = by_y(keep_q[t], yq_in[t, 0])
        ref[:, cols(1)] = by_y(yq_in[t, 0], keep_q[t])
        mask = chunk_rows(z, x) >= long_start
        ref[:, cols(2)] = by_side(mask, yq_out[t, 1], yq_in[t, 1])[0]

    def project(n):
        return dot_nn(attn[...], feature(n)).astype(BF)

    send(1, go_hbm.at[second], go_relay.at[1], "back")
    load[4].wait()
    pair_out[0, 0] = by_y(q_ref[:, cols(1)], q_ref[:, cols(0)])
    pair_out[0, 1] = q_ref[:, cols(2)]
    send(6, pair_out.at[0], pair_in.at[0], "pair")
    qg_ref[0, z, y] = by_y(q_ref[:, cols(0)], q_ref[:, cols(1)])
    z_own(0)
    c = y * NX + x
    pair_y = 1 - y
    for t, (ref, text) in enumerate(((k_ref, tk_ref), (v_ref, tv_ref))):
        load[2 * t].wait()
        load[2 * t + 1].wait()
        st_pair[t, 0:TR] = by_y(ref[:, cols(1)], ref[:, cols(0)])
        st_pair[t, TR:BR] = by_y(text[:, cols(1)], text[:, cols(0)])
        st_pair[t, SHARED_TEXT:SHARED] = text[:, cols(2)]
        st_pair[t, SHARED:CHUNK] = ref[:, cols(2)]
        if t == 0:
            send(7, st_pair.at[0], kv_ref.at[0, c], "pair")
        kv_ref[t, c, 0:TR] = by_y(ref[:, cols(0)], ref[:, cols(1)])
        kv_ref[t, c, TR:BR] = by_y(text[:, cols(0)], text[:, cols(1)])
        kv_ref[t, c, SHARED_TEXT:SHARED] = text[:, cols(2)]
        x_send(0, t, y)
    send(2, go_hbm, goall.at[head], "core")
    load[7].wait()
    load[8].wait()
    key_side()
    send(0, go_hbm.at[first], go_relay.at[0], "pair")
    pair_rows(0, q_ref[:, cols(2)])
    z_pair(0)
    lax.fori_loop(0, BLOCKS, query_side, 0)
    z_own_forward(0)
    pair_keys(0, k_ref)
    load[5].wait()
    load[6].wait()
    acc[...] = dot_nt(go_ref[...], feature(head))
    x_forward(0, 0, y)
    x_forward(0, 1, y)
    z_pair_forward(0)
    z_own_finish(0)
    z_pair_finish(0)
    take_rows(0, keep_query)
    arrived(0, go_relay.at[0])
    send(3, go_relay.at[0], goall.at[head, first], "back")
    arrived(1, go_relay.at[1])
    send(4, go_relay.at[1], goall.at[other_head, second], "pair")
    x_forward(1, 0, pair_y)
    score(0)
    arrived(2, goall.at[core_head])
    acc[...] += dot_nt(goall[core_head], feature(core_head))
    x_near_finish(0, 0, y)
    x_near_finish(1, 0, pair_y)
    score(1)
    send(8, st_pair.at[1], kv_ref.at[1, c], "pair")
    score(3)
    arrived(3, goall.at[other_head, first])
    arrived(4, goall.at[other_head, second])
    send(5, goall.at[other_head], goall.at[other_head], "core")
    acc[...] += dot_nt(goall[other_head], feature(other_head))
    arrived(5, goall.at[core_other])
    grad = (acc[...] + dot_nt(goall[core_other], feature(core_other))).astype(BF)
    pair_out[1, 0] = by_y(grad[:, cols(1)], grad[:, cols(0)])
    pair_out[1, 1] = grad[:, cols(2)]
    send(9, pair_out.at[1], pair_in.at[1], "pair")
    qg_ref[1, z, y] = by_y(grad[:, cols(0)], grad[:, cols(1)])
    z_own(1)
    x_far_finish(0, 0, y)
    x_far_finish(1, 0, pair_y)
    score(2)
    pair_keys(1, v_ref)
    score_text()
    pair_rows(1, pair_out[1, 1])
    z_pair(1)
    z_own_forward(1)
    x_near_finish(0, 1, y)
    x_far_finish(0, 1, y)
    take_column(1, 0)
    x_forward(1, 1, pair_y)
    x_near_finish(1, 1, pair_y)
    take_column(1, 1)
    take_column(1, 3)
    mix_near()
    z_pair_forward(1)
    x_far_finish(1, 1, pair_y)
    take_column(1, 2)
    mix_far(zf)
    z_far(0)
    mix_far(zu)
    mix_far(zd)
    z_near(0)
    mix_far(z)

    z_own_finish(1)
    z_pair_finish(1)
    take_rows(1, keep_grad)
    key_grads_text(1)
    key_grads(1, 2)
    x_far(1)
    z_relay(0)
    key_grads(1, 3)
    key_grads(1, 1)
    x_near(1)
    slope_text()
    z_total(0, 1.0)
    slope(2)
    x_relay(1)
    key_grads_text(0)
    key_grads(0, 2)
    x_far(0)
    key_grads(1, 0)
    take_attn(0, attn)
    part[0] = project(core_other)
    rsend(28, part.at[0], core_in.at[0], "core")
    part[2] = project(other_head)
    to_pair(1)
    slope(1)
    rarrived(28, core_in.at[0])
    pair_sum[...] = (wide(part[2]) + wide(core_in[0])).astype(BF)
    rsend(30, pair_sum.at[first], out_relay.at[0], "pair")
    rsend(31, pair_sum.at[second], out_relay.at[1], "back")
    slope(3)
    for zq in (zf, zu, zd, z):
        slope_row(0, zq)
        finish_dq(zq)
        if zq is zf:
            z_far(1)
        elif zq is zd:
            z_near(1)
    key_grads(0, 1)
    key_grads(0, 3)
    x_relay(0)
    x_near(0)
    part[1] = project(core_head)
    rsend(29, part.at[1], core_in.at[1], "core")
    rarrived(30, out_relay.at[0])
    rsend(32, out_relay.at[0], far_in.at[first], "back")
    rarrived(31, out_relay.at[1])
    rsend(33, out_relay.at[1], far_in.at[second], "pair")
    z_relay(1)
    key_grads(0, 0)
    part[3] = project(head)
    z_total(1, factor)
    to_pair(0)

    stores = []

    def store(src, dst):
        copy = pltpu.make_async_copy(src, dst, store_sem.at[len(stores)])
        copy.start()
        stores.append(copy)

    results = ((gk_ref, gtk_ref, gk_hbm, gtk_hbm), (gv_ref, gtv_ref, gv_hbm, gtv_hbm))
    rarrived(29, core_in.at[1])
    rarrived(32, far_in.at[first])
    rarrived(33, far_in.at[second])
    out_ref[...] = (wide(part[3]) + wide(core_in[1]) + wide(far_in[...])).astype(BF)
    store(out_ref, out_hbm)
    for t, (ref, text, to, text_to) in enumerate(results):
        own = x_total(t, 0)
        rarrived(26 + t, yk_in.at[t])
        mine, other = own[0:BR].astype(BF), yk_in[t, 0:BR]
        mask = chunk_rows(z, x) >= long_start
        both = by_side(mask, yk_out[t, SHARED:CHUNK], yk_in[t, SHARED:CHUNK])[0]
        for h, value in ((0, by_y(mine, other)), (1, by_y(other, mine))):
            ref[:, cols(h)] = value[0:TR]
            text[:, cols(h)] = value[TR:BR]
        ref[:, cols(2)] = both
        text[:, cols(2)] = (own[BR:SHARED] + wide(yk_in[t, SHARED_TEXT:SHARED])).astype(BF)
        store(ref, to)
        store(text, text_to)
    take_attn(1, gq_ref)
    store(gq_ref, gq_hbm)
    for copy in sent:
        copy.wait_send()
    for copy in stores:
        copy.wait()


def store_kernel(*refs):
    count = (len(refs) - 2) // 3
    held, result, buffers = refs[:count], refs[count : 2 * count], refs[2 * count : 3 * count]
    load_sem, store_sem = refs[-2:]
    loads = [
        pltpu.make_async_copy(held[n], buffers[n], load_sem.at[n]) for n in range(count)
    ]
    stores = [
        pltpu.make_async_copy(buffers[n], result[n], store_sem.at[n]) for n in range(count)
    ]
    for copy in loads:
        copy.start()
    for load, copy in zip(loads, stores):
        load.wait()
        copy.start()
    for copy in stores:
        copy.wait()


def shards(
    queries,
    keys,
    values,
    text_keys,
    text_values,
    head_bias,
    out_weight,
    grad_out,
    clip_lengths,
    tile_mask,
    caption_order,
):
    smem = pl.BlockSpec(memory_space=pltpu.SMEM)
    hbm = pl.BlockSpec(memory_space=pltpu.HBM)
    dma = pltpu.SemaphoreType.DMA
    qg_shape = (2, NZ, NH, TR, HS)
    kv_shape = (2, NY * NX, CHUNK, HS)
    out_cols = grad_out.shape[1]
    order = caption_order.reshape(CLIPS, CAP)
    token = pltpu.VMEM((TR, NH * HS), BF)
    text = pltpu.VMEM((CR, NH * HS), BF)
    wide_out = pltpu.VMEM((TR, out_cols), BF)
    halves = pltpu.VMEM((2, HALF, out_cols), BF)
    token_shape = jax.ShapeDtypeStruct((TR, NH * HS), BF)
    text_shape = jax.ShapeDtypeStruct((CR, NH * HS), BF)
    result = (
        jax.ShapeDtypeStruct((TR, out_cols), BF),
        token_shape,
        token_shape,
        token_shape,
        text_shape,
        text_shape,
    )
    held = pl.pallas_call(
        fused_kernel,
        out_shape=result,
        in_specs=[hbm] * 9 + [smem] * 2,
        out_specs=(hbm,) * len(result),
        scratch_shapes=[
            token,
            token,
            token,
            text,
            text,
            wide_out,
            pltpu.VMEM(out_weight.shape, BF),
            pltpu.VMEM(tile_mask.shape, jnp.int32),
            pltpu.VMEM(order.shape, jnp.int32),
            wide_out,
            token,
            token,
            token,
            text,
            text,
            pltpu.VMEM(qg_shape, BF),
            pltpu.VMEM(kv_shape, BF),
            pltpu.VMEM((2, CHUNK, HS), BF),
            pltpu.VMEM((2, 2, TR, HS), BF),
            pltpu.VMEM((2, 2, TR, HS), BF),
            pltpu.VMEM((4, TR, out_cols), BF),
            halves,
            pltpu.VMEM((TR, NH * HS), F32),
            pltpu.VMEM((NH, SIDE + TEXT, 2 * HS), BF),
            pltpu.VMEM((NH, SIDE + TEXT, HS), BF),
            pltpu.VMEM((BLOCKS, TR, 2 * HS), BF),
            pltpu.VMEM((BLOCKS, TR, HS), BF),
            pltpu.VMEM((BLOCKS * TR, SIDE + TEXT), BF),
            pltpu.VMEM((BLOCKS * TR, SIDE + TEXT), BF),
            pltpu.VMEM((HS, BLOCKS * TR), BF),
            pltpu.VMEM((HS, BLOCKS * TR), BF),
            pltpu.VMEM((BLOCKS, TR, HS), F32),
            pltpu.VMEM((BLOCKS, TR, HS), F32),
            pltpu.VMEM(qg_shape, BF),
            pltpu.VMEM(kv_shape, BF),
            pltpu.VMEM((2, 6, NH, HALF, HS), BF),
            pltpu.VMEM((2, 2, NH, HALF, HS), BF),
            pltpu.VMEM((2, NY, 3, CHUNK, HS), BF),
            pltpu.VMEM((2, NY, CHUNK, HS), BF),
            pltpu.VMEM((2, 2, TR, HS), BF),
            pltpu.VMEM((2, 2, TR, HS), BF),
            pltpu.VMEM((2, CHUNK, HS), BF),
            pltpu.VMEM((2, CHUNK, HS), BF),
            pltpu.VMEM((2, TR, HS), BF),
            token,
            pltpu.VMEM((4, TR, out_cols), BF),
            pltpu.VMEM((2, TR, out_cols), BF),
            wide_out,
            halves,
            wide_out,
            dma((42,)),
            dma((42,)),
            dma((34,)),
            dma((34,)),
            dma((9,)),
            dma((len(result),)),
        ],
        compiler_params=pltpu.CompilerParams(
            collective_id=0, has_side_effects=True, vmem_limit_bytes=VMEM_LIMIT
        ),
    )(
        queries,
        keys,
        values,
        text_keys,
        text_values,
        grad_out,
        out_weight,
        tile_mask,
        order,
        clip_lengths,
        head_bias,
    )
    return pl.pallas_call(
        store_kernel,
        out_shape=result,
        in_specs=[hbm] * len(result),
        out_specs=(hbm,) * len(result),
        scratch_shapes=[pltpu.VMEM(array.shape, array.dtype) for array in result]
        + [dma((len(result),)), dma((len(result),))],
        compiler_params=pltpu.CompilerParams(vmem_limit_bytes=VMEM_LIMIT),
    )(*held)


def solution(mesh):
    in_specs = (
        P("seq", "head"),
        P("seq", "head"),
        P("seq", "head"),
        P("seq", "head"),
        P("seq", "head"),
        P("head"),
        P("head", None),
        P("seq", "head"),
        P(),
        P(),
        P(),
    )
    out_specs = (P("seq", "head"),) * 6
    return jax.shard_map(shards, mesh=mesh, in_specs=in_specs, out_specs=out_specs, check_vma=False)
```

```python
import jax
import jax.numpy as jnp
from jax import lax
from jax.experimental import pallas as pl
from jax.experimental.pallas import tpu as pltpu
from jax.sharding import PartitionSpec as P

MESH = pl.DeviceIdType.MESH
BF = jnp.bfloat16
F32 = jnp.float32

NX, NZ, NY = 4, 4, 2
HS = 128
NH = 3
TR = 256
CR = 16
BR = TR + CR
HALF = TR // 2
CLIPS = 4
CAP = 128
TILE = 64
MASKED = -32768.0
BLOCKS = NH * NZ
SIDE = NX * TR
SHARED_TEXT = BR
SHARED = BR + CR
CHUNK = BR + BR
TEXT = NY * NX * CR
VMEM_LIMIT = 58 * 1024 * 1024


def place():
    seq = lax.axis_index("seq")
    head = lax.axis_index("head")
    y = seq // (NZ * NX)
    z = (seq // NX) % NZ
    x = seq % NX
    return seq, head, y, z, x


def peers(seq, head, y, z, x):
    def at(yy, zz, xx):
        return (yy * NZ + zz) * NX + xx

    other_head = (head + 2) % 4
    core_head = head + 1 - 2 * (head % 2)
    return {
        "pair": (at(1 - y, z, x), head),
        "back": (at(1 - y, z, x), other_head),
        "core": (seq, core_head),
        "right": (at(y, z, (x + 1) % NX), head),
        "left": (at(y, z, (x + NX - 1) % NX), head),
        "up": (at(y, (z + 1) % NZ, x), head),
        "down": (at(y, (z + NZ - 1) % NZ, x), head),
    }


def greet(peer):
    barrier = pltpu.get_barrier_semaphore()
    for device in peer.values():
        pl.semaphore_signal(barrier, inc=1, device_id=device, device_id_type=MESH)
    pl.semaphore_wait(barrier, len(peer))


def sender(peer, send_sem, recv_sem, sent):
    def send(n, src, dst, to):
        copy = pltpu.make_async_remote_copy(
            src_ref=src,
            dst_ref=dst,
            send_sem=send_sem.at[n],
            recv_sem=recv_sem.at[n],
            device_id=peer[to],
            device_id_type=MESH,
        )
        copy.start()
        sent.append(copy)

    def arrived(n, dst):
        pltpu.make_async_remote_copy(
            src_ref=dst,
            dst_ref=dst,
            send_sem=send_sem.at[n],
            recv_sem=recv_sem.at[n],
            device_id=peer["core"],
            device_id_type=MESH,
        ).wait_recv()

    return send, arrived


def dot_nt(a, b):
    return lax.dot_general(a, b, (((1,), (1,)), ((), ())), preferred_element_type=F32)


def dot_nn(a, b):
    return lax.dot_general(a, b, (((1,), (0,)), ((), ())), preferred_element_type=F32)


def fused_kernel(
    q_hbm,
    k_hbm,
    v_hbm,
    tk_hbm,
    tv_hbm,
    go_hbm,
    w_hbm,
    tile_hbm,
    order_hbm,
    len_ref,
    bias_ref,
    out_hbm,
    gq_hbm,
    gk_hbm,
    gv_hbm,
    gtk_hbm,
    gtv_hbm,
    q_ref,
    k_ref,
    v_ref,
    tk_ref,
    tv_ref,
    go_ref,
    w_ref,
    tile_ref,
    order_ref,
    out_ref,
    gq_ref,
    gk_ref,
    gv_ref,
    gtk_ref,
    gtv_ref,
    qg_ref,
    kv_ref,
    st_pair,
    pair_out,
    pair_in,
    goall,
    go_relay,
    acc,
    kaug,
    vals,
    qaug,
    gsel,
    weights,
    slopes,
    queries_t,
    grads_t,
    oacc,
    qacc,
    oq_ref,
    kvg_ref,
    z_in,
    z_sum,
    x_in,
    x_sum,
    yq_out,
    yq_in,
    yk_out,
    yk_in,
    keep_q,
    attn,
    part,
    core_in,
    pair_sum,
    out_relay,
    far_in,
    g_send,
    g_recv,
    r_send,
    r_recv,
    local_sem,
    store_sem,
):
    seq, head, y, z, x = place()
    peer = peers(seq, head, y, z, x)
    zu, zd, zf = (z + 1) % NZ, (z + NZ - 1) % NZ, (z + 2) % NZ
    xr, xl, xf = (x + 1) % NX, (x + NX - 1) % NX, (x + 2) % NX
    other_head = (head + 2) % 4
    core_head = head + 1 - 2 * (head % 2)
    core_other = core_head + 2 - 4 * (core_head // 2)
    first, second = pl.ds(0, HALF), pl.ds(HALF, HALF)
    sent = []
    send, arrived = sender(peer, g_send, g_recv, sent)
    rsend, rarrived = sender(peer, r_send, r_recv, sent)
    cols = lambda h: slice(h * HS, (h + 1) * HS)
    by_y = lambda a, b: jnp.where(y == 0, a, b)
    wide = lambda a: a.astype(F32)
    factor = HS ** (-0.5)

    load = []
    for n, (src, dst) in enumerate(
        (
            (k_hbm, k_ref),
            (tk_hbm, tk_ref),
            (v_hbm, v_ref),
            (tv_hbm, tv_ref),
            (q_hbm, q_ref),
            (go_hbm, go_ref),
            (w_hbm, w_ref),
            (tile_hbm, tile_ref),
            (order_hbm, order_ref),
        )
    ):
        copy = pltpu.make_async_copy(src, dst, local_sem.at[n])
        copy.start()
        load.append(copy)

    greet(peer)


    def chunk_of(a, t, index):
        return kv_ref.at[t, index, pl.ds(0, (SHARED, CHUNK)[a])]

    def x_send(a, t, yy):
        chunk = chunk_of(a, t, yy * NX + x)
        send(10 + 6 * a + 2 * t, chunk, chunk, ("right", "left")[t])
        send(11 + 6 * a + 2 * t, chunk, chunk, ("left", "right")[t])

    def x_forward(a, t, yy):
        base = 10 + 6 * a
        chunk = chunk_of(a, t, yy * NX + (xl, xr)[t])
        arrived(base + 2 * t, chunk)
        send(base + 4 + t, chunk, chunk, ("right", "left")[t])

    def x_near_finish(a, t, yy):
        arrived(10 + 6 * a + 1 + 2 * t, chunk_of(a, t, yy * NX + (xr, xl)[t]))

    def x_far_finish(a, t, yy):
        arrived(10 + 6 * a + 4 + t, chunk_of(a, t, yy * NX + xf))

    def z_pair(t):
        base = 22 + 10 * t
        send(base + 0, qg_ref.at[t, z, 2], qg_ref.at[t, z, 2], "up")
        send(base + 1, qg_ref.at[t, z, 1 - y], qg_ref.at[t, z, 1 - y], "down")
        send(base + 2, qg_ref.at[t, z, 1 - y], qg_ref.at[t, z, 1 - y], "up")
        send(base + 3, qg_ref.at[t, z, 2], qg_ref.at[t, z, 2], "down")

    def z_pair_forward(t):
        base = 22 + 10 * t
        arrived(base + 0, qg_ref.at[t, zd, 2])
        send(base + 4, qg_ref.at[t, zd, 2], qg_ref.at[t, zd, 2], "up")
        arrived(base + 1, qg_ref.at[t, zu, 1 - y])
        send(base + 5, qg_ref.at[t, zu, 1 - y], qg_ref.at[t, zu, 1 - y], "down")

    def z_own(t):
        base = 22 + 10 * t
        send(base + 6, qg_ref.at[t, z, y], qg_ref.at[t, z, y], "up")
        send(base + 7, qg_ref.at[t, z, y], qg_ref.at[t, z, y], "down")

    def z_own_forward(t):
        base = 22 + 10 * t
        arrived(base + 6, qg_ref.at[t, zd, y])
        src = qg_ref.at[t, zd, y, first]
        send(base + 8, src, src, "up")
        arrived(base + 7, qg_ref.at[t, zu, y])
        src = qg_ref.at[t, zu, y, second]
        send(base + 9, src, src, "down")

    def z_pair_finish(t):
        base = 22 + 10 * t
        arrived(base + 2, qg_ref.at[t, zd, 1 - y])
        arrived(base + 3, qg_ref.at[t, zu, 2])
        arrived(base + 4, qg_ref.at[t, zf, 2])
        arrived(base + 5, qg_ref.at[t, zf, 1 - y])

    def z_own_finish(t):
        base = 22 + 10 * t
        arrived(base + 8, qg_ref.at[t, zf, y, first])
        arrived(base + 9, qg_ref.at[t, zf, y, second])

    def pair_rows(t, shared):
        arrived((6, 9)[t], pair_in.at[t])
        qg_ref[t, z, 1 - y] = pair_in[t, 0]
        mask = chunk_rows(z, x) >= long_start
        qg_ref[t, z, 2] = by_side(mask, shared, pair_in[t, 1])[0]

    def pair_keys(t, ref):
        index = (1 - y) * NX + x
        arrived(7 + t, kv_ref.at[t, index])
        mask = chunk_rows(z, x) >= long_start
        rows = pl.ds(SHARED, TR)
        kv_ref[t, index, rows] = by_side(mask, ref[:, cols(2)], kv_ref[t, index, rows])[0]
        x_send(1, t, 1 - y)

    def feature(n):
        return w_ref[:, pl.ds(pl.multiple_of(n * 768, 128), 768)]

    half_rows = NZ * NX * TR
    ends = [len_ref[0]]
    for c in range(1, CLIPS):
        ends.append(ends[-1] + len_ref[c])
    long_start = 0
    for c in range(1, CLIPS):
        long_start = jnp.where(len_ref[c] == half_rows, ends[c - 1], long_start)

    def clip_at(pos):
        total = 0
        for c in range(CLIPS - 1):
            total = total + jnp.where(pos >= ends[c], 1, 0)
        return total

    row_index = lax.broadcasted_iota(jnp.int32, (TR, HS), 0)

    def chunk_rows(zz, xx):
        return (zz * NX + xx) * TR + row_index

    def own_is_long(zz, xx):
        t = chunk_rows(zz, xx)
        return jnp.where(y == 0, t - long_start, long_start - 1 - t) >= 0

    def by_side(mask, mine, other):
        mine, other = wide(mine), wide(other)
        return jnp.where(mask, mine, other).astype(BF), jnp.where(mask, other, mine).astype(BF)

    lane = lax.broadcasted_iota(jnp.int32, (1, HS), 1)
    tiles_here = (lane % 64) // 16 == z
    clip_lane = ((z + 1) % NZ) * 16
    bias_lane = clip_lane + CLIPS
    bias_ones = jnp.where((lane >= bias_lane) & (lane < bias_lane + 3), 1.0, 0.0)

    def kv_index(n):
        return ((y + n % 2) % NY) * NX + (x + n // 2) % NX

    def key_columns(pos):
        hit = (tiles_here & ((pos >> 6) == lane)) | (clip_at(pos) == lane - clip_lane)
        return jnp.where(hit, 1.0, bias_ones).astype(BF)

    def key_side():
        for d in range(NX):
            t = chunk_rows(z, (x + d) % NX)
            rows = slice(d * TR, (d + 1) * TR)
            sides = by_side(t >= long_start, key_columns(t), key_columns(t + half_rows))
            for side, value in enumerate(sides + (by_y(*sides),)):
                kaug[side, rows, HS:] = value
        row = lax.broadcasted_iota(jnp.int32, (TEXT, HS), 0)
        n = row // CR
        plane = ((y + n % 2) % NY) * NZ + z
        text_row = (plane * NX + (x + n // 2) % NX) * CR + row % CR
        aug = jnp.broadcast_to(bias_ones, text_row.shape)
        for c in range(CLIPS):
            listed = jnp.where(order_ref[c : c + 1, :] == text_row, 1.0, 0.0)
            found = jnp.max(listed, axis=1, keepdims=True)
            aug = jnp.where(lane == clip_lane + c, found, aug)
        for g in range(NH):
            kaug[g, SIDE:, HS:] = aug.astype(BF)

    log_len = [
        jnp.log(jnp.full((1, HS), len_ref[c] + CAP, jnp.int32).astype(F32)) for c in range(CLIPS)
    ]

    def query_side(n, carry):
        g, zq = n // NZ, n % NZ
        t = chunk_rows(zq, x)
        side = jnp.where(g == 2, y, g)
        in_high = jnp.where(side == 0, long_start - 1 - t, t - long_start) >= 0
        pos = t + jnp.where(in_high, half_rows, 0)
        head_bias = bias_ref[jnp.where(g == 2, 2, y)]
        clip = clip_at(pos)
        offset = jnp.broadcast_to(log_len[CLIPS - 1], (TR, HS))
        for c in range(CLIPS - 2, -1, -1):
            offset = jnp.where(pos < ends[c], log_len[c], offset)
        total = (head_bias - offset) * (HS**0.5)
        hi = total.astype(BF).astype(F32)
        mid = (total - hi).astype(BF).astype(F32)
        low = total - hi - mid
        in_bias = jnp.where(lane == bias_lane, hi, jnp.where(lane == bias_lane + 1, mid, low))
        in_bias = jnp.where((lane >= bias_lane) & (lane < bias_lane + 3), in_bias, 0.0)
        in_clip = (lane >= clip_lane) & (lane < clip_lane + CLIPS) & (lane - clip_lane != clip)
        side = jnp.where(in_clip, MASKED, in_bias)
        for u in range(TR // TILE):
            rows = slice(u * TILE, (u + 1) * TILE)
            tile = (zq * NX + x) * (TR // TILE) + u
            off = []
            for p in range(NY):
                at = tile + p * (half_rows // TILE)
                mask_row = tile_ref[pl.ds(at, 1), :]
                off.append(jnp.where((mask_row == 0) & (lane != at) & tiles_here, 1.0, 0.0))
            masked = jnp.where(in_high[rows], off[1], off[0]) > 0.5
            qaug[n, rows, HS:] = jnp.where(masked, MASKED, side[rows]).astype(BF)
        return carry

    def keep_query(n, value):
        qaug[n, :, 0:HS] = value
        queries_t[:, n * TR : (n + 1) * TR] = value.T

    def keep_grad(n, value):
        gsel[n] = value
        grads_t[:, n * TR : (n + 1) * TR] = value.T

    def take_rows(t, keep):
        for zq in range(NZ):
            mask = own_is_long(zq, x)
            sides = by_side(mask, qg_ref[t, zq, y], qg_ref[t, zq, 1 - y])
            for g, value in enumerate(sides + (qg_ref[t, zq, 2],)):
                keep(g * NZ + zq, value)

    def take_column(t, d):
        lanes = slice(0, HS)
        ref = (kaug, vals)[t]
        mask = own_is_long(z, (x + d) % NX)
        mine, other = kv_index(2 * d), kv_index(2 * d + 1)
        sides = by_side(mask, kv_ref[t, mine, 0:TR], kv_ref[t, other, 0:TR])
        for g, value in enumerate(sides + (kv_ref[t, other, SHARED:CHUNK],)):
            ref[g, d * TR : (d + 1) * TR, lanes] = value
        for r in range(2):
            index = kv_index(2 * d + r)
            rows = slice(SIDE + (2 * d + r) * CR, SIDE + (2 * d + r + 1) * CR)
            for g in range(NH):
                low = SHARED_TEXT if g == 2 else TR
                ref[g, rows, lanes] = kv_ref[t, index, low : low + CR]

    def block_rows(n):
        return pl.ds(pl.multiple_of(n * TR, TR), TR)

    def weigh(block, columns):
        scores = dot_nt(qaug[block], kaug[block // NZ, columns, :])
        half = jnp.tanh(scores * (0.5 * factor))
        twice = 1.0 + half
        weights[block_rows(block), columns] = twice.astype(BF)
        slopes[block_rows(block), columns] = (twice * (1.0 - half)).astype(BF)

    def every_block(body):
        def step(zq, carry):
            for g in range(NH):
                body(g * NZ + zq)
            return carry

        lax.fori_loop(0, NZ, step, 0)

    def column(d):
        return slice(d * TR, (d + 1) * TR)

    text_columns = slice(SIDE, SIDE + TEXT)

    def score(d):
        take_column(0, d)
        every_block(lambda block: weigh(block, column(d)))

    def score_text():
        every_block(lambda block: weigh(block, text_columns))

    def mix(block, columns):
        return dot_nn(weights[block_rows(block), columns], vals[block // NZ, columns, :])

    def mix_near():
        def body(block):
            oacc[block] = mix(block, slice(0, 2 * TR)) + mix(block, column(3))

        every_block(body)

    def mix_far(zq):
        totals = []
        for g in range(NH):
            block = g * NZ + zq
            total = oacc[block] + mix(block, column(2)) + mix(block, text_columns)
            totals.append(total * 0.5)
        mine, other = by_side(own_is_long(zq, x), totals[0], totals[1])
        oq_ref[0, zq, y] = mine
        oq_ref[0, zq, 1 - y] = other
        oq_ref[0, zq, 2] = totals[2].astype(BF)

    def slope_step(block, columns, fresh=False):
        rows, g = block_rows(block), block // NZ
        slope = (dot_nt(gsel[block], vals[g, columns, :]) * wide(slopes[rows, columns])).astype(BF)
        slopes[rows, columns] = slope
        share = dot_nn(slope, kaug[g, columns, 0:HS])
        if fresh:
            qacc[block] = share
        else:
            qacc[block] += share

    def slope(d):
        every_block(lambda block: slope_step(block, column(d)))

    def slope_text():
        every_block(lambda block: slope_step(block, text_columns, True))

    def slope_row(d, zq):
        for g in range(NH):
            slope_step(g * NZ + zq, column(d))

    def finish_dq(zq):
        mine, other = by_side(own_is_long(zq, x), qacc[zq] * 0.25, qacc[NZ + zq] * 0.25)
        oq_ref[1, zq, y] = mine
        oq_ref[1, zq, 1 - y] = other
        oq_ref[1, zq, 2] = (qacc[2 * NZ + zq] * 0.25).astype(BF)

    left_of = (queries_t, grads_t)
    scale_of = (0.25, 0.5)

    def key_grads(t, d):
        sides = []
        for g in range(NH):
            rows = slice(g * SIDE, (g + 1) * SIDE)
            total = dot_nn(left_of[t][:, rows], (slopes, weights)[t][rows, column(d)])
            sides.append((total * scale_of[t]).astype(BF).T)
        mine, other = by_side(own_is_long(z, (x + d) % NX), sides[0], sides[1])
        kvg_ref[t, kv_index(2 * d), 0:TR] = mine
        kvg_ref[t, kv_index(2 * d + 1), 0:TR] = other
        kvg_ref[t, kv_index(2 * d + 1), SHARED:CHUNK] = sides[2]

    def key_grads_text(t):
        for low, high, at in ((0, 2 * SIDE, TR), (2 * SIDE, 3 * SIDE, SHARED_TEXT)):
            right = (slopes, weights)[t][low:high, text_columns]
            text_rows = (dot_nn(left_of[t][:, low:high], right) * scale_of[t]).astype(BF).T
            for n in range(NY * NX):
                kvg_ref[t, kv_index(n), at : at + CR] = text_rows[n * CR : (n + 1) * CR]


    def z_far(t):
        rsend(6 * t + 0, oq_ref.at[t, zf, :, first], z_in.at[t, 0], "up")
        rsend(6 * t + 3, oq_ref.at[t, zf, :, second], z_in.at[t, 3], "down")

    def z_near(t):
        rsend(6 * t + 1, oq_ref.at[t, zd, :, first], z_in.at[t, 1], "down")
        rsend(6 * t + 4, oq_ref.at[t, zu, :, second], z_in.at[t, 4], "up")

    def z_relay(t):
        base = 6 * t
        rarrived(base + 0, z_in.at[t, 0])
        z_sum[t, 0] = (wide(z_in[t, 0]) + wide(oq_ref[t, zu, :, first])).astype(BF)
        rsend(base + 2, z_sum.at[t, 0], z_in.at[t, 2], "up")
        rarrived(base + 3, z_in.at[t, 3])
        z_sum[t, 1] = (wide(z_in[t, 3]) + wide(oq_ref[t, zd, :, second])).astype(BF)
        rsend(base + 5, z_sum.at[t, 1], z_in.at[t, 5], "down")

    def z_total(t, scale):
        base = 6 * t
        for n in (1, 2, 4, 5):
            rarrived(base + n, z_in.at[t, n])
        for rows, one, two in ((first, 1, 2), (second, 4, 5)):

            def total(j):
                value = wide(oq_ref[t, z, j, rows]) + wide(z_in[t, one, j]) + wide(z_in[t, two, j])
                return (value * scale).astype(BF) if scale != 1.0 else value.astype(BF)

            yq_out[t, 0, rows] = total(1 - y)
            yq_out[t, 1, rows] = total(2)
            keep_q[t, rows] = total(y)
        rsend(24 + t, yq_out.at[t], yq_in.at[t], "pair")

    def x_base(t, a):
        return 12 + 6 * t + 3 * a

    ring = (("right", "left"), ("left", "right"))
    ahead = ((xr, xl), (xl, xr))
    plane = (y, 1 - y)

    def sums_of(a):
        return pl.ds(0, (SHARED, CHUNK)[a])

    def x_far(t):
        for a in (1, 0):
            src = kvg_ref.at[t, plane[a] * NX + xf, sums_of(a)]
            rsend(x_base(t, a), src, x_in.at[t, a, 0, sums_of(a)], ring[a][0])

    def x_near(t):
        for a in (1, 0):
            src = kvg_ref.at[t, plane[a] * NX + ahead[a][1], sums_of(a)]
            rsend(x_base(t, a) + 1, src, x_in.at[t, a, 1, sums_of(a)], ring[a][1])

    def x_relay(t):
        for a in (1, 0):
            rows = sums_of(a)
            rarrived(x_base(t, a), x_in.at[t, a, 0, rows])
            mine = wide(kvg_ref[t, plane[a] * NX + ahead[a][0], rows])
            x_sum[t, a, rows] = (wide(x_in[t, a, 0, rows]) + mine).astype(BF)
            rsend(x_base(t, a) + 2, x_sum.at[t, a, rows], x_in.at[t, a, 2, rows], ring[a][0])

    def to_pair(t):
        yk_out[t] = x_total(t, 1).astype(BF)
        rsend(26 + t, yk_out.at[t], yk_in.at[t], "pair")

    def x_total(t, a):
        rows = sums_of(a)
        rarrived(x_base(t, a) + 1, x_in.at[t, a, 1, rows])
        rarrived(x_base(t, a) + 2, x_in.at[t, a, 2, rows])
        value = wide(kvg_ref[t, plane[a] * NX + x, rows])
        value = value + wide(x_in[t, a, 1, rows]) + wide(x_in[t, a, 2, rows])
        return value * factor if t == 0 else value

    def take_attn(t, ref):
        rarrived(24 + t, yq_in.at[t])
        ref[:, cols(0)] = by_y(keep_q[t], yq_in[t, 0])
        ref[:, cols(1)] = by_y(yq_in[t, 0], keep_q[t])
        mask = chunk_rows(z, x) >= long_start
        ref[:, cols(2)] = by_side(mask, yq_out[t, 1], yq_in[t, 1])[0]

    def project(n):
        return dot_nn(attn[...], feature(n)).astype(BF)

    send(1, go_hbm.at[second], go_relay.at[1], "back")
    load[4].wait()
    pair_out[0, 0] = by_y(q_ref[:, cols(1)], q_ref[:, cols(0)])
    pair_out[0, 1] = q_ref[:, cols(2)]
    send(6, pair_out.at[0], pair_in.at[0], "pair")
    qg_ref[0, z, y] = by_y(q_ref[:, cols(0)], q_ref[:, cols(1)])
    z_own(0)
    c = y * NX + x
    pair_y = 1 - y
    for t, (ref, text) in enumerate(((k_ref, tk_ref), (v_ref, tv_ref))):
        load[2 * t].wait()
        load[2 * t + 1].wait()
        st_pair[t, 0:TR] = by_y(ref[:, cols(1)], ref[:, cols(0)])
        st_pair[t, TR:BR] = by_y(text[:, cols(1)], text[:, cols(0)])
        st_pair[t, SHARED_TEXT:SHARED] = text[:, cols(2)]
        st_pair[t, SHARED:CHUNK] = ref[:, cols(2)]
        if t == 0:
            send(7, st_pair.at[0], kv_ref.at[0, c], "pair")
        kv_ref[t, c, 0:TR] = by_y(ref[:, cols(0)], ref[:, cols(1)])
        kv_ref[t, c, TR:BR] = by_y(text[:, cols(0)], text[:, cols(1)])
        kv_ref[t, c, SHARED_TEXT:SHARED] = text[:, cols(2)]
        x_send(0, t, y)
    send(2, go_hbm, goall.at[head], "core")
    load[7].wait()
    load[8].wait()
    key_side()
    pair_rows(0, q_ref[:, cols(2)])
    z_pair(0)
    send(0, go_hbm.at[first], go_relay.at[0], "pair")
    lax.fori_loop(0, BLOCKS, query_side, 0)
    z_own_forward(0)
    pair_keys(0, k_ref)
    load[5].wait()
    load[6].wait()
    acc[...] = dot_nt(go_ref[...], feature(head))
    x_forward(0, 0, y)
    x_forward(0, 1, y)
    z_pair_forward(0)
    z_own_finish(0)
    z_pair_finish(0)
    take_rows(0, keep_query)
    arrived(0, go_relay.at[0])
    send(3, go_relay.at[0], goall.at[head, first], "back")
    arrived(1, go_relay.at[1])
    send(4, go_relay.at[1], goall.at[other_head, second], "pair")
    send(8, st_pair.at[1], kv_ref.at[1, c], "pair")
    x_forward(1, 0, pair_y)
    score(0)
    arrived(2, goall.at[core_head])
    acc[...] += dot_nt(goall[core_head], feature(core_head))
    x_near_finish(0, 0, y)
    x_near_finish(1, 0, pair_y)
    score(1)
    score(3)
    arrived(3, goall.at[other_head, first])
    arrived(4, goall.at[other_head, second])
    send(5, goall.at[other_head], goall.at[other_head], "core")
    acc[...] += dot_nt(goall[other_head], feature(other_head))
    pair_keys(1, v_ref)
    arrived(5, goall.at[core_other])
    grad = (acc[...] + dot_nt(goall[core_other], feature(core_other))).astype(BF)
    pair_out[1, 0] = by_y(grad[:, cols(1)], grad[:, cols(0)])
    pair_out[1, 1] = grad[:, cols(2)]
    send(9, pair_out.at[1], pair_in.at[1], "pair")
    qg_ref[1, z, y] = by_y(grad[:, cols(0)], grad[:, cols(1)])
    z_own(1)
    x_far_finish(0, 0, y)
    x_far_finish(1, 0, pair_y)
    score(2)
    x_forward(1, 1, pair_y)
    pair_rows(1, pair_out[1, 1])
    z_pair(1)
    z_own_forward(1)
    score_text()
    x_near_finish(0, 1, y)
    x_far_finish(0, 1, y)
    take_column(1, 0)
    x_near_finish(1, 1, pair_y)
    take_column(1, 1)
    take_column(1, 3)
    mix_near()
    z_pair_forward(1)
    x_far_finish(1, 1, pair_y)
    take_column(1, 2)
    mix_far(zf)
    z_far(0)
    mix_far(zu)
    mix_far(zd)
    z_near(0)
    mix_far(z)

    z_own_finish(1)
    z_pair_finish(1)
    take_rows(1, keep_grad)
    key_grads_text(1)
    key_grads(1, 2)
    x_far(1)
    z_relay(0)
    key_grads(1, 3)
    key_grads(1, 1)
    x_near(1)
    slope_text()
    slope(2)
    x_relay(1)
    z_total(0, 1.0)
    key_grads_text(0)
    key_grads(0, 2)
    x_far(0)
    slope(1)
    take_attn(0, attn)
    part[0] = project(core_other)
    rsend(28, part.at[0], core_in.at[0], "core")
    part[2] = project(other_head)
    key_grads(1, 0)
    to_pair(1)
    slope(3)
    rarrived(28, core_in.at[0])
    pair_sum[...] = (wide(part[2]) + wide(core_in[0])).astype(BF)
    rsend(30, pair_sum.at[first], out_relay.at[0], "pair")
    rsend(31, pair_sum.at[second], out_relay.at[1], "back")
    key_grads(0, 1)
    key_grads(0, 3)
    x_relay(0)
    x_near(0)
    for zq in (zf, zu, zd, z):
        slope_row(0, zq)
        finish_dq(zq)
        if zq is zf:
            z_far(1)
        elif zq is zd:
            z_near(1)
    part[1] = project(core_head)
    rsend(29, part.at[1], core_in.at[1], "core")
    part[3] = project(head)
    rarrived(30, out_relay.at[0])
    rsend(32, out_relay.at[0], far_in.at[first], "back")
    rarrived(31, out_relay.at[1])
    rsend(33, out_relay.at[1], far_in.at[second], "pair")
    z_relay(1)
    key_grads(0, 0)
    to_pair(0)
    z_total(1, factor)

    stores = []

    def store(src, dst):
        copy = pltpu.make_async_copy(src, dst, store_sem.at[len(stores)])
        copy.start()
        stores.append(copy)

    results = ((gk_ref, gtk_ref, gk_hbm, gtk_hbm), (gv_ref, gtv_ref, gv_hbm, gtv_hbm))
    rarrived(29, core_in.at[1])
    rarrived(32, far_in.at[first])
    rarrived(33, far_in.at[second])
    out_ref[...] = (wide(part[3]) + wide(core_in[1]) + wide(far_in[...])).astype(BF)
    store(out_ref, out_hbm)
    for t, (ref, text, to, text_to) in enumerate(results):
        own = x_total(t, 0)
        rarrived(26 + t, yk_in.at[t])
        mine, other = own[0:BR].astype(BF), yk_in[t, 0:BR]
        mask = chunk_rows(z, x) >= long_start
        both = by_side(mask, yk_out[t, SHARED:CHUNK], yk_in[t, SHARED:CHUNK])[0]
        for h, value in ((0, by_y(mine, other)), (1, by_y(other, mine))):
            ref[:, cols(h)] = value[0:TR]
            text[:, cols(h)] = value[TR:BR]
        ref[:, cols(2)] = both
        text[:, cols(2)] = (own[BR:SHARED] + wide(yk_in[t, SHARED_TEXT:SHARED])).astype(BF)
        store(ref, to)
        store(text, text_to)
    take_attn(1, gq_ref)
    store(gq_ref, gq_hbm)
    for copy in sent:
        copy.wait_send()
    for copy in stores:
        copy.wait()


def store_kernel(*refs):
    count = (len(refs) - 2) // 3
    held, result, buffers = refs[:count], refs[count : 2 * count], refs[2 * count : 3 * count]
    load_sem, store_sem = refs[-2:]
    loads = [
        pltpu.make_async_copy(held[n], buffers[n], load_sem.at[n]) for n in range(count)
    ]
    stores = [
        pltpu.make_async_copy(buffers[n], result[n], store_sem.at[n]) for n in range(count)
    ]
    for copy in loads:
        copy.start()
    for load, copy in zip(loads, stores):
        load.wait()
        copy.start()
    for copy in stores:
        copy.wait()


def shards(
    queries,
    keys,
    values,
    text_keys,
    text_values,
    head_bias,
    out_weight,
    grad_out,
    clip_lengths,
    tile_mask,
    caption_order,
):
    smem = pl.BlockSpec(memory_space=pltpu.SMEM)
    hbm = pl.BlockSpec(memory_space=pltpu.HBM)
    dma = pltpu.SemaphoreType.DMA
    qg_shape = (2, NZ, NH, TR, HS)
    kv_shape = (2, NY * NX, CHUNK, HS)
    out_cols = grad_out.shape[1]
    order = caption_order.reshape(CLIPS, CAP)
    token = pltpu.VMEM((TR, NH * HS), BF)
    text = pltpu.VMEM((CR, NH * HS), BF)
    wide_out = pltpu.VMEM((TR, out_cols), BF)
    halves = pltpu.VMEM((2, HALF, out_cols), BF)
    token_shape = jax.ShapeDtypeStruct((TR, NH * HS), BF)
    text_shape = jax.ShapeDtypeStruct((CR, NH * HS), BF)
    result = (
        jax.ShapeDtypeStruct((TR, out_cols), BF),
        token_shape,
        token_shape,
        token_shape,
        text_shape,
        text_shape,
    )
    held = pl.pallas_call(
        fused_kernel,
        out_shape=result,
        in_specs=[hbm] * 9 + [smem] * 2,
        out_specs=(hbm,) * len(result),
        scratch_shapes=[
            token,
            token,
            token,
            text,
            text,
            wide_out,
            pltpu.VMEM(out_weight.shape, BF),
            pltpu.VMEM(tile_mask.shape, jnp.int32),
            pltpu.VMEM(order.shape, jnp.int32),
            wide_out,
            token,
            token,
            token,
            text,
            text,
            pltpu.VMEM(qg_shape, BF),
            pltpu.VMEM(kv_shape, BF),
            pltpu.VMEM((2, CHUNK, HS), BF),
            pltpu.VMEM((2, 2, TR, HS), BF),
            pltpu.VMEM((2, 2, TR, HS), BF),
            pltpu.VMEM((4, TR, out_cols), BF),
            halves,
            pltpu.VMEM((TR, NH * HS), F32),
            pltpu.VMEM((NH, SIDE + TEXT, 2 * HS), BF),
            pltpu.VMEM((NH, SIDE + TEXT, HS), BF),
            pltpu.VMEM((BLOCKS, TR, 2 * HS), BF),
            pltpu.VMEM((BLOCKS, TR, HS), BF),
            pltpu.VMEM((BLOCKS * TR, SIDE + TEXT), BF),
            pltpu.VMEM((BLOCKS * TR, SIDE + TEXT), BF),
            pltpu.VMEM((HS, BLOCKS * TR), BF),
            pltpu.VMEM((HS, BLOCKS * TR), BF),
            pltpu.VMEM((BLOCKS, TR, HS), F32),
            pltpu.VMEM((BLOCKS, TR, HS), F32),
            pltpu.VMEM(qg_shape, BF),
            pltpu.VMEM(kv_shape, BF),
            pltpu.VMEM((2, 6, NH, HALF, HS), BF),
            pltpu.VMEM((2, 2, NH, HALF, HS), BF),
            pltpu.VMEM((2, NY, 3, CHUNK, HS), BF),
            pltpu.VMEM((2, NY, CHUNK, HS), BF),
            pltpu.VMEM((2, 2, TR, HS), BF),
            pltpu.VMEM((2, 2, TR, HS), BF),
            pltpu.VMEM((2, CHUNK, HS), BF),
            pltpu.VMEM((2, CHUNK, HS), BF),
            pltpu.VMEM((2, TR, HS), BF),
            token,
            pltpu.VMEM((4, TR, out_cols), BF),
            pltpu.VMEM((2, TR, out_cols), BF),
            wide_out,
            halves,
            wide_out,
            dma((42,)),
            dma((42,)),
            dma((34,)),
            dma((34,)),
            dma((9,)),
            dma((len(result),)),
        ],
        compiler_params=pltpu.CompilerParams(
            collective_id=0, has_side_effects=True, vmem_limit_bytes=VMEM_LIMIT
        ),
    )(
        queries,
        keys,
        values,
        text_keys,
        text_values,
        grad_out,
        out_weight,
        tile_mask,
        order,
        clip_lengths,
        head_bias,
    )
    return pl.pallas_call(
        store_kernel,
        out_shape=result,
        in_specs=[hbm] * len(result),
        out_specs=(hbm,) * len(result),
        scratch_shapes=[pltpu.VMEM(array.shape, array.dtype) for array in result]
        + [dma((len(result),)), dma((len(result),))],
        compiler_params=pltpu.CompilerParams(vmem_limit_bytes=VMEM_LIMIT),
    )(*held)


def solution(mesh):
    in_specs = (
        P("seq", "head"),
        P("seq", "head"),
        P("seq", "head"),
        P("seq", "head"),
        P("seq", "head"),
        P("head"),
        P("head", None),
        P("seq", "head"),
        P(),
        P(),
        P(),
    )
    out_specs = (P("seq", "head"),) * 6
    return jax.shard_map(shards, mesh=mesh, in_specs=in_specs, out_specs=out_specs, check_vma=False)
```
